32 devices in a mesh: seq: 8 (over z, x), chan: 4 (over y, core).
Axes of the slice: x: 2, y: 2, z: 4, core: 2. Of those that a mesh axis runs over, the one named last changes fastest.
Arguments:
- token_ids: int32 [8, 1024], P(None, 'seq'), may hold values from 0 to 255
- valid_counts: int32 [8], replicated, may hold values from 1 to 1024, as said below
- embed: bfloat16 [256, 512], replicated, may hold values from -4 to 4
- attn_gain: float32 [512], replicated, may hold values from 0.5 to 1.5
- ema_in: float32 [512, 16], P('chan'), may hold values from -1.5 to 1.5
- ema_keep: float32 [512, 16], P('chan'), may hold values from 0 to 1, as said below
- ema_out: float32 [512, 16], P('chan'), may hold values from -1.5 to 1.5
- ema_skip: float32 [512], P('chan'), may hold values from -1.5 to 1.5
- z_proj: bfloat16 [512, 128], P('chan'), may hold values from -0.25 to 0.25
- q_gain: float32 [128], replicated, may hold values from -2 to 2
- k_gain: float32 [128], replicated, may hold values from -2 to 2
- q_bias: float32 [128], replicated, may hold values from -1 to 1
- v_proj: bfloat16 [512, 1024], P(None, 'chan'), may hold values from -0.25 to 0.25
- r_proj: bfloat16 [512, 1024], P(None, 'chan'), may hold values from -0.25 to 0.25
- o_proj: bfloat16 [1024, 512], P('chan'), may hold values from -0.75 to 0.75
- ffn_gain: float32 [512], replicated, may hold values from 0.5 to 1.5
- up_proj: bfloat16 [512, 1024], P(None, 'chan'), may hold values from -0.25 to 0.25
- down_proj: bfloat16 [1024, 512], P('chan'), may hold values from -0.1875 to 0.1875
- grad_out: bfloat16 [8, 1024, 512], P(None, 'seq'), may hold values from -6 to 6
Outputs:
- output: bfloat16 [8, 1024, 512], P(None, 'seq')
- embed_grad: float32 [256, 512], replicated
- attn_gain_grad: float32 [512], replicated
- ema_in_grad: float32 [512, 16], P('chan')
- ema_keep_grad: float32 [512, 16], P('chan')
- ema_out_grad: float32 [512, 16], P('chan')
- ema_skip_grad: float32 [512], P('chan')
- z_proj_grad: float32 [512, 128], P('chan')
- q_gain_grad: float32 [128], replicated
- k_gain_grad: float32 [128], replicated
- q_bias_grad: float32 [128], replicated
- v_proj_grad: float32 [512, 1024], P(None, 'chan')
- r_proj_grad: float32 [512, 1024], P(None, 'chan')
- o_proj_grad: float32 [1024, 512], P('chan')
- ffn_gain_grad: float32 [512], replicated
- up_proj_grad: float32 [512, 1024], P(None, 'chan')
- down_proj_grad: float32 [1024, 512], P('chan')
The draws below stay inside these ranges and needn't reach their ends.
Inputs may be any that keep to these rules, and one draw needn't show every extreme that they name: `valid_counts`: each sequence has a count from 1 to 1024; in every draw some sequence, chosen by the seed, has all 1024 positions valid. `ema_keep`: decay factors lie strictly between 0 and 1.
All inputs are finite; a program needn't handle non-finite values.
Results may differ from the reference program's by a relative error of at most 0.02.
The reference program's roundings to bfloat16 on the way count: a program that leaves them out, or rounds other values in their place, can miss the bound.
Values may be sent and summed in bfloat16 or wider, within the bound.
No kernel may reach another device: no remote copies, remote signals or barrier semaphores. Data moves between devices by JAX's collectives and lax.ppermute only.
A program may use at most 192 MiB of HBM per device.

```python
import math
import jax
import jax.numpy as jnp
import numpy as np
from jax import lax

D = 512
NDIM = 16
Z = 128
V = 1024
FF = 1024
VOCAB = 256
GROUP = 128
ROWS = 8
LEN = 1024
SPAN = 1024
PIECES = 1


def draw_valid_counts(key, part):
    key = jax.random.fold_in(key, 5)
    count_key, row_key = jax.random.split(key)
    total = ROWS * PIECES
    counts = jax.random.randint(count_key, (total,), 1, SPAN + 1)
    full_row = jax.random.randint(row_key, (), 0, total)
    return jnp.where(jnp.arange(total) == full_row, SPAN, counts).astype(jnp.int32)


def draw_ema_keep(key, part):
    key = jax.random.fold_in(key, 11)
    pick_key, slow_key, fast_key = jax.random.split(key, 3)
    share = 0.5
    slow = jax.random.uniform(pick_key, (D, NDIM), jnp.float32) < share
    slow_rate = jnp.exp(jax.random.uniform(slow_key, (D, NDIM), jnp.float32, jnp.log(0.3 / SPAN), jnp.log(2.0 / SPAN)))
    fast_rate = jnp.exp(jax.random.uniform(fast_key, (D, NDIM), jnp.float32, jnp.log(1.0 / 50.0), jnp.log(1.0 / 20.0)))
    return jnp.exp(-jnp.where(slow, slow_rate, fast_rate)).astype(jnp.float32)


def plant(entries, key, least, top_value):
    spot = [jax.random.randint(jax.random.fold_in(key, axis), (), 0, length) for axis, length in enumerate(entries.shape)]
    main_axis = entries.shape.index(max(entries.shape))
    next_to = spot[:main_axis] + [(spot[main_axis] + 1) % entries.shape[main_axis]] + spot[main_axis + 1:]
    return entries.at[tuple(spot)].set(least).at[tuple(next_to)].set(top_value)


def shard_levels(stream_key, shape, cuts, low, top_value):
    factor_of = 1.0
    for axis_at, blocks in cuts:
        draws = jax.random.uniform(jax.random.fold_in(jax.random.fold_in(stream_key, 6), axis_at), (blocks,), jnp.float32, low / len(cuts), top_value / len(cuts))
        factor_of = factor_of * jnp.repeat(jnp.exp(draws), shape[axis_at] // blocks).reshape((-1,) + (1,) * (len(shape) - 1 - axis_at))
    return factor_of


def cumulative_ranks(amount, skew):
    portions = [(1 << 20) // math.isqrt(standing ** skew) + 1 for standing in range(1, amount + 1)]
    scale = 1 + sum(portions) // (1 << 30)
    return np.cumsum(np.array([max(1, weight // scale) for weight in portions]))


def skewed_ids(stream_key, shape, count, slope):
    table = cumulative_ranks(count, slope)
    lot = jax.random.randint(jax.random.fold_in(stream_key, 1), shape, 0, int(table[count - 1]))
    rank = jnp.searchsorted(jnp.asarray(table, jnp.int32), lot, side="right")
    return jax.random.permutation(jax.random.fold_in(stream_key, 2), count)[rank].astype(jnp.int32)


def bell_draw(own_key, extent, spread, most, cuts=(), kind=jnp.bfloat16):
    loudness = shard_levels(own_key, extent, cuts, -0.22, 0.18) if cuts else 1.0
    values = jax.random.normal(own_key, extent, jnp.float32) * spread * loudness
    return jnp.minimum(jnp.maximum(values, -most), most).astype(kind)


def setup_inputs(seed: int = 0) -> dict:
    key_list = jax.random.split(jax.random.key(seed), 20)
    return {
        "token_ids": plant(skewed_ids(key_list[0], (ROWS, LEN), VOCAB, 2), jax.random.fold_in(key_list[0], 3), 0, VOCAB - 1).astype(jnp.int32),
        "valid_counts": draw_valid_counts(jax.random.fold_in(key_list[19], 71), 0),
        "embed": bell_draw(key_list[2], (VOCAB, D), 1.0, 4.0),
        "attn_gain": jnp.clip(1.0 + 0.1 * jax.random.normal(key_list[3], (D,), jnp.float32), 0.5, 1.5),
        "ema_in": jnp.clip(jax.random.uniform(key_list[4], (D, NDIM), jnp.float32, -1.5, 1.5) * shard_levels(key_list[4], (D, NDIM), ((0, 4),), -0.4, 0.0), -1.5, 1.5),
        "ema_keep": draw_ema_keep(jax.random.fold_in(key_list[19], 71), 0),
        "ema_out": bell_draw(key_list[6], (D, NDIM), NDIM ** -0.5, 1.5, ((0, 4),), jnp.float32),
        "ema_skip": jnp.clip(jax.random.uniform(key_list[7], (D,), jnp.float32, -1.5, 1.5) * shard_levels(key_list[7], (D,), ((0, 4),), -0.4, 0.0), -1.5, 1.5),
        "z_proj": bell_draw(key_list[8], (D, Z), D ** -0.5, 0.25, ((0, 4),)),
        "q_gain": jnp.clip(jax.random.uniform(key_list[9], (Z,), jnp.float32, -2.0, 2.0), -2.0, 2.0),
        "k_gain": jnp.clip(jax.random.uniform(key_list[10], (Z,), jnp.float32, -2.0, 2.0), -2.0, 2.0),
        "q_bias": jnp.clip(jax.random.uniform(key_list[11], (Z,), jnp.float32, -1.0, 1.0), -1.0, 1.0),
        "v_proj": bell_draw(key_list[12], (D, V), D ** -0.5, 0.25, ((1, 4),)),
        "r_proj": bell_draw(key_list[13], (D, V), D ** -0.5, 0.25, ((1, 4),)),
        "o_proj": bell_draw(key_list[14], (V, D), (V // 16) ** -0.5, 0.75, ((0, 4),)),
        "ffn_gain": jnp.clip(1.0 + 0.1 * jax.random.normal(key_list[15], (D,), jnp.float32), 0.5, 1.5),
        "up_proj": bell_draw(key_list[16], (D, FF), D ** -0.5, 0.25, ((1, 4),)),
        "down_proj": bell_draw(key_list[17], (FF, D), FF ** -0.5, 0.1875, ((0, 4),)),
        "grad_out": bell_draw(key_list[18], (ROWS, LEN, D), 1.0, 6.0, ((1, 8),)),
    }


HIGH = lax.Precision.HIGHEST
EPS = 1e-06

@jax.custom_vjp
def low(v):
    return lax.optimization_barrier(v.astype(jnp.bfloat16)).astype(jnp.float32)

@jax.custom_vjp
def low_back(v):
    return v

def low_keep(v):
    return (low(v), None)

def low_pass(kept, grad):
    return (grad,)

def back_keep(v):
    return (v, None)

def back_low(kept, grad):
    return (low(grad),)
low.defvjp(low_keep, low_pass)
low_back.defvjp(back_keep, back_low)

def scaled_norm(values, gain):
    return values * lax.rsqrt(lax.optimization_barrier(jnp.mean(values * values, axis=-1, keepdims=True)) + EPS) * gain

def ema_local(rows_in, state_in, ema_in, ema_keep, ema_out):
    width = rows_in.shape[1]
    lags = jnp.arange(width, dtype=jnp.float32)
    log_keep = jnp.log(ema_keep)
    powers = jnp.exp(log_keep[:, :, None] * lags[None, None, :])
    drive = ema_in * jnp.sqrt(1.0 - ema_keep * ema_keep)
    kernel = lax.optimization_barrier(jnp.sum((ema_out * drive)[:, :, None] * powers, axis=1))
    offsets = jnp.arange(width, dtype=jnp.int32)[:, None] - jnp.arange(width, dtype=jnp.int32)[None, :]
    toeplitz = jnp.where(offsets[None] >= 0, kernel[:, jnp.maximum(offsets, 0)], 0.0)
    local = jnp.einsum('cts,rsc->rtc', toeplitz, rows_in, precision=HIGH)
    carried = jnp.einsum('ckt,rck->rtc', (ema_out * ema_keep)[:, :, None] * powers, state_in, precision=HIGH)
    tail = drive[:, :, None] * powers[:, :, ::-1]
    state_end = jnp.einsum('cks,rsc->rck', tail, rows_in, precision=HIGH)
    whole = jnp.exp(log_keep * width)
    return (local + carried, whole[None] * state_in + state_end)

def forward(embed, attn_gain, ema_in, ema_keep, ema_out, ema_skip, z_proj, q_gain, k_gain, q_bias, v_proj, r_proj, o_proj, ffn_gain, up_proj, down_proj, token_ids, valid_counts):
    rows, length = token_ids.shape
    dim = embed.shape[1]
    blocks = length // GROUP
    inputs = jnp.take(embed, token_ids, axis=0)
    normed = scaled_norm(inputs, attn_gain)
    normed_low = low(normed)
    pieces = normed.reshape(rows, blocks, GROUP, dim).transpose(1, 0, 2, 3)

    def advance(state, piece):
        smooth_piece, state_next = ema_local(piece, state, ema_in, ema_keep, ema_out)
        return (state_next, smooth_piece)
    start = jnp.zeros((rows, dim, ema_in.shape[1]), jnp.float32)
    _, smooth = lax.scan(jax.checkpoint(advance), start, pieces)
    smooth = smooth.transpose(1, 0, 2, 3).reshape(rows, length, dim)
    mixed_pre = smooth + ema_skip * normed
    mixed_low = low(jax.nn.silu(mixed_pre))
    z_pre = jnp.einsum('rtd,dz->rtz', mixed_low, z_proj, precision=HIGH)
    zeta = jax.nn.silu(z_pre)
    queries = low(zeta * q_gain + q_bias).reshape(rows, blocks, GROUP, -1)
    keys = low(zeta * k_gain).reshape(rows, blocks, GROUP, -1)
    scores = jnp.einsum('rbtz,rbsz->rbts', queries, keys, precision=HIGH) * Z ** (-0.5)
    positions = jnp.arange(length, dtype=jnp.int32).reshape(blocks, GROUP)
    key_valid = positions[None] < valid_counts[:, None, None]
    starts = jnp.arange(blocks, dtype=jnp.int32) * GROUP
    any_valid = (valid_counts[:, None] > starts[None]).astype(jnp.float32)
    mask = key_valid[:, :, None, :]
    masked = jnp.where(mask, scores, -1e+30)
    top = lax.optimization_barrier(jnp.max(masked, axis=-1, keepdims=True))
    weights = jnp.exp(masked - top) * mask.astype(jnp.float32)
    attn = weights / (lax.optimization_barrier(jnp.sum(weights, axis=-1, keepdims=True)) + (1.0 - any_valid)[:, :, None, None])
    v_pre = low_back(jnp.einsum('rtd,dv->rtv', normed_low, v_proj, precision=HIGH))
    values_low = low(jax.nn.silu(v_pre)).reshape(rows, blocks, GROUP, -1)
    r_pre = low_back(jnp.einsum('rtd,dv->rtv', normed_low, r_proj, precision=HIGH))
    reset = jax.nn.silu(r_pre)
    context = low_back(jnp.einsum('rbts,rbsv->rbtv', low(attn), values_low, precision=HIGH))
    context = context.reshape(rows, length, -1)
    gated_low = low(reset * context)
    branch = low_back(jnp.einsum('rtv,vd->rtd', gated_low, o_proj, precision=HIGH))
    middle = inputs + branch
    ffn_low = low(scaled_norm(middle, ffn_gain))
    up_pre = low_back(jnp.einsum('rtd,df->rtf', ffn_low, up_proj, precision=HIGH))
    hidden_low = low(jax.nn.silu(up_pre))
    return middle + jnp.einsum('rtf,fd->rtd', hidden_low, down_proj, precision=HIGH)

def reference(token_ids, valid_counts, embed, attn_gain, ema_in, ema_keep, ema_out, ema_skip, z_proj, q_gain, k_gain, q_bias, v_proj, r_proj, o_proj, ffn_gain, up_proj, down_proj, grad_out):
    rows, length = token_ids.shape
    sequence_ids = token_ids.reshape(-1, SPAN)

    def layer(*weights):
        return forward(*weights, sequence_ids, valid_counts)
    weights = [item.astype(jnp.float32) for item in (embed, attn_gain, ema_in, ema_keep, ema_out, ema_skip, z_proj, q_gain, k_gain, q_bias, v_proj, r_proj, o_proj, ffn_gain, up_proj, down_proj)]
    output, pull = jax.vjp(layer, *weights)
    grads = pull(grad_out.astype(jnp.float32).reshape(-1, SPAN, grad_out.shape[2]))
    output = output.reshape(rows, length, -1)
    return (output.astype(jnp.bfloat16), grads[0], grads[1], grads[2], grads[3], grads[4], grads[5], grads[6], grads[7], grads[8], grads[9], grads[10], grads[11], grads[12], grads[13], grads[14], grads[15])
```

```python
import functools

import jax
import jax.numpy as jnp
from jax import lax
from jax.experimental import pallas as pl
from jax.experimental.pallas import tpu as pltpu
from jax.sharding import PartitionSpec as P

SEQMAX = 4096
HIGH = lax.Precision.HIGHEST
EPS = 1e-06
F32 = jnp.float32
BF16 = jnp.bfloat16
LANES = 128
SUBS = 8
MIB = 1024 * 1024


def sigmoid(u):
    return 0.5 * jnp.tanh(0.5 * u) + 0.5


def silu_slope(pre):
    sigma = sigmoid(pre)
    return sigma * (1.0 + pre * (1.0 - sigma))


def mm(left, right, dims, precision=None):
    return lax.dot_general(
        left, right, ((dims[0], dims[1]), ((), ())), precision=precision, preferred_element_type=F32
    )


def dot(left, right):
    return mm(left, right, ((1,), (0,)))


def dot_rows(left, right):
    return mm(left, right, ((0,), (0,)))


def dot_cols(left, right):
    return mm(left, right, ((1,), (1,)))


def exact(left, right, dims):
    return mm(left.astype(F32), right.astype(F32), dims, HIGH)


def shape_of(dims, dtype=F32):
    return jax.ShapeDtypeStruct(dims, dtype)


TOKENS = {}


def call(
    kernel, outs, args, name, scratch=(), smem=(), hbm=(), free=(), far=(), out_hbm=(), out_free=(), out_far=(), after=(), limit=16
):

    waits = [TOKENS[key] for key in after]
    hbm, out_hbm = {*hbm, *far}, {*out_hbm, *out_far}
    count, made = len(args), len(outs)

    def run(*refs):
        rest = refs[count + len(waits) :]
        kernel(*refs[:count], *rest[:made], *rest[made + 1 :])

    def spec(at):
        if at >= count or (at in hbm and at not in far):
            return pl.BlockSpec(memory_space=pltpu.HBM)
        return pl.BlockSpec(memory_space=pltpu.SMEM if at in smem else pltpu.VMEM)

    def held(at, value):
        if at < count and (at in smem or at in free):
            return value
        return pltpu.with_memory_space_constraint(value, pltpu.HBM if at in hbm or at >= count else pltpu.VMEM)

    def result(at, out):
        if at in out_free:
            return out
        return (pltpu.HBM if at in out_hbm or at == made else pltpu.VMEM)(out.shape, out.dtype)

    shapes = list(outs) + [shape_of((SUBS, LANES))]
    *results, TOKENS[name] = pl.pallas_call(
        run,
        out_shape=[result(at, out) for at, out in enumerate(shapes)],
        in_specs=[spec(at) for at in range(count + len(waits))],
        out_specs=[
            pl.BlockSpec(memory_space=pltpu.HBM if (at in out_hbm and at not in out_far) or at == made else pltpu.VMEM)
            for at in range(made + 1)
        ],
        scratch_shapes=list(scratch),
        name=name,
        cost_estimate=pl.CostEstimate(flops=1, bytes_accessed=1, transcendentals=0),
        compiler_params=pltpu.CompilerParams(vmem_limit_bytes=limit * MIB),
    )(*[held(at, value) for at, value in enumerate([*args, *waits])])
    return results


def move(copies, sems):
    for copy in run_copies(copies, sems):
        copy.wait()


def run_copies(copies, sems):
    started = [pltpu.make_async_copy(src, dst, sems.at[at]) for at, (src, dst) in enumerate(copies)]
    for copy in started:
        copy.start()
    return started


def pack_params(in_ref, keep_ref, out_ref, skip_ref, p_ref, buf, sems):
    nd, lanes = in_ref.shape
    copies = [(ref, buf.at[at * nd : (at + 1) * nd, :]) for at, ref in enumerate((in_ref, keep_ref, out_ref))]
    copies.append((skip_ref, buf.at[3 * nd : 3 * nd + 1, :]))
    for copy in run_copies(copies, sems):
        copy.wait()
    rest = buf.shape[0] - 3 * nd
    buf[3 * nd :, :] = jnp.broadcast_to(buf[3 * nd : 3 * nd + 1, :], (rest, lanes))
    started = run_copies([(buf, p_ref.at[at]) for at in range(p_ref.shape[0])], sems)
    for copy in started:
        copy.wait()


def pack_first(v_ref, r_ref, z_ref, out_ref, buf, sems):
    dim = v_ref.shape[0]
    zrows = z_ref.shape[0] // 2
    copies = [(v_ref, buf.at[0:dim, :]), (r_ref, buf.at[dim : 2 * dim, :])]
    for half in range(2):
        copies.append(
            (
                z_ref.at[half * zrows : (half + 1) * zrows, :],
                buf.at[2 * dim : 2 * dim + zrows, half * LANES : (half + 1) * LANES],
            )
        )
    move(copies, sems)
    move([(buf, out_ref)], sems)


def pack_second(up_ref, o_ref, down_ref, out_ref, buf, sems):
    dim, units = up_ref.shape
    urows = o_ref.shape[0]
    copies = [(up_ref, buf.at[0:dim, :])]
    for at, ref in enumerate((o_ref, down_ref)):
        for half in range(dim // units):
            start = dim + (dim // units * at + half) * urows
            copies.append((ref.at[:, half * units : (half + 1) * units], buf.at[start : start + urows, :]))
    move(copies, sems)
    move([(buf, out_ref)], sems)


def embed_kernel(nc, ids_at, table_at, gain_at, x_to, xt_ref, low_to, ids_ref, embed_ref, gain_ref, x_ref, low_ref, sems):
    started = run_copies([(ids_at, ids_ref), (table_at, embed_ref), (gain_at, gain_ref)], sems)
    rp = x_ref.shape[0] // ids_ref.shape[1]
    width = ids_ref.shape[1]
    vocab = embed_ref.shape[0]
    chan = lax.axis_index("chan")
    for copy in started:
        copy.wait()
    for row in range(rp):
        ids = ids_ref[pl.ds(chan * rp + row, 1), :]
        onehot = jnp.where(lax.broadcasted_iota(jnp.int32, (vocab, width), 0) == ids, 1.0, 0.0).astype(BF16)
        x = dot_rows(onehot, embed_ref[...])
        x_ref[row * width : (row + 1) * width, :] = x.astype(BF16)
        normed = x * lax.rsqrt(jnp.mean(x * x, axis=-1, keepdims=True) + EPS) * gain_ref[...]
        low_ref[row * width : (row + 1) * width, :] = normed.astype(BF16)
        for chunk in range(nc):
            xt_ref[pl.ds(row * nc + chunk, width, stride=SUBS), :] = normed[
                :, chunk * LANES : (chunk + 1) * LANES
            ]
    move([(x_ref, x_to), (low_ref, low_to)], sems)


def tile(ref, at):
    return ref[at * SUBS : (at + 1) * SUBS, :]


def step_tile(ref, t):
    return ref[pl.ds(pl.multiple_of(t * SUBS, SUBS), SUBS), :]


def scan_end_kernel(nc, nd, p_ref, xt_ref, pt_ref, end_ref, buf, sems):
    width = xt_ref.shape[0] // SUBS
    prows = p_ref.shape[1]
    for sub in range(SUBS):
        pt_ref[pl.ds(sub, prows, stride=SUBS), :] = p_ref[sub % nc]
    keep = [tile(pt_ref, nd + k) for k in range(nd)]

    def step(block, states):
        states = list(states)
        for u in range(8):
            x = step_tile(xt_ref, block * 8 + u)
            states = [q * s + x for q, s in zip(keep, states)]
        return tuple(states)

    zero = jnp.zeros((SUBS, LANES), F32)
    states = lax.fori_loop(0, width // 8, step, (zero,) * nd)
    buf[...] = jnp.concatenate(states, axis=0)
    for copy in run_copies([(buf, end_ref.at[at]) for at in range(end_ref.shape[0])], sems):
        copy.wait()


def project_kernel(
    dim, low_at, h0, h1, h2, h3, vpre_to, rpre_ref, val_ref, z_ref, val_to, low_ref, vpre_ref, buf, sems, out_sems
):
    chan = lax.axis_index("chan")
    units = h0.shape[1]
    zrows = h0.shape[0] - 2 * dim
    started = run_copies([(low_at, low_ref)] + [(ref, buf.at[j]) for j, ref in enumerate((h0, h1, h2, h3))], sems)
    started[0].wait()
    low = low_ref[...]
    leaving = []
    for j in range(4):
        started[1 + j].wait()
        w = buf.at[j]
        cols = slice(j * units, (j + 1) * units)
        v_pre = dot(low, w[0:dim, :])
        vpre_ref[:, cols] = v_pre
        val_ref[:, cols] = (v_pre * sigmoid(v_pre)).astype(BF16)
        leaving += run_copies(
            [(vpre_ref.at[:, cols], vpre_to.at[:, cols]), (val_ref.at[:, cols], val_to.at[:, cols])],
            out_sems.at[2 * j : 2 * j + 2],
        )
        rpre_ref[:, cols] = dot(low, w[dim : 2 * dim, :])
        start = pl.multiple_of(jnp.bitwise_xor(chan, j) * 2 * zrows, 2 * zrows)
        half = w[2 * dim : 2 * dim + zrows, :]
        z_ref[pl.ds(start, 2 * zrows), :] = jnp.concatenate([half[:, :LANES], half[:, LANES:]], axis=0)
    for copy in leaving:
        copy.wait()


def whole_keep(keep, width):
    whole = keep
    power = 1
    while power < width:
        whole = whole * whole
        power *= 2
    return whole


def weights_of(pt_ref, nd):
    amp = pt_ref[0 : nd * SUBS, :]
    keep = pt_ref[nd * SUBS : 2 * nd * SUBS, :]
    out = pt_ref[2 * nd * SUBS : 3 * nd * SUBS, :]
    root = jnp.sqrt(1.0 - keep * keep)
    return amp, keep, out, root


def split_tiles(value, nd):
    return [value[k * SUBS : (k + 1) * SUBS, :] for k in range(nd)]


def tree_sum(values):
    values = list(values)
    while len(values) > 1:
        values = [sum(values[i : i + 2][1:], values[i]) for i in range(0, len(values), 2)]
    return values[0]


def scale_of(x):
    return lax.rsqrt(jnp.mean(x * x, axis=-1, keepdims=True) + EPS)


def mix_kernel(
    nc, nd, span, counts_ref, ends_ref, xt_ref, pt_ref, z_ref, val_ref, rpre_ref, qg_ref, kg_ref, qb_ref,
    mpre_ref, mlow_to, zpre_ref, attn_ref, ctx_ref, gated_ref, sin_to, sm_ref, sin_ref, mlow_ref, sems,
):
    width = xt_ref.shape[0] // SUBS
    rp = SUBS // nc
    place = lax.axis_index("seq")
    chan = lax.axis_index("chan")
    amp, keep_all, out_all, root = weights_of(pt_ref, nd)
    whole = whole_keep(keep_all, width)
    per = span // width
    first = place // per * per

    def gather(n, state):
        return state * whole + ends_ref[n].astype(F32)

    start = lax.fori_loop(first, place, gather, jnp.zeros_like(whole))
    sin_ref[...] = start
    (leaving,) = run_copies([(sin_ref, sin_to)], sems.at[:1])
    keep = split_tiles(keep_all, nd)
    weight = split_tiles(out_all * amp * root, nd)

    def step(block, states):
        states = list(states)
        for u in range(8):
            t = block * 8 + u
            x = step_tile(xt_ref, t)
            states = [q * s + x for q, s in zip(keep, states)]
            sm_ref[pl.ds(pl.multiple_of(t * SUBS, SUBS), SUBS), :] = tree_sum(
                [w * s for w, s in zip(weight, states)]
            )
        return tuple(states)

    lax.fori_loop(0, width // 8, step, tuple(split_tiles(start, nd)))
    skip = pt_ref[3 * nd * SUBS : 3 * nd * SUBS + SUBS, :]
    for row in range(rp):
        rows = slice(row * width, (row + 1) * width)
        for chunk in range(nc):
            at = row * nc + chunk
            lanes = slice(chunk * LANES, (chunk + 1) * LANES)
            own = xt_ref[pl.ds(at, width, stride=SUBS), :]
            pre = sm_ref[pl.ds(at, width, stride=SUBS), :] + skip[at : at + 1, :] * own
            mpre_ref[rows, lanes] = pre
            mlow_ref[rows, lanes] = (pre * sigmoid(pre)).astype(BF16)
    (left,) = run_copies([(mlow_ref, mlow_to)], sems.at[1:])
    z_pre = dot(mlow_ref[...], z_ref[...])
    zpre_ref[...] = z_pre
    zeta = z_pre * sigmoid(z_pre)
    queries = (zeta * qg_ref[...] + qb_ref[...]).astype(BF16)
    keys = (zeta * kg_ref[...]).astype(BF16)
    scale = z_pre.shape[1] ** (-0.5)
    pieces = counts_ref.shape[0] // (rp * nc)
    begin = place * width
    piece = begin // span
    inner = begin - piece * span
    for row in range(rp):
        rows = slice(row * width, (row + 1) * width)
        count = counts_ref[(chan * rp + row) * pieces + piece]
        valid = lax.broadcasted_iota(jnp.int32, (width, width), 1) < count - inner
        scores = jnp.where(valid, dot_cols(queries[rows, :], keys[rows, :]) * scale, -1e30)
        top = jnp.max(scores, axis=-1, keepdims=True)
        weights = jnp.where(valid, jnp.exp(scores - top), 0.0)
        empty = jnp.where(count > inner, 0.0, 1.0)
        attn = weights / (jnp.sum(weights, axis=-1, keepdims=True) + empty)
        attn_ref[rows, :] = attn
        context = dot(attn.astype(BF16), val_ref[rows, :])
        ctx_ref[rows, :] = context
        r_pre = rpre_ref[rows, :]
        gated_ref[rows, :] = (r_pre * sigmoid(r_pre) * context).astype(BF16)
    leaving.wait()
    left.wait()


def ffn_kernel(
    nc, dim, gated_ref, h0, h1, h2, h3, x_at, grad_ref, fgain_ref,
    out_to, gmid_to, ggated_ref, keep_to, send_to, fg_ref, hid_ref, gup_ref, g_ref, out_ref, gmid_ref, x_ref, buf,
    part_ref, sems, part_sems,
):
    units = h0.shape[1]
    rp = grad_ref.shape[0] // nc
    width = grad_ref.shape[1]
    chan = lax.axis_index("chan")
    urows = (h0.shape[0] - dim) // 4
    split = (slice(dim, dim + 2 * urows), slice(0, dim), slice(dim + 2 * urows, dim + 4 * urows))
    hs = (h0, h1, h2, h3)
    copies = [(x_at, x_ref)]
    copies += [(hs[j].at[split[0], :], buf.at[j, split[0], :]) for j in range(4)]
    copies += [(grad_ref.at[chan * rp + row], g_ref.at[row * width : (row + 1) * width, :]) for row in range(rp)]
    copies += [(hs[j].at[part, :], buf.at[j, part, :]) for j in range(4) for part in split[1:]]
    started = run_copies(copies, sems)
    started[0].wait()
    ws = [buf.at[j] for j in range(4)]
    halves = dim // units

    def shard(j, which):
        start = dim + which * halves * urows
        return [ws[j][start + half * urows : start + (half + 1) * urows, :] for half in range(halves)]

    def cols(j):
        return slice(j * units, (j + 1) * units)

    branch = [None] * halves
    for j in range(4):
        started[1 + j].wait()
        for half, part in enumerate(shard(j, 0)):
            term = dot(gated_ref[:, cols(j)], part)
            branch[half] = term if j == 0 else branch[half] + term
    middle = x_ref[...].astype(F32) + jnp.concatenate(branch, axis=1)
    r = scale_of(middle)
    n = middle * r
    fgain = fgain_ref[...]
    for copy in started[5 : 5 + rp]:
        copy.wait()
    g = g_ref[...]
    ffn_low = (n * fgain).astype(BF16)
    ffn_out = [None] * halves
    g_in = None
    for j in range(4):
        for copy in started[5 + rp + 2 * j : 7 + rp + 2 * j]:
            copy.wait()
        up = ws[j][0:dim, :]
        up_pre = dot(ffn_low, up)
        sigma = sigmoid(up_pre)
        hidden = (up_pre * sigma).astype(BF16)
        hid_ref[:, cols(j)] = hidden
        down = shard(j, 1)
        back = None
        for half, part in enumerate(down):
            term = dot(hidden, part)
            ffn_out[half] = term if j == 0 else ffn_out[half] + term
            term = dot_cols(g[:, half * units : (half + 1) * units], part)
            back = term if half == 0 else back + term
        g_up = (back * (sigma * (1.0 + up_pre * (1.0 - sigma)))).astype(BF16)
        gup_ref[:, cols(j)] = g_up
        term = dot_cols(g_up, up)
        g_in = term if j == 0 else g_in + term
    toks = g_ref.shape[0]
    for half in range(halves):
        out_ref[half * toks : (half + 1) * toks, :] = (middle[:, half * units : (half + 1) * units] + ffn_out[half]).astype(
            BF16
        )
    fg_ref[...] = jnp.sum(g_in * n, axis=0, keepdims=True)
    h = g_in * fgain
    g_mid = g.astype(F32) + r * (h - n * jnp.mean(h * n, axis=-1, keepdims=True))
    gmid_ref[...] = g_mid
    leaving = run_copies([(out_ref, out_to), (gmid_ref, gmid_to)], sems)
    g_branch = g_mid.astype(BF16)
    for j in range(4):
        total = None
        for half, part in enumerate(shard(j, 0)):
            term = dot_cols(g_branch[:, half * units : (half + 1) * units], part)
            total = term if half == 0 else total + term
        ggated_ref[:, cols(j)] = total
    for j in (1, 3, 0, 2):
        part_ref[j, 0:dim, :] = dot_rows(ffn_low, gup_ref[:, cols(j)]).astype(BF16)
        for which, (left, right) in enumerate(((gated_ref, g_branch), (hid_ref, g))):
            grad = dot_rows(left[:, cols(j)], right).astype(BF16)
            for half in range(halves):
                start = dim + (which * halves + half) * urows
                part_ref[j, start : start + urows, :] = grad[:, half * units : (half + 1) * units]
        leaving += run_copies([(part_ref.at[j], (keep_to, send_to)[j % 2].at[j // 2])], part_sems.at[j : j + 1])
    for copy in leaving:
        copy.wait()


def attn_back_kernel(
    nc, nd, ggated_ref, rpre_ref, vpre_ref, ctx_ref, attn_ref, val_ref, zpre_ref, mpre_ref, xt_ref, z_ref, pt_ref,
    qg_ref, kg_ref, qb_ref,
    gv_to, gr_to, gz_ref, gmt_ref, carry_ref, small_ref, skip_ref, buf, gv_ref, gr_ref, sems, out_sems,
):
    width = xt_ref.shape[0] // SUBS
    rp = SUBS // nc
    z_pre = zpre_ref[...]
    sigma = sigmoid(z_pre)
    zeta = z_pre * sigma
    queries = (zeta * qg_ref[...] + qb_ref[...]).astype(BF16)
    keys = (zeta * kg_ref[...]).astype(BF16)
    scale = z_pre.shape[1] ** (-0.5)
    parts_q, parts_k = [], []
    for row in range(rp):
        rows = slice(row * width, (row + 1) * width)
        g_gated = ggated_ref[rows, :]
        r_pre = rpre_ref[rows, :]
        sr = sigmoid(r_pre)
        g_context = (g_gated * (r_pre * sr)).astype(BF16)
        gr_ref[rows, :] = (g_gated * ctx_ref[rows, :] * (sr * (1.0 + r_pre * (1.0 - sr)))).astype(BF16)
        attn = attn_ref[rows, :]
        g_values = dot_rows(attn.astype(BF16), g_context)
        gv_ref[rows, :] = (g_values * silu_slope(vpre_ref[rows, :])).astype(BF16)
        g_attn = dot_cols(g_context, val_ref[rows, :])
        g_scores = attn * (g_attn - jnp.sum(attn * g_attn, axis=-1, keepdims=True))
        parts_q.append(exact(g_scores, keys[rows, :], ((1,), (0,))) * scale)
        parts_k.append(exact(g_scores, queries[rows, :], ((0,), (0,))) * scale)
    leaving = run_copies([(gv_ref, gv_to), (gr_ref, gr_to)], out_sems)
    g_q = jnp.concatenate(parts_q, axis=0)
    g_k = jnp.concatenate(parts_k, axis=0)
    small_ref[...] = jnp.concatenate(
        [
            jnp.sum(g_q * zeta, axis=0, keepdims=True),
            jnp.sum(g_k * zeta, axis=0, keepdims=True),
            jnp.sum(g_q, axis=0, keepdims=True),
            jnp.zeros((SUBS - 3, z_pre.shape[1]), F32),
        ],
        axis=0,
    )
    g_z = (g_q * qg_ref[...] + g_k * kg_ref[...]) * (sigma * (1.0 + z_pre * (1.0 - sigma)))
    gz_ref[...] = g_z
    skips = []
    for row in range(rp):
        rows = slice(row * width, (row + 1) * width)
        for chunk in range(nc):
            at = row * nc + chunk
            lanes = slice(chunk * LANES, (chunk + 1) * LANES)
            g_mixed = exact(g_z[rows, :], z_ref[lanes, :], ((1,), (1,))) * silu_slope(mpre_ref[rows, lanes])
            gmt_ref[pl.ds(at, width, stride=SUBS), :] = g_mixed
            skips.append(jnp.sum(g_mixed * xt_ref[pl.ds(at, width, stride=SUBS), :], axis=0, keepdims=True))
    skip_ref[...] = jnp.concatenate(skips, axis=0)
    keep = [tile(pt_ref, nd + k) for k in range(nd)]

    def step(block, carries):
        carries = list(carries)
        for u in range(8):
            gm = step_tile(gmt_ref, width - 1 - (block * 8 + u))
            carries = [q * (c + gm) for q, c in zip(keep, carries)]
        return tuple(carries)

    zero = jnp.zeros((SUBS, LANES), F32)
    carries = lax.fori_loop(0, width // 8, step, (zero,) * nd)
    buf[...] = jnp.concatenate(carries, axis=0).astype(BF16)
    for copy in leaving:
        copy.wait()
    for copy in run_copies([(buf, carry_ref.at[at]) for at in range(carry_ref.shape[0])], sems):
        copy.wait()


def grads_kernel(
    nc, dim, zrows, low_at, gv_at, gr_at, mlow_at, gz_ref, keep_to, send1_to, send3_to,
    zg_ref, low_ref, gv_ref, gr_ref, mlow_ref, part_ref, sems, part_sems,
):
    units = gv_ref.shape[1] // nc
    chan = lax.axis_index("chan")
    started = run_copies([(mlow_at, mlow_ref), (low_at, low_ref), (gv_at, gv_ref), (gr_at, gr_ref)], sems)
    started[0].wait()
    zg_ref[...] = exact(mlow_ref[...], gz_ref[...], ((0,), (0,)))
    for copy in started[1:]:
        copy.wait()
    low = low_ref[...]
    used = 2 * dim + zrows
    spare = part_ref.shape[1] - used
    leaving = []
    for j in (1, 3, 0, 2):
        cols = slice(j * units, (j + 1) * units)
        part_ref[j, 0:dim, :] = dot_rows(low, gv_ref[:, cols]).astype(BF16)
        part_ref[j, dim : 2 * dim, :] = dot_rows(low, gr_ref[:, cols]).astype(BF16)
        start = pl.multiple_of(jnp.bitwise_xor(chan, j) * 2 * zrows, 2 * zrows)
        block = zg_ref[pl.ds(start, 2 * zrows), :]
        part_ref[j, 2 * dim : used, :] = jnp.concatenate([block[:zrows, :], block[zrows:, :]], axis=1).astype(BF16)
        part_ref[j, used:, :] = jnp.zeros((spare, units), BF16)
        to = (keep_to.at[0], send1_to, keep_to.at[1], send3_to)[j]
        leaving += run_copies([(part_ref.at[j], to)], part_sems.at[j : j + 1])
    for copy in leaving:
        copy.wait()


def scans_kernel(
    nd, dim, gv_at, gr_at, h0, h1, h2, h3, pt_ref, sin_at, xt_ref, gmt_ref,
    shared_to, acc_to, shared_ref, acc_ref, sin_ref, buf, gv_ref, gr_ref, sems,
):
    units = h0.shape[1]
    width = xt_ref.shape[0] // SUBS
    started = run_copies(
        [(sin_at, sin_ref), (gv_at, gv_ref), (gr_at, gr_ref)]
        + [(ref.at[0 : 2 * dim, :], buf.at[j]) for j, ref in enumerate((h0, h1, h2, h3))],
        sems,
    )
    started[0].wait()
    group = 8
    for begin in range(0, nd, group):
        ks = list(range(begin, begin + group))
        keep = [tile(pt_ref, nd + k) for k in ks]

        def step(block, carry):
            s, d, a, b = [list(part) for part in carry]
            for u in range(4):
                t = block * 4 + u
                x = step_tile(xt_ref, t)
                gm = step_tile(gmt_ref, t)
                d = [q * di + si for q, di, si in zip(keep, d, s)]
                s = [q * si + x for q, si in zip(keep, s)]
                a = [ai + gm * si for ai, si in zip(a, s)]
                b = [bi + gm * di for bi, di in zip(b, d)]
            return tuple(s), tuple(d), tuple(a), tuple(b)

        zero = (jnp.zeros((SUBS, LANES), F32),) * group
        init = tuple(tile(sin_ref, k) for k in ks)
        s, d, a, b = lax.fori_loop(0, width // 4, step, (init, zero, zero, zero))
        rows = slice(begin * SUBS, (begin + group) * SUBS)
        acc_ref[0, rows, :] = jnp.concatenate(a, axis=0)
        acc_ref[1, rows, :] = jnp.concatenate(b, axis=0)
        acc_ref[2, rows, :] = jnp.concatenate(d, axis=0)
    for copy in started[1:3]:
        copy.wait()
    (last,) = run_copies([(acc_ref, acc_to)], sems)
    shared = None
    for j in range(4):
        cols = slice(j * units, (j + 1) * units)
        started[3 + j].wait()
        term = dot_cols(gv_ref[:, cols], buf[j, 0:dim, :]) + dot_cols(gr_ref[:, cols], buf[j, dim:, :])
        shared = term if j == 0 else shared + term
    shared_ref[...] = shared
    move([(shared_ref, shared_to)], sems.at[1:])
    last.wait()


def small_rows(nc, nd):
    return -(-(nc * (3 * nd + 3) + 3) // 16) * 16


def last_kernel(
    nc, nd, ns, span, carry_ref, gmt_ref, pt_ref, shared_at, x_at, gain_at, gmid_at, ids_at, sums_at,
    small_ref, skip_ref, fg_ref,
    to_ref, yt_ref, acc_ref, f_ref, shared_ref, x_ref, gain_ref, gmid_ref, ids_ref, sums_ref, sems,
):
    started = run_copies(
        [
            (shared_at, shared_ref), (x_at, x_ref), (gain_at, gain_ref), (gmid_at, gmid_ref), (ids_at, ids_ref),
            (sums_at, sums_ref),
        ],
        sems,
    )
    width = gmt_ref.shape[0] // SUBS
    rp = SUBS // nc
    vocab = acc_ref.shape[0]
    place = lax.axis_index("seq")
    chan = lax.axis_index("chan")
    amp, keep_all, out_all, root = weights_of(pt_ref, nd)
    whole = whole_keep(keep_all, width)
    per = span // width
    last = place // per * per + per - 1

    def gather(n, state):
        return state * whole + carry_ref[last - n].astype(F32)

    start = lax.fori_loop(0, last - place, gather, jnp.zeros_like(whole))
    drive = amp * root
    weight_all = out_all * drive
    keep = split_tiles(keep_all, nd)
    weight = split_tiles(weight_all, nd)

    def step(block, carries):
        carries = list(carries)
        for u in range(8):
            t = width - 1 - (block * 8 + u)
            gm = step_tile(gmt_ref, t)
            adj = [c + gm for c in carries]
            yt_ref[pl.ds(pl.multiple_of(t * SUBS, SUBS), SUBS), :] = tree_sum(
                [w * s for w, s in zip(weight, adj)]
            )
            carries = [q * s for q, s in zip(keep, adj)]
        return tuple(carries)

    lax.fori_loop(0, width // 8, step, tuple(split_tiles(start, nd)))
    for copy in started:
        copy.wait()
    a = sums_ref[0]
    g_drive = out_all * a
    grad_out = drive * a
    grad_in = g_drive * root
    grad_keep = weight_all * (sums_ref[1] + sums_ref[2] * start) - g_drive * amp * keep_all / root
    base = nc * vocab
    pad = f_ref.shape[0] - base
    rows = []

    def fold(value):
        total = value[0:nc, :]
        for row in range(1, rp):
            total = total + value[row * nc : (row + 1) * nc, :]
        return total

    for grad in (grad_in, grad_keep, grad_out):
        for k in range(nd):
            rows.append(fold(grad[k * SUBS : (k + 1) * SUBS, :]))
    rows.append(fold(skip_ref[...]))
    skip = pt_ref[3 * nd * SUBS : 3 * nd * SUBS + SUBS, :]
    gain = gain_ref[...]
    for row in range(rp):
        toks = slice(row * width, (row + 1) * width)
        pieces = []
        for chunk in range(nc):
            at = row * nc + chunk
            lanes = slice(chunk * LANES, (chunk + 1) * LANES)
            gm = gmt_ref[pl.ds(at, width, stride=SUBS), :]
            pieces.append(
                shared_ref[toks, lanes] + skip[at : at + 1, :] * gm + yt_ref[pl.ds(at, width, stride=SUBS), :]
            )
        g_normed = jnp.concatenate(pieces, axis=1)
        x = x_ref[toks, :].astype(F32)
        r = scale_of(x)
        n = x * r
        h = g_normed * gain
        g_x = gmid_ref[toks, :] + r * (h - n * jnp.mean(h * n, axis=-1, keepdims=True))
        part = jnp.sum(g_normed * n, axis=0, keepdims=True)
        ag = part if row == 0 else ag + part
        ids = ids_ref[pl.ds(chan * rp + row, 1), :]
        onehot = jnp.where(lax.broadcasted_iota(jnp.int32, (vocab, width), 0) == ids, 1.0, 0.0)
        term = exact(onehot, g_x, ((1,), (0,)))
        acc_ref[...] = term if row == 0 else acc_ref[...] + term
    for chunk in range(nc):
        f_ref[chunk * vocab : (chunk + 1) * vocab, :] = acc_ref[:, chunk * LANES : (chunk + 1) * LANES].astype(BF16)
    for chunk in range(nc):
        rows.append(ag[:, chunk * LANES : (chunk + 1) * LANES])
    for chunk in range(nc):
        rows.append(fg_ref[:, chunk * LANES : (chunk + 1) * LANES])
    rows.append(small_ref[0:3, :])
    used = nc * (3 * nd + 3) + 3
    room = small_rows(nc, nd)
    rows.append(jnp.zeros((room - used, LANES), F32))
    value = jnp.concatenate(rows, axis=0)
    high = value.astype(BF16)
    f_ref[base : base + room, :] = high
    f_ref[base + room : base + 2 * room, :] = (value - high.astype(F32)).astype(BF16)
    f_ref[base + 2 * room :, :] = jnp.zeros((pad - 2 * room, LANES), BF16)
    move([(f_ref, to_ref)], sems)


def sum_kernel(in_ref, out_ref, buf, sems):
    total = in_ref[0].astype(F32)
    for at in range(1, in_ref.shape[0]):
        total = total + in_ref[at].astype(F32)
    buf[...] = total.astype(BF16)
    for copy in run_copies([(buf, out_ref.at[at]) for at in range(out_ref.shape[0])], sems):
        copy.wait()


def spread(parts, name, after=()):
    scratch = [pltpu.VMEM(parts.shape[1:], BF16), pltpu.SemaphoreType.DMA((parts.shape[0],))]
    return call(sum_kernel, (shape_of(parts.shape, BF16),), (parts,), name, scratch=scratch, out_hbm=(0,), after=after)[0]


def finish_kernel(nc, nd, f_ref, embed_ref, ag_ref, ei_ref, ek_ref, eo_ref, es_ref, fg_ref, qg_ref, kg_ref, qb_ref, s_ref):
    vocab = embed_ref.shape[0]
    chan = lax.axis_index("chan")
    base = nc * vocab
    room = small_rows(nc, nd)
    for chunk in range(nc):
        lanes = slice(chunk * LANES, (chunk + 1) * LANES)
        embed_ref[:, lanes] = f_ref[chunk * vocab : (chunk + 1) * vocab, :].astype(F32)
    s_ref[...] = f_ref[base : base + room, :].astype(F32) + f_ref[base + room : base + 2 * room, :].astype(F32)
    for at, ref in enumerate((ei_ref, ek_ref, eo_ref)):
        ref[...] = s_ref[pl.ds(at * nd * nc + chan, nd, stride=nc), :]
    start = 3 * nd * nc
    es_ref[...] = s_ref[pl.ds(start + chan, 1), :]
    for at, ref in enumerate((ag_ref, fg_ref)):
        for chunk in range(nc):
            row = start + nc * (1 + at) + chunk
            ref[:, chunk * LANES : (chunk + 1) * LANES] = s_ref[row : row + 1, :]
    start += 3 * nc
    for at, ref in enumerate((qg_ref, kg_ref, qb_ref)):
        ref[...] = s_ref[start + at : start + at + 1, :]


def unpack_first(dim, urows, u_ref, v_ref, up_ref, o_ref, down_ref, s_ref):
    join(u_ref, v_ref, s_ref)
    units = s_ref.shape[1]
    up_ref[...] = s_ref[0:dim, :].astype(F32)
    for at, ref in enumerate((o_ref, down_ref)):
        for half in range(dim // units):
            start = dim + (at * (dim // units) + half) * urows
            ref[:, half * units : (half + 1) * units] = s_ref[start : start + urows, :].astype(F32)


def unpack_second(dim, zrows, u_ref, x_ref, v_ref, r_ref, z_ref, s_ref):
    join(u_ref, x_ref, s_ref)
    v_ref[...] = s_ref[0:dim, :].astype(F32)
    r_ref[...] = s_ref[dim : 2 * dim, :].astype(F32)
    block = s_ref[2 * dim : 2 * dim + zrows, :].astype(F32)
    z_ref[0:zrows, :] = block[:, :LANES]
    z_ref[zrows:, :] = block[:, LANES:]


def join(mine_ref, other_ref, to_ref):
    half = mine_ref.shape[0]
    if half == to_ref.shape[0]:
        to_ref[...] = mine_ref[...]
        return
    bit = jnp.bitwise_and(lax.axis_index("seq"), 1)
    to_ref[pl.ds(pl.multiple_of(bit * half, 16), half), :] = mine_ref[...]
    to_ref[pl.ds(pl.multiple_of((1 - bit) * half, 16), half), :] = other_ref[...]


def plus(left, right):
    return (left.astype(F32) + right.astype(F32)).astype(BF16)


def add_core_first(keep_ref, got_ref, out_ref, mine_ref, theirs_ref):
    rows = keep_ref.shape[1]
    mine_ref[...] = plus(keep_ref[0], got_ref[0])
    theirs_ref[0:rows, :] = plus(keep_ref[1], got_ref[1])
    theirs_ref[rows:, :] = out_ref[...]


def add_core_second(keep_ref, got_ref, other_ref, mine_ref, theirs_ref):
    mine_ref[...] = plus(keep_ref[0], got_ref[...])
    theirs_ref[...] = plus(keep_ref[1], other_ref[...])


def add_far_first(mine_ref, got_ref, keep_ref, send_ref, out_ref):
    add_halves(0, mine_ref, got_ref, keep_ref, send_ref)
    out_ref[...] = got_ref[mine_ref.shape[0] :, :]


def add_plain(mine_ref, got_ref, out_ref):
    out_ref[...] = plus(mine_ref[...], got_ref[...])


def seq_bit(level):
    return jnp.bitwise_and(lax.shift_right_logical(lax.axis_index("seq"), level), 1)


def add_halves(level, mine_ref, got_ref, keep_ref, send_ref):
    half = keep_ref.shape[0]
    bit = seq_bit(level)
    for side, ref in ((bit, keep_ref), (1 - bit, send_ref)):
        rows = pl.ds(pl.multiple_of(side * half, 16), half)
        ref[...] = plus(mine_ref[rows, :], got_ref[rows, :])


def join_halves(level, mine_ref, got_ref, out_ref):
    half = mine_ref.shape[0]
    bit = seq_bit(level)
    for side, ref in ((bit, mine_ref), (1 - bit, got_ref)):
        out_ref[pl.ds(pl.multiple_of(side * half, 16), half), :] = ref[...]


def output_kernel(w0, w1, w2, w3, out_ref):
    rows, width, dim = out_ref.shape
    units = w0.shape[1]
    toks = w0.shape[0] // (dim // units)
    chan = lax.axis_index("chan")
    for j, ref in enumerate((w0, w1, w2, w3)):
        for row in range(toks // width):
            for half in range(dim // units):
                start = half * toks + row * width
                out_ref[jnp.bitwise_xor(chan, j) * (toks // width) + row, :, half * units : (half + 1) * units] = ref[
                    start : start + width, :
                ]


def swap(value, mask, axis="chan"):
    return lax.ppermute(value, axis, [(at, at ^ mask) for at in range(lax.axis_size(axis))])


def exchange(value, axis):
    return lax.all_to_all(value, axis, 0, 0, tiled=True)


def add_pair(kernel, args, rows, name, after):
    shape = shape_of((rows, args[0].shape[-1]), BF16)
    return call(kernel, (shape, shape), args, name, free=range(3), out_free=(0, 1), after=after)


def seq_sum(value, ns, name):
    rows = value.shape[0]
    parts = exchange(value.reshape(ns, rows // ns, value.shape[1]), "seq")
    return exchange(spread(parts, name), "seq").reshape(value.shape)


def body(
    token_ids, valid_counts, embed, attn_gain, ema_in, ema_keep, ema_out, ema_skip, z_proj, q_gain, k_gain, q_bias,
    v_proj, r_proj, o_proj, ffn_gain, up_proj, down_proj, grad_out,
):
    rows, width = token_ids.shape
    vocab, dim = embed.shape
    nd = ema_in.shape[1]
    units = v_proj.shape[1]
    zdim = z_proj.shape[1]
    nc = lax.axis_size("chan")
    ns = lax.axis_size("seq")
    ndev = nc * ns
    rp = rows // nc
    toks = rp * width
    span = min(width * ns, SEQMAX)
    urows = o_proj.shape[0]
    zrows = z_proj.shape[0] // 2
    prows = 3 * nd + SUBS
    w1_rows = 2 * dim + zrows
    w2_rows = 3 * dim
    row = lambda vector: vector.reshape(1, -1)

    dma = pltpu.SemaphoreType.DMA
    (packed_params,) = call(
        pack_params, (shape_of((nc, prows, LANES)),), (ema_in.T, ema_keep.T, ema_out.T, row(ema_skip)), "pack_params",
        scratch=[pltpu.VMEM((prows, LANES), F32), dma((max(nc, 4),))], hbm=range(4), out_hbm=(0,), limit=8,
    )
    params = exchange(packed_params, "chan")
    x, xt, low = call(
        functools.partial(embed_kernel, nc),
        (shape_of((toks, dim), BF16), shape_of((width * SUBS, LANES)), shape_of((toks, dim), BF16)),
        (token_ids, embed, row(attn_gain)), "embed",
        scratch=[
            pltpu.VMEM((rows, width), jnp.int32), pltpu.VMEM((vocab, dim), BF16), pltpu.VMEM((1, dim), F32),
            pltpu.VMEM((toks, dim), BF16), pltpu.VMEM((toks, dim), BF16), dma((3,)),
        ],
        hbm=range(3), out_hbm=(0, 2), after=("pack_params",), limit=8,
    )
    (own1,) = call(
        pack_first, (shape_of((w1_rows, units), BF16),), (v_proj, r_proj, z_proj), "pack_first",
        scratch=[pltpu.VMEM((w1_rows, units), BF16), dma((4,))], hbm=range(3), out_hbm=(0,), after=("embed",), limit=8,
    )
    (own2,) = call(
        pack_second, (shape_of((w2_rows, units), BF16),), (up_proj, o_proj, down_proj), "pack_second",
        scratch=[pltpu.VMEM((w2_rows, units), BF16), dma((5,))], hbm=range(3), out_hbm=(0,), after=("pack_first",), limit=8,
    )
    own1, own2, params = lax.optimization_barrier((own1, own2, params))
    far1 = swap(own1, 2)
    near1 = swap(own1, 1)
    far2 = swap(own2, 2)
    near2 = swap(own2, 1)
    pt, ends = call(
        functools.partial(scan_end_kernel, nc, nd),
        (shape_of((prows * SUBS, LANES)), shape_of((ns, nd * SUBS, LANES))),
        (params, xt), "scan_end", scratch=[pltpu.VMEM((nd * SUBS, LANES), F32), dma((ns,))], out_hbm=(1,), after=("pack_second",), limit=8,
    )
    far1, _ = lax.optimization_barrier((far1, pt))
    both1 = swap(far1, 1)
    first = (own1, near1, far1, both1)
    ends = exchange(ends, "seq")
    v_pre, r_pre, values, z_all, values_far = call(
        functools.partial(project_kernel, dim),
        (
            shape_of((toks, nc * units)), shape_of((toks, nc * units)), shape_of((toks, nc * units), BF16),
            shape_of((dim, zdim), BF16), shape_of((toks, nc * units), BF16),
        ),
        (low,) + first, "project",
        scratch=[
            pltpu.VMEM((toks, dim), BF16), pltpu.VMEM((toks, nc * units), F32), pltpu.VMEM((4, w1_rows, units), BF16),
            dma((5,)), dma((8,)),
        ],
        hbm=range(5), out_hbm=(0, 4), after=("scan_end",), limit=16,
    )
    mixed_pre, mixed_low, z_pre, attn, context, gated, state_in = call(
        functools.partial(mix_kernel, nc, nd, span),
        (
            shape_of((toks, dim)), shape_of((toks, dim), BF16), shape_of((toks, zdim)), shape_of((toks, width)),
            shape_of((toks, nc * units)), shape_of((toks, nc * units), BF16), shape_of((nd * SUBS, LANES)),
        ),
        (
            valid_counts, ends, xt, pt, z_all, values, r_pre, row(q_gain), row(k_gain), row(q_bias),
        ),
        "mix", scratch=[pltpu.VMEM((width * SUBS, LANES), F32), pltpu.VMEM((nd * SUBS, LANES), F32), pltpu.VMEM((toks, dim), BF16), dma((2,))],
        smem=(0,), free=range(7, 10), out_hbm=(1, 6), after=("project",), limit=16,
    )
    far2, gated = lax.optimization_barrier((far2, gated))
    both2 = swap(far2, 1)
    second = (own2, near2, far2, both2)
    out_rows = toks * (dim // units)
    out, g_mid, g_gated, keep1, send1, ffn_grad = call(
        functools.partial(ffn_kernel, nc, dim),
        (
            shape_of((out_rows, units), BF16), shape_of((toks, dim)), shape_of((toks, nc * units)),
            shape_of((2, w2_rows, units), BF16), shape_of((2, w2_rows, units), BF16), shape_of((1, dim)),
        ),
        (gated,) + second + (x, grad_out, row(ffn_gain)),
        "ffn",
        scratch=[
            pltpu.VMEM((toks, nc * units), BF16), pltpu.VMEM((toks, nc * units), BF16),
            pltpu.VMEM((toks, dim), BF16), pltpu.VMEM((out_rows, units), BF16), pltpu.VMEM((toks, dim), F32),
            pltpu.VMEM((toks, dim), BF16), pltpu.VMEM((4, w2_rows, units), BF16), pltpu.VMEM((4, w2_rows, units), BF16),
            dma((13 + rp,)), dma((4,)),
        ],
        hbm=range(1, 7), free=(7,), out_hbm=(0, 1, 3, 4), after=("mix",), limit=32,
    )
    got1 = swap(send1, 1)
    grad_v, grad_r, g_z, gmt, carries, small, skip_grad = call(
        functools.partial(attn_back_kernel, nc, nd),
        (
            shape_of((toks, nc * units), BF16), shape_of((toks, nc * units), BF16), shape_of((toks, zdim)),
            shape_of((width * SUBS, LANES)), shape_of((ns, nd * SUBS, LANES), BF16), shape_of((SUBS, zdim)),
            shape_of((SUBS, LANES)),
        ),
        (
            g_gated, r_pre, v_pre, context, attn, values_far, z_pre, mixed_pre, xt, z_all, pt, row(q_gain), row(k_gain),
            row(q_bias),
        ),
        "attn_back",
        scratch=[
            pltpu.VMEM((nd * SUBS, LANES), BF16), pltpu.VMEM((toks, nc * units), BF16), pltpu.VMEM((toks, nc * units), BF16),
            dma((ns,)), dma((2,)),
        ],
        free=(2, 5, 11, 12, 13), out_hbm=(0, 1, 4), after=("ffn",), limit=20,
    )
    carries = exchange(carries, "seq")
    fast = ns == 8
    mine1, theirs1 = call(
        add_core_first, (shape_of((w2_rows, units), BF16), shape_of((w2_rows + out_rows, units), BF16)),
        (keep1, got1, out), "add_core_first", far=range(3), out_far=range(2), after=("attn_back",),
    )
    far_got1 = swap(theirs1, 2)
    out_near = swap(out, 1)
    g2_rows = -(-w1_rows // (16 * ns)) * 16 * ns
    keep2, send2, send4 = call(
        functools.partial(grads_kernel, nc, dim, zrows),
        (shape_of((2, g2_rows, units), BF16), shape_of((g2_rows, units), BF16), shape_of((g2_rows, units), BF16)),
        (low, grad_v, grad_r, mixed_low, g_z), "grads",
        scratch=[
            pltpu.VMEM((dim, zdim), F32), pltpu.VMEM((toks, dim), BF16), pltpu.VMEM((toks, nc * units), BF16),
            pltpu.VMEM((toks, nc * units), BF16), pltpu.VMEM((toks, dim), BF16), pltpu.VMEM((4, g2_rows, units), BF16),
            dma((4,)), dma((4,)),
        ],
        hbm=range(4), out_hbm=range(3), after=("add_core_first",), limit=24,
    )
    got2, got4 = swap(send2, 1), swap(send4, 1)
    shared, sums = call(
        functools.partial(scans_kernel, nd, dim),
        (shape_of((toks, dim)), shape_of((3, nd * SUBS, LANES))),
        (grad_v, grad_r) + first + (pt, state_in, xt, gmt), "scans",
        scratch=[
            pltpu.VMEM((toks, dim), F32), pltpu.VMEM((3, nd * SUBS, LANES), F32), pltpu.VMEM((nd * SUBS, LANES), F32),
            pltpu.VMEM((4, 2 * dim, units), BF16), pltpu.VMEM((toks, nc * units), BF16),
            pltpu.VMEM((toks, nc * units), BF16), dma((7,)),
        ],
        hbm=(0, 1, 2, 3, 4, 5, 7), out_hbm=range(2), after=("grads",), limit=24,
    )
    mine2, theirs2 = call(
        add_core_second, (shape_of((g2_rows, units), BF16),) * 2, (keep2, got2, got4), "add_core_second",
        far=range(3), out_far=range(2), after=("scans",),
    )
    far_got2 = swap(theirs2, 2)
    halves = lambda level, args, name, after: add_pair(
        functools.partial(add_halves, level), args, args[0].shape[0] // 2, name, after
    )
    joined = lambda level, args, name, after: call(
        functools.partial(join_halves, level), (shape_of((2 * args[0].shape[0], units), BF16),), args, name,
        free=range(2), out_free=(0,), after=after,
    )[0]
    add_two = lambda args, name, after: call(
        add_plain, (shape_of(args[0].shape, BF16),), args, name, free=range(2), out_free=(0,), after=after
    )[0]
    used = nc * vocab + 2 * small_rows(nc, nd)
    per = -(-used // (ndev * 16)) * 16
    (packed,) = call(
        functools.partial(last_kernel, nc, nd, ns, span),
        (shape_of((per * ndev, LANES), BF16),),
        (carries, gmt, pt, shared, x, row(attn_gain), g_mid, token_ids, sums, small, skip_grad, ffn_grad),
        "last",
        scratch=[
            pltpu.VMEM((width * SUBS, LANES), F32), pltpu.VMEM((vocab, dim), F32), pltpu.VMEM((per * ndev, LANES), BF16),
            pltpu.VMEM((toks, dim), F32), pltpu.VMEM((toks, dim), BF16), pltpu.VMEM((1, dim), F32),
            pltpu.VMEM((toks, dim), F32), pltpu.VMEM((rows, width), jnp.int32), pltpu.VMEM((3, nd * SUBS, LANES), F32),
            dma((6,)),
        ],
        hbm=range(3, 9), out_hbm=(0,), after=("add_core_second",), limit=16,
    )
    parts = exchange(packed.reshape(ndev, per, LANES), ("seq", "chan"))
    if fast:
        keep1, send1, out_far = call(
            add_far_first, (shape_of((w2_rows // 2, units), BF16),) * 2 + (shape_of((out_rows, units), BF16),),
            (mine1, far_got1), "x_first", far=range(2), out_far=range(3), after=("last",),
        )
        x_got1 = swap(send1, 1, "seq")
        keep2, send2 = halves(0, (mine2, far_got2), "x_second", ("x_first",))
        got2 = swap(send2, 1, "seq")
        keep1, send1 = halves(1, (keep1, x_got1), "z_first", ("x_second",))
        got1 = swap(send1, 2, "seq")
        keep2, send2 = halves(1, (keep2, got2), "z_second", ("z_first",))
        got2 = swap(send2, 2, "seq")
    else:
        far_got1, out_far = far_got1[:w2_rows], far_got1[w2_rows:]
    out_both = swap(out_far, 1)
    total = spread(parts, "sum_last", ("z_second",) if fast else ())
    whole = exchange(total, ("seq", "chan")).reshape(ndev * per, LANES)

    def gather_output(after):
        return call(
            output_kernel, (shape_of((rows, width, dim), BF16),), (out, out_near, out_far, out_both), "output",
            free=range(4), out_free=(0,), after=after, limit=8,
        )[0]

    def finish(after):
        return call(
            functools.partial(finish_kernel, nc, nd),
            (
                shape_of((vocab, dim)), shape_of((1, dim)), shape_of((nd, LANES)), shape_of((nd, LANES)),
                shape_of((nd, LANES)), shape_of((1, LANES)), shape_of((1, dim)), shape_of((1, zdim)),
                shape_of((1, zdim)), shape_of((1, zdim)),
            ),
            (whole,), "finish", out_free=range(10), scratch=[pltpu.VMEM((small_rows(nc, nd), LANES), F32)],
            after=after, limit=8,
        )

    if fast:
        keep1, send1 = halves(2, (keep1, got1), "zz_first", ("sum_last",))
        got1 = swap(send1, 4, "seq")
        keep2, send2 = halves(2, (keep2, got2), "zz_second", ("zz_first",))
        got2 = swap(send2, 4, "seq")
        keep1 = add_two((keep1, got1), "sum_first", ("zz_second",))
        got1 = swap(keep1, 4, "seq")
        keep2 = add_two((keep2, got2), "sum_second", ("sum_first",))
        got2 = swap(keep2, 4, "seq")
        keep1 = joined(2, (keep1, got1), "join_zz_first", ("sum_second",))
        got1 = swap(keep1, 2, "seq")
        keep2 = joined(2, (keep2, got2), "join_zz_second", ("join_zz_first",))
        got2 = swap(keep2, 2, "seq")
        u1 = joined(1, (keep1, got1), "join_z_first", ("join_zz_second",))
        v1 = swap(u1, 1, "seq")
        output = gather_output(("join_z_first",))
        finished = finish(("output",))
        u2 = joined(1, (keep2, got2), "join_z_second", ("finish",))
        v2 = swap(u2, 1, "seq")
    else:
        finished = finish(())
        output = gather_output(("finish",))
        u1 = v1 = seq_sum(add_two((mine1, far_got1), "add_first", ()), ns, "sum_first")
        u2 = v2 = seq_sum(add_two((mine2, far_got2), "add_second", ()), ns, "sum_second")
    embed_grad, ag, gi, gk, go, gs, fg, qg, kg, qb = finished
    up_grad, o_grad, down_grad = call(
        functools.partial(unpack_first, dim, urows),
        (shape_of(up_proj.shape), shape_of(o_proj.shape), shape_of(down_proj.shape)),
        (u1, v1), "unpack_first", free=range(2), out_free=range(3), scratch=[pltpu.VMEM((w2_rows, units), BF16)],
        after=("join_z_second",) if fast else ("output",),
    )
    v_grad, r_grad, z_grad = call(
        functools.partial(unpack_second, dim, zrows),
        (shape_of(v_proj.shape), shape_of(r_proj.shape), shape_of(z_proj.shape)),
        (u2, v2), "unpack_second", free=range(2), out_free=range(3), scratch=[pltpu.VMEM((g2_rows, units), BF16)],
        after=("unpack_first",),
    )
    flat = lambda value: value.reshape(-1)
    return (
        output, embed_grad, flat(ag), gi.T, gk.T, go.T, flat(gs), z_grad, flat(qg), flat(kg), flat(qb), v_grad, r_grad,
        o_grad, flat(fg), up_grad, down_grad,
    )


def solution(mesh):
    placed = (
        P(None, "seq"), P(), P(), P(), P("chan", None), P("chan", None), P("chan", None), P("chan"), P("chan", None),
        P(), P(), P(), P(None, "chan"), P(None, "chan"), P("chan", None), P(), P(None, "chan"), P("chan", None),
        P(None, "seq", None),
    )
    return jax.shard_map(
        body,
        mesh=mesh,
        in_specs=placed,
        out_specs=(
            P(None, "seq", None), P(), P(), P("chan", None), P("chan", None), P("chan", None), P("chan"),
            P("chan", None), P(), P(), P(), P(None, "chan"), P(None, "chan"), P("chan", None), P(), P(None, "chan"),
            P("chan", None),
        ),
        check_vma=False,
    )
```

```python
import functools

import jax
import jax.numpy as jnp
from jax import lax
from jax.experimental import pallas as pl
from jax.experimental.pallas import tpu as pltpu
from jax.sharding import PartitionSpec as P

SEQMAX = 4096
HIGH = lax.Precision.HIGHEST
EPS = 1e-06
F32 = jnp.float32
BF16 = jnp.bfloat16
LANES = 128
SUBS = 8
MIB = 1024 * 1024


def sigmoid(u):
    return 0.5 * jnp.tanh(0.5 * u) + 0.5


def silu_slope(pre):
    sigma = sigmoid(pre)
    return sigma * (1.0 + pre * (1.0 - sigma))


def mm(left, right, dims, precision=None):
    return lax.dot_general(
        left, right, ((dims[0], dims[1]), ((), ())), precision=precision, preferred_element_type=F32
    )


def dot(left, right):
    return mm(left, right, ((1,), (0,)))


def dot_rows(left, right):
    return mm(left, right, ((0,), (0,)))


def dot_cols(left, right):
    return mm(left, right, ((1,), (1,)))


def exact(left, right, dims):
    return mm(left.astype(F32), right.astype(F32), dims, HIGH)


def shape_of(dims, dtype=F32):
    return jax.ShapeDtypeStruct(dims, dtype)


TOKENS = {}


def call(
    kernel, outs, args, name, scratch=(), smem=(), hbm=(), free=(), far=(), out_hbm=(), out_free=(), out_far=(), after=(), limit=16
):

    waits = [TOKENS[key] for key in after]
    hbm, out_hbm = {*hbm, *far}, {*out_hbm, *out_far}
    count, made = len(args), len(outs)

    def run(*refs):
        rest = refs[count + len(waits) :]
        kernel(*refs[:count], *rest[:made], *rest[made + 1 :])

    def spec(at):
        if at >= count or (at in hbm and at not in far):
            return pl.BlockSpec(memory_space=pltpu.HBM)
        return pl.BlockSpec(memory_space=pltpu.SMEM if at in smem else pltpu.VMEM)

    def held(at, value):
        if at < count and (at in smem or at in free):
            return value
        return pltpu.with_memory_space_constraint(value, pltpu.HBM if at in hbm or at >= count else pltpu.VMEM)

    def result(at, out):
        if at in out_free:
            return out
        return (pltpu.HBM if at in out_hbm or at == made else pltpu.VMEM)(out.shape, out.dtype)

    shapes = list(outs) + [shape_of((SUBS, LANES))]
    *results, TOKENS[name] = pl.pallas_call(
        run,
        out_shape=[result(at, out) for at, out in enumerate(shapes)],
        in_specs=[spec(at) for at in range(count + len(waits))],
        out_specs=[
            pl.BlockSpec(memory_space=pltpu.HBM if (at in out_hbm and at not in out_far) or at == made else pltpu.VMEM)
            for at in range(made + 1)
        ],
        scratch_shapes=list(scratch),
        name=name,
        cost_estimate=pl.CostEstimate(flops=1, bytes_accessed=1, transcendentals=0),
        compiler_params=pltpu.CompilerParams(vmem_limit_bytes=limit * MIB),
    )(*[held(at, value) for at, value in enumerate([*args, *waits])])
    return results


def move(copies, sems):
    for copy in run_copies(copies, sems):
        copy.wait()


def run_copies(copies, sems):
    started = [pltpu.make_async_copy(src, dst, sems.at[at]) for at, (src, dst) in enumerate(copies)]
    for copy in started:
        copy.start()
    return started


def pack_params(in_ref, keep_ref, out_ref, skip_ref, p_ref, buf, sems):
    nd, lanes = in_ref.shape
    copies = [(ref, buf.at[at * nd : (at + 1) * nd, :]) for at, ref in enumerate((in_ref, keep_ref, out_ref))]
    copies.append((skip_ref, buf.at[3 * nd : 3 * nd + 1, :]))
    for copy in run_copies(copies, sems):
        copy.wait()
    rest = buf.shape[0] - 3 * nd
    buf[3 * nd :, :] = jnp.broadcast_to(buf[3 * nd : 3 * nd + 1, :], (rest, lanes))
    started = run_copies([(buf, p_ref.at[at]) for at in range(p_ref.shape[0])], sems)
    for copy in started:
        copy.wait()


def first_copies(v_ref, r_ref, z_ref, buf):
    dim = v_ref.shape[0]
    zrows = z_ref.shape[0] // 2
    copies = [(v_ref, buf.at[0:dim, :]), (r_ref, buf.at[dim : 2 * dim, :])]
    for half in range(2):
        copies.append(
            (
                z_ref.at[half * zrows : (half + 1) * zrows, :],
                buf.at[2 * dim : 2 * dim + zrows, half * LANES : (half + 1) * LANES],
            )
        )
    return copies


def second_copies(up_ref, o_ref, down_ref, buf):
    dim, units = up_ref.shape
    urows = o_ref.shape[0]
    copies = [(up_ref, buf.at[0:dim, :])]
    for at, ref in enumerate((o_ref, down_ref)):
        for half in range(dim // units):
            start = dim + (dim // units * at + half) * urows
            copies.append((ref.at[:, half * units : (half + 1) * units], buf.at[start : start + urows, :]))
    return copies


def prepare_kernel(
    nc, ids_at, table_at, gain_at, v_at, r_at, z_at, up_at, o_at, down_at,
    x_to, xt_ref, low_to, w1_to, w2_to,
    ids_ref, embed_ref, gain_ref, x_ref, low_ref, w1_ref, w2_ref, sems, w_sems, out_sems,
):
    entering = run_copies(first_copies(v_at, r_at, z_at, w1_ref), w_sems.at[0:4])
    started = run_copies([(ids_at, ids_ref), (table_at, embed_ref), (gain_at, gain_ref)], sems)
    later = run_copies(second_copies(up_at, o_at, down_at, w2_ref), w_sems.at[4:9])
    for copy in entering:
        copy.wait()
    leaving = run_copies([(w1_ref, w1_to)], out_sems.at[0:1])
    rp = x_ref.shape[0] // ids_ref.shape[1]
    width = ids_ref.shape[1]
    vocab = embed_ref.shape[0]
    chan = lax.axis_index("chan")
    for copy in started:
        copy.wait()
    for row in range(rp):
        ids = ids_ref[pl.ds(chan * rp + row, 1), :]
        onehot = jnp.where(lax.broadcasted_iota(jnp.int32, (vocab, width), 0) == ids, 1.0, 0.0).astype(BF16)
        x = dot_rows(onehot, embed_ref[...])
        x_ref[row * width : (row + 1) * width, :] = x.astype(BF16)
        normed = x * lax.rsqrt(jnp.mean(x * x, axis=-1, keepdims=True) + EPS) * gain_ref[...]
        low_ref[row * width : (row + 1) * width, :] = normed.astype(BF16)
        for chunk in range(nc):
            xt_ref[pl.ds(row * nc + chunk, width, stride=SUBS), :] = normed[
                :, chunk * LANES : (chunk + 1) * LANES
            ]
        for copy in later:
            copy.wait()
        later = []
        leaving += run_copies([(w2_ref, w2_to)], out_sems.at[1:2]) if row == 0 else []
    leaving += run_copies([(x_ref, x_to), (low_ref, low_to)], out_sems.at[2:4])
    for copy in leaving:
        copy.wait()


def tile(ref, at):
    return ref[at * SUBS : (at + 1) * SUBS, :]


def step_tile(ref, t):
    return ref[pl.ds(pl.multiple_of(t * SUBS, SUBS), SUBS), :]


def scan_end_kernel(nc, nd, p_ref, xt_ref, pt_ref, end_ref, buf, sems):
    width = xt_ref.shape[0] // SUBS
    prows = p_ref.shape[1]
    for sub in range(SUBS):
        pt_ref[pl.ds(sub, prows, stride=SUBS), :] = p_ref[sub % nc]
    keep = [tile(pt_ref, nd + k) for k in range(nd)]

    def step(block, states):
        states = list(states)
        for u in range(8):
            x = step_tile(xt_ref, block * 8 + u)
            states = [q * s + x for q, s in zip(keep, states)]
        return tuple(states)

    zero = jnp.zeros((SUBS, LANES), F32)
    states = lax.fori_loop(0, width // 8, step, (zero,) * nd)
    buf[...] = jnp.concatenate(states, axis=0)
    for copy in run_copies([(buf, end_ref.at[at]) for at in range(end_ref.shape[0])], sems):
        copy.wait()


def project_kernel(
    dim, low_at, h0, h1, h2, h3, vpre_to, rpre_ref, val_ref, z_ref, val_to, low_ref, vpre_ref, buf, sems, out_sems
):
    chan = lax.axis_index("chan")
    units = h0.shape[1]
    zrows = h0.shape[0] - 2 * dim
    started = run_copies([(low_at, low_ref)] + [(ref, buf.at[j]) for j, ref in enumerate((h0, h1, h2, h3))], sems)
    started[0].wait()
    low = low_ref[...]
    leaving = []
    for j in range(4):
        started[1 + j].wait()
        w = buf.at[j]
        cols = slice(j * units, (j + 1) * units)
        v_pre = dot(low, w[0:dim, :])
        vpre_ref[:, cols] = v_pre
        val_ref[:, cols] = (v_pre * sigmoid(v_pre)).astype(BF16)
        leaving += run_copies(
            [(vpre_ref.at[:, cols], vpre_to.at[:, cols]), (val_ref.at[:, cols], val_to.at[:, cols])],
            out_sems.at[2 * j : 2 * j + 2],
        )
        rpre_ref[:, cols] = dot(low, w[dim : 2 * dim, :])
        start = pl.multiple_of(jnp.bitwise_xor(chan, j) * 2 * zrows, 2 * zrows)
        half = w[2 * dim : 2 * dim + zrows, :]
        z_ref[pl.ds(start, 2 * zrows), :] = jnp.concatenate([half[:, :LANES], half[:, LANES:]], axis=0)
    for copy in leaving:
        copy.wait()


def whole_keep(keep, width):
    whole = keep
    power = 1
    while power < width:
        whole = whole * whole
        power *= 2
    return whole


def weights_of(pt_ref, nd):
    amp = pt_ref[0 : nd * SUBS, :]
    keep = pt_ref[nd * SUBS : 2 * nd * SUBS, :]
    out = pt_ref[2 * nd * SUBS : 3 * nd * SUBS, :]
    root = jnp.sqrt(1.0 - keep * keep)
    return amp, keep, out, root


def split_tiles(value, nd):
    return [value[k * SUBS : (k + 1) * SUBS, :] for k in range(nd)]


def tree_sum(values):
    values = list(values)
    while len(values) > 1:
        values = [sum(values[i : i + 2][1:], values[i]) for i in range(0, len(values), 2)]
    return values[0]


def scale_of(x):
    return lax.rsqrt(jnp.mean(x * x, axis=-1, keepdims=True) + EPS)


def mix_kernel(
    nc, nd, span, counts_ref, ends_ref, xt_ref, pt_ref, z_ref, val_ref, rpre_ref, qg_ref, kg_ref, qb_ref,
    mpre_ref, mlow_to, zpre_ref, attn_ref, ctx_ref, gated_ref, sin_to, sm_ref, sin_ref, mlow_ref, sems,
):
    width = xt_ref.shape[0] // SUBS
    rp = SUBS // nc
    place = lax.axis_index("seq")
    chan = lax.axis_index("chan")
    amp, keep_all, out_all, root = weights_of(pt_ref, nd)
    whole = whole_keep(keep_all, width)
    per = span // width
    first = place // per * per

    def gather(n, state):
        return state * whole + ends_ref[n].astype(F32)

    start = lax.fori_loop(first, place, gather, jnp.zeros_like(whole))
    sin_ref[...] = start
    (leaving,) = run_copies([(sin_ref, sin_to)], sems.at[:1])
    keep = split_tiles(keep_all, nd)
    weight = split_tiles(out_all * amp * root, nd)

    def step(block, states):
        states = list(states)
        for u in range(8):
            t = block * 8 + u
            x = step_tile(xt_ref, t)
            states = [q * s + x for q, s in zip(keep, states)]
            sm_ref[pl.ds(pl.multiple_of(t * SUBS, SUBS), SUBS), :] = tree_sum(
                [w * s for w, s in zip(weight, states)]
            )
        return tuple(states)

    lax.fori_loop(0, width // 8, step, tuple(split_tiles(start, nd)))
    skip = pt_ref[3 * nd * SUBS : 3 * nd * SUBS + SUBS, :]
    for row in range(rp):
        rows = slice(row * width, (row + 1) * width)
        for chunk in range(nc):
            at = row * nc + chunk
            lanes = slice(chunk * LANES, (chunk + 1) * LANES)
            own = xt_ref[pl.ds(at, width, stride=SUBS), :]
            pre = sm_ref[pl.ds(at, width, stride=SUBS), :] + skip[at : at + 1, :] * own
            mpre_ref[rows, lanes] = pre
            mlow_ref[rows, lanes] = (pre * sigmoid(pre)).astype(BF16)
    (left,) = run_copies([(mlow_ref, mlow_to)], sems.at[1:])
    z_pre = dot(mlow_ref[...], z_ref[...])
    zpre_ref[...] = z_pre
    zeta = z_pre * sigmoid(z_pre)
    queries = (zeta * qg_ref[...] + qb_ref[...]).astype(BF16)
    keys = (zeta * kg_ref[...]).astype(BF16)
    scale = z_pre.shape[1] ** (-0.5)
    pieces = counts_ref.shape[0] // (rp * nc)
    begin = place * width
    piece = begin // span
    inner = begin - piece * span
    for row in range(rp):
        rows = slice(row * width, (row + 1) * width)
        count = counts_ref[(chan * rp + row) * pieces + piece]
        valid = lax.broadcasted_iota(jnp.int32, (width, width), 1) < count - inner
        scores = jnp.where(valid, dot_cols(queries[rows, :], keys[rows, :]) * scale, -1e30)
        top = jnp.max(scores, axis=-1, keepdims=True)
        weights = jnp.where(valid, jnp.exp(scores - top), 0.0)
        empty = jnp.where(count > inner, 0.0, 1.0)
        attn = weights / (jnp.sum(weights, axis=-1, keepdims=True) + empty)
        attn_ref[rows, :] = attn
        context = dot(attn.astype(BF16), val_ref[rows, :])
        ctx_ref[rows, :] = context
        r_pre = rpre_ref[rows, :]
        gated_ref[rows, :] = (r_pre * sigmoid(r_pre) * context).astype(BF16)
    leaving.wait()
    left.wait()


def ffn_kernel(
    nc, dim, gated_ref, h0, h1, h2, h3, x_at, grad_ref, fgain_ref,
    out_to, gmid_to, ggated_ref, keep_to, send_to, fg_ref, hid_ref, gup_ref, g_ref, out_ref, gmid_ref, x_ref, buf,
    part_ref, sems, part_sems,
):
    units = h0.shape[1]
    rp = grad_ref.shape[0] // nc
    width = grad_ref.shape[1]
    chan = lax.axis_index("chan")
    urows = (h0.shape[0] - dim) // 4
    split = (slice(dim, dim + 2 * urows), slice(0, dim), slice(dim + 2 * urows, dim + 4 * urows))
    hs = (h0, h1, h2, h3)
    copies = [(x_at, x_ref)]
    copies += [(hs[j].at[split[0], :], buf.at[j, split[0], :]) for j in range(4)]
    copies += [(grad_ref.at[chan * rp + row], g_ref.at[row * width : (row + 1) * width, :]) for row in range(rp)]
    copies += [(hs[j].at[part, :], buf.at[j, part, :]) for j in range(4) for part in split[1:]]
    started = run_copies(copies, sems)
    started[0].wait()
    ws = [buf.at[j] for j in range(4)]
    halves = dim // units

    def shard(j, which):
        start = dim + which * halves * urows
        return [ws[j][start + half * urows : start + (half + 1) * urows, :] for half in range(halves)]

    def cols(j):
        return slice(j * units, (j + 1) * units)

    branch = [None] * halves
    for j in range(4):
        started[1 + j].wait()
        for half, part in enumerate(shard(j, 0)):
            term = dot(gated_ref[:, cols(j)], part)
            branch[half] = term if j == 0 else branch[half] + term
    middle = x_ref[...].astype(F32) + jnp.concatenate(branch, axis=1)
    r = scale_of(middle)
    n = middle * r
    fgain = fgain_ref[...]
    for copy in started[5 : 5 + rp]:
        copy.wait()
    g = g_ref[...]
    ffn_low = (n * fgain).astype(BF16)
    ffn_out = [None] * halves
    g_in = None
    for j in range(4):
        for copy in started[5 + rp + 2 * j : 7 + rp + 2 * j]:
            copy.wait()
        up = ws[j][0:dim, :]
        up_pre = dot(ffn_low, up)
        sigma = sigmoid(up_pre)
        hidden = (up_pre * sigma).astype(BF16)
        hid_ref[:, cols(j)] = hidden
        down = shard(j, 1)
        back = None
        for half, part in enumerate(down):
            term = dot(hidden, part)
            ffn_out[half] = term if j == 0 else ffn_out[half] + term
            term = dot_cols(g[:, half * units : (half + 1) * units], part)
            back = term if half == 0 else back + term
        g_up = (back * (sigma * (1.0 + up_pre * (1.0 - sigma)))).astype(BF16)
        gup_ref[:, cols(j)] = g_up
        term = dot_cols(g_up, up)
        g_in = term if j == 0 else g_in + term
    toks = g_ref.shape[0]
    for half in range(halves):
        out_ref[half * toks : (half + 1) * toks, :] = (middle[:, half * units : (half + 1) * units] + ffn_out[half]).astype(
            BF16
        )
    fg_ref[...] = jnp.sum(g_in * n, axis=0, keepdims=True)
    h = g_in * fgain
    g_mid = g.astype(F32) + r * (h - n * jnp.mean(h * n, axis=-1, keepdims=True))
    gmid_ref[...] = g_mid
    leaving = run_copies([(out_ref, out_to), (gmid_ref, gmid_to)], sems)
    g_branch = g_mid.astype(BF16)
    for j in range(4):
        total = None
        for half, part in enumerate(shard(j, 0)):
            term = dot_cols(g_branch[:, half * units : (half + 1) * units], part)
            total = term if half == 0 else total + term
        ggated_ref[:, cols(j)] = total
    for j in (1, 3, 0, 2):
        part_ref[j, 0:dim, :] = dot_rows(ffn_low, gup_ref[:, cols(j)]).astype(BF16)
        for which, (left, right) in enumerate(((gated_ref, g_branch), (hid_ref, g))):
            grad = dot_rows(left[:, cols(j)], right).astype(BF16)
            for half in range(halves):
                start = dim + (which * halves + half) * urows
                part_ref[j, start : start + urows, :] = grad[:, half * units : (half + 1) * units]
        leaving += run_copies([(part_ref.at[j], (keep_to, send_to)[j % 2].at[j // 2])], part_sems.at[j : j + 1])
    for copy in leaving:
        copy.wait()


def attn_back_kernel(
    nc, nd, ggated_ref, rpre_ref, vpre_ref, ctx_ref, attn_ref, val_ref, zpre_ref, mpre_ref, xt_ref, z_ref, pt_ref,
    qg_ref, kg_ref, qb_ref,
    gv_to, gr_to, gz_ref, gmt_ref, carry_ref, small_ref, skip_ref, buf, gv_ref, gr_ref, sems, out_sems,
):
    width = xt_ref.shape[0] // SUBS
    rp = SUBS // nc
    z_pre = zpre_ref[...]
    sigma = sigmoid(z_pre)
    zeta = z_pre * sigma
    queries = (zeta * qg_ref[...] + qb_ref[...]).astype(BF16)
    keys = (zeta * kg_ref[...]).astype(BF16)
    scale = z_pre.shape[1] ** (-0.5)
    parts_q, parts_k = [], []
    for row in range(rp):
        rows = slice(row * width, (row + 1) * width)
        g_gated = ggated_ref[rows, :]
        r_pre = rpre_ref[rows, :]
        sr = sigmoid(r_pre)
        g_context = (g_gated * (r_pre * sr)).astype(BF16)
        gr_ref[rows, :] = (g_gated * ctx_ref[rows, :] * (sr * (1.0 + r_pre * (1.0 - sr)))).astype(BF16)
        attn = attn_ref[rows, :]
        g_values = dot_rows(attn.astype(BF16), g_context)
        gv_ref[rows, :] = (g_values * silu_slope(vpre_ref[rows, :])).astype(BF16)
        g_attn = dot_cols(g_context, val_ref[rows, :])
        g_scores = attn * (g_attn - jnp.sum(attn * g_attn, axis=-1, keepdims=True))
        parts_q.append(exact(g_scores, keys[rows, :], ((1,), (0,))) * scale)
        parts_k.append(exact(g_scores, queries[rows, :], ((0,), (0,))) * scale)
    leaving = run_copies([(gv_ref, gv_to), (gr_ref, gr_to)], out_sems)
    g_q = jnp.concatenate(parts_q, axis=0)
    g_k = jnp.concatenate(parts_k, axis=0)
    small_ref[...] = jnp.concatenate(
        [
            jnp.sum(g_q * zeta, axis=0, keepdims=True),
            jnp.sum(g_k * zeta, axis=0, keepdims=True),
            jnp.sum(g_q, axis=0, keepdims=True),
            jnp.zeros((SUBS - 3, z_pre.shape[1]), F32),
        ],
        axis=0,
    )
    g_z = (g_q * qg_ref[...] + g_k * kg_ref[...]) * (sigma * (1.0 + z_pre * (1.0 - sigma)))
    gz_ref[...] = g_z
    skips = []
    for row in range(rp):
        rows = slice(row * width, (row + 1) * width)
        for chunk in range(nc):
            at = row * nc + chunk
            lanes = slice(chunk * LANES, (chunk + 1) * LANES)
            g_mixed = exact(g_z[rows, :], z_ref[lanes, :], ((1,), (1,))) * silu_slope(mpre_ref[rows, lanes])
            gmt_ref[pl.ds(at, width, stride=SUBS), :] = g_mixed
            skips.append(jnp.sum(g_mixed * xt_ref[pl.ds(at, width, stride=SUBS), :], axis=0, keepdims=True))
    skip_ref[...] = jnp.concatenate(skips, axis=0)
    keep = [tile(pt_ref, nd + k) for k in range(nd)]

    def step(block, carries):
        carries = list(carries)
        for u in range(8):
            gm = step_tile(gmt_ref, width - 1 - (block * 8 + u))
            carries = [q * (c + gm) for q, c in zip(keep, carries)]
        return tuple(carries)

    zero = jnp.zeros((SUBS, LANES), F32)
    carries = lax.fori_loop(0, width // 8, step, (zero,) * nd)
    buf[...] = jnp.concatenate(carries, axis=0).astype(BF16)
    for copy in leaving:
        copy.wait()
    for copy in run_copies([(buf, carry_ref.at[at]) for at in range(carry_ref.shape[0])], sems):
        copy.wait()


def grads_kernel(
    nc, dim, zrows, low_at, gv_at, gr_at, mlow_at, gz_ref, keep_to, send1_to, send3_to,
    zg_ref, low_ref, gv_ref, gr_ref, mlow_ref, part_ref, sems, part_sems,
):
    units = gv_ref.shape[1] // nc
    chan = lax.axis_index("chan")
    started = run_copies([(mlow_at, mlow_ref), (low_at, low_ref), (gv_at, gv_ref), (gr_at, gr_ref)], sems)
    started[0].wait()
    zg_ref[...] = exact(mlow_ref[...], gz_ref[...], ((0,), (0,)))
    for copy in started[1:]:
        copy.wait()
    low = low_ref[...]
    used = 2 * dim + zrows
    spare = part_ref.shape[1] - used
    leaving = []
    for j in (1, 3, 0, 2):
        cols = slice(j * units, (j + 1) * units)
        part_ref[j, 0:dim, :] = dot_rows(low, gv_ref[:, cols]).astype(BF16)
        part_ref[j, dim : 2 * dim, :] = dot_rows(low, gr_ref[:, cols]).astype(BF16)
        start = pl.multiple_of(jnp.bitwise_xor(chan, j) * 2 * zrows, 2 * zrows)
        block = zg_ref[pl.ds(start, 2 * zrows), :]
        part_ref[j, 2 * dim : used, :] = jnp.concatenate([block[:zrows, :], block[zrows:, :]], axis=1).astype(BF16)
        part_ref[j, used:, :] = jnp.zeros((spare, units), BF16)
        to = (keep_to.at[0], send1_to, keep_to.at[1], send3_to)[j]
        leaving += run_copies([(part_ref.at[j], to)], part_sems.at[j : j + 1])
    for copy in leaving:
        copy.wait()


def scans_kernel(
    nd, dim, gv_at, gr_at, h0, h1, h2, h3, pt_ref, sin_at, xt_ref, gmt_ref,
    shared_to, acc_to, shared_ref, acc_ref, sin_ref, buf, gv_ref, gr_ref, sems,
):
    units = h0.shape[1]
    width = xt_ref.shape[0] // SUBS
    started = run_copies(
        [(sin_at, sin_ref), (gv_at, gv_ref), (gr_at, gr_ref)]
        + [(ref.at[0 : 2 * dim, :], buf.at[j]) for j, ref in enumerate((h0, h1, h2, h3))],
        sems,
    )
    started[0].wait()
    group = 8
    for begin in range(0, nd, group):
        ks = list(range(begin, begin + group))
        keep = [tile(pt_ref, nd + k) for k in ks]

        def step(block, carry):
            s, d, a, b = [list(part) for part in carry]
            for u in range(4):
                t = block * 4 + u
                x = step_tile(xt_ref, t)
                gm = step_tile(gmt_ref, t)
                d = [q * di + si for q, di, si in zip(keep, d, s)]
                s = [q * si + x for q, si in zip(keep, s)]
                a = [ai + gm * si for ai, si in zip(a, s)]
                b = [bi + gm * di for bi, di in zip(b, d)]
            return tuple(s), tuple(d), tuple(a), tuple(b)

        zero = (jnp.zeros((SUBS, LANES), F32),) * group
        init = tuple(tile(sin_ref, k) for k in ks)
        s, d, a, b = lax.fori_loop(0, width // 4, step, (init, zero, zero, zero))
        rows = slice(begin * SUBS, (begin + group) * SUBS)
        acc_ref[0, rows, :] = jnp.concatenate(a, axis=0)
        acc_ref[1, rows, :] = jnp.concatenate(b, axis=0)
        acc_ref[2, rows, :] = jnp.concatenate(d, axis=0)
    for copy in started[1:3]:
        copy.wait()
    (last,) = run_copies([(acc_ref, acc_to)], sems)
    shared = None
    for j in range(4):
        cols = slice(j * units, (j + 1) * units)
        started[3 + j].wait()
        term = dot_cols(gv_ref[:, cols], buf[j, 0:dim, :]) + dot_cols(gr_ref[:, cols], buf[j, dim:, :])
        shared = term if j == 0 else shared + term
    shared_ref[...] = shared
    move([(shared_ref, shared_to)], sems.at[1:])
    last.wait()


def rest_rows(nd):
    return -(-(3 * nd + 4) // 16) * 16


def last_kernel(
    nc, nd, ns, span, carry_ref, gmt_ref, pt_ref, shared_at, x_at, gain_at, gmid_at, ids_at, sums_at,
    small_ref, skip_ref, fg_ref,
    keep_ref, send_ref, yt_ref, acc_ref, ema_ref, rest_ref, shared_ref, x_ref, gain_ref, gmid_ref, ids_ref, sums_ref,
    sems,
):
    started = run_copies(
        [
            (shared_at, shared_ref), (x_at, x_ref), (gain_at, gain_ref), (gmid_at, gmid_ref), (ids_at, ids_ref),
            (sums_at, sums_ref),
        ],
        sems,
    )
    width = gmt_ref.shape[0] // SUBS
    rp = SUBS // nc
    vocab = acc_ref.shape[0]
    place = lax.axis_index("seq")
    chan = lax.axis_index("chan")
    amp, keep_all, out_all, root = weights_of(pt_ref, nd)
    whole = whole_keep(keep_all, width)
    per = span // width
    last = place // per * per + per - 1

    def gather(n, state):
        return state * whole + carry_ref[last - n].astype(F32)

    start = lax.fori_loop(0, last - place, gather, jnp.zeros_like(whole))
    drive = amp * root
    weight_all = out_all * drive
    keep = split_tiles(keep_all, nd)
    weight = split_tiles(weight_all, nd)

    def step(block, carries):
        carries = list(carries)
        for u in range(8):
            t = width - 1 - (block * 8 + u)
            gm = step_tile(gmt_ref, t)
            adj = [c + gm for c in carries]
            yt_ref[pl.ds(pl.multiple_of(t * SUBS, SUBS), SUBS), :] = tree_sum(
                [w * s for w, s in zip(weight, adj)]
            )
            carries = [q * s for q, s in zip(keep, adj)]
        return tuple(carries)

    lax.fori_loop(0, width // 8, step, tuple(split_tiles(start, nd)))
    for copy in started:
        copy.wait()
    a = sums_ref[0]
    g_drive = out_all * a
    grad_out = drive * a
    grad_in = g_drive * root
    grad_keep = weight_all * (sums_ref[1] + sums_ref[2] * start) - g_drive * amp * keep_all / root
    for at, grad in enumerate((grad_in, grad_keep, grad_out)):
        ema_ref[at * nd * SUBS : (at + 1) * nd * SUBS, :] = grad
    skip = pt_ref[3 * nd * SUBS : 3 * nd * SUBS + SUBS, :]
    gain = gain_ref[...]
    for row in range(rp):
        toks = slice(row * width, (row + 1) * width)
        pieces = []
        for chunk in range(nc):
            at = row * nc + chunk
            lanes = slice(chunk * LANES, (chunk + 1) * LANES)
            gm = gmt_ref[pl.ds(at, width, stride=SUBS), :]
            pieces.append(
                shared_ref[toks, lanes] + skip[at : at + 1, :] * gm + yt_ref[pl.ds(at, width, stride=SUBS), :]
            )
        g_normed = jnp.concatenate(pieces, axis=1)
        x = x_ref[toks, :].astype(F32)
        r = scale_of(x)
        n = x * r
        h = g_normed * gain
        g_x = gmid_ref[toks, :] + r * (h - n * jnp.mean(h * n, axis=-1, keepdims=True))
        part = jnp.sum(g_normed * n, axis=0, keepdims=True)
        ag = part if row == 0 else ag + part
        ids = ids_ref[pl.ds(chan * rp + row, 1), :]
        onehot = jnp.where(lax.broadcasted_iota(jnp.int32, (vocab, width), 0) == ids, 1.0, 0.0)
        term = exact(onehot, g_x, ((1,), (0,)))
        acc_ref[...] = term if row == 0 else acc_ref[...] + term
    rest_ref[...] = jnp.zeros_like(rest_ref)
    for chunk in range(nc):
        lanes = slice(chunk * LANES, (chunk + 1) * LANES)
        for at in range(3):
            total = None
            for row in range(rp):
                term = ema_ref[pl.ds(at * nd * SUBS + row * nc + chunk, nd, stride=SUBS), :]
                total = term if row == 0 else total + term
            rest_ref[chunk, at * nd : (at + 1) * nd, :] = total
        at = 3 * nd
        rest_ref[chunk, at : at + 1, :] = sum(
            skip_ref[row * nc + chunk : row * nc + chunk + 1, :] for row in range(rp)
        )
        rest_ref[chunk, at + 1 : at + 2, :] = ag[:, lanes]
        rest_ref[chunk, at + 2 : at + 3, :] = fg_ref[:, lanes]
        if chunk < 3:
            rest_ref[chunk, at + 3 : at + 4, :] = small_ref[chunk : chunk + 1, :]
    half = vocab // 2
    room = rest_ref.shape[1]
    for j in range(4):
        to = (keep_ref, send_ref)[j % 2]
        owner = jnp.bitwise_xor(chan, j)
        block = acc_ref[:, pl.ds(pl.multiple_of(owner * LANES, LANES), LANES)]
        to[j // 2, 0:half, :] = jnp.concatenate([block[:half, :], block[half:, :]], axis=1).astype(BF16)
        rest = rest_ref[owner]
        high = rest.astype(BF16)
        low = (rest - high.astype(F32)).astype(BF16)
        to[j // 2, half : half + room, :] = jnp.concatenate([high, low], axis=1)
        to[j // 2, half + room :, :] = jnp.zeros((to.shape[1] - half - room, to.shape[2]), BF16)


def sum_kernel(in_ref, out_ref, buf, sems):
    total = in_ref[0].astype(F32)
    for at in range(1, in_ref.shape[0]):
        total = total + in_ref[at].astype(F32)
    buf[...] = total.astype(BF16)
    for copy in run_copies([(buf, out_ref.at[at]) for at in range(out_ref.shape[0])], sems):
        copy.wait()


def spread(parts, name, after=()):
    scratch = [pltpu.VMEM(parts.shape[1:], BF16), pltpu.SemaphoreType.DMA((parts.shape[0],))]
    return call(sum_kernel, (shape_of(parts.shape, BF16),), (parts,), name, scratch=scratch, out_hbm=(0,), after=after)[0]


def finish_kernel(
    nc, nd, w0, w1, w2, w3, embed_ref, ag_ref, ei_ref, ek_ref, eo_ref, es_ref, fg_ref, qg_ref, kg_ref, qb_ref, rest_ref
):
    half = embed_ref.shape[0] // 2
    room = rest_ref.shape[1]
    chan = lax.axis_index("chan")
    for j, ref in enumerate((w0, w1, w2, w3)):
        owner = jnp.bitwise_xor(chan, j)
        lanes = pl.ds(pl.multiple_of(owner * LANES, LANES), LANES)
        block = ref[0:half, :].astype(F32)
        embed_ref[0:half, lanes] = block[:, :LANES]
        embed_ref[half:, lanes] = block[:, LANES:]
        rest = ref[half : half + room, :].astype(F32)
        rest = rest[:, :LANES] + rest[:, LANES:]
        rest_ref[owner] = rest
        if j == 0:
            for at, to in enumerate((ei_ref, ek_ref, eo_ref)):
                to[...] = rest[at * nd : (at + 1) * nd, :]
            es_ref[...] = rest[3 * nd : 3 * nd + 1, :]
        ag_ref[:, lanes] = rest[3 * nd + 1 : 3 * nd + 2, :]
        fg_ref[:, lanes] = rest[3 * nd + 2 : 3 * nd + 3, :]
    for at, to in enumerate((qg_ref, kg_ref, qb_ref)):
        to[...] = rest_ref[at, 3 * nd + 3 : 3 * nd + 4, :]


def unpack_first(dim, urows, u_ref, v_ref, up_ref, o_ref, down_ref, s_ref):
    join(u_ref, v_ref, s_ref)
    units = s_ref.shape[1]
    up_ref[...] = s_ref[0:dim, :].astype(F32)
    for at, ref in enumerate((o_ref, down_ref)):
        for half in range(dim // units):
            start = dim + (at * (dim // units) + half) * urows
            ref[:, half * units : (half + 1) * units] = s_ref[start : start + urows, :].astype(F32)


def unpack_second(dim, zrows, u_ref, x_ref, v_ref, r_ref, z_ref, s_ref):
    join(u_ref, x_ref, s_ref)
    v_ref[...] = s_ref[0:dim, :].astype(F32)
    r_ref[...] = s_ref[dim : 2 * dim, :].astype(F32)
    block = s_ref[2 * dim : 2 * dim + zrows, :].astype(F32)
    z_ref[0:zrows, :] = block[:, :LANES]
    z_ref[zrows:, :] = block[:, LANES:]


def join(mine_ref, other_ref, to_ref):
    if mine_ref.shape[0] >= to_ref.shape[0]:
        to_ref[...] = mine_ref[0 : to_ref.shape[0], :]
    else:
        join_part(0, mine_ref, other_ref, to_ref)


def plus(left, right):
    return (left.astype(F32) + right.astype(F32)).astype(BF16)


def add_core_first(keep_ref, got_ref, mine_to, theirs_to, mine_ref, theirs_ref, sems):
    rows = keep_ref.shape[1] // 4
    leaving = []
    for at in range(4):
        part = slice(at * rows, (at + 1) * rows)
        theirs_ref[part, :] = plus(keep_ref[1, part, :], got_ref[1, part, :])
        mine_ref[part, :] = plus(keep_ref[0, part, :], got_ref[0, part, :])
        leaving += run_copies(
            [(theirs_ref.at[part, :], theirs_to.at[part, :]), (mine_ref.at[part, :], mine_to.at[part, :])],
            sems.at[2 * at : 2 * at + 2],
        )
    for copy in leaving:
        copy.wait()


def add_core(keep_ref, got_ref, mine_ref, theirs_ref):
    mine_ref[...] = plus(keep_ref[0], got_ref[0])
    theirs_ref[...] = plus(keep_ref[1], got_ref[1])


def add_core_second(keep_ref, got_ref, other_ref, mine_ref, theirs_ref):
    mine_ref[...] = plus(keep_ref[0], got_ref[...])
    theirs_ref[...] = plus(keep_ref[1], other_ref[...])


def add_plain(mine_ref, got_ref, out_ref):
    out_ref[...] = plus(mine_ref[...], got_ref[...])


def seq_bit(level):
    return jnp.bitwise_and(lax.shift_right_logical(lax.axis_index("seq"), level), 1)


def add_halves(level, parts, *refs):
    pairs, (keep_ref, send_ref) = refs[:-2], refs[-2:]
    bit = seq_bit(level)
    begin = 0
    for at in range(0, len(pairs), 2):
        mine_ref, got_ref = pairs[at : at + 2]
        inner = 0
        for rows in parts[at // 2]:
            half = rows // 2
            for side, ref in ((bit, keep_ref), (1 - bit, send_ref)):
                at_rows = pl.ds(pl.multiple_of(inner + side * half, 16), half)
                ref[begin : begin + half, :] = plus(mine_ref[at_rows, :], got_ref[at_rows, :])
            inner += rows
            begin += half


def join_halves(level, parts, mine_ref, got_ref, out_ref):
    bit = seq_bit(level)
    begin = 0
    for rows in parts:
        for side, ref in ((bit, mine_ref), (1 - bit, got_ref)):
            out_ref[pl.ds(pl.multiple_of(2 * begin + side * rows, 16), rows), :] = ref[begin : begin + rows, :]
        begin += rows


def join_part(begin, mine_ref, got_ref, out_ref):
    half = out_ref.shape[0] // 2
    bit = seq_bit(0)
    for side, ref in ((bit, mine_ref), (1 - bit, got_ref)):
        out_ref[pl.ds(pl.multiple_of(side * half, 16), half), :] = ref[begin : begin + half, :]


def output_kernel(w0, w1, w2, w3, out_ref):
    rows, width, dim = out_ref.shape
    units = w0.shape[1]
    toks = w0.shape[0] // (dim // units)
    chan = lax.axis_index("chan")
    for j, ref in enumerate((w0, w1, w2, w3)):
        for row in range(toks // width):
            for half in range(dim // units):
                start = half * toks + row * width
                out_ref[jnp.bitwise_xor(chan, j) * (toks // width) + row, :, half * units : (half + 1) * units] = ref[
                    start : start + width, :
                ]


def swap(value, mask, axis="chan"):
    return lax.ppermute(value, axis, [(at, at ^ mask) for at in range(lax.axis_size(axis))])


def exchange(value, axis):
    return lax.all_to_all(value, axis, 0, 0, tiled=True)


def add_pair(kernel, args, rows, name, after):
    shape = shape_of((rows, args[0].shape[-1]), BF16)
    return call(kernel, (shape, shape), args, name, free=range(3), out_free=(0, 1), after=after)


def seq_sum(value, ns, name):
    rows = value.shape[0]
    parts = exchange(value.reshape(ns, rows // ns, value.shape[1]), "seq")
    return exchange(spread(parts, name), "seq").reshape(value.shape)


def body(
    token_ids, valid_counts, embed, attn_gain, ema_in, ema_keep, ema_out, ema_skip, z_proj, q_gain, k_gain, q_bias,
    v_proj, r_proj, o_proj, ffn_gain, up_proj, down_proj, grad_out,
):
    rows, width = token_ids.shape
    vocab, dim = embed.shape
    nd = ema_in.shape[1]
    units = v_proj.shape[1]
    zdim = z_proj.shape[1]
    nc = lax.axis_size("chan")
    ns = lax.axis_size("seq")
    ndev = nc * ns
    rp = rows // nc
    toks = rp * width
    span = min(width * ns, SEQMAX)
    urows = o_proj.shape[0]
    zrows = z_proj.shape[0] // 2
    prows = 3 * nd + SUBS
    w1_rows = 2 * dim + zrows
    w2_rows = 3 * dim
    row = lambda vector: vector.reshape(1, -1)

    dma = pltpu.SemaphoreType.DMA
    (packed_params,) = call(
        pack_params, (shape_of((nc, prows, LANES)),), (ema_in.T, ema_keep.T, ema_out.T, row(ema_skip)), "pack_params",
        scratch=[pltpu.VMEM((prows, LANES), F32), dma((max(nc, 4),))], hbm=range(4), out_hbm=(0,), limit=8,
    )
    params = exchange(packed_params, "chan")
    x, xt, low, own1, own2 = call(
        functools.partial(prepare_kernel, nc),
        (
            shape_of((toks, dim), BF16), shape_of((width * SUBS, LANES)), shape_of((toks, dim), BF16),
            shape_of((w1_rows, units), BF16), shape_of((w2_rows, units), BF16),
        ),
        (token_ids, embed, row(attn_gain), v_proj, r_proj, z_proj, up_proj, o_proj, down_proj), "prepare",
        scratch=[
            pltpu.VMEM((rows, width), jnp.int32), pltpu.VMEM((vocab, dim), BF16), pltpu.VMEM((1, dim), F32),
            pltpu.VMEM((toks, dim), BF16), pltpu.VMEM((toks, dim), BF16), pltpu.VMEM((w1_rows, units), BF16),
            pltpu.VMEM((w2_rows, units), BF16), dma((3,)), dma((9,)), dma((4,)),
        ],
        hbm=range(9), out_hbm=(0, 2, 3, 4), after=("pack_params",),
    )
    own1, own2, params = lax.optimization_barrier((own1, own2, params))
    far1 = swap(own1, 2)
    near1 = swap(own1, 1)
    far2 = swap(own2, 2)
    near2 = swap(own2, 1)
    pt, ends = call(
        functools.partial(scan_end_kernel, nc, nd),
        (shape_of((prows * SUBS, LANES)), shape_of((ns, nd * SUBS, LANES))),
        (params, xt), "scan_end", scratch=[pltpu.VMEM((nd * SUBS, LANES), F32), dma((ns,))], out_hbm=(1,), after=("prepare",), limit=8,
    )
    far1, _ = lax.optimization_barrier((far1, pt))
    both1 = swap(far1, 1)
    first = (own1, near1, far1, both1)
    ends = exchange(ends, "seq")
    v_pre, r_pre, values, z_all, values_far = call(
        functools.partial(project_kernel, dim),
        (
            shape_of((toks, nc * units)), shape_of((toks, nc * units)), shape_of((toks, nc * units), BF16),
            shape_of((dim, zdim), BF16), shape_of((toks, nc * units), BF16),
        ),
        (low,) + first, "project",
        scratch=[
            pltpu.VMEM((toks, dim), BF16), pltpu.VMEM((toks, nc * units), F32), pltpu.VMEM((4, w1_rows, units), BF16),
            dma((5,)), dma((8,)),
        ],
        hbm=range(5), out_hbm=(0, 4), after=("scan_end",), limit=16,
    )
    mixed_pre, mixed_low, z_pre, attn, context, gated, state_in = call(
        functools.partial(mix_kernel, nc, nd, span),
        (
            shape_of((toks, dim)), shape_of((toks, dim), BF16), shape_of((toks, zdim)), shape_of((toks, width)),
            shape_of((toks, nc * units)), shape_of((toks, nc * units), BF16), shape_of((nd * SUBS, LANES)),
        ),
        (
            valid_counts, ends, xt, pt, z_all, values, r_pre, row(q_gain), row(k_gain), row(q_bias),
        ),
        "mix", scratch=[pltpu.VMEM((width * SUBS, LANES), F32), pltpu.VMEM((nd * SUBS, LANES), F32), pltpu.VMEM((toks, dim), BF16), dma((2,))],
        smem=(0,), free=range(7, 10), out_hbm=(1, 6), after=("project",), limit=16,
    )
    far2, gated = lax.optimization_barrier((far2, gated))
    both2 = swap(far2, 1)
    second = (own2, near2, far2, both2)
    out_rows = toks * (dim // units)
    out, g_mid, g_gated, keep1, send1, ffn_grad = call(
        functools.partial(ffn_kernel, nc, dim),
        (
            shape_of((out_rows, units), BF16), shape_of((toks, dim)), shape_of((toks, nc * units)),
            shape_of((2, w2_rows, units), BF16), shape_of((2, w2_rows, units), BF16), shape_of((1, dim)),
        ),
        (gated,) + second + (x, grad_out, row(ffn_gain)),
        "ffn",
        scratch=[
            pltpu.VMEM((toks, nc * units), BF16), pltpu.VMEM((toks, nc * units), BF16),
            pltpu.VMEM((toks, dim), BF16), pltpu.VMEM((out_rows, units), BF16), pltpu.VMEM((toks, dim), F32),
            pltpu.VMEM((toks, dim), BF16), pltpu.VMEM((4, w2_rows, units), BF16), pltpu.VMEM((4, w2_rows, units), BF16),
            dma((13 + rp,)), dma((4,)),
        ],
        hbm=range(1, 7), free=(7,), out_hbm=(0, 1, 3, 4), after=("mix",), limit=32,
    )
    got1 = swap(send1, 1)
    grad_v, grad_r, g_z, gmt, carries, small, skip_grad = call(
        functools.partial(attn_back_kernel, nc, nd),
        (
            shape_of((toks, nc * units), BF16), shape_of((toks, nc * units), BF16), shape_of((toks, zdim)),
            shape_of((width * SUBS, LANES)), shape_of((ns, nd * SUBS, LANES), BF16), shape_of((SUBS, zdim)),
            shape_of((SUBS, LANES)),
        ),
        (
            g_gated, r_pre, v_pre, context, attn, values_far, z_pre, mixed_pre, xt, z_all, pt, row(q_gain), row(k_gain),
            row(q_bias),
        ),
        "attn_back",
        scratch=[
            pltpu.VMEM((nd * SUBS, LANES), BF16), pltpu.VMEM((toks, nc * units), BF16), pltpu.VMEM((toks, nc * units), BF16),
            dma((ns,)), dma((2,)),
        ],
        free=(2, 5, 11, 12, 13), out_hbm=(0, 1, 4), after=("ffn",), limit=20,
    )
    carries = exchange(carries, "seq")
    fast = ns == 8
    mine1, theirs1 = call(
        add_core_first, (shape_of((w2_rows, units), BF16),) * 2, (keep1, got1), "add_core_first",
        scratch=[pltpu.VMEM((w2_rows, units), BF16), pltpu.VMEM((w2_rows, units), BF16), dma((8,))],
        free=range(2), out_hbm=range(2), after=("attn_back",),
    )
    far_got1 = swap(theirs1, 2)
    g2_rows = -(-w1_rows // (16 * ns)) * 16 * ns
    keep2, send2, send4 = call(
        functools.partial(grads_kernel, nc, dim, zrows),
        (shape_of((2, g2_rows, units), BF16), shape_of((g2_rows, units), BF16), shape_of((g2_rows, units), BF16)),
        (low, grad_v, grad_r, mixed_low, g_z), "grads",
        scratch=[
            pltpu.VMEM((dim, zdim), F32), pltpu.VMEM((toks, dim), BF16), pltpu.VMEM((toks, nc * units), BF16),
            pltpu.VMEM((toks, nc * units), BF16), pltpu.VMEM((toks, dim), BF16), pltpu.VMEM((4, g2_rows, units), BF16),
            dma((4,)), dma((4,)),
        ],
        hbm=range(4), out_hbm=range(3), after=("add_core_first",), limit=24,
    )
    got2, got4 = swap(send2, 1), swap(send4, 1)
    shared, sums = call(
        functools.partial(scans_kernel, nd, dim),
        (shape_of((toks, dim)), shape_of((3, nd * SUBS, LANES))),
        (grad_v, grad_r) + first + (pt, state_in, xt, gmt), "scans",
        scratch=[
            pltpu.VMEM((toks, dim), F32), pltpu.VMEM((3, nd * SUBS, LANES), F32), pltpu.VMEM((nd * SUBS, LANES), F32),
            pltpu.VMEM((4, 2 * dim, units), BF16), pltpu.VMEM((toks, nc * units), BF16),
            pltpu.VMEM((toks, nc * units), BF16), dma((7,)),
        ],
        hbm=(0, 1, 2, 3, 4, 5, 7), out_hbm=range(2), after=("grads",), limit=24,
    )
    mine2, theirs2 = call(
        add_core_second, (shape_of((g2_rows, units), BF16),) * 2, (keep2, got2, got4), "add_core_second",
        far=range(3), out_far=range(2), after=("scans",),
    )
    far_got2 = swap(theirs2, 2)
    half_parts = lambda parts: tuple(rows // 2 for rows in parts)

    def halves(level, pairs, parts, name, after):
        rows = sum(sum(part) for part in parts) // 2
        return call(
            functools.partial(add_halves, level, parts), (shape_of((rows, units), BF16),) * 2, pairs, name,
            free=range(len(pairs)), out_free=range(2), after=after,
        )

    def joined(level, pair, parts, name, after):
        return call(
            functools.partial(join_halves, level, parts), (shape_of((2 * pair[0].shape[0], units), BF16),), pair, name,
            free=range(2), out_free=(0,), after=after,
        )[0]

    def add_two(pair, name, after):
        return call(
            add_plain, (shape_of(pair[0].shape, BF16),), pair, name, free=range(2), out_free=(0,), after=after
        )[0]

    if fast:
        keep1, send1 = halves(0, (mine1, far_got1), ((w2_rows,),), "x_first", ("add_core_second",))
        x_got1 = swap(send1, 1, "seq")
    room = rest_rows(nd)
    f_rows = -(-(vocab // 2 + room) // (16 * ns)) * 16 * ns
    f_keep, f_send = call(
        functools.partial(last_kernel, nc, nd, ns, span),
        (shape_of((2, f_rows, units), BF16),) * 2,
        (carries, gmt, pt, shared, x, row(attn_gain), g_mid, token_ids, sums, small, skip_grad, ffn_grad),
        "last",
        scratch=[
            pltpu.VMEM((width * SUBS, LANES), F32), pltpu.VMEM((vocab, dim), F32),
            pltpu.VMEM((3 * nd * SUBS, LANES), F32), pltpu.VMEM((nc, room, LANES), F32),
            pltpu.VMEM((toks, dim), F32), pltpu.VMEM((toks, dim), BF16), pltpu.VMEM((1, dim), F32),
            pltpu.VMEM((toks, dim), F32), pltpu.VMEM((rows, width), jnp.int32), pltpu.VMEM((3, nd * SUBS, LANES), F32),
            dma((6,)),
        ],
        hbm=range(3, 9), out_free=range(2), after=("x_first",) if fast else ("add_core_second",), limit=16,
    )
    f_got = swap(f_send, 1)
    f_mine, f_theirs = call(
        add_core, (shape_of((f_rows, units), BF16),) * 2, (f_keep, f_got), "add_core_last", free=range(2),
        out_free=range(2), after=("last",),
    )
    f_far = swap(f_theirs, 2)
    if fast:
        parts1, parts2 = (w2_rows // 2,), (g2_rows // 2, f_rows // 2)
        keep1, send1 = halves(1, (keep1, x_got1), (parts1,), "z_first", ("add_core_last",))
        got1 = swap(send1, 2, "seq")
        keep2, send2 = halves(
            0, (mine2, far_got2, f_mine, f_far), ((g2_rows,), (f_rows,)), "x_second", ("z_first",)
        )
        got2 = swap(send2, 1, "seq")
        parts1 = half_parts(parts1)
        keep1, send1 = halves(2, (keep1, got1), (parts1,), "zz_first", ("x_second",))
        got1 = swap(send1, 4, "seq")
        out, keep2 = lax.optimization_barrier((out, keep2))
        out_far, out_near = swap(out, 2), swap(out, 1)
        keep2, send2 = halves(1, (keep2, got2), (parts2,), "z_second", ("zz_first",))
        got2 = swap(send2, 2, "seq")
        parts1, parts2 = half_parts(parts1), half_parts(parts2)
        keep1 = add_two((keep1, got1), "sum_first", ("z_second",))
        got1 = swap(keep1, 4, "seq")
        keep2, send2 = halves(2, (keep2, got2), (parts2,), "zz_second", ("sum_first",))
        got2 = swap(send2, 4, "seq")
        parts2 = half_parts(parts2)
        keep1 = joined(2, (keep1, got1), parts1, "join_zz_first", ("zz_second",))
        got1 = swap(keep1, 2, "seq")
        keep2 = add_two((keep2, got2), "sum_second", ("join_zz_first",))
        got2 = swap(keep2, 4, "seq")
        out_far, keep2 = lax.optimization_barrier((out_far, keep2))
        out_both = swap(out_far, 1)
        u1 = joined(1, (keep1, got1), tuple(2 * rows for rows in parts1), "join_z_first", ("sum_second",))
        v1 = swap(u1, 1, "seq")
        keep2 = joined(2, (keep2, got2), parts2, "join_zz_second", ("join_z_first",))
        got2 = swap(keep2, 2, "seq")
        follow = ("join_zz_second",)
    else:
        out_far, out_near = swap(out, 2), swap(out, 1)
        out_both = swap(out_far, 1)
        u1 = v1 = seq_sum(add_two((mine1, far_got1), "add_first", ()), ns, "sum_first")
        u2 = v2 = seq_sum(add_two((mine2, far_got2), "add_second", ()), ns, "sum_second")
        f_own = seq_sum(add_two((f_mine, f_far), "add_last", ()), ns, "sum_last")
        follow = ()
    (output,) = call(
        output_kernel, (shape_of((rows, width, dim), BF16),), (out, out_near, out_far, out_both), "output",
        free=range(4), out_free=(0,), after=follow, limit=8,
    )
    if fast:
        u2 = joined(1, (keep2, got2), tuple(2 * rows for rows in parts2), "join_z_second", ("output",))
        v2 = swap(u2, 1, "seq")
    up_grad, o_grad, down_grad = call(
        functools.partial(unpack_first, dim, urows),
        (shape_of(up_proj.shape), shape_of(o_proj.shape), shape_of(down_proj.shape)),
        (u1, v1), "unpack_first", free=range(2), out_free=range(3), scratch=[pltpu.VMEM((w2_rows, units), BF16)],
        after=("join_z_second",) if fast else ("output",),
    )
    if fast:
        (f_own,) = call(
            functools.partial(join_part, g2_rows // 2), (shape_of((f_rows, units), BF16),), (u2, v2), "collect",
            free=range(2), out_free=(0,), after=("unpack_first",),
        )
    f_far, f_near = swap(f_own, 2), swap(f_own, 1)
    v_grad, r_grad, z_grad = call(
        functools.partial(unpack_second, dim, zrows),
        (shape_of(v_proj.shape), shape_of(r_proj.shape), shape_of(z_proj.shape)),
        (u2, v2), "unpack_second", free=range(2), out_free=range(3), scratch=[pltpu.VMEM((g2_rows, units), BF16)],
        after=("collect",) if fast else ("unpack_first",),
    )
    embed_grad, ag, gi, gk, go, gs, fg, qg, kg, qb = call(
        functools.partial(finish_kernel, nc, nd),
        (
            shape_of((vocab, dim)), shape_of((1, dim)), shape_of((nd, LANES)), shape_of((nd, LANES)),
            shape_of((nd, LANES)), shape_of((1, LANES)), shape_of((1, dim)), shape_of((1, zdim)),
            shape_of((1, zdim)), shape_of((1, zdim)),
        ),
        (f_own, f_near, f_far, swap(f_far, 1)), "finish", free=range(4), out_free=range(10),
        scratch=[pltpu.VMEM((nc, room, LANES), F32)], after=("unpack_second",), limit=8,
    )
    flat = lambda value: value.reshape(-1)
    return (
        output, embed_grad, flat(ag), gi.T, gk.T, go.T, flat(gs), z_grad, flat(qg), flat(kg), flat(qb), v_grad, r_grad,
        o_grad, flat(fg), up_grad, down_grad,
    )


def solution(mesh):
    placed = (
        P(None, "seq"), P(), P(), P(), P("chan", None), P("chan", None), P("chan", None), P("chan"), P("chan", None),
        P(), P(), P(), P(None, "chan"), P(None, "chan"), P("chan", None), P(), P(None, "chan"), P("chan", None),
        P(None, "seq", None),
    )
    return jax.shard_map(
        body,
        mesh=mesh,
        in_specs=placed,
        out_specs=(
            P(None, "seq", None), P(), P(), P("chan", None), P("chan", None), P("chan", None), P("chan"),
            P("chan", None), P(), P(), P(), P(None, "chan"), P(None, "chan"), P("chan", None), P(), P(None, "chan"),
            P("chan", None),
        ),
        check_vma=False,
    )
```

```python
import functools

import jax
import jax.numpy as jnp
from jax import lax
from jax.experimental import pallas as pl
from jax.experimental.pallas import tpu as pltpu
from jax.sharding import PartitionSpec as P

SEQMAX = 4096
HIGH = lax.Precision.HIGHEST
EPS = 1e-06
F32 = jnp.float32
BF16 = jnp.bfloat16
LANES = 128
SUBS = 8
MIB = 1024 * 1024


def sigmoid(u):
    return 0.5 * jnp.tanh(0.5 * u) + 0.5


def silu_slope(pre):
    sigma = sigmoid(pre)
    return sigma * (1.0 + pre * (1.0 - sigma))


def mm(left, right, dims, precision=None):
    return lax.dot_general(
        left, right, ((dims[0], dims[1]), ((), ())), precision=precision, preferred_element_type=F32
    )


def dot(left, right):
    return mm(left, right, ((1,), (0,)))


def dot_rows(left, right):
    return mm(left, right, ((0,), (0,)))


def dot_cols(left, right):
    return mm(left, right, ((1,), (1,)))


def exact(left, right, dims):
    return mm(left.astype(F32), right.astype(F32), dims, HIGH)


def shape_of(dims, dtype=F32):
    return jax.ShapeDtypeStruct(dims, dtype)


TOKENS = {}


def call(
    kernel, outs, args, name, scratch=(), smem=(), hbm=(), free=(), far=(), out_hbm=(), out_free=(), out_far=(), after=(), limit=16
):

    waits = [TOKENS[key] for key in after]
    hbm, out_hbm = {*hbm, *far}, {*out_hbm, *out_far}
    count, made = len(args), len(outs)

    def run(*refs):
        rest = refs[count + len(waits) :]
        kernel(*refs[:count], *rest[:made], *rest[made + 1 :])

    def spec(at):
        if at >= count or (at in hbm and at not in far):
            return pl.BlockSpec(memory_space=pltpu.HBM)
        return pl.BlockSpec(memory_space=pltpu.SMEM if at in smem else pltpu.VMEM)

    def held(at, value):
        if at < count and (at in smem or at in free):
            return value
        return pltpu.with_memory_space_constraint(value, pltpu.HBM if at in hbm or at >= count else pltpu.VMEM)

    def result(at, out):
        if at in out_free:
            return out
        return (pltpu.HBM if at in out_hbm or at == made else pltpu.VMEM)(out.shape, out.dtype)

    shapes = list(outs) + [shape_of((SUBS, LANES))]
    *results, TOKENS[name] = pl.pallas_call(
        run,
        out_shape=[result(at, out) for at, out in enumerate(shapes)],
        in_specs=[spec(at) for at in range(count + len(waits))],
        out_specs=[
            pl.BlockSpec(memory_space=pltpu.HBM if (at in out_hbm and at not in out_far) or at == made else pltpu.VMEM)
            for at in range(made + 1)
        ],
        scratch_shapes=list(scratch),
        name=name,
        cost_estimate=pl.CostEstimate(flops=1, bytes_accessed=1, transcendentals=0),
        compiler_params=pltpu.CompilerParams(vmem_limit_bytes=limit * MIB),
    )(*[held(at, value) for at, value in enumerate([*args, *waits])])
    return results


def move(copies, sems):
    for copy in run_copies(copies, sems):
        copy.wait()


def run_copies(copies, sems):
    started = [pltpu.make_async_copy(src, dst, sems.at[at]) for at, (src, dst) in enumerate(copies)]
    for copy in started:
        copy.start()
    return started


def pack_params(in_ref, keep_ref, out_ref, skip_ref, p_ref, sems):
    nd, lanes = in_ref.shape
    copies = [(ref, p_ref.at[at * nd : (at + 1) * nd, :]) for at, ref in enumerate((in_ref, keep_ref, out_ref))]
    copies.append((skip_ref, p_ref.at[3 * nd : 3 * nd + 1, :]))
    move(copies, sems)
    rest = p_ref.shape[0] - 3 * nd
    p_ref[3 * nd :, :] = jnp.broadcast_to(p_ref[3 * nd : 3 * nd + 1, :], (rest, lanes))


def first_copies(v_ref, r_ref, z_ref, buf):
    dim = v_ref.shape[0]
    zrows = z_ref.shape[0] // 2
    copies = [(v_ref, buf.at[0:dim, :]), (r_ref, buf.at[dim : 2 * dim, :])]
    for half in range(2):
        copies.append(
            (
                z_ref.at[half * zrows : (half + 1) * zrows, :],
                buf.at[2 * dim : 2 * dim + zrows, half * LANES : (half + 1) * LANES],
            )
        )
    return copies


def second_copies(up_ref, o_ref, down_ref, buf):
    dim, units = up_ref.shape
    urows = o_ref.shape[0]
    copies = [(up_ref, buf.at[0:dim, :])]
    for at, ref in enumerate((o_ref, down_ref)):
        for half in range(dim // units):
            start = dim + (dim // units * at + half) * urows
            copies.append((ref.at[:, half * units : (half + 1) * units], buf.at[start : start + urows, :]))
    return copies


def prepare_kernel(
    nc, ids_at, table_at, gain_at, v_at, r_at, z_at, up_at, o_at, down_at,
    x_to, xt_ref, low_to, w1_to, w2_to,
    ids_ref, embed_ref, gain_ref, x_ref, low_ref, w1_ref, w2_ref, sems, w_sems, out_sems,
):
    entering = run_copies(first_copies(v_at, r_at, z_at, w1_ref), w_sems.at[0:4])
    started = run_copies([(ids_at, ids_ref), (table_at, embed_ref), (gain_at, gain_ref)], sems)
    later = run_copies(second_copies(up_at, o_at, down_at, w2_ref), w_sems.at[4:9])
    for copy in entering:
        copy.wait()
    leaving = run_copies([(w1_ref, w1_to)], out_sems.at[0:1])
    rp = x_ref.shape[0] // ids_ref.shape[1]
    width = ids_ref.shape[1]
    vocab = embed_ref.shape[0]
    chan = lax.axis_index("chan")
    for copy in started:
        copy.wait()
    for row in range(rp):
        ids = ids_ref[pl.ds(chan * rp + row, 1), :]
        onehot = jnp.where(lax.broadcasted_iota(jnp.int32, (vocab, width), 0) == ids, 1.0, 0.0).astype(BF16)
        x = dot_rows(onehot, embed_ref[...])
        x_ref[row * width : (row + 1) * width, :] = x.astype(BF16)
        normed = x * lax.rsqrt(jnp.mean(x * x, axis=-1, keepdims=True) + EPS) * gain_ref[...]
        low_ref[row * width : (row + 1) * width, :] = normed.astype(BF16)
        for chunk in range(nc):
            xt_ref[pl.ds(row * nc + chunk, width, stride=SUBS), :] = normed[
                :, chunk * LANES : (chunk + 1) * LANES
            ]
        for copy in later:
            copy.wait()
        later = []
        leaving += run_copies([(w2_ref, w2_to)], out_sems.at[1:2]) if row == 0 else []
    leaving += run_copies([(x_ref, x_to), (low_ref, low_to)], out_sems.at[2:4])
    for copy in leaving:
        copy.wait()


def tile(ref, at):
    return ref[at * SUBS : (at + 1) * SUBS, :]


def step_tile(ref, t):
    return ref[pl.ds(pl.multiple_of(t * SUBS, SUBS), SUBS), :]


def scan_end_kernel(nc, nd, p0, p1, p2, p3, xt_ref, pt_ref, end_ref, p_ref, buf, sems):
    width = xt_ref.shape[0] // SUBS
    prows = p_ref.shape[1]
    chan = lax.axis_index("chan")
    for j, ref in enumerate((p0, p1, p2, p3)):
        p_ref[jnp.bitwise_xor(chan, j)] = ref[...]
    for sub in range(SUBS):
        pt_ref[pl.ds(sub, prows, stride=SUBS), :] = p_ref[sub % nc]
    keep = [tile(pt_ref, nd + k) for k in range(nd)]

    def step(block, states):
        states = list(states)
        for u in range(8):
            x = step_tile(xt_ref, block * 8 + u)
            states = [q * s + x for q, s in zip(keep, states)]
        return tuple(states)

    zero = jnp.zeros((SUBS, LANES), F32)
    states = lax.fori_loop(0, width // 8, step, (zero,) * nd)
    buf[...] = jnp.concatenate(states, axis=0)
    for copy in run_copies([(buf, end_ref.at[at]) for at in range(end_ref.shape[0])], sems):
        copy.wait()


def project_kernel(
    dim, low_at, h0, h1, h2, h3, vpre_to, rpre_ref, val_ref, z_ref, val_to, low_ref, vpre_ref, buf, sems, out_sems
):
    chan = lax.axis_index("chan")
    units = h0.shape[1]
    zrows = h0.shape[0] - 2 * dim
    started = run_copies([(low_at, low_ref)] + [(ref, buf.at[j]) for j, ref in enumerate((h0, h1, h2, h3))], sems)
    started[0].wait()
    low = low_ref[...]
    leaving = []
    for j in range(4):
        started[1 + j].wait()
        w = buf.at[j]
        cols = slice(j * units, (j + 1) * units)
        v_pre = dot(low, w[0:dim, :])
        vpre_ref[:, cols] = v_pre
        val_ref[:, cols] = (v_pre * sigmoid(v_pre)).astype(BF16)
        leaving += run_copies(
            [(vpre_ref.at[:, cols], vpre_to.at[:, cols]), (val_ref.at[:, cols], val_to.at[:, cols])],
            out_sems.at[2 * j : 2 * j + 2],
        )
        rpre_ref[:, cols] = dot(low, w[dim : 2 * dim, :])
        start = pl.multiple_of(jnp.bitwise_xor(chan, j) * 2 * zrows, 2 * zrows)
        half = w[2 * dim : 2 * dim + zrows, :]
        z_ref[pl.ds(start, 2 * zrows), :] = jnp.concatenate([half[:, :LANES], half[:, LANES:]], axis=0)
    for copy in leaving:
        copy.wait()


def whole_keep(keep, width):
    whole = keep
    power = 1
    while power < width:
        whole = whole * whole
        power *= 2
    return whole


def weights_of(pt_ref, nd):
    amp = pt_ref[0 : nd * SUBS, :]
    keep = pt_ref[nd * SUBS : 2 * nd * SUBS, :]
    out = pt_ref[2 * nd * SUBS : 3 * nd * SUBS, :]
    root = jnp.sqrt(1.0 - keep * keep)
    return amp, keep, out, root


def split_tiles(value, nd):
    return [value[k * SUBS : (k + 1) * SUBS, :] for k in range(nd)]


def tree_sum(values):
    values = list(values)
    while len(values) > 1:
        values = [sum(values[i : i + 2][1:], values[i]) for i in range(0, len(values), 2)]
    return values[0]


def scale_of(x):
    return lax.rsqrt(jnp.mean(x * x, axis=-1, keepdims=True) + EPS)


def mix_kernel(
    nc, nd, span, counts_ref, ends_ref, xt_ref, pt_ref, z_ref, val_ref, rpre_ref, qg_ref, kg_ref, qb_ref,
    mpre_ref, mlow_to, zpre_ref, attn_ref, ctx_ref, gated_ref, sin_to, sm_ref, sin_ref, mlow_ref, sems,
):
    width = xt_ref.shape[0] // SUBS
    rp = SUBS // nc
    place = lax.axis_index("seq")
    chan = lax.axis_index("chan")
    amp, keep_all, out_all, root = weights_of(pt_ref, nd)
    whole = whole_keep(keep_all, width)
    per = span // width
    first = place // per * per

    def gather(n, state):
        return state * whole + ends_ref[n].astype(F32)

    start = lax.fori_loop(first, place, gather, jnp.zeros_like(whole))
    sin_ref[...] = start
    (leaving,) = run_copies([(sin_ref, sin_to)], sems.at[:1])
    keep = split_tiles(keep_all, nd)
    weight = split_tiles(out_all * amp * root, nd)

    def step(block, states):
        states = list(states)
        for u in range(8):
            t = block * 8 + u
            x = step_tile(xt_ref, t)
            states = [q * s + x for q, s in zip(keep, states)]
            sm_ref[pl.ds(pl.multiple_of(t * SUBS, SUBS), SUBS), :] = tree_sum(
                [w * s for w, s in zip(weight, states)]
            )
        return tuple(states)

    lax.fori_loop(0, width // 8, step, tuple(split_tiles(start, nd)))
    skip = pt_ref[3 * nd * SUBS : 3 * nd * SUBS + SUBS, :]
    for row in range(rp):
        rows = slice(row * width, (row + 1) * width)
        for chunk in range(nc):
            at = row * nc + chunk
            lanes = slice(chunk * LANES, (chunk + 1) * LANES)
            own = xt_ref[pl.ds(at, width, stride=SUBS), :]
            pre = sm_ref[pl.ds(at, width, stride=SUBS), :] + skip[at : at + 1, :] * own
            mpre_ref[rows, lanes] = pre
            mlow_ref[rows, lanes] = (pre * sigmoid(pre)).astype(BF16)
    (left,) = run_copies([(mlow_ref, mlow_to)], sems.at[1:])
    z_pre = dot(mlow_ref[...], z_ref[...])
    zpre_ref[...] = z_pre
    zeta = z_pre * sigmoid(z_pre)
    queries = (zeta * qg_ref[...] + qb_ref[...]).astype(BF16)
    keys = (zeta * kg_ref[...]).astype(BF16)
    scale = z_pre.shape[1] ** (-0.5)
    pieces = counts_ref.shape[0] // (rp * nc)
    begin = place * width
    piece = begin // span
    inner = begin - piece * span
    for row in range(rp):
        rows = slice(row * width, (row + 1) * width)
        count = counts_ref[(chan * rp + row) * pieces + piece]
        valid = lax.broadcasted_iota(jnp.int32, (width, width), 1) < count - inner
        scores = jnp.where(valid, dot_cols(queries[rows, :], keys[rows, :]) * scale, -1e30)
        top = jnp.max(scores, axis=-1, keepdims=True)
        weights = jnp.where(valid, jnp.exp(scores - top), 0.0)
        empty = jnp.where(count > inner, 0.0, 1.0)
        attn = weights / (jnp.sum(weights, axis=-1, keepdims=True) + empty)
        attn_ref[rows, :] = attn
        context = dot(attn.astype(BF16), val_ref[rows, :])
        ctx_ref[rows, :] = context
        r_pre = rpre_ref[rows, :]
        gated_ref[rows, :] = (r_pre * sigmoid(r_pre) * context).astype(BF16)
    leaving.wait()
    left.wait()


def ffn_kernel(
    nc, dim, gated_ref, h0, h1, h2, h3, x_at, grad_ref, fgain_ref,
    out_to, gmid_to, ggated_ref, keep_to, send_to, fg_ref,
    hid_ref, gup_ref, g_ref, out_ref, gmid_ref, x_ref, up_ref, o_ref, down_ref, part_ref, sems, out_sems, part_sems,
):
    units = h0.shape[1]
    rp = grad_ref.shape[0] // nc
    width = grad_ref.shape[1]
    chan = lax.axis_index("chan")
    urows = (h0.shape[0] - dim) // 4
    halves = dim // units
    hs = (h0, h1, h2, h3)

    def shards(ref, which):
        return [
            (
                h.at[dim + (which * halves + half) * urows : dim + (which * halves + half + 1) * urows, :],
                ref.at[j * urows : (j + 1) * urows, half * units : (half + 1) * units],
            )
            for j, h in enumerate(hs)
            for half in range(halves)
        ]

    copies = [(x_at, x_ref)] + shards(o_ref, 0)
    copies += [(h.at[0:dim, :], up_ref.at[:, j * units : (j + 1) * units]) for j, h in enumerate(hs)]
    copies += [(grad_ref.at[chan * rp + row], g_ref.at[row * width : (row + 1) * width, :]) for row in range(rp)]
    copies += shards(down_ref, 1)
    started = run_copies(copies, sems)
    first = 1 + 4 * halves
    for copy in started[:first]:
        copy.wait()
    middle = x_ref[...].astype(F32) + dot(gated_ref[...], o_ref[...])
    r = scale_of(middle)
    n = middle * r
    fgain = fgain_ref[...]
    ffn_low = (n * fgain).astype(BF16)
    for copy in started[first:]:
        copy.wait()
    g = g_ref[...]
    up_pre = dot(ffn_low, up_ref[...])
    sigma = sigmoid(up_pre)
    hid_ref[...] = (up_pre * sigma).astype(BF16)
    gup_ref[...] = (dot_cols(g, down_ref[...]) * (sigma * (1.0 + up_pre * (1.0 - sigma)))).astype(BF16)
    g_in = dot_cols(gup_ref[...], up_ref[...])
    h = g_in * fgain
    g_mid = g.astype(F32) + r * (h - n * jnp.mean(h * n, axis=-1, keepdims=True))
    gmid_ref[...] = g_mid
    g_branch = g_mid.astype(BF16)
    leaving = run_copies([(gmid_ref, gmid_to)], out_sems.at[0:1])
    fg_ref[...] = jnp.sum(g_in * n, axis=0, keepdims=True)

    def leave(begin, rows, which):
        part = slice(begin, begin + rows)
        return run_copies(
            [(part_ref.at[j, part, :], (keep_to, send_to)[j % 2].at[j // 2, part, :]) for j in (1, 3, 0, 2)],
            part_sems.at[4 * which : 4 * which + 4],
        )

    grad = dot_rows(ffn_low, gup_ref[...]).astype(BF16)
    for j in range(4):
        part_ref[j, 0:dim, :] = grad[:, j * units : (j + 1) * units]
    leaving += leave(0, dim, 0)
    for which, (left, right) in enumerate(((hid_ref, g), (gated_ref, g_branch))):
        grad = dot_rows(left[...], right).astype(BF16)
        begin = dim + (1 - which) * halves * urows
        for j in range(4):
            for half in range(halves):
                part_ref[j, begin + half * urows : begin + (half + 1) * urows, :] = grad[
                    j * urows : (j + 1) * urows, half * units : (half + 1) * units
                ]
        leaving += leave(begin, halves * urows, 1 + which)
    ggated_ref[...] = dot_cols(g_branch, o_ref[...])
    out = (middle + dot(hid_ref[...], down_ref[...])).astype(BF16)
    toks = g_ref.shape[0]
    for half in range(halves):
        out_ref[half * toks : (half + 1) * toks, :] = out[:, half * units : (half + 1) * units]
    leaving += run_copies([(out_ref, out_to)], out_sems.at[1:2])
    for copy in leaving:
        copy.wait()


def attn_back_kernel(
    nc, nd, ggated_ref, rpre_ref, vpre_ref, ctx_ref, attn_ref, val_ref, zpre_ref, mpre_ref, xt_ref, z_ref, pt_ref,
    qg_ref, kg_ref, qb_ref,
    gv_to, gr_to, gz_ref, gmt_ref, carry_ref, small_ref, skip_ref, buf, gv_ref, gr_ref, sems, out_sems,
):
    width = xt_ref.shape[0] // SUBS
    rp = SUBS // nc
    z_pre = zpre_ref[...]
    sigma = sigmoid(z_pre)
    zeta = z_pre * sigma
    queries = (zeta * qg_ref[...] + qb_ref[...]).astype(BF16)
    keys = (zeta * kg_ref[...]).astype(BF16)
    scale = z_pre.shape[1] ** (-0.5)
    parts_q, parts_k = [], []
    for row in range(rp):
        rows = slice(row * width, (row + 1) * width)
        g_gated = ggated_ref[rows, :]
        r_pre = rpre_ref[rows, :]
        sr = sigmoid(r_pre)
        g_context = (g_gated * (r_pre * sr)).astype(BF16)
        gr_ref[rows, :] = (g_gated * ctx_ref[rows, :] * (sr * (1.0 + r_pre * (1.0 - sr)))).astype(BF16)
        attn = attn_ref[rows, :]
        g_values = dot_rows(attn.astype(BF16), g_context)
        gv_ref[rows, :] = (g_values * silu_slope(vpre_ref[rows, :])).astype(BF16)
        g_attn = dot_cols(g_context, val_ref[rows, :])
        g_scores = attn * (g_attn - jnp.sum(attn * g_attn, axis=-1, keepdims=True))
        parts_q.append(exact(g_scores, keys[rows, :], ((1,), (0,))) * scale)
        parts_k.append(exact(g_scores, queries[rows, :], ((0,), (0,))) * scale)
    leaving = run_copies([(gv_ref, gv_to), (gr_ref, gr_to)], out_sems)
    g_q = jnp.concatenate(parts_q, axis=0)
    g_k = jnp.concatenate(parts_k, axis=0)
    small_ref[...] = jnp.concatenate(
        [
            jnp.sum(g_q * zeta, axis=0, keepdims=True),
            jnp.sum(g_k * zeta, axis=0, keepdims=True),
            jnp.sum(g_q, axis=0, keepdims=True),
            jnp.zeros((SUBS - 3, z_pre.shape[1]), F32),
        ],
        axis=0,
    )
    g_z = (g_q * qg_ref[...] + g_k * kg_ref[...]) * (sigma * (1.0 + z_pre * (1.0 - sigma)))
    gz_ref[...] = g_z
    skips = []
    for row in range(rp):
        rows = slice(row * width, (row + 1) * width)
        for chunk in range(nc):
            at = row * nc + chunk
            lanes = slice(chunk * LANES, (chunk + 1) * LANES)
            g_mixed = exact(g_z[rows, :], z_ref[lanes, :], ((1,), (1,))) * silu_slope(mpre_ref[rows, lanes])
            gmt_ref[pl.ds(at, width, stride=SUBS), :] = g_mixed
            skips.append(jnp.sum(g_mixed * xt_ref[pl.ds(at, width, stride=SUBS), :], axis=0, keepdims=True))
    skip_ref[...] = jnp.concatenate(skips, axis=0)
    keep = [tile(pt_ref, nd + k) for k in range(nd)]

    def step(block, carries):
        carries = list(carries)
        for u in range(8):
            gm = step_tile(gmt_ref, width - 1 - (block * 8 + u))
            carries = [q * (c + gm) for q, c in zip(keep, carries)]
        return tuple(carries)

    zero = jnp.zeros((SUBS, LANES), F32)
    carries = lax.fori_loop(0, width // 8, step, (zero,) * nd)
    buf[...] = jnp.concatenate(carries, axis=0).astype(BF16)
    for copy in leaving:
        copy.wait()
    for copy in run_copies([(buf, carry_ref.at[at]) for at in range(carry_ref.shape[0])], sems):
        copy.wait()


def grads_kernel(
    nc, dim, zrows, low_at, gv_at, gr_at, mlow_at, gz_ref, keep_to, send1_to, more1_to, send3_to, more3_to,
    zg_ref, low_ref, gv_ref, gr_ref, mlow_ref, part_ref, sems, part_sems,
):
    units = gv_ref.shape[1] // nc
    chan = lax.axis_index("chan")
    started = run_copies([(mlow_at, mlow_ref), (low_at, low_ref), (gv_at, gv_ref), (gr_at, gr_ref)], sems)
    started[0].wait()
    zg_ref[...] = exact(mlow_ref[...], gz_ref[...], ((0,), (0,)))
    for copy in started[1:]:
        copy.wait()
    low = low_ref[...]
    used = 2 * dim + zrows
    spare = part_ref.shape[1] - used
    leaving = []
    for j in (1, 3, 0, 2):
        cols = slice(j * units, (j + 1) * units)
        part_ref[j, 0:dim, :] = dot_rows(low, gv_ref[:, cols]).astype(BF16)
        part_ref[j, dim : 2 * dim, :] = dot_rows(low, gr_ref[:, cols]).astype(BF16)
        start = pl.multiple_of(jnp.bitwise_xor(chan, j) * 2 * zrows, 2 * zrows)
        block = zg_ref[pl.ds(start, 2 * zrows), :]
        part_ref[j, 2 * dim : used, :] = jnp.concatenate([block[:zrows, :], block[zrows:, :]], axis=1).astype(BF16)
        part_ref[j, used:, :] = jnp.zeros((spare, units), BF16)
        if j % 2:
            half = send1_to.shape[0]
            first, second = ((send1_to, more1_to), (send3_to, more3_to))[j // 2]
            copies = [(part_ref.at[j, 0:half, :], first), (part_ref.at[j, half:, :], second)]
        else:
            copies = [(part_ref.at[j], keep_to.at[j // 2])]
        leaving += run_copies(copies, part_sems.at[2 * j : 2 * j + len(copies)])
    for copy in leaving:
        copy.wait()


def scans_kernel(
    nd, dim, gv_at, gr_at, h0, h1, h2, h3, pt_ref, sin_at, xt_ref, gmt_ref,
    shared_to, acc_to, shared_ref, acc_ref, sin_ref, buf, gv_ref, gr_ref, sems,
):
    units = h0.shape[1]
    width = xt_ref.shape[0] // SUBS
    started = run_copies(
        [(sin_at, sin_ref), (gv_at, gv_ref), (gr_at, gr_ref)]
        + [(ref.at[0 : 2 * dim, :], buf.at[j]) for j, ref in enumerate((h0, h1, h2, h3))],
        sems,
    )
    started[0].wait()
    group = 8
    for begin in range(0, nd, group):
        ks = list(range(begin, begin + group))
        keep = [tile(pt_ref, nd + k) for k in ks]

        def step(block, carry):
            s, d, a, b = [list(part) for part in carry]
            for u in range(4):
                t = block * 4 + u
                x = step_tile(xt_ref, t)
                gm = step_tile(gmt_ref, t)
                d = [q * di + si for q, di, si in zip(keep, d, s)]
                s = [q * si + x for q, si in zip(keep, s)]
                a = [ai + gm * si for ai, si in zip(a, s)]
                b = [bi + gm * di for bi, di in zip(b, d)]
            return tuple(s), tuple(d), tuple(a), tuple(b)

        zero = (jnp.zeros((SUBS, LANES), F32),) * group
        init = tuple(tile(sin_ref, k) for k in ks)
        s, d, a, b = lax.fori_loop(0, width // 4, step, (init, zero, zero, zero))
        rows = slice(begin * SUBS, (begin + group) * SUBS)
        acc_ref[0, rows, :] = jnp.concatenate(a, axis=0)
        acc_ref[1, rows, :] = jnp.concatenate(b, axis=0)
        acc_ref[2, rows, :] = jnp.concatenate(d, axis=0)
    for copy in started[1:3]:
        copy.wait()
    (last,) = run_copies([(acc_ref, acc_to)], sems)
    shared = None
    for j in range(4):
        cols = slice(j * units, (j + 1) * units)
        started[3 + j].wait()
        term = dot_cols(gv_ref[:, cols], buf[j, 0:dim, :]) + dot_cols(gr_ref[:, cols], buf[j, dim:, :])
        shared = term if j == 0 else shared + term
    shared_ref[...] = shared
    move([(shared_ref, shared_to)], sems.at[1:])
    last.wait()


def rest_rows(nd):
    return -(-(3 * nd + 4) // 16) * 16


def last_kernel(
    nc, nd, ns, span, carry_ref, gmt_ref, pt_ref, shared_at, x_at, gain_at, gmid_at, ids_at, sums_at,
    small_ref, skip_ref, fg_ref,
    keep_ref, send1_ref, send3_ref, yt_ref, acc_ref, ema_ref, rest_ref, shared_ref, x_ref, gain_ref, gmid_ref, ids_ref, sums_ref,
    sems,
):
    started = run_copies(
        [
            (shared_at, shared_ref), (x_at, x_ref), (gain_at, gain_ref), (gmid_at, gmid_ref), (ids_at, ids_ref),
            (sums_at, sums_ref),
        ],
        sems,
    )
    width = gmt_ref.shape[0] // SUBS
    rp = SUBS // nc
    vocab = acc_ref.shape[0]
    place = lax.axis_index("seq")
    chan = lax.axis_index("chan")
    amp, keep_all, out_all, root = weights_of(pt_ref, nd)
    whole = whole_keep(keep_all, width)
    per = span // width
    last = place // per * per + per - 1

    def gather(n, state):
        return state * whole + carry_ref[last - n].astype(F32)

    start = lax.fori_loop(0, last - place, gather, jnp.zeros_like(whole))
    drive = amp * root
    weight_all = out_all * drive
    keep = split_tiles(keep_all, nd)
    weight = split_tiles(weight_all, nd)

    def step(block, carries):
        carries = list(carries)
        for u in range(8):
            t = width - 1 - (block * 8 + u)
            gm = step_tile(gmt_ref, t)
            adj = [c + gm for c in carries]
            yt_ref[pl.ds(pl.multiple_of(t * SUBS, SUBS), SUBS), :] = tree_sum(
                [w * s for w, s in zip(weight, adj)]
            )
            carries = [q * s for q, s in zip(keep, adj)]
        return tuple(carries)

    lax.fori_loop(0, width // 8, step, tuple(split_tiles(start, nd)))
    for copy in started:
        copy.wait()
    a = sums_ref[0]
    g_drive = out_all * a
    grad_out = drive * a
    grad_in = g_drive * root
    grad_keep = weight_all * (sums_ref[1] + sums_ref[2] * start) - g_drive * amp * keep_all / root
    for at, grad in enumerate((grad_in, grad_keep, grad_out)):
        ema_ref[at * nd * SUBS : (at + 1) * nd * SUBS, :] = grad
    skip = pt_ref[3 * nd * SUBS : 3 * nd * SUBS + SUBS, :]
    gain = gain_ref[...]
    for row in range(rp):
        toks = slice(row * width, (row + 1) * width)
        pieces = []
        for chunk in range(nc):
            at = row * nc + chunk
            lanes = slice(chunk * LANES, (chunk + 1) * LANES)
            gm = gmt_ref[pl.ds(at, width, stride=SUBS), :]
            pieces.append(
                shared_ref[toks, lanes] + skip[at : at + 1, :] * gm + yt_ref[pl.ds(at, width, stride=SUBS), :]
            )
        g_normed = jnp.concatenate(pieces, axis=1)
        x = x_ref[toks, :].astype(F32)
        r = scale_of(x)
        n = x * r
        h = g_normed * gain
        g_x = gmid_ref[toks, :] + r * (h - n * jnp.mean(h * n, axis=-1, keepdims=True))
        part = jnp.sum(g_normed * n, axis=0, keepdims=True)
        ag = part if row == 0 else ag + part
        ids = ids_ref[pl.ds(chan * rp + row, 1), :]
        onehot = jnp.where(lax.broadcasted_iota(jnp.int32, (vocab, width), 0) == ids, 1.0, 0.0)
        term = exact(onehot, g_x, ((1,), (0,)))
        acc_ref[...] = term if row == 0 else acc_ref[...] + term
    rest_ref[...] = jnp.zeros_like(rest_ref)
    for chunk in range(nc):
        lanes = slice(chunk * LANES, (chunk + 1) * LANES)
        for at in range(3):
            total = None
            for row in range(rp):
                term = ema_ref[pl.ds(at * nd * SUBS + row * nc + chunk, nd, stride=SUBS), :]
                total = term if row == 0 else total + term
            rest_ref[chunk, at * nd : (at + 1) * nd, :] = total
        at = 3 * nd
        rest_ref[chunk, at : at + 1, :] = sum(
            skip_ref[row * nc + chunk : row * nc + chunk + 1, :] for row in range(rp)
        )
        rest_ref[chunk, at + 1 : at + 2, :] = ag[:, lanes]
        rest_ref[chunk, at + 2 : at + 3, :] = fg_ref[:, lanes]
        if chunk < 3:
            rest_ref[chunk, at + 3 : at + 4, :] = small_ref[chunk : chunk + 1, :]
    half = vocab // 2
    room = rest_ref.shape[1]
    for j in range(4):
        to = (keep_ref.at[0], send1_ref, keep_ref.at[1], send3_ref)[j]
        owner = jnp.bitwise_xor(chan, j)
        block = acc_ref[:, pl.ds(pl.multiple_of(owner * LANES, LANES), LANES)]
        to[0:half, :] = jnp.concatenate([block[:half, :], block[half:, :]], axis=1).astype(BF16)
        rest = rest_ref[owner]
        high = rest.astype(BF16)
        low = (rest - high.astype(F32)).astype(BF16)
        to[half : half + room, :] = jnp.concatenate([high, low], axis=1)
        to[half + room :, :] = jnp.zeros((to.shape[0] - half - room, to.shape[1]), BF16)


def sum_kernel(in_ref, out_ref, buf, sems):
    total = in_ref[0].astype(F32)
    for at in range(1, in_ref.shape[0]):
        total = total + in_ref[at].astype(F32)
    buf[...] = total.astype(BF16)
    for copy in run_copies([(buf, out_ref.at[at]) for at in range(out_ref.shape[0])], sems):
        copy.wait()


def spread(parts, name, after=()):
    scratch = [pltpu.VMEM(parts.shape[1:], BF16), pltpu.SemaphoreType.DMA((parts.shape[0],))]
    return call(sum_kernel, (shape_of(parts.shape, BF16),), (parts,), name, scratch=scratch, out_hbm=(0,), after=after)[0]


def finish_kernel(
    nc, nd, w0, w1, w2, w3, embed_ref, ag_ref, ei_ref, ek_ref, eo_ref, es_ref, fg_ref, qg_ref, kg_ref, qb_ref, rest_ref
):
    half = embed_ref.shape[0] // 2
    room = rest_ref.shape[1]
    chan = lax.axis_index("chan")
    for j, ref in enumerate((w0, w1, w2, w3)):
        owner = jnp.bitwise_xor(chan, j)
        lanes = pl.ds(pl.multiple_of(owner * LANES, LANES), LANES)
        block = ref[0:half, :].astype(F32)
        embed_ref[0:half, lanes] = block[:, :LANES]
        embed_ref[half:, lanes] = block[:, LANES:]
        rest = ref[half : half + room, :].astype(F32)
        rest = rest[:, :LANES] + rest[:, LANES:]
        rest_ref[owner] = rest
        if j == 0:
            for at, to in enumerate((ei_ref, ek_ref, eo_ref)):
                to[...] = rest[at * nd : (at + 1) * nd, :]
            es_ref[...] = rest[3 * nd : 3 * nd + 1, :]
        ag_ref[:, lanes] = rest[3 * nd + 1 : 3 * nd + 2, :]
        fg_ref[:, lanes] = rest[3 * nd + 2 : 3 * nd + 3, :]
    for at, to in enumerate((qg_ref, kg_ref, qb_ref)):
        to[...] = rest_ref[at, 3 * nd + 3 : 3 * nd + 4, :]


def unpack_first(dim, urows, parts, u_ref, v_ref, up_ref, o_ref, down_ref, s_ref):
    join(parts, u_ref, v_ref, s_ref)
    units = s_ref.shape[1]
    up_ref[...] = s_ref[0:dim, :].astype(F32)
    for at, ref in enumerate((o_ref, down_ref)):
        for half in range(dim // units):
            start = dim + (at * (dim // units) + half) * urows
            ref[:, half * units : (half + 1) * units] = s_ref[start : start + urows, :].astype(F32)


def unpack_second(dim, zrows, parts, u_ref, x_ref, v_ref, r_ref, z_ref, s_ref):
    join(parts, u_ref, x_ref, s_ref)
    v_ref[...] = s_ref[0:dim, :].astype(F32)
    r_ref[...] = s_ref[dim : 2 * dim, :].astype(F32)
    block = s_ref[2 * dim : 2 * dim + zrows, :].astype(F32)
    z_ref[0:zrows, :] = block[:, :LANES]
    z_ref[zrows:, :] = block[:, LANES:]


def join(parts, mine_ref, other_ref, to_ref):
    if parts is None:
        to_ref[...] = mine_ref[...]
    else:
        join_halves(0, parts, mine_ref, other_ref, to_ref)


def plus(left, right):
    return (left.astype(F32) + right.astype(F32)).astype(BF16)


def piece_sum(keep_ref, got, chunk, begin, rows):
    each = got[0].shape[0]
    pieces = []
    while rows:
        at = chunk * keep_ref.shape[1] + begin
        inner = at % each
        take = min(rows, each - inner)
        pieces.append(plus(keep_ref[chunk, begin : begin + take, :], got[at // each][inner : inner + take, :]))
        begin, rows = begin + take, rows - take
    return pieces[0] if len(pieces) == 1 else jnp.concatenate(pieces, axis=0)


def add_core_split(split, keep_ref, *refs):
    got, refs = refs[:-8], refs[-8:]
    (mine_to, theirs_to, keep_to, send_to), (mine_ref, theirs_ref, halves_ref, sems) = refs[:4], refs[4:]
    half = (keep_ref.shape[1] - split) // 2
    theirs_ref[...] = piece_sum(keep_ref, got, 1, 0, split)
    leaving = run_copies([(theirs_ref, theirs_to)], sems.at[0:1])
    for chunk in range(2):
        for side in range(2):
            halves_ref[side, chunk * half : (chunk + 1) * half, :] = piece_sum(
                keep_ref, got, chunk, split + side * half, half
            )
    bit = seq_bit(0)
    leaving += run_copies([(halves_ref.at[1 - bit], send_to), (halves_ref.at[bit], keep_to)], sems.at[1:3])
    mine_ref[...] = piece_sum(keep_ref, got, 0, 0, split)
    leaving += run_copies([(mine_ref, mine_to)], sems.at[3:4])
    for copy in leaving:
        copy.wait()


def turn_kernel(mine_ref, got_ref, keep_ref, other_ref, kept_ref, send_ref, own_ref, theirs_ref):
    half = kept_ref.shape[0]
    bit = seq_bit(0)
    for side, ref in ((bit, kept_ref), (1 - bit, send_ref)):
        rows = pl.ds(pl.multiple_of(side * half, 16), half)
        ref[...] = plus(mine_ref[rows, :], got_ref[rows, :])
    half = own_ref.shape[0]
    own_ref[...] = plus(keep_ref[0:half, :], other_ref[0:half, :])
    theirs_ref[...] = plus(keep_ref[half:, :], other_ref[half:, :])


def add_core_far(keep_ref, *refs):
    got, (mine_to, theirs_to, mine_ref, theirs_ref, sems) = refs[:-5], refs[-5:]
    leaving = []
    for chunk, ref, to in ((1, theirs_ref, theirs_to), (0, mine_ref, mine_to)):
        ref[...] = piece_sum(keep_ref, got, chunk, 0, keep_ref.shape[1])
        leaving += run_copies([(ref, to)], sems.at[chunk : chunk + 1])
    for copy in leaving:
        copy.wait()


def add_core(keep_ref, got_ref, other_ref, mine_ref, theirs_ref):
    mine_ref[...] = plus(keep_ref[0], got_ref[...])
    theirs_ref[...] = plus(keep_ref[1], other_ref[...])


def add_plain(mine_ref, got_ref, out_ref):
    out_ref[...] = plus(mine_ref[...], got_ref[...])


def seq_bit(level):
    return jnp.bitwise_and(lax.shift_right_logical(lax.axis_index("seq"), level), 1)


def add_halves(level, parts, *refs):
    pairs, (keep_ref, send_ref) = refs[:-2], refs[-2:]
    bit = seq_bit(level)
    begin = 0
    for at in range(0, len(pairs), 2):
        mine_ref, got_ref = pairs[at : at + 2]
        inner = 0
        for rows in parts[at // 2]:
            half = rows // 2
            for side, ref in ((bit, keep_ref), (1 - bit, send_ref)):
                at_rows = pl.ds(pl.multiple_of(inner + side * half, 16), half)
                ref[begin : begin + half, :] = plus(mine_ref[at_rows, :], got_ref[at_rows, :])
            inner += rows
            begin += half


def join_halves(level, parts, mine_ref, got_ref, out_ref):
    bit = seq_bit(level)
    begin = 0
    for rows in parts:
        for side, ref in ((bit, mine_ref), (1 - bit, got_ref)):
            out_ref[pl.ds(pl.multiple_of(2 * begin + side * rows, 16), rows), :] = ref[begin : begin + rows, :]
        begin += rows


def join_part(begin, mine_ref, got_ref, out_ref):
    half = out_ref.shape[0] // 2
    bit = seq_bit(0)
    for side, ref in ((bit, mine_ref), (1 - bit, got_ref)):
        out_ref[pl.ds(pl.multiple_of(side * half, 16), half), :] = ref[begin : begin + half, :]


def output_kernel(w0, w1, w2, w3, out_ref):
    rows, width, dim = out_ref.shape
    units = w0.shape[1]
    toks = w0.shape[0] // (dim // units)
    chan = lax.axis_index("chan")
    for j, ref in enumerate((w0, w1, w2, w3)):
        for row in range(toks // width):
            for half in range(dim // units):
                start = half * toks + row * width
                out_ref[jnp.bitwise_xor(chan, j) * (toks // width) + row, :, half * units : (half + 1) * units] = ref[
                    start : start + width, :
                ]


def swap(value, mask, axis="chan"):
    return lax.ppermute(value, axis, [(at, at ^ mask) for at in range(lax.axis_size(axis))])


def exchange(value, axis):
    return lax.all_to_all(value, axis, 0, 0, tiled=True)


def add_pair(kernel, args, rows, name, after):
    shape = shape_of((rows, args[0].shape[-1]), BF16)
    return call(kernel, (shape, shape), args, name, free=range(3), out_free=(0, 1), after=after)


def seq_sum(value, ns, name):
    rows = value.shape[0]
    parts = exchange(value.reshape(ns, rows // ns, value.shape[1]), "seq")
    return exchange(spread(parts, name), "seq").reshape(value.shape)


def body(
    token_ids, valid_counts, embed, attn_gain, ema_in, ema_keep, ema_out, ema_skip, z_proj, q_gain, k_gain, q_bias,
    v_proj, r_proj, o_proj, ffn_gain, up_proj, down_proj, grad_out,
):
    rows, width = token_ids.shape
    vocab, dim = embed.shape
    nd = ema_in.shape[1]
    units = v_proj.shape[1]
    zdim = z_proj.shape[1]
    nc = lax.axis_size("chan")
    ns = lax.axis_size("seq")
    ndev = nc * ns
    rp = rows // nc
    toks = rp * width
    span = min(width * ns, SEQMAX)
    urows = o_proj.shape[0]
    zrows = z_proj.shape[0] // 2
    prows = 3 * nd + SUBS
    w1_rows = 2 * dim + zrows
    w2_rows = 3 * dim
    row = lambda vector: vector.reshape(1, -1)

    dma = pltpu.SemaphoreType.DMA
    (p_own,) = call(
        pack_params, (shape_of((prows, LANES)),), (ema_in.T, ema_keep.T, ema_out.T, row(ema_skip)), "pack_params",
        scratch=[dma((4,))], hbm=range(4), out_free=(0,), limit=8,
    )
    p_far, p_near = swap(p_own, 2), swap(p_own, 1)
    x, xt, low, own1, own2 = call(
        functools.partial(prepare_kernel, nc),
        (
            shape_of((toks, dim), BF16), shape_of((width * SUBS, LANES)), shape_of((toks, dim), BF16),
            shape_of((w1_rows, units), BF16), shape_of((w2_rows, units), BF16),
        ),
        (token_ids, embed, row(attn_gain), v_proj, r_proj, z_proj, up_proj, o_proj, down_proj), "prepare",
        scratch=[
            pltpu.VMEM((rows, width), jnp.int32), pltpu.VMEM((vocab, dim), BF16), pltpu.VMEM((1, dim), F32),
            pltpu.VMEM((toks, dim), BF16), pltpu.VMEM((toks, dim), BF16), pltpu.VMEM((w1_rows, units), BF16),
            pltpu.VMEM((w2_rows, units), BF16), dma((3,)), dma((9,)), dma((4,)),
        ],
        hbm=range(9), out_hbm=(0, 2, 3, 4), after=("pack_params",),
    )
    own1, own2, p_far = lax.optimization_barrier((own1, own2, p_far))
    p_both = swap(p_far, 1)
    far1 = swap(own1, 2)
    near1 = swap(own1, 1)
    far2 = swap(own2, 2)
    near2 = swap(own2, 1)
    pt, ends = call(
        functools.partial(scan_end_kernel, nc, nd),
        (shape_of((prows * SUBS, LANES)), shape_of((ns, nd * SUBS, LANES))),
        (p_own, p_near, p_far, p_both, xt), "scan_end",
        scratch=[pltpu.VMEM((nc, prows, LANES), F32), pltpu.VMEM((nd * SUBS, LANES), F32), dma((ns,))],
        free=range(4), out_hbm=(1,), after=("prepare",), limit=8,
    )
    far1, _ = lax.optimization_barrier((far1, pt))
    both1 = swap(far1, 1)
    first = (own1, near1, far1, both1)
    ends = exchange(ends, "seq")
    v_pre, r_pre, values, z_all, values_far = call(
        functools.partial(project_kernel, dim),
        (
            shape_of((toks, nc * units)), shape_of((toks, nc * units)), shape_of((toks, nc * units), BF16),
            shape_of((dim, zdim), BF16), shape_of((toks, nc * units), BF16),
        ),
        (low,) + first, "project",
        scratch=[
            pltpu.VMEM((toks, dim), BF16), pltpu.VMEM((toks, nc * units), F32), pltpu.VMEM((4, w1_rows, units), BF16),
            dma((5,)), dma((8,)),
        ],
        hbm=range(4), free=(4,), out_hbm=(0, 4), after=("scan_end",), limit=16,
    )
    mixed_pre, mixed_low, z_pre, attn, context, gated, state_in = call(
        functools.partial(mix_kernel, nc, nd, span),
        (
            shape_of((toks, dim)), shape_of((toks, dim), BF16), shape_of((toks, zdim)), shape_of((toks, width)),
            shape_of((toks, nc * units)), shape_of((toks, nc * units), BF16), shape_of((nd * SUBS, LANES)),
        ),
        (
            valid_counts, ends, xt, pt, z_all, values, r_pre, row(q_gain), row(k_gain), row(q_bias),
        ),
        "mix", scratch=[pltpu.VMEM((width * SUBS, LANES), F32), pltpu.VMEM((nd * SUBS, LANES), F32), pltpu.VMEM((toks, dim), BF16), dma((2,))],
        smem=(0,), free=range(7, 10), out_hbm=(1, 6), after=("project",), limit=16,
    )
    far2, gated = lax.optimization_barrier((far2, gated))
    both2 = swap(far2, 1)
    second = (own2, near2, far2, both2)
    out_rows = toks * (dim // units)
    out, g_mid, g_gated, keep1, send1, ffn_grad = call(
        functools.partial(ffn_kernel, nc, dim),
        (
            shape_of((out_rows, units), BF16), shape_of((toks, dim)), shape_of((toks, nc * units)),
            shape_of((2, w2_rows, units), BF16), shape_of((2, w2_rows, units), BF16), shape_of((1, dim)),
        ),
        (gated,) + second + (x, grad_out, row(ffn_gain)),
        "ffn",
        scratch=[
            pltpu.VMEM((toks, nc * units), BF16), pltpu.VMEM((toks, nc * units), BF16),
            pltpu.VMEM((toks, dim), BF16), pltpu.VMEM((out_rows, units), BF16), pltpu.VMEM((toks, dim), F32),
            pltpu.VMEM((toks, dim), BF16), pltpu.VMEM((dim, nc * units), BF16), pltpu.VMEM((nc * urows, dim), BF16),
            pltpu.VMEM((nc * urows, dim), BF16), pltpu.VMEM((4, w2_rows, units), BF16),
            dma((1 + 8 * (dim // units) + 4 + rp,)), dma((2,)), dma((12,)),
        ],
        hbm=(1, 2, 3, 5, 6), free=(4, 7), out_hbm=(0, 1, 3, 4), after=("mix",), limit=32,
    )
    got1 = swap(send1, 1)
    grad_v, grad_r, g_z, gmt, carries, small, skip_grad = call(
        functools.partial(attn_back_kernel, nc, nd),
        (
            shape_of((toks, nc * units), BF16), shape_of((toks, nc * units), BF16), shape_of((toks, zdim)),
            shape_of((width * SUBS, LANES)), shape_of((ns, nd * SUBS, LANES), BF16), shape_of((SUBS, zdim)),
            shape_of((SUBS, LANES)),
        ),
        (
            g_gated, r_pre, v_pre, context, attn, values_far, z_pre, mixed_pre, xt, z_all, pt, row(q_gain), row(k_gain),
            row(q_bias),
        ),
        "attn_back",
        scratch=[
            pltpu.VMEM((nd * SUBS, LANES), BF16), pltpu.VMEM((toks, nc * units), BF16), pltpu.VMEM((toks, nc * units), BF16),
            dma((ns,)), dma((2,)),
        ],
        free=(2, 5, 11, 12, 13), out_hbm=(0, 1, 4), after=("ffn",), limit=20,
    )
    carries = exchange(carries, "seq")
    fast = ns == 8
    mine1, theirs1 = call(
        add_core_far, (shape_of((w2_rows, units), BF16),) * 2, (keep1, got1.reshape(2 * w2_rows, units)),
        "add_core_first",
        scratch=[pltpu.VMEM((w2_rows, units), BF16), pltpu.VMEM((w2_rows, units), BF16), dma((2,))],
        free=range(2), out_hbm=range(2), after=("attn_back",),
    )
    far_got1 = swap(theirs1, 2)
    g2_rows = -(-w1_rows // (16 * ns)) * 16 * ns
    keep2, *sends2 = call(
        functools.partial(grads_kernel, nc, dim, zrows),
        (shape_of((2, g2_rows, units), BF16),) + (shape_of((g2_rows // 2, units), BF16),) * 4,
        (low, grad_v, grad_r, mixed_low, g_z), "grads",
        scratch=[
            pltpu.VMEM((dim, zdim), F32), pltpu.VMEM((toks, dim), BF16), pltpu.VMEM((toks, nc * units), BF16),
            pltpu.VMEM((toks, nc * units), BF16), pltpu.VMEM((toks, dim), BF16), pltpu.VMEM((4, g2_rows, units), BF16),
            dma((4,)), dma((8,)),
        ],
        hbm=range(4), out_hbm=range(5), after=("add_core_first",), limit=24,
    )
    gots2 = [swap(value, 1) for value in sends2]
    shared, sums = call(
        functools.partial(scans_kernel, nd, dim),
        (shape_of((toks, dim)), shape_of((3, nd * SUBS, LANES))),
        (grad_v, grad_r) + first + (pt, state_in, xt, gmt), "scans",
        scratch=[
            pltpu.VMEM((toks, dim), F32), pltpu.VMEM((3, nd * SUBS, LANES), F32), pltpu.VMEM((nd * SUBS, LANES), F32),
            pltpu.VMEM((4, 2 * dim, units), BF16), pltpu.VMEM((toks, nc * units), BF16),
            pltpu.VMEM((toks, nc * units), BF16), dma((7,)),
        ],
        hbm=(0, 1, 2, 3, 4, 5, 7), out_hbm=range(2), after=("grads",), limit=24,
    )
    split2 = g2_rows - 256 if fast else g2_rows
    if fast:
        near, far = shape_of((split2, units), BF16), shape_of((g2_rows - split2, units), BF16)
        mine2, theirs2, kept2, send2 = call(
            functools.partial(add_core_split, split2), (near, near, far, far), (keep2, *gots2), "add_core_second",
            scratch=[
                pltpu.VMEM((split2, units), BF16), pltpu.VMEM((split2, units), BF16),
                pltpu.VMEM((2, g2_rows - split2, units), BF16), dma((4,)),
            ],
            free=range(5), out_hbm=range(4), after=("scans",),
        )
        sums2 = (mine2, swap(theirs2, 2), kept2, swap(send2, 1, "seq"))
    else:
        mine2, theirs2 = call(
            add_core_far, (shape_of((g2_rows, units), BF16),) * 2, (keep2, *gots2), "add_core_second",
            scratch=[pltpu.VMEM((g2_rows, units), BF16), pltpu.VMEM((g2_rows, units), BF16), dma((2,))],
            free=range(5), out_hbm=range(2), after=("scans",),
        )
        sums2 = (mine2, swap(theirs2, 2))
    half_parts = lambda parts: tuple(rows // 2 for rows in parts)

    def halves(level, pairs, parts, name, after):
        rows = sum(sum(part) for part in parts) // 2
        return call(
            functools.partial(add_halves, level, parts), (shape_of((rows, units), BF16),) * 2, pairs, name,
            free=range(len(pairs)), out_free=range(2), after=after,
        )

    def joined(level, pair, parts, name, after):
        return call(
            functools.partial(join_halves, level, parts), (shape_of((2 * pair[0].shape[0], units), BF16),), pair, name,
            free=range(2), out_free=(0,), after=after,
        )[0]

    def add_two(pair, name, after):
        return call(
            add_plain, (shape_of(pair[0].shape, BF16),), pair, name, free=range(2), out_free=(0,), after=after
        )[0]

    if fast:
        keep1, send1 = halves(0, (mine1, far_got1), ((w2_rows,),), "x_first", ("add_core_second",))
        x_got1 = swap(send1, 1, "seq")
    room = rest_rows(nd)
    f_rows = -(-(vocab // 2 + room) // (16 * ns)) * 16 * ns
    f_keep, f_send, f_other = call(
        functools.partial(last_kernel, nc, nd, ns, span),
        (shape_of((2, f_rows, units), BF16),) + (shape_of((f_rows, units), BF16),) * 2,
        (carries, gmt, pt, shared, x, row(attn_gain), g_mid, token_ids, sums, small, skip_grad, ffn_grad),
        "last",
        scratch=[
            pltpu.VMEM((width * SUBS, LANES), F32), pltpu.VMEM((vocab, dim), F32),
            pltpu.VMEM((3 * nd * SUBS, LANES), F32), pltpu.VMEM((nc, room, LANES), F32),
            pltpu.VMEM((toks, dim), F32), pltpu.VMEM((toks, dim), BF16), pltpu.VMEM((1, dim), F32),
            pltpu.VMEM((toks, dim), F32), pltpu.VMEM((rows, width), jnp.int32), pltpu.VMEM((3, nd * SUBS, LANES), F32),
            dma((6,)),
        ],
        hbm=range(3, 9), out_free=range(3), after=("x_first",) if fast else ("add_core_second",), limit=16,
    )
    f_mine, f_theirs = call(
        add_core, (shape_of((f_rows, units), BF16),) * 2, (f_keep, swap(f_send, 1), swap(f_other, 1)), "add_core_last",
        free=range(3),
        out_free=range(2), after=("last",),
    )
    f_far = swap(f_theirs, 2)
    if fast:
        parts1, parts2 = (w2_rows // 2,), (split2 // 2, (g2_rows - split2) // 2, f_rows // 2)
        keep1, send1 = halves(1, (keep1, x_got1), (parts1,), "z_first", ("add_core_last",))
        got1 = swap(send1, 2, "seq")
        near, far = shape_of((split2 // 2, units), BF16), shape_of(((g2_rows - split2) // 2, units), BF16)
        kept2, send2, own2, theirs2 = call(
            turn_kernel, (near, near, far, far), sums2, "turn_second", free=range(4), out_free=range(4),
            after=("z_first",),
        )
        sums2 = (kept2, swap(send2, 1, "seq"), own2, swap(theirs2, 2))
        keepf, sendf = halves(0, (f_mine, f_far), ((f_rows,),), "x_last", ("turn_second",))
        sums2 += (keepf, swap(sendf, 1, "seq"))
        parts1 = half_parts(parts1)
        keep1 = add_two((keep1, got1), "zz_first", ("x_last",))
        got1 = swap(keep1, 4, "seq")
        keep2, send2 = halves(1, sums2, tuple((rows,) for rows in parts2), "z_second", ("zz_first",))
        got2 = swap(send2, 2, "seq")
        out, keep2 = lax.optimization_barrier((out, keep2))
        out_far, out_near = swap(out, 2), swap(out, 1)
        parts2 = half_parts(parts2)
        keep2 = add_two((keep2, got2), "zz_second", ("z_second",))
        got2 = swap(keep2, 4, "seq")
        keep1 = add_two((keep1, got1), "sum_first", ("zz_second",))
        got1 = swap(keep1, 2, "seq")
        out_far, keep1 = lax.optimization_barrier((out_far, keep1))
        out_both = swap(out_far, 1)
        u1 = joined(1, (keep1, got1), parts1, "join_z_first", ("sum_first",))
        v1 = swap(u1, 1, "seq")
        keep2 = add_two((keep2, got2), "sum_second", ("join_z_first",))
        got2 = swap(keep2, 2, "seq")
        follow = ("sum_second",)
    else:
        out_far, out_near = swap(out, 2), swap(out, 1)
        out_both = swap(out_far, 1)
        follow = ()
    (output,) = call(
        output_kernel, (shape_of((rows, width, dim), BF16),), (out, out_near, out_far, out_both), "output",
        free=range(4), out_free=(0,), after=follow, limit=8,
    )
    if fast:
        u2 = joined(1, (keep2, got2), parts2, "join_z_second", ("output",))
        v2 = swap(u2, 1, "seq")
    else:
        u1 = v1 = seq_sum(add_two((mine1, far_got1), "add_first", ()), ns, "sum_first")
        u2 = v2 = seq_sum(add_two(sums2, "add_second", ()), ns, "sum_second")
        f_own = seq_sum(add_two((f_mine, f_far), "add_last", ()), ns, "sum_last")
    up_grad, o_grad, down_grad = call(
        functools.partial(unpack_first, dim, urows, (w2_rows // 2,) if fast else None),
        (shape_of(up_proj.shape), shape_of(o_proj.shape), shape_of(down_proj.shape)),
        (u1, v1), "unpack_first", free=range(2), out_free=range(3), scratch=[pltpu.VMEM((w2_rows, units), BF16)],
        after=("join_z_second",) if fast else ("output",),
    )
    if fast:
        (f_own,) = call(
            functools.partial(join_part, g2_rows // 2), (shape_of((f_rows, units), BF16),), (u2, v2), "collect",
            free=range(2), out_free=(0,), after=("unpack_first",),
        )
    f_far, f_near = swap(f_own, 2), swap(f_own, 1)
    v_grad, r_grad, z_grad = call(
        functools.partial(
            unpack_second, dim, zrows, (split2 // 2, (g2_rows - split2) // 2) if fast else None
        ),
        (shape_of(v_proj.shape), shape_of(r_proj.shape), shape_of(z_proj.shape)),
        (u2, v2), "unpack_second", free=range(2), out_free=range(3), scratch=[pltpu.VMEM((g2_rows, units), BF16)],
        after=("collect",) if fast else ("unpack_first",),
    )
    embed_grad, ag, gi, gk, go, gs, fg, qg, kg, qb = call(
        functools.partial(finish_kernel, nc, nd),
        (
            shape_of((vocab, dim)), shape_of((1, dim)), shape_of((nd, LANES)), shape_of((nd, LANES)),
            shape_of((nd, LANES)), shape_of((1, LANES)), shape_of((1, dim)), shape_of((1, zdim)),
            shape_of((1, zdim)), shape_of((1, zdim)),
        ),
        (f_own, f_near, f_far, swap(f_far, 1)), "finish", free=range(4), out_free=range(10),
        scratch=[pltpu.VMEM((nc, room, LANES), F32)], after=("unpack_second",), limit=8,
    )
    flat = lambda value: value.reshape(-1)
    return (
        output, embed_grad, flat(ag), gi.T, gk.T, go.T, flat(gs), z_grad, flat(qg), flat(kg), flat(qb), v_grad, r_grad,
        o_grad, flat(fg), up_grad, down_grad,
    )


def solution(mesh):
    placed = (
        P(None, "seq"), P(), P(), P(), P("chan", None), P("chan", None), P("chan", None), P("chan"), P("chan", None),
        P(), P(), P(), P(None, "chan"), P(None, "chan"), P("chan", None), P(), P(None, "chan"), P("chan", None),
        P(None, "seq", None),
    )
    return jax.shard_map(
        body,
        mesh=mesh,
        in_specs=placed,
        out_specs=(
            P(None, "seq", None), P(), P(), P("chan", None), P("chan", None), P("chan", None), P("chan"),
            P("chan", None), P(), P(), P(), P(None, "chan"), P(None, "chan"), P("chan", None), P(), P(None, "chan"),
            P("chan", None),
        ),
        check_vma=False,
    )
```

```python
import functools

import jax
import jax.numpy as jnp
from jax import lax
from jax.experimental import pallas as pl
from jax.experimental.pallas import tpu as pltpu
from jax.sharding import PartitionSpec as P

SEQMAX = 4096
EPS = 1e-06
F32 = jnp.float32
BF16 = jnp.bfloat16
LANES = 128
SUBS = 8
MIB = 1024 * 1024


def sigmoid(u):
    return 0.5 * jnp.tanh(0.5 * u) + 0.5


def silu_slope(pre):
    sigma = sigmoid(pre)
    return sigma * (1.0 + pre * (1.0 - sigma))


def mm(left, right, dims, precision=None):
    return lax.dot_general(
        left, right, ((dims[0], dims[1]), ((), ())), precision=precision, preferred_element_type=F32
    )


def dot(left, right):
    return mm(left, right, ((1,), (0,)))


def dot_rows(left, right):
    return mm(left, right, ((0,), (0,)))


def dot_cols(left, right):
    return mm(left, right, ((1,), (1,)))


def two_parts(value):
    high = value.astype(BF16)
    return high, (value - high.astype(F32)).astype(BF16)


def exact(left, right, dims):
    if left.dtype == BF16:
        high, low = two_parts(right)
        return mm(left, high, dims) + mm(left, low, dims)
    high, low = two_parts(left)
    return mm(high, right, dims) + mm(low, right, dims)


def shape_of(dims, dtype=F32):
    return jax.ShapeDtypeStruct(dims, dtype)


TOKENS = {}
ORDER = (
    "attn_back", "core_first", "grads", "move_carry", "scans", "core_second", "x_first", "last", "core_last", "z_first", "turn_second", "zz_first", "z_second", "move_out", "x_last", "z_last", "zz_second", "sum_first", "zz_last", "join_first", "sum_second", "sum_last", "move_both", "join_second", "join_last", "output", "unpack_first", "collect", "unpack_second", "finish",
)
PLAIN = (
    "attn_back", "move_carry", "core_first", "grads", "scans", "core_second", "last", "core_last", "move_out", "move_both", "output",
    "plain_sums", "unpack_first", "unpack_second", "finish",
)
X_FIRST = 128
X_ROWS = 384
PIECES = 4


def call(
    kernel, outs, args, name, scratch=(), smem=(), hbm=(), free=(), far=(), out_hbm=(), out_free=(), out_far=(), after=(), limit=16
):

    waits = [TOKENS[key] for key in after]
    hbm, out_hbm = {*hbm, *far}, {*out_hbm, *out_far}
    count, made = len(args), len(outs)

    def run(*refs):
        rest = refs[count + len(waits) :]
        kernel(*refs[:count], *rest[:made], *rest[made + 1 :])

    def spec(at):
        if at >= count or (at in hbm and at not in far):
            return pl.BlockSpec(memory_space=pltpu.HBM)
        return pl.BlockSpec(memory_space=pltpu.SMEM if at in smem else pltpu.VMEM)

    def held(at, value):
        if at < count and (at in smem or at in free):
            return value
        return pltpu.with_memory_space_constraint(value, pltpu.HBM if at in hbm or at >= count else pltpu.VMEM)

    def result(at, out):
        if at in out_free:
            return out
        return (pltpu.HBM if at in out_hbm or at == made else pltpu.VMEM)(out.shape, out.dtype)

    shapes = list(outs) + [shape_of((SUBS, LANES))]
    *results, TOKENS[name] = pl.pallas_call(
        run,
        out_shape=[result(at, out) for at, out in enumerate(shapes)],
        in_specs=[spec(at) for at in range(count + len(waits))],
        out_specs=[
            pl.BlockSpec(memory_space=pltpu.HBM if (at in out_hbm and at not in out_far) or at == made else pltpu.VMEM)
            for at in range(made + 1)
        ],
        scratch_shapes=list(scratch),
        name=name,
        cost_estimate=pl.CostEstimate(flops=1, bytes_accessed=1, transcendentals=0),
        compiler_params=pltpu.CompilerParams(vmem_limit_bytes=limit * MIB),
    )(*[held(at, value) for at, value in enumerate([*args, *waits])])
    return results


def move(copies, sems):
    for copy in run_copies(copies, sems):
        copy.wait()


def run_copies(copies, sems):
    started = [pltpu.make_async_copy(src, dst, sems.at[at]) for at, (src, dst) in enumerate(copies)]
    for copy in started:
        copy.start()
    return started


def pack_params(in_ref, keep_ref, out_ref, skip_ref, p_ref, sems):
    nd, lanes = in_ref.shape
    copies = [(ref, p_ref.at[at * nd : (at + 1) * nd, :]) for at, ref in enumerate((in_ref, keep_ref, out_ref))]
    copies.append((skip_ref, p_ref.at[3 * nd : 3 * nd + 1, :]))
    move(copies, sems)
    rest = p_ref.shape[0] - 3 * nd
    p_ref[3 * nd :, :] = jnp.broadcast_to(p_ref[3 * nd : 3 * nd + 1, :], (rest, lanes))


def first_copies(v_ref, r_ref, z_ref, buf):
    dim = v_ref.shape[0]
    zrows = z_ref.shape[0] // 2
    copies = [(v_ref, buf.at[0:dim, :]), (r_ref, buf.at[dim : 2 * dim, :])]
    for half in range(2):
        copies.append(
            (
                z_ref.at[half * zrows : (half + 1) * zrows, :],
                buf.at[2 * dim : 2 * dim + zrows, half * LANES : (half + 1) * LANES],
            )
        )
    return copies


def second_copies(up_ref, o_ref, down_ref, buf):
    dim, units = up_ref.shape
    urows = o_ref.shape[0]
    copies = [(up_ref, buf.at[0:dim, :])]
    for at, ref in enumerate((o_ref, down_ref)):
        for half in range(dim // units):
            start = dim + (dim // units * at + half) * urows
            copies.append((ref.at[:, half * units : (half + 1) * units], buf.at[start : start + urows, :]))
    return copies


def prepare_kernel(
    nc, ids_at, table_at, gain_at, v_at, r_at, z_at, up_at, o_at, down_at,
    x_to, xt_ref, low_to, w1_to, w2_to,
    ids_ref, embed_ref, gain_ref, x_ref, low_ref, w1_ref, w2_ref, sems, w_sems, out_sems,
):
    entering = run_copies(first_copies(v_at, r_at, z_at, w1_ref), w_sems.at[0:4])
    started = run_copies([(ids_at, ids_ref), (table_at, embed_ref), (gain_at, gain_ref)], sems)
    later = run_copies(second_copies(up_at, o_at, down_at, w2_ref), w_sems.at[4:9])
    for copy in entering:
        copy.wait()
    leaving = run_copies([(w1_ref, w1_to)], out_sems.at[0:1])
    rp = x_ref.shape[0] // ids_ref.shape[1]
    width = ids_ref.shape[1]
    vocab = embed_ref.shape[0]
    chan = lax.axis_index("chan")
    for copy in started:
        copy.wait()
    for row in range(rp):
        ids = ids_ref[pl.ds(chan * rp + row, 1), :]
        onehot = jnp.where(lax.broadcasted_iota(jnp.int32, (vocab, width), 0) == ids, 1.0, 0.0).astype(BF16)
        x = dot_rows(onehot, embed_ref[...])
        x_ref[row * width : (row + 1) * width, :] = x.astype(BF16)
        normed = x * lax.rsqrt(jnp.mean(x * x, axis=-1, keepdims=True) + EPS) * gain_ref[...]
        low_ref[row * width : (row + 1) * width, :] = normed.astype(BF16)
        for chunk in range(nc):
            xt_ref[pl.ds(row * nc + chunk, width, stride=SUBS), :] = normed[
                :, chunk * LANES : (chunk + 1) * LANES
            ]
        for copy in later:
            copy.wait()
        later = []
        leaving += run_copies([(w2_ref, w2_to)], out_sems.at[1:2]) if row == 0 else []
    leaving += run_copies([(x_ref, x_to), (low_ref, low_to)], out_sems.at[2:4])
    for copy in leaving:
        copy.wait()


def tile(ref, at):
    return ref[at * SUBS : (at + 1) * SUBS, :]


def step_tile(ref, t):
    return ref[pl.ds(pl.multiple_of(t * SUBS, SUBS), SUBS), :]


def scan_end_kernel(nc, nd, p0, p1, p2, p3, xt_ref, pt_ref, end_ref, p_ref, buf, sems):
    width = xt_ref.shape[0] // SUBS
    prows = p_ref.shape[1]
    chan = lax.axis_index("chan")
    for j, ref in enumerate((p0, p1, p2, p3)):
        p_ref[jnp.bitwise_xor(chan, j)] = ref[...]
    for sub in range(SUBS):
        pt_ref[pl.ds(sub, prows, stride=SUBS), :] = p_ref[sub % nc]
    keep = [tile(pt_ref, nd + k) for k in range(nd)]

    def step(block, states):
        states = list(states)
        for u in range(8):
            x = step_tile(xt_ref, block * 8 + u)
            states = [q * s + x for q, s in zip(keep, states)]
        return tuple(states)

    zero = jnp.zeros((SUBS, LANES), F32)
    states = lax.fori_loop(0, width // 8, step, (zero,) * nd)
    buf[...] = jnp.concatenate(states, axis=0)
    for copy in run_copies([(buf, end_ref.at[at]) for at in range(end_ref.shape[0])], sems):
        copy.wait()


def project_kernel(
    dim, low_at, h0, h1, h2, h3, vpre_to, rpre_ref, val_ref, z_ref, val_to, low_ref, vpre_ref, buf, sems, out_sems
):
    chan = lax.axis_index("chan")
    units = h0.shape[1]
    zrows = h0.shape[0] - 2 * dim
    started = run_copies([(low_at, low_ref)] + [(ref, buf.at[j]) for j, ref in enumerate((h0, h1, h2, h3))], sems)
    started[0].wait()
    low = low_ref[...]
    leaving = []
    for j in range(4):
        started[1 + j].wait()
        w = buf.at[j]
        cols = slice(j * units, (j + 1) * units)
        v_pre = dot(low, w[0:dim, :])
        vpre_ref[:, cols] = v_pre
        val_ref[:, cols] = (v_pre * sigmoid(v_pre)).astype(BF16)
        leaving += run_copies(
            [(vpre_ref.at[:, cols], vpre_to.at[:, cols]), (val_ref.at[:, cols], val_to.at[:, cols])],
            out_sems.at[2 * j : 2 * j + 2],
        )
        rpre_ref[:, cols] = dot(low, w[dim : 2 * dim, :])
        start = pl.multiple_of(jnp.bitwise_xor(chan, j) * 2 * zrows, 2 * zrows)
        half = w[2 * dim : 2 * dim + zrows, :]
        z_ref[pl.ds(start, 2 * zrows), :] = jnp.concatenate([half[:, :LANES], half[:, LANES:]], axis=0)
    for copy in leaving:
        copy.wait()


def whole_keep(keep, width):
    whole = keep
    power = 1
    while power < width:
        whole = whole * whole
        power *= 2
    return whole


def weights_of(pt_ref, nd):
    amp = pt_ref[0 : nd * SUBS, :]
    keep = pt_ref[nd * SUBS : 2 * nd * SUBS, :]
    out = pt_ref[2 * nd * SUBS : 3 * nd * SUBS, :]
    root = jnp.sqrt(1.0 - keep * keep)
    return amp, keep, out, root


def split_tiles(value, nd):
    return [value[k * SUBS : (k + 1) * SUBS, :] for k in range(nd)]


def tree_sum(values):
    values = list(values)
    while len(values) > 1:
        values = [sum(values[i : i + 2][1:], values[i]) for i in range(0, len(values), 2)]
    return values[0]


def scale_of(x):
    return lax.rsqrt(jnp.mean(x * x, axis=-1, keepdims=True) + EPS)


def mix_kernel(
    nc, nd, span, counts_ref, ends_ref, xt_ref, pt_ref, z_ref, val_ref, rpre_ref, qg_ref, kg_ref, qb_ref,
    mpre_ref, mlow_to, zpre_ref, attn_ref, ctx_ref, gated_ref, sin_to, sm_ref, sin_ref, mlow_ref, sems,
):
    width = xt_ref.shape[0] // SUBS
    rp = SUBS // nc
    place = lax.axis_index("seq")
    chan = lax.axis_index("chan")
    amp, keep_all, out_all, root = weights_of(pt_ref, nd)
    whole = whole_keep(keep_all, width)
    per = span // width
    first = place // per * per

    def gather(n, state):
        return state * whole + ends_ref[n].astype(F32)

    start = lax.fori_loop(first, place, gather, jnp.zeros_like(whole))
    sin_ref[...] = start
    (leaving,) = run_copies([(sin_ref, sin_to)], sems.at[:1])
    keep = split_tiles(keep_all, nd)
    weight = split_tiles(out_all * amp * root, nd)

    def step(block, states):
        states = list(states)
        for u in range(8):
            t = block * 8 + u
            x = step_tile(xt_ref, t)
            states = [q * s + x for q, s in zip(keep, states)]
            sm_ref[pl.ds(pl.multiple_of(t * SUBS, SUBS), SUBS), :] = tree_sum(
                [w * s for w, s in zip(weight, states)]
            )
        return tuple(states)

    lax.fori_loop(0, width // 8, step, tuple(split_tiles(start, nd)))
    skip = pt_ref[3 * nd * SUBS : 3 * nd * SUBS + SUBS, :]
    for row in range(rp):
        rows = slice(row * width, (row + 1) * width)
        for chunk in range(nc):
            at = row * nc + chunk
            lanes = slice(chunk * LANES, (chunk + 1) * LANES)
            own = xt_ref[pl.ds(at, width, stride=SUBS), :]
            pre = sm_ref[pl.ds(at, width, stride=SUBS), :] + skip[at : at + 1, :] * own
            mpre_ref[rows, lanes] = pre
            mlow_ref[rows, lanes] = (pre * sigmoid(pre)).astype(BF16)
    (left,) = run_copies([(mlow_ref, mlow_to)], sems.at[1:])
    z_pre = dot(mlow_ref[...], z_ref[...])
    zpre_ref[...] = z_pre
    zeta = z_pre * sigmoid(z_pre)
    queries = (zeta * qg_ref[...] + qb_ref[...]).astype(BF16)
    keys = (zeta * kg_ref[...]).astype(BF16)
    scale = z_pre.shape[1] ** (-0.5)
    pieces = counts_ref.shape[0] // (rp * nc)
    begin = place * width
    piece = begin // span
    inner = begin - piece * span
    for row in range(rp):
        rows = slice(row * width, (row + 1) * width)
        count = counts_ref[(chan * rp + row) * pieces + piece]
        valid = lax.broadcasted_iota(jnp.int32, (width, width), 1) < count - inner
        scores = jnp.where(valid, dot_cols(queries[rows, :], keys[rows, :]) * scale, -1e30)
        top = jnp.max(scores, axis=-1, keepdims=True)
        weights = jnp.where(valid, jnp.exp(scores - top), 0.0)
        empty = jnp.where(count > inner, 0.0, 1.0)
        attn = weights / (jnp.sum(weights, axis=-1, keepdims=True) + empty)
        attn_ref[rows, :] = attn
        context = dot(attn.astype(BF16), val_ref[rows, :])
        ctx_ref[rows, :] = context
        r_pre = rpre_ref[rows, :]
        gated_ref[rows, :] = (r_pre * sigmoid(r_pre) * context).astype(BF16)
    leaving.wait()
    left.wait()


def ffn_kernel(
    nc, dim, gated_ref, h0, h1, h2, h3, x_at, grad_ref, fgain_ref,
    out_to, gmid_to, ggated_ref, keep_to, send_to, fg_ref,
    hid_ref, gup_ref, g_ref, out_ref, gmid_ref, x_ref, up_ref, o_ref, down_ref, part_ref, sems, out_sems, part_sems,
):
    units = h0.shape[1]
    rp = grad_ref.shape[0] // nc
    width = grad_ref.shape[1]
    chan = lax.axis_index("chan")
    urows = (h0.shape[0] - dim) // 4
    halves = dim // units
    hs = (h0, h1, h2, h3)

    def shards(ref, which):
        return [
            (
                h.at[dim + (which * halves + half) * urows : dim + (which * halves + half + 1) * urows, :],
                ref.at[j * urows : (j + 1) * urows, half * units : (half + 1) * units],
            )
            for j, h in enumerate(hs)
            for half in range(halves)
        ]

    copies = [(x_at, x_ref)] + shards(o_ref, 0)
    copies += [(h.at[0:dim, :], up_ref.at[:, j * units : (j + 1) * units]) for j, h in enumerate(hs)]
    copies += [(grad_ref.at[chan * rp + row], g_ref.at[row * width : (row + 1) * width, :]) for row in range(rp)]
    copies += shards(down_ref, 1)
    started = run_copies(copies, sems)
    first = 1 + 4 * halves
    for copy in started[:first]:
        copy.wait()
    middle = x_ref[...].astype(F32) + dot(gated_ref[...], o_ref[...])
    r = scale_of(middle)
    n = middle * r
    fgain = fgain_ref[...]
    ffn_low = (n * fgain).astype(BF16)
    for copy in started[first:]:
        copy.wait()
    g = g_ref[...]
    up_pre = dot(ffn_low, up_ref[...])
    sigma = sigmoid(up_pre)
    hid_ref[...] = (up_pre * sigma).astype(BF16)
    gup_ref[...] = (dot_cols(g, down_ref[...]) * (sigma * (1.0 + up_pre * (1.0 - sigma)))).astype(BF16)
    g_in = dot_cols(gup_ref[...], up_ref[...])
    h = g_in * fgain
    g_mid = g.astype(F32) + r * (h - n * jnp.mean(h * n, axis=-1, keepdims=True))
    gmid_ref[...] = g_mid
    g_branch = g_mid.astype(BF16)
    leaving = run_copies([(gmid_ref, gmid_to)], out_sems.at[0:1])
    fg_ref[...] = jnp.sum(g_in * n, axis=0, keepdims=True)

    def leave(begin, rows, which):
        part = slice(begin, begin + rows)
        return run_copies(
            [(part_ref.at[j, part, :], (keep_to, send_to)[j % 2].at[j // 2, part, :]) for j in (1, 3, 0, 2)],
            part_sems.at[4 * which : 4 * which + 4],
        )

    grad = dot_rows(ffn_low, gup_ref[...]).astype(BF16)
    for j in range(4):
        part_ref[j, 0:dim, :] = grad[:, j * units : (j + 1) * units]
    leaving += leave(0, dim, 0)
    for which, (left, right) in enumerate(((hid_ref, g), (gated_ref, g_branch))):
        grad = dot_rows(left[...], right).astype(BF16)
        begin = dim + (1 - which) * halves * urows
        for j in range(4):
            for half in range(halves):
                part_ref[j, begin + half * urows : begin + (half + 1) * urows, :] = grad[
                    j * urows : (j + 1) * urows, half * units : (half + 1) * units
                ]
        leaving += leave(begin, halves * urows, 1 + which)
    ggated_ref[...] = dot_cols(g_branch, o_ref[...])
    out = (middle + dot(hid_ref[...], down_ref[...])).astype(BF16)
    toks = g_ref.shape[0]
    for half in range(halves):
        out_ref[half * toks : (half + 1) * toks, :] = out[:, half * units : (half + 1) * units]
    leaving += run_copies([(out_ref, out_to)], out_sems.at[1:2])
    for copy in leaving:
        copy.wait()


def attn_back_kernel(
    nc, nd, ggated_ref, rpre_ref, vpre_ref, ctx_ref, attn_ref, val_ref, zpre_ref, mpre_ref, xt_ref, z_ref, pt_ref,
    qg_ref, kg_ref, qb_ref,
    gv_to, gr_to, gz_ref, gmt_ref, carry_ref, small_ref, skip_ref, buf, gv_ref, gr_ref, sems, out_sems,
):
    width = xt_ref.shape[0] // SUBS
    rp = SUBS // nc
    z_pre = zpre_ref[...]
    sigma = sigmoid(z_pre)
    zeta = z_pre * sigma
    queries = (zeta * qg_ref[...] + qb_ref[...]).astype(BF16)
    keys = (zeta * kg_ref[...]).astype(BF16)
    scale = z_pre.shape[1] ** (-0.5)
    parts_q, parts_k = [], []
    for row in range(rp):
        rows = slice(row * width, (row + 1) * width)
        g_gated = ggated_ref[rows, :]
        r_pre = rpre_ref[rows, :]
        sr = sigmoid(r_pre)
        g_context = (g_gated * (r_pre * sr)).astype(BF16)
        gr_ref[rows, :] = (g_gated * ctx_ref[rows, :] * (sr * (1.0 + r_pre * (1.0 - sr)))).astype(BF16)
        attn = attn_ref[rows, :]
        g_values = dot_rows(attn.astype(BF16), g_context)
        gv_ref[rows, :] = (g_values * silu_slope(vpre_ref[rows, :])).astype(BF16)
        g_attn = dot_cols(g_context, val_ref[rows, :])
        g_scores = attn * (g_attn - jnp.sum(attn * g_attn, axis=-1, keepdims=True))
        parts_q.append(exact(g_scores, keys[rows, :], ((1,), (0,))) * scale)
        parts_k.append(exact(g_scores, queries[rows, :], ((0,), (0,))) * scale)
    leaving = run_copies([(gv_ref, gv_to), (gr_ref, gr_to)], out_sems)
    g_q = jnp.concatenate(parts_q, axis=0)
    g_k = jnp.concatenate(parts_k, axis=0)
    small_ref[...] = jnp.concatenate(
        [
            jnp.sum(g_q * zeta, axis=0, keepdims=True),
            jnp.sum(g_k * zeta, axis=0, keepdims=True),
            jnp.sum(g_q, axis=0, keepdims=True),
            jnp.zeros((SUBS - 3, z_pre.shape[1]), F32),
        ],
        axis=0,
    )
    g_z = (g_q * qg_ref[...] + g_k * kg_ref[...]) * (sigma * (1.0 + z_pre * (1.0 - sigma)))
    gz_ref[...] = g_z
    for row in range(rp):
        rows = slice(row * width, (row + 1) * width)
        for chunk in range(nc):
            at = row * nc + chunk
            lanes = slice(chunk * LANES, (chunk + 1) * LANES)
            g_mixed = exact(g_z[rows, :], z_ref[lanes, :], ((1,), (1,))) * silu_slope(mpre_ref[rows, lanes])
            gmt_ref[pl.ds(at, width, stride=SUBS), :] = g_mixed
    keep = [tile(pt_ref, nd + k) for k in range(nd)]

    def step(block, carries):
        carries = list(carries)
        for u in range(8):
            gm = step_tile(gmt_ref, width - 1 - (block * 8 + u))
            carries = [q * (c + gm) for q, c in zip(keep, carries)]
        return tuple(carries)

    zero = jnp.zeros((SUBS, LANES), F32)
    carries = lax.fori_loop(0, width // 8, step, (zero,) * nd)
    buf[...] = jnp.concatenate(carries, axis=0).astype(BF16)
    leaving += run_copies([(buf, carry_ref.at[at]) for at in range(carry_ref.shape[0])], sems)
    skips = []
    for at in range(SUBS):
        every = pl.ds(at, width, stride=SUBS)
        skips.append(jnp.sum(gmt_ref[every, :] * xt_ref[every, :], axis=0, keepdims=True))
    skip_ref[...] = jnp.concatenate(skips, axis=0)
    for copy in leaving:
        copy.wait()


def grads_kernel(
    nc, dim, zrows, low_at, gv_at, gr_at, mlow_at, gz_ref, keep_to, *refs
):
    sends, (zg_ref, low_ref, gv_ref, gr_ref, mlow_ref, part_ref, sems, part_sems) = refs[:-8], refs[-8:]
    units = gv_ref.shape[1] // nc
    chan = lax.axis_index("chan")
    started = run_copies([(mlow_at, mlow_ref), (low_at, low_ref), (gv_at, gv_ref), (gr_at, gr_ref)], sems)
    started[0].wait()
    zg_ref[...] = exact(mlow_ref[...], gz_ref[...], ((0,), (0,)))
    for copy in started[1:]:
        copy.wait()
    low = low_ref[...]
    used = 2 * dim + zrows
    spare = part_ref.shape[1] - used
    leaving = []
    for j in (1, 3, 0, 2):
        cols = slice(j * units, (j + 1) * units)
        part_ref[j, 0:dim, :] = dot_rows(low, gv_ref[:, cols]).astype(BF16)
        part_ref[j, dim : 2 * dim, :] = dot_rows(low, gr_ref[:, cols]).astype(BF16)
        start = pl.multiple_of(jnp.bitwise_xor(chan, j) * 2 * zrows, 2 * zrows)
        block = zg_ref[pl.ds(start, 2 * zrows), :]
        part_ref[j, 2 * dim : used, :] = jnp.concatenate([block[:zrows, :], block[zrows:, :]], axis=1).astype(BF16)
        part_ref[j, used:, :] = jnp.zeros((spare, units), BF16)
        if j % 2:
            copies = []
            total, each = part_ref.shape[1], sends[0].shape[0]
            begin = 0
            while begin < total:
                at = j // 2 * total + begin
                take = min(total - begin, each - at % each)
                to = sends[at // each].at[at % each : at % each + take, :]
                copies.append((part_ref.at[j, begin : begin + take, :], to))
                begin += take
        else:
            copies = [(part_ref.at[j], keep_to.at[j // 2])]
        leaving += run_copies(copies, part_sems.at[4 * j : 4 * j + len(copies)])
    for copy in leaving:
        copy.wait()


def scans_kernel(
    nd, dim, gv_at, gr_at, h0, h1, h2, h3, pt_ref, sin_at, xt_ref, gmt_ref,
    shared_to, acc_to, shared_ref, acc_ref, sin_ref, buf, gv_ref, gr_ref, sems,
):
    units = h0.shape[1]
    width = xt_ref.shape[0] // SUBS
    started = run_copies(
        [(sin_at, sin_ref), (gv_at, gv_ref), (gr_at, gr_ref)]
        + [(ref.at[0 : 2 * dim, :], buf.at[j]) for j, ref in enumerate((h0, h1, h2, h3))],
        sems,
    )
    started[0].wait()
    group = nd // 2

    def scan(begin):
        ks = list(range(begin, begin + group))
        keep = [tile(pt_ref, nd + k) for k in ks]

        def step(block, carry):
            s, d, a, b = [list(part) for part in carry]
            for u in range(8):
                t = block * 8 + u
                x = step_tile(xt_ref, t)
                gm = step_tile(gmt_ref, t)
                d = [q * di + si for q, di, si in zip(keep, d, s)]
                s = [q * si + x for q, si in zip(keep, s)]
                a = [ai + gm * si for ai, si in zip(a, s)]
                b = [bi + gm * di for bi, di in zip(b, d)]
            return tuple(s), tuple(d), tuple(a), tuple(b)

        zero = (jnp.zeros((SUBS, LANES), F32),) * group
        init = tuple(tile(sin_ref, k) for k in ks)
        s, d, a, b = lax.fori_loop(0, width // 8, step, (init, zero, zero, zero))
        rows = slice(begin * SUBS, (begin + group) * SUBS)
        acc_ref[0, rows, :] = jnp.concatenate(a, axis=0)
        acc_ref[1, rows, :] = jnp.concatenate(b, axis=0)
        acc_ref[2, rows, :] = jnp.concatenate(d, axis=0)

    scan(0)
    for copy in started[1:3]:
        copy.wait()
    shared = None
    for j in range(4):
        cols = slice(j * units, (j + 1) * units)
        started[3 + j].wait()
        term = dot_cols(gv_ref[:, cols], buf[j, 0:dim, :]) + dot_cols(gr_ref[:, cols], buf[j, dim:, :])
        shared = term if j == 0 else shared + term
    shared_ref[...] = shared
    leaving = run_copies([(shared_ref, shared_to)], sems.at[1:])
    scan(group)
    leaving += run_copies([(acc_ref, acc_to)], sems)
    for copy in leaving:
        copy.wait()


def rest_rows(nd):
    return -(-(3 * nd + 4) // 16) * 16


def last_kernel(
    nc, nd, ns, span, carry_ref, gmt_ref, pt_ref, shared_at, x_at, gain_at, gmid_at, ids_at, sums_at,
    small_ref, skip_ref, fg_ref,
    keep_ref, send1_ref, send3_ref, yt_ref, acc_ref, ema_ref, rest_ref, shared_ref, x_ref, gain_ref, gmid_ref, ids_ref, sums_ref,
    sems,
):
    started = run_copies(
        [
            (shared_at, shared_ref), (x_at, x_ref), (gain_at, gain_ref), (gmid_at, gmid_ref), (ids_at, ids_ref),
            (sums_at, sums_ref),
        ],
        sems,
    )
    width = gmt_ref.shape[0] // SUBS
    rp = SUBS // nc
    vocab = acc_ref.shape[0]
    place = lax.axis_index("seq")
    chan = lax.axis_index("chan")
    amp, keep_all, out_all, root = weights_of(pt_ref, nd)
    whole = whole_keep(keep_all, width)
    per = span // width
    last = place // per * per + per - 1

    def gather(n, state):
        return state * whole + carry_ref[last - n].astype(F32)

    start = lax.fori_loop(0, last - place, gather, jnp.zeros_like(whole))
    drive = amp * root
    weight_all = out_all * drive
    keep = split_tiles(keep_all, nd)
    weight = split_tiles(weight_all, nd)

    def step(block, carries):
        carries = list(carries)
        for u in range(8):
            t = width - 1 - (block * 8 + u)
            gm = step_tile(gmt_ref, t)
            adj = [c + gm for c in carries]
            yt_ref[pl.ds(pl.multiple_of(t * SUBS, SUBS), SUBS), :] = tree_sum(
                [w * s for w, s in zip(weight, adj)]
            )
            carries = [q * s for q, s in zip(keep, adj)]
        return tuple(carries)

    lax.fori_loop(0, width // 8, step, tuple(split_tiles(start, nd)))
    for copy in started:
        copy.wait()
    a = sums_ref[0]
    g_drive = out_all * a
    grad_out = drive * a
    grad_in = g_drive * root
    grad_keep = weight_all * (sums_ref[1] + sums_ref[2] * start) - g_drive * amp * keep_all / root
    for at, grad in enumerate((grad_in, grad_keep, grad_out)):
        ema_ref[at * nd * SUBS : (at + 1) * nd * SUBS, :] = grad
    skip = pt_ref[3 * nd * SUBS : 3 * nd * SUBS + SUBS, :]
    gain = gain_ref[...]
    for row in range(rp):
        toks = slice(row * width, (row + 1) * width)
        pieces = []
        for chunk in range(nc):
            at = row * nc + chunk
            lanes = slice(chunk * LANES, (chunk + 1) * LANES)
            gm = gmt_ref[pl.ds(at, width, stride=SUBS), :]
            pieces.append(
                shared_ref[toks, lanes] + skip[at : at + 1, :] * gm + yt_ref[pl.ds(at, width, stride=SUBS), :]
            )
        g_normed = jnp.concatenate(pieces, axis=1)
        x = x_ref[toks, :].astype(F32)
        r = scale_of(x)
        n = x * r
        h = g_normed * gain
        g_x = gmid_ref[toks, :] + r * (h - n * jnp.mean(h * n, axis=-1, keepdims=True))
        part = jnp.sum(g_normed * n, axis=0, keepdims=True)
        ag = part if row == 0 else ag + part
        ids = ids_ref[pl.ds(chan * rp + row, 1), :]
        onehot = jnp.where(lax.broadcasted_iota(jnp.int32, (vocab, width), 0) == ids, 1.0, 0.0).astype(BF16)
        term = exact(onehot, g_x, ((1,), (0,)))
        acc_ref[...] = term if row == 0 else acc_ref[...] + term
    rest_ref[...] = jnp.zeros_like(rest_ref)
    for chunk in range(nc):
        lanes = slice(chunk * LANES, (chunk + 1) * LANES)
        for at in range(3):
            total = None
            for row in range(rp):
                term = ema_ref[pl.ds(at * nd * SUBS + row * nc + chunk, nd, stride=SUBS), :]
                total = term if row == 0 else total + term
            rest_ref[chunk, at * nd : (at + 1) * nd, :] = total
        at = 3 * nd
        rest_ref[chunk, at : at + 1, :] = sum(
            skip_ref[row * nc + chunk : row * nc + chunk + 1, :] for row in range(rp)
        )
        rest_ref[chunk, at + 1 : at + 2, :] = ag[:, lanes]
        rest_ref[chunk, at + 2 : at + 3, :] = fg_ref[:, lanes]
        if chunk < 3:
            rest_ref[chunk, at + 3 : at + 4, :] = small_ref[chunk : chunk + 1, :]
    half = vocab // 2
    room = rest_ref.shape[1]
    for j in range(4):
        to = (keep_ref.at[0], send1_ref, keep_ref.at[1], send3_ref)[j]
        owner = jnp.bitwise_xor(chan, j)
        block = acc_ref[:, pl.ds(pl.multiple_of(owner * LANES, LANES), LANES)]
        to[0:half, :] = jnp.concatenate([block[:half, :], block[half:, :]], axis=1).astype(BF16)
        rest = rest_ref[owner]
        high = rest.astype(BF16)
        low = (rest - high.astype(F32)).astype(BF16)
        to[half : half + room, :] = jnp.concatenate([high, low], axis=1)
        to[half + room :, :] = jnp.zeros((to.shape[0] - half - room, to.shape[1]), BF16)


def sum_kernel(in_ref, out_ref, buf, sems):
    total = in_ref[0].astype(F32)
    for at in range(1, in_ref.shape[0]):
        total = total + in_ref[at].astype(F32)
    buf[...] = total.astype(BF16)
    for copy in run_copies([(buf, out_ref.at[at]) for at in range(out_ref.shape[0])], sems):
        copy.wait()


def spread(parts, name, after=()):
    scratch = [pltpu.VMEM(parts.shape[1:], BF16), pltpu.SemaphoreType.DMA((parts.shape[0],))]
    return call(sum_kernel, (shape_of(parts.shape, BF16),), (parts,), name, scratch=scratch, out_hbm=(0,), after=after)[0]


def finish_kernel(
    nc, nd, w0, w1, w2, w3, embed_ref, ag_ref, ei_ref, ek_ref, eo_ref, es_ref, fg_ref, qg_ref, kg_ref, qb_ref, rest_ref
):
    half = embed_ref.shape[0] // 2
    room = rest_ref.shape[1]
    chan = lax.axis_index("chan")
    for j, ref in enumerate((w0, w1, w2, w3)):
        owner = jnp.bitwise_xor(chan, j)
        lanes = pl.ds(pl.multiple_of(owner * LANES, LANES), LANES)
        block = ref[0:half, :].astype(F32)
        embed_ref[0:half, lanes] = block[:, :LANES]
        embed_ref[half:, lanes] = block[:, LANES:]
        rest = ref[half : half + room, :].astype(F32)
        rest = rest[:, :LANES] + rest[:, LANES:]
        rest_ref[owner] = rest
        if j == 0:
            for at, to in enumerate((ei_ref, ek_ref, eo_ref)):
                to[...] = rest[at * nd : (at + 1) * nd, :]
            es_ref[...] = rest[3 * nd : 3 * nd + 1, :]
        ag_ref[:, lanes] = rest[3 * nd + 1 : 3 * nd + 2, :]
        fg_ref[:, lanes] = rest[3 * nd + 2 : 3 * nd + 3, :]
    for at, to in enumerate((qg_ref, kg_ref, qb_ref)):
        to[...] = rest_ref[at, 3 * nd + 3 : 3 * nd + 4, :]


def unpack_first(dim, urows, parts, u_ref, v_ref, up_ref, o_ref, down_ref, s_ref):
    join(parts, u_ref, v_ref, s_ref)
    units = s_ref.shape[1]
    up_ref[...] = s_ref[0:dim, :].astype(F32)
    for at, ref in enumerate((o_ref, down_ref)):
        for half in range(dim // units):
            start = dim + (at * (dim // units) + half) * urows
            ref[:, half * units : (half + 1) * units] = s_ref[start : start + urows, :].astype(F32)


def unpack_second(dim, zrows, parts, u_ref, x_ref, v_ref, r_ref, z_ref, s_ref):
    join(parts, u_ref, x_ref, s_ref)
    v_ref[...] = s_ref[0:dim, :].astype(F32)
    r_ref[...] = s_ref[dim : 2 * dim, :].astype(F32)
    block = s_ref[2 * dim : 2 * dim + zrows, :].astype(F32)
    z_ref[0:zrows, :] = block[:, :LANES]
    z_ref[zrows:, :] = block[:, LANES:]


def join(parts, mine_ref, other_ref, to_ref):
    if parts is None:
        to_ref[...] = mine_ref[...]
    else:
        join_halves(0, parts, mine_ref, other_ref, to_ref)


def plus(left, right):
    return (left.astype(F32) + right.astype(F32)).astype(BF16)


def piece_sum(keep_ref, got, chunk, begin, rows):
    each = got[0].shape[0]
    pieces = []
    while rows:
        at = chunk * keep_ref.shape[1] + begin
        inner = at % each
        take = min(rows, each - inner)
        pieces.append(plus(keep_ref[chunk, begin : begin + take, :], got[at // each][inner : inner + take, :]))
        begin, rows = begin + take, rows - take
    return pieces[0] if len(pieces) == 1 else jnp.concatenate(pieces, axis=0)


def add_core_split(split, keep_ref, *refs):
    got, refs = refs[:-8], refs[-8:]
    (mine_to, theirs_to, keep_to, send_to), (mine_ref, theirs_ref, halves_ref, sems) = refs[:4], refs[4:]
    half = (keep_ref.shape[1] - split) // 2
    theirs_ref[...] = piece_sum(keep_ref, got, 1, 0, split)
    leaving = run_copies([(theirs_ref, theirs_to)], sems.at[0:1])
    for chunk in range(2):
        for side in range(2):
            halves_ref[side, chunk * half : (chunk + 1) * half, :] = piece_sum(
                keep_ref, got, chunk, split + side * half, half
            )
    bit = seq_bit(0)
    leaving += run_copies([(halves_ref.at[1 - bit], send_to), (halves_ref.at[bit], keep_to)], sems.at[1:3])
    mine_ref[...] = piece_sum(keep_ref, got, 0, 0, split)
    leaving += run_copies([(mine_ref, mine_to)], sems.at[3:4])
    for copy in leaving:
        copy.wait()


def turn_kernel(mine_ref, got_ref, keep_ref, other_ref, kept_ref, send_ref, own_ref, theirs_ref):
    half = kept_ref.shape[0]
    bit = seq_bit(0)
    for side, ref in ((bit, kept_ref), (1 - bit, send_ref)):
        rows = pl.ds(pl.multiple_of(side * half, 16), half)
        ref[...] = plus(mine_ref[rows, :], got_ref[rows, :])
    half = own_ref.shape[0]
    own_ref[...] = plus(keep_ref[0:half, :], other_ref[0:half, :])
    theirs_ref[...] = plus(keep_ref[half:, :], other_ref[half:, :])


def add_core_far(keep_ref, *refs):
    got, (mine_to, theirs_to, mine_ref, theirs_ref, sems) = refs[:-5], refs[-5:]
    leaving = []
    for chunk, ref, to in ((1, theirs_ref, theirs_to), (0, mine_ref, mine_to)):
        ref[...] = piece_sum(keep_ref, got, chunk, 0, keep_ref.shape[1])
        leaving += run_copies([(ref, to)], sems.at[chunk : chunk + 1])
    for copy in leaving:
        copy.wait()


def add_core(keep_ref, got_ref, other_ref, mine_ref, theirs_ref):
    mine_ref[...] = plus(keep_ref[0], got_ref[...])
    theirs_ref[...] = plus(keep_ref[1], other_ref[...])


def add_plain(mine_ref, got_ref, out_ref):
    out_ref[...] = plus(mine_ref[...], got_ref[...])


def seq_bit(level):
    return jnp.bitwise_and(lax.shift_right_logical(lax.axis_index("seq"), level), 1)


def add_halves(level, parts, *refs):
    pairs, (keep_ref, send_ref) = refs[:-2], refs[-2:]
    bit = seq_bit(level)
    begin = 0
    for at in range(0, len(pairs), 2):
        mine_ref, got_ref = pairs[at : at + 2]
        inner = 0
        for rows in parts[at // 2]:
            half = rows // 2
            for side, ref in ((bit, keep_ref), (1 - bit, send_ref)):
                at_rows = pl.ds(pl.multiple_of(inner + side * half, 16), half)
                ref[begin : begin + half, :] = plus(mine_ref[at_rows, :], got_ref[at_rows, :])
            inner += rows
            begin += half


def join_halves(level, parts, mine_ref, got_ref, out_ref):
    bit = seq_bit(level)
    begin = 0
    for rows in parts:
        for side, ref in ((bit, mine_ref), (1 - bit, got_ref)):
            out_ref[pl.ds(pl.multiple_of(2 * begin + side * rows, 16), rows), :] = ref[begin : begin + rows, :]
        begin += rows


def join_part(begin, mine_ref, got_ref, out_ref):
    half = out_ref.shape[0] // 2
    bit = seq_bit(0)
    for side, ref in ((bit, mine_ref), (1 - bit, got_ref)):
        out_ref[pl.ds(pl.multiple_of(side * half, 16), half), :] = ref[begin : begin + half, :]


def output_kernel(w0, w1, w2, w3, out_ref):
    rows, width, dim = out_ref.shape
    units = w0.shape[1]
    toks = w0.shape[0] // (dim // units)
    chan = lax.axis_index("chan")
    for j, ref in enumerate((w0, w1, w2, w3)):
        for row in range(toks // width):
            for half in range(dim // units):
                start = half * toks + row * width
                out_ref[jnp.bitwise_xor(chan, j) * (toks // width) + row, :, half * units : (half + 1) * units] = ref[
                    start : start + width, :
                ]


def swap(value, mask, axis="chan"):
    return lax.ppermute(value, axis, [(at, at ^ mask) for at in range(lax.axis_size(axis))])


def exchange(value, axis):
    return lax.all_to_all(value, axis, 0, 0, tiled=True)


def add_pair(kernel, args, rows, name, after):
    shape = shape_of((rows, args[0].shape[-1]), BF16)
    return call(kernel, (shape, shape), args, name, free=range(3), out_free=(0, 1), after=after)


def seq_sum(value, ns, name):
    rows = value.shape[0]
    parts = exchange(value.reshape(ns, rows // ns, value.shape[1]), "seq")
    return exchange(spread(parts, name), "seq").reshape(value.shape)


def body(
    token_ids, valid_counts, embed, attn_gain, ema_in, ema_keep, ema_out, ema_skip, z_proj, q_gain, k_gain, q_bias,
    v_proj, r_proj, o_proj, ffn_gain, up_proj, down_proj, grad_out,
):
    rows, width = token_ids.shape
    vocab, dim = embed.shape
    nd = ema_in.shape[1]
    units = v_proj.shape[1]
    zdim = z_proj.shape[1]
    nc = lax.axis_size("chan")
    ns = lax.axis_size("seq")
    ndev = nc * ns
    rp = rows // nc
    toks = rp * width
    span = min(width * ns, SEQMAX)
    urows = o_proj.shape[0]
    zrows = z_proj.shape[0] // 2
    prows = 3 * nd + SUBS
    w1_rows = 2 * dim + zrows
    w2_rows = 3 * dim
    row = lambda vector: vector.reshape(1, -1)
    TOKENS.clear()

    dma = pltpu.SemaphoreType.DMA
    (p_own,) = call(
        pack_params, (shape_of((prows, LANES)),), (ema_in.T, ema_keep.T, ema_out.T, row(ema_skip)), "pack_params",
        scratch=[dma((4,))], hbm=range(4), out_free=(0,), limit=8,
    )
    p_far, p_near = swap(p_own, 2), swap(p_own, 1)
    x, xt, low, own1, own2 = call(
        functools.partial(prepare_kernel, nc),
        (
            shape_of((toks, dim), BF16), shape_of((width * SUBS, LANES)), shape_of((toks, dim), BF16),
            shape_of((w1_rows, units), BF16), shape_of((w2_rows, units), BF16),
        ),
        (token_ids, embed, row(attn_gain), v_proj, r_proj, z_proj, up_proj, o_proj, down_proj), "prepare",
        scratch=[
            pltpu.VMEM((rows, width), jnp.int32), pltpu.VMEM((vocab, dim), BF16), pltpu.VMEM((1, dim), F32),
            pltpu.VMEM((toks, dim), BF16), pltpu.VMEM((toks, dim), BF16), pltpu.VMEM((w1_rows, units), BF16),
            pltpu.VMEM((w2_rows, units), BF16), dma((3,)), dma((9,)), dma((4,)),
        ],
        hbm=range(9), out_hbm=(0, 2, 3, 4), after=("pack_params",),
    )
    own1, own2, p_far = lax.optimization_barrier((own1, own2, p_far))
    p_both = swap(p_far, 1)
    far1 = swap(own1, 2)
    near1 = swap(own1, 1)
    far2 = swap(own2, 2)
    near2 = swap(own2, 1)
    pt, ends = call(
        functools.partial(scan_end_kernel, nc, nd),
        (shape_of((prows * SUBS, LANES)), shape_of((ns, nd * SUBS, LANES))),
        (p_own, p_near, p_far, p_both, xt), "scan_end",
        scratch=[pltpu.VMEM((nc, prows, LANES), F32), pltpu.VMEM((nd * SUBS, LANES), F32), dma((ns,))],
        free=range(4), out_hbm=(1,), after=("prepare",), limit=8,
    )
    far1, _ = lax.optimization_barrier((far1, pt))
    both1 = swap(far1, 1)
    first = (own1, near1, far1, both1)
    ends = exchange(ends, "seq")
    v_pre, r_pre, values, z_all, values_far = call(
        functools.partial(project_kernel, dim),
        (
            shape_of((toks, nc * units)), shape_of((toks, nc * units)), shape_of((toks, nc * units), BF16),
            shape_of((dim, zdim), BF16), shape_of((toks, nc * units), BF16),
        ),
        (low,) + first, "project",
        scratch=[
            pltpu.VMEM((toks, dim), BF16), pltpu.VMEM((toks, nc * units), F32), pltpu.VMEM((4, w1_rows, units), BF16),
            dma((5,)), dma((8,)),
        ],
        hbm=range(4), free=(4,), out_hbm=(0, 4), after=("scan_end",), limit=16,
    )
    mixed_pre, mixed_low, z_pre, attn, context, gated, state_in = call(
        functools.partial(mix_kernel, nc, nd, span),
        (
            shape_of((toks, dim)), shape_of((toks, dim), BF16), shape_of((toks, zdim)), shape_of((toks, width)),
            shape_of((toks, nc * units)), shape_of((toks, nc * units), BF16), shape_of((nd * SUBS, LANES)),
        ),
        (
            valid_counts, ends, xt, pt, z_all, values, r_pre, row(q_gain), row(k_gain), row(q_bias),
        ),
        "mix", scratch=[pltpu.VMEM((width * SUBS, LANES), F32), pltpu.VMEM((nd * SUBS, LANES), F32), pltpu.VMEM((toks, dim), BF16), dma((2,))],
        smem=(0,), free=range(7, 10), out_hbm=(1, 6), after=("project",), limit=16,
    )
    far2, gated = lax.optimization_barrier((far2, gated))
    both2 = swap(far2, 1)
    second = (own2, near2, far2, both2)
    out_rows = toks * (dim // units)
    out, g_mid, g_gated, keep1, send1, ffn_grad = call(
        functools.partial(ffn_kernel, nc, dim),
        (
            shape_of((out_rows, units), BF16), shape_of((toks, dim)), shape_of((toks, nc * units)),
            shape_of((2, w2_rows, units), BF16), shape_of((2, w2_rows, units), BF16), shape_of((1, dim)),
        ),
        (gated,) + second + (x, grad_out, row(ffn_gain)),
        "ffn",
        scratch=[
            pltpu.VMEM((toks, nc * units), BF16), pltpu.VMEM((toks, nc * units), BF16),
            pltpu.VMEM((toks, dim), BF16), pltpu.VMEM((out_rows, units), BF16), pltpu.VMEM((toks, dim), F32),
            pltpu.VMEM((toks, dim), BF16), pltpu.VMEM((dim, nc * units), BF16), pltpu.VMEM((nc * urows, dim), BF16),
            pltpu.VMEM((nc * urows, dim), BF16), pltpu.VMEM((4, w2_rows, units), BF16),
            dma((1 + 8 * (dim // units) + 4 + rp,)), dma((2,)), dma((12,)),
        ],
        hbm=(1, 2, 3, 5, 6), free=(4, 7), out_hbm=(0, 1, 3, 4), after=("mix",), limit=32,
    )
    got1 = swap(send1, 1).reshape(2 * w2_rows, units)
    fast = ns == 8
    g2_rows = -(-w1_rows // (16 * ns)) * 16 * ns
    split1 = w2_rows - X_FIRST if fast else w2_rows
    split2 = g2_rows - X_ROWS if fast else g2_rows
    pieces = PIECES if fast else 2
    room = rest_rows(nd)
    f_rows = -(-(vocab // 2 + room) // (16 * ns)) * 16 * ns
    state = {"out": out}
    parts_of = lambda rows, split: tuple(part // 2 for part in (split, rows - split) if part)
    parts1, parts2 = parts_of(w2_rows, split1), parts_of(g2_rows, split2)
    half_of = lambda parts: tuple(part // 2 for part in parts)
    bf = lambda rows: shape_of((rows, units), BF16)

    def halves(level, pairs, parts, name, after):
        rows = sum(sum(part) for part in parts) // 2
        return call(
            functools.partial(add_halves, level, parts), (bf(rows),) * 2, pairs, name, free=range(len(pairs)),
            out_free=range(2), after=after,
        )

    def joined(level, pair, parts, name, after):
        return call(
            functools.partial(join_halves, level, parts), (bf(2 * pair[0].shape[0]),), pair, name, free=range(2),
            out_free=(0,), after=after,
        )[0]

    def add_two(pair, name, after):
        return call(add_plain, (bf(pair[0].shape[0]),), pair, name, free=range(2), out_free=(0,), after=after)[0]

    def over_seq(value, mask):
        return swap(value, mask, "seq")

    def core_whole(keep, gots, rows, name, after):
        mine, theirs = call(
            add_core_far, (bf(rows),) * 2, (keep, *gots), name,
            scratch=[pltpu.VMEM((rows, units), BF16), pltpu.VMEM((rows, units), BF16), dma((2,))],
            free=range(1 + len(gots)), out_hbm=range(2), after=after,
        )
        return mine, swap(theirs, 2)

    def tied(value, after):
        value, TOKENS[after[0]] = lax.optimization_barrier((value, TOKENS[after[0]]))
        return value

    def attn_back(after):
        grad_v, grad_r, g_z, gmt, carries, small, skip_grad = call(
            functools.partial(attn_back_kernel, nc, nd),
            (
                shape_of((toks, nc * units), BF16), shape_of((toks, nc * units), BF16), shape_of((toks, zdim)),
                shape_of((width * SUBS, LANES)), shape_of((ns, nd * SUBS, LANES), BF16), shape_of((SUBS, zdim)),
                shape_of((SUBS, LANES)),
            ),
            (
                g_gated, r_pre, v_pre, context, attn, values_far, z_pre, mixed_pre, xt, z_all, pt, row(q_gain),
                row(k_gain), row(q_bias),
            ),
            "attn_back",
            scratch=[
                pltpu.VMEM((nd * SUBS, LANES), BF16), pltpu.VMEM((toks, nc * units), BF16),
                pltpu.VMEM((toks, nc * units), BF16), dma((ns,)), dma((2,)),
            ],
            free=(2, 5, 11, 12, 13), out_hbm=(0, 1, 4), after=after, limit=20,
        )
        state.update(
            grad_v=grad_v, grad_r=grad_r, g_z=g_z, gmt=gmt, carries=carries, small=small, skip_grad=skip_grad,
        )

    def core_parted(keep, gots, rows, split, name, after):
        if split == rows:
            return core_whole(keep, gots, rows, name, after)
        mine, theirs, kept, send = call(
            functools.partial(add_core_split, split), (bf(split),) * 2 + (bf(rows - split),) * 2, (keep, *gots), name,
            scratch=[
                pltpu.VMEM((split, units), BF16), pltpu.VMEM((split, units), BF16),
                pltpu.VMEM((2, rows - split, units), BF16), dma((4,)),
            ],
            free=range(1 + len(gots)), out_hbm=range(4), after=after,
        )
        return mine, swap(theirs, 2), kept, over_seq(send, 1)

    def turned(sums, name, after):
        if len(sums) == 2:
            keep, send = halves(0, sums, ((sums[0].shape[0],),), name, after)
            return keep, over_seq(send, 1)
        near, far = sums[0].shape[0] // 2, sums[2].shape[0] // 2
        kept, send, own, theirs = call(
            turn_kernel, (bf(near), bf(near), bf(far), bf(far)), sums, name, free=range(4), out_free=range(4), after=after
        )
        return kept, over_seq(send, 1), own, swap(theirs, 2)

    def move_carry(after):
        state["carries"] = exchange(tied(state["carries"], after), "seq")

    def core_first(after):
        state["sums1"] = core_parted(keep1, (got1,), w2_rows, split1, "core_first", after)

    def grads(after):
        keep2, *sends = call(
            functools.partial(grads_kernel, nc, dim, zrows),
            (shape_of((2, g2_rows, units), BF16),) + (bf(2 * g2_rows // pieces),) * pieces,
            (low, state["grad_v"], state["grad_r"], mixed_low, state["g_z"]), "grads",
            scratch=[
                pltpu.VMEM((dim, zdim), F32), pltpu.VMEM((toks, dim), BF16), pltpu.VMEM((toks, nc * units), BF16),
                pltpu.VMEM((toks, nc * units), BF16), pltpu.VMEM((toks, dim), BF16),
                pltpu.VMEM((4, g2_rows, units), BF16), dma((4,)), dma((16,)),
            ],
            hbm=range(4), out_hbm=range(1 + pieces), after=after, limit=24,
        )
        state.update(keep2=keep2, gots2=[swap(value, 1) for value in sends])

    def scans(after):
        state["shared"], state["sums"] = call(
            functools.partial(scans_kernel, nd, dim), (shape_of((toks, dim)), shape_of((3, nd * SUBS, LANES))),
            (state["grad_v"], state["grad_r"]) + first + (pt, state_in, xt, state["gmt"]), "scans",
            scratch=[
                pltpu.VMEM((toks, dim), F32), pltpu.VMEM((3, nd * SUBS, LANES), F32), pltpu.VMEM((nd * SUBS, LANES), F32),
                pltpu.VMEM((4, 2 * dim, units), BF16), pltpu.VMEM((toks, nc * units), BF16),
                pltpu.VMEM((toks, nc * units), BF16), dma((7,)),
            ],
            hbm=(0, 1, 2, 3, 4, 5, 7), out_hbm=range(2), after=after, limit=24,
        )

    def core_second(after):
        state["sums2"] = core_parted(state["keep2"], state["gots2"], g2_rows, split2, "core_second", after)

    def x_first(after):
        state["sums1"] = turned(state["sums1"], "x_first", after)

    def last(after):
        state["f"] = call(
            functools.partial(last_kernel, nc, nd, ns, span),
            (shape_of((2, f_rows, units), BF16),) + (bf(f_rows),) * 2,
            (
                state["carries"], state["gmt"], pt, state["shared"], x, row(attn_gain), g_mid, token_ids, state["sums"],
                state["small"], state["skip_grad"], ffn_grad,
            ),
            "last",
            scratch=[
                pltpu.VMEM((width * SUBS, LANES), F32), pltpu.VMEM((vocab, dim), F32),
                pltpu.VMEM((3 * nd * SUBS, LANES), F32), pltpu.VMEM((nc, room, LANES), F32),
                pltpu.VMEM((toks, dim), F32), pltpu.VMEM((toks, dim), BF16), pltpu.VMEM((1, dim), F32),
                pltpu.VMEM((toks, dim), F32), pltpu.VMEM((rows, width), jnp.int32),
                pltpu.VMEM((3, nd * SUBS, LANES), F32), dma((6,)),
            ],
            hbm=range(3, 9), out_free=range(3), after=after, limit=16,
        )

    def core_last(after):
        keep, send, other = state["f"]
        mine, theirs = call(
            add_core, (bf(f_rows),) * 2, (keep, swap(send, 1), swap(other, 1)), "core_last", free=range(3),
            out_free=range(2), after=after,
        )
        state["sumsf"] = (mine, swap(theirs, 2))

    def x_last(after):
        keep, send = halves(0, state["sumsf"], ((f_rows,),), "x_last", after)
        state["sumsf"] = (keep, over_seq(send, 1))

    def turn_second(after):
        state["sums2"] = turned(state["sums2"], "turn_second", after)

    def z_first(after):
        keep, send = halves(1, state["sums1"], tuple((rows,) for rows in parts1), "z_first", after)
        state["sums1"] = (keep, over_seq(send, 2))

    def z_second(after):
        keep, send = halves(1, state["sums2"], tuple((rows,) for rows in parts2), "z_second", after)
        state["sums2"] = (keep, over_seq(send, 2))

    def add_step(key, mask, name):
        def step(after):
            value = add_two(state[key], name, after)
            state[key] = (value, over_seq(value, mask))

        return step

    def join_first(after):
        whole = joined(1, state["sums1"], half_of(parts1), "join_first", after)
        state["sums1"] = (whole, over_seq(whole, 1))

    def join_second(after):
        whole = joined(1, state["sums2"], half_of(parts2), "join_second", after)
        state["sums2"] = (whole, over_seq(whole, 1))

    def z_last(after):
        keep, send = halves(1, state["sumsf"], ((f_rows // 2,),), "z_last", after)
        state["sumsf"] = (keep, over_seq(send, 2))

    def join_last(after):
        whole = joined(1, state["sumsf"], (f_rows // 4,), "join_last", after)
        state["sumsf"] = (whole, over_seq(whole, 1))

    def move_out(after):
        state["out"] = tied(state["out"], after)
        state.update(out_far=swap(state["out"], 2), out_near=swap(state["out"], 1))

    def move_both(after):
        state["out_far"] = tied(state["out_far"], after)
        state["out_both"] = swap(state["out_far"], 1)

    def output(after):
        state["output"] = call(
            output_kernel, (shape_of((rows, width, dim), BF16),),
            (state["out"], state["out_near"], state["out_far"], state["out_both"]), "output", free=range(4),
            out_free=(0,), after=after, limit=8,
        )[0]

    def plain_sums(after):
        for key, name in (("sums1", "sum_first"), ("sums2", "sum_second"), ("sumsf", "sum_last")):
            total = seq_sum(add_two(state[key], "add_" + name, ()), ns, name)
            state[key] = (total, total)
        state["f_own"] = state["sumsf"][0]

    def unpack_first_step(after):
        state["first"] = call(
            functools.partial(unpack_first, dim, urows, parts1 if fast else None),
            (shape_of(up_proj.shape), shape_of(o_proj.shape), shape_of(down_proj.shape)), state["sums1"],
            "unpack_first", free=range(2), out_free=range(3), scratch=[pltpu.VMEM((w2_rows, units), BF16)], after=after,
        )

    def unpack_second_step(after):
        state["second"] = call(
            functools.partial(unpack_second, dim, zrows, parts2 if fast else None),
            (shape_of(v_proj.shape), shape_of(r_proj.shape), shape_of(z_proj.shape)), state["sums2"],
            "unpack_second", free=range(2), out_free=range(3), scratch=[pltpu.VMEM((g2_rows, units), BF16)],
            after=after,
        )

    def collect(after):
        (state["f_own"],) = call(
            functools.partial(join_part, 0), (bf(f_rows),), state["sumsf"], "collect", free=range(2),
            out_free=(0,), after=after,
        )

    def finish(after):
        own = state["f_own"]
        far = swap(own, 2)
        state["finish"] = call(
            functools.partial(finish_kernel, nc, nd),
            (
                shape_of((vocab, dim)), shape_of((1, dim)), shape_of((nd, LANES)), shape_of((nd, LANES)),
                shape_of((nd, LANES)), shape_of((1, LANES)), shape_of((1, dim)), shape_of((1, zdim)),
                shape_of((1, zdim)), shape_of((1, zdim)),
            ),
            (own, swap(own, 1), far, swap(far, 1)), "finish", free=range(4), out_free=range(10),
            scratch=[pltpu.VMEM((nc, room, LANES), F32)], after=after, limit=8,
        )

    steps = {
        "attn_back": attn_back, "core_first": core_first, "grads": grads, "scans": scans, "core_second": core_second,
        "x_first": x_first, "last": last, "core_last": core_last, "z_first": z_first, "turn_second": turn_second,
        "zz_first": add_step("sums1", 4, "zz_first"), "x_last": x_last, "z_second": z_second, "move_out": move_out,
        "zz_second": add_step("sums2", 4, "zz_second"), "sum_first": add_step("sums1", 2, "sum_first"),
        "z_last": z_last, "zz_last": add_step("sumsf", 4, "zz_last"), "sum_last": add_step("sumsf", 2, "sum_last"),
        "join_last": join_last, "move_carry": move_carry, "move_both": move_both, "join_first": join_first, "sum_second": add_step("sums2", 2, "sum_second"),
        "output": output, "join_second": join_second, "unpack_first": unpack_first_step, "collect": collect,
        "unpack_second": unpack_second_step, "finish": finish, "plain_sums": plain_sums,
    }
    previous = "ffn"
    for name in ORDER if fast else PLAIN:
        steps[name]((previous,))
        previous = name if name in TOKENS else previous
    output = state["output"]
    up_grad, o_grad, down_grad = state["first"]
    v_grad, r_grad, z_grad = state["second"]
    embed_grad, ag, gi, gk, go, gs, fg, qg, kg, qb = state["finish"]
    flat = lambda value: value.reshape(-1)
    return (
        output, embed_grad, flat(ag), gi.T, gk.T, go.T, flat(gs), z_grad, flat(qg), flat(kg), flat(qb), v_grad, r_grad,
        o_grad, flat(fg), up_grad, down_grad,
    )


def solution(mesh):
    placed = (
        P(None, "seq"), P(), P(), P(), P("chan", None), P("chan", None), P("chan", None), P("chan"), P("chan", None),
        P(), P(), P(), P(None, "chan"), P(None, "chan"), P("chan", None), P(), P(None, "chan"), P("chan", None),
        P(None, "seq", None),
    )
    return jax.shard_map(
        body,
        mesh=mesh,
        in_specs=placed,
        out_specs=(
            P(None, "seq", None), P(), P(), P("chan", None), P("chan", None), P("chan", None), P("chan"),
            P("chan", None), P(), P(), P(), P(None, "chan"), P(None, "chan"), P("chan", None), P(), P(None, "chan"),
            P("chan", None),
        ),
        check_vma=False,
    )
```

```python
import functools
import types

import jax
import jax.numpy as jnp
from jax import lax
from jax.experimental import pallas as pl
from jax.experimental.pallas import tpu as pltpu
from jax.sharding import PartitionSpec as P

SEQMAX = 4096
CHAN, SEQ = "chan", "seq"
EPS = 1e-06
F32 = jnp.float32
BF16 = jnp.bfloat16
LANES = 128
SUBS = 8
MIB = 1024 * 1024


def sigmoid(u):
    return 0.5 * jnp.tanh(0.5 * u) + 0.5


def silu_slope(pre):
    sigma = sigmoid(pre)
    return sigma * (1.0 + pre * (1.0 - sigma))


def mm(left, right, dims, precision=None):
    return lax.dot_general(
        left, right, ((dims[0], dims[1]), ((), ())), precision=precision, preferred_element_type=F32
    )


def dot(left, right):
    return mm(left, right, ((1,), (0,)))


def dot_rows(left, right):
    return mm(left, right, ((0,), (0,)))


def dot_cols(left, right):
    return mm(left, right, ((1,), (1,)))


def two_parts(value):
    high = value.astype(BF16)
    return high, (value - high.astype(F32)).astype(BF16)


def exact(left, right, dims):
    if left.dtype == BF16:
        high, low = two_parts(right)
        return mm(left, high, dims) + mm(left, low, dims)
    high, low = two_parts(left)
    return mm(high, right, dims) + mm(low, right, dims)


def shape_of(dims, dtype=F32):
    return jax.ShapeDtypeStruct(dims, dtype)


TOKEN = []
X_FIRST = 128
X_ROWS = 384
PIECES = 4


def call(
    kernel, outs, args, scratch=(), smem=(), hbm=(), free=(), far=(), out_hbm=(), out_free=(), out_far=(), limit=16
):
    waits = list(TOKEN)
    hbm, out_hbm = {*hbm, *far}, {*out_hbm, *out_far}
    count, made = len(args), len(outs)
    inner = kernel.func if isinstance(kernel, functools.partial) else kernel

    def run(*refs):
        rest = refs[count + len(waits) :]
        kernel(*refs[:count], *rest[:made], *rest[made + 1 :])

    def spec(at):
        if at >= count or (at in hbm and at not in far):
            return pl.BlockSpec(memory_space=pltpu.HBM)
        return pl.BlockSpec(memory_space=pltpu.SMEM if at in smem else pltpu.VMEM)

    def held(at, value):
        if at < count and (at in smem or at in free):
            return value
        return pltpu.with_memory_space_constraint(value, pltpu.HBM if at in hbm or at >= count else pltpu.VMEM)

    def result(at, out):
        if at in out_free:
            return out
        return (pltpu.HBM if at in out_hbm or at == made else pltpu.VMEM)(out.shape, out.dtype)

    shapes = list(outs) + [shape_of((SUBS, LANES))]
    *results, token = pl.pallas_call(
        run,
        out_shape=[result(at, out) for at, out in enumerate(shapes)],
        in_specs=[spec(at) for at in range(count + len(waits))],
        out_specs=[
            pl.BlockSpec(memory_space=pltpu.HBM if (at in out_hbm and at not in out_far) or at == made else pltpu.VMEM)
            for at in range(made + 1)
        ],
        scratch_shapes=list(scratch),
        name=inner.__name__,
        cost_estimate=pl.CostEstimate(flops=1, bytes_accessed=1, transcendentals=0),
        compiler_params=pltpu.CompilerParams(vmem_limit_bytes=limit * MIB),
    )(*[held(at, value) for at, value in enumerate([*args, *waits])])
    TOKEN[:] = [token]
    return results


def move(copies, sems):
    for copy in run_copies(copies, sems):
        copy.wait()


def run_copies(copies, sems):
    started = [pltpu.make_async_copy(src, dst, sems.at[at]) for at, (src, dst) in enumerate(copies)]
    for copy in started:
        copy.start()
    return started


def pack_params(in_ref, keep_ref, out_ref, skip_ref, p_ref, sems):
    nd, lanes = in_ref.shape
    copies = [(ref, p_ref.at[at * nd : (at + 1) * nd, :]) for at, ref in enumerate((in_ref, keep_ref, out_ref))]
    copies.append((skip_ref, p_ref.at[3 * nd : 3 * nd + 1, :]))
    move(copies, sems)
    rest = p_ref.shape[0] - 3 * nd
    p_ref[3 * nd :, :] = jnp.broadcast_to(p_ref[3 * nd : 3 * nd + 1, :], (rest, lanes))


def first_copies(v_ref, r_ref, z_ref, buf):
    dim = v_ref.shape[0]
    zrows = z_ref.shape[0] // 2
    copies = [(v_ref, buf.at[0:dim, :]), (r_ref, buf.at[dim : 2 * dim, :])]
    for half in range(2):
        copies.append(
            (
                z_ref.at[half * zrows : (half + 1) * zrows, :],
                buf.at[2 * dim : 2 * dim + zrows, half * LANES : (half + 1) * LANES],
            )
        )
    return copies


def second_copies(up_ref, o_ref, down_ref, buf):
    dim, units = up_ref.shape
    urows = o_ref.shape[0]
    copies = [(up_ref, buf.at[0:dim, :])]
    for at, ref in enumerate((o_ref, down_ref)):
        for half in range(dim // units):
            start = dim + (dim // units * at + half) * urows
            copies.append((ref.at[:, half * units : (half + 1) * units], buf.at[start : start + urows, :]))
    return copies


def prepare_kernel(
    nc, ids_at, table_at, gain_at, v_at, r_at, z_at, up_at, o_at, down_at,
    x_to, xt_ref, low_to, w1_to, w2_to,
    ids_ref, embed_ref, gain_ref, x_ref, low_ref, w1_ref, w2_ref, sems, w_sems, out_sems,
):
    entering = run_copies(first_copies(v_at, r_at, z_at, w1_ref), w_sems.at[0:4])
    started = run_copies([(ids_at, ids_ref), (table_at, embed_ref), (gain_at, gain_ref)], sems)
    later = run_copies(second_copies(up_at, o_at, down_at, w2_ref), w_sems.at[4:9])
    for copy in entering:
        copy.wait()
    leaving = run_copies([(w1_ref, w1_to)], out_sems.at[0:1])
    rp = x_ref.shape[0] // ids_ref.shape[1]
    width = ids_ref.shape[1]
    vocab = embed_ref.shape[0]
    chan = lax.axis_index(CHAN)
    for copy in started:
        copy.wait()
    for row in range(rp):
        ids = ids_ref[pl.ds(chan * rp + row, 1), :]
        onehot = jnp.where(lax.broadcasted_iota(jnp.int32, (vocab, width), 0) == ids, 1.0, 0.0).astype(BF16)
        x = dot_rows(onehot, embed_ref[...])
        x_ref[row * width : (row + 1) * width, :] = x.astype(BF16)
        normed = x * lax.rsqrt(jnp.mean(x * x, axis=-1, keepdims=True) + EPS) * gain_ref[...]
        low_ref[row * width : (row + 1) * width, :] = normed.astype(BF16)
        for chunk in range(nc):
            xt_ref[pl.ds(row * nc + chunk, width, stride=SUBS), :] = normed[
                :, chunk * LANES : (chunk + 1) * LANES
            ]
        for copy in later:
            copy.wait()
        later = []
        leaving += run_copies([(w2_ref, w2_to)], out_sems.at[1:2]) if row == 0 else []
    leaving += run_copies([(x_ref, x_to), (low_ref, low_to)], out_sems.at[2:4])
    for copy in leaving:
        copy.wait()


def tile(ref, at):
    return ref[at * SUBS : (at + 1) * SUBS, :]


def step_tile(ref, t):
    return ref[pl.ds(pl.multiple_of(t * SUBS, SUBS), SUBS), :]


def scan_end_kernel(nc, nd, p0, p1, p2, p3, xt_ref, pt_ref, end_ref, p_ref, buf, sems):
    width = xt_ref.shape[0] // SUBS
    prows = p_ref.shape[1]
    chan = lax.axis_index(CHAN)
    for j, ref in enumerate((p0, p1, p2, p3)):
        p_ref[jnp.bitwise_xor(chan, j)] = ref[...]
    for sub in range(SUBS):
        pt_ref[pl.ds(sub, prows, stride=SUBS), :] = p_ref[sub % nc]
    keep = [tile(pt_ref, nd + k) for k in range(nd)]

    def step(block, states):
        states = list(states)
        for u in range(8):
            x = step_tile(xt_ref, block * 8 + u)
            states = [q * s + x for q, s in zip(keep, states)]
        return tuple(states)

    zero = jnp.zeros((SUBS, LANES), F32)
    states = lax.fori_loop(0, width // 8, step, (zero,) * nd)
    buf[...] = jnp.concatenate(states, axis=0)
    for copy in run_copies([(buf, end_ref.at[at]) for at in range(end_ref.shape[0])], sems):
        copy.wait()


def project_kernel(
    dim, low_at, h0, h1, h2, h3, vpre_to, rpre_ref, val_ref, z_ref, val_to, low_ref, vpre_ref, buf, sems, out_sems
):
    chan = lax.axis_index(CHAN)
    units = h0.shape[1]
    zrows = h0.shape[0] - 2 * dim
    started = run_copies([(low_at, low_ref)] + [(ref, buf.at[j]) for j, ref in enumerate((h0, h1, h2, h3))], sems)
    started[0].wait()
    low = low_ref[...]
    leaving = []
    for j in range(4):
        started[1 + j].wait()
        w = buf.at[j]
        cols = slice(j * units, (j + 1) * units)
        v_pre = dot(low, w[0:dim, :])
        vpre_ref[:, cols] = v_pre
        val_ref[:, cols] = (v_pre * sigmoid(v_pre)).astype(BF16)
        leaving += run_copies(
            [(vpre_ref.at[:, cols], vpre_to.at[:, cols]), (val_ref.at[:, cols], val_to.at[:, cols])],
            out_sems.at[2 * j : 2 * j + 2],
        )
        rpre_ref[:, cols] = dot(low, w[dim : 2 * dim, :])
        start = pl.multiple_of(jnp.bitwise_xor(chan, j) * 2 * zrows, 2 * zrows)
        half = w[2 * dim : 2 * dim + zrows, :]
        z_ref[pl.ds(start, 2 * zrows), :] = jnp.concatenate([half[:, :LANES], half[:, LANES:]], axis=0)
    for copy in leaving:
        copy.wait()


def whole_keep(keep, width):
    whole = keep
    power = 1
    while power < width:
        whole = whole * whole
        power *= 2
    return whole


def weights_of(pt_ref, nd):
    amp = pt_ref[0 : nd * SUBS, :]
    keep = pt_ref[nd * SUBS : 2 * nd * SUBS, :]
    out = pt_ref[2 * nd * SUBS : 3 * nd * SUBS, :]
    root = jnp.sqrt(1.0 - keep * keep)
    return amp, keep, out, root


def split_tiles(value, nd):
    return [value[k * SUBS : (k + 1) * SUBS, :] for k in range(nd)]


def tree_sum(values):
    values = list(values)
    while len(values) > 1:
        values = [sum(values[i : i + 2][1:], values[i]) for i in range(0, len(values), 2)]
    return values[0]


def scale_of(x):
    return lax.rsqrt(jnp.mean(x * x, axis=-1, keepdims=True) + EPS)


def mix_kernel(
    nc, nd, span, counts_ref, ends_ref, xt_ref, pt_ref, z_ref, val_ref, rpre_ref, qg_ref, kg_ref, qb_ref,
    mpre_ref, mlow_to, zpre_ref, attn_ref, ctx_ref, gated_ref, sin_to, sm_ref, sin_ref, mlow_ref, sems,
):
    width = xt_ref.shape[0] // SUBS
    rp = SUBS // nc
    place = lax.axis_index(SEQ)
    chan = lax.axis_index(CHAN)
    amp, keep_all, out_all, root = weights_of(pt_ref, nd)
    whole = whole_keep(keep_all, width)
    per = span // width
    first = place // per * per

    def gather(n, state):
        return state * whole + ends_ref[n].astype(F32)

    start = lax.fori_loop(first, place, gather, jnp.zeros_like(whole))
    sin_ref[...] = start
    (leaving,) = run_copies([(sin_ref, sin_to)], sems.at[:1])
    keep = split_tiles(keep_all, nd)
    weight = split_tiles(out_all * amp * root, nd)

    def step(block, states):
        states = list(states)
        for u in range(8):
            t = block * 8 + u
            x = step_tile(xt_ref, t)
            states = [q * s + x for q, s in zip(keep, states)]
            sm_ref[pl.ds(pl.multiple_of(t * SUBS, SUBS), SUBS), :] = tree_sum(
                [w * s for w, s in zip(weight, states)]
            )
        return tuple(states)

    lax.fori_loop(0, width // 8, step, tuple(split_tiles(start, nd)))
    skip = pt_ref[3 * nd * SUBS : 3 * nd * SUBS + SUBS, :]
    for row in range(rp):
        rows = slice(row * width, (row + 1) * width)
        for chunk in range(nc):
            at = row * nc + chunk
            lanes = slice(chunk * LANES, (chunk + 1) * LANES)
            own = xt_ref[pl.ds(at, width, stride=SUBS), :]
            pre = sm_ref[pl.ds(at, width, stride=SUBS), :] + skip[at : at + 1, :] * own
            mpre_ref[rows, lanes] = pre
            mlow_ref[rows, lanes] = (pre * sigmoid(pre)).astype(BF16)
    (left,) = run_copies([(mlow_ref, mlow_to)], sems.at[1:])
    z_pre = dot(mlow_ref[...], z_ref[...])
    zpre_ref[...] = z_pre
    zeta = z_pre * sigmoid(z_pre)
    queries = (zeta * qg_ref[...] + qb_ref[...]).astype(BF16)
    keys = (zeta * kg_ref[...]).astype(BF16)
    scale = z_pre.shape[1] ** (-0.5)
    pieces = counts_ref.shape[0] // (rp * nc)
    begin = place * width
    piece = begin // span
    inner = begin - piece * span
    for row in range(rp):
        rows = slice(row * width, (row + 1) * width)
        count = counts_ref[(chan * rp + row) * pieces + piece]
        valid = lax.broadcasted_iota(jnp.int32, (width, width), 1) < count - inner
        scores = jnp.where(valid, dot_cols(queries[rows, :], keys[rows, :]) * scale, -1e30)
        top = jnp.max(scores, axis=-1, keepdims=True)
        weights = jnp.where(valid, jnp.exp(scores - top), 0.0)
        empty = jnp.where(count > inner, 0.0, 1.0)
        attn = weights / (jnp.sum(weights, axis=-1, keepdims=True) + empty)
        attn_ref[rows, :] = attn
        context = dot(attn.astype(BF16), val_ref[rows, :])
        ctx_ref[rows, :] = context
        r_pre = rpre_ref[rows, :]
        gated_ref[rows, :] = (r_pre * sigmoid(r_pre) * context).astype(BF16)
    leaving.wait()
    left.wait()


def ffn_kernel(
    nc, dim, gated_ref, h0, h1, h2, h3, x_at, grad_ref, fgain_ref,
    out_to, gmid_to, ggated_ref, keep_to, send_to, fg_ref,
    hid_ref, gup_ref, g_ref, out_ref, gmid_ref, x_ref, up_ref, o_ref, down_ref, part_ref, sems, out_sems, part_sems,
):
    units = h0.shape[1]
    rp = grad_ref.shape[0] // nc
    width = grad_ref.shape[1]
    chan = lax.axis_index(CHAN)
    urows = (h0.shape[0] - dim) // 4
    halves = dim // units
    hs = (h0, h1, h2, h3)

    def shards(ref, which):
        return [
            (
                h.at[dim + (which * halves + half) * urows : dim + (which * halves + half + 1) * urows, :],
                ref.at[j * urows : (j + 1) * urows, half * units : (half + 1) * units],
            )
            for j, h in enumerate(hs)
            for half in range(halves)
        ]

    copies = [(x_at, x_ref)] + shards(o_ref, 0)
    copies += [(h.at[0:dim, :], up_ref.at[:, j * units : (j + 1) * units]) for j, h in enumerate(hs)]
    copies += [(grad_ref.at[chan * rp + row], g_ref.at[row * width : (row + 1) * width, :]) for row in range(rp)]
    copies += shards(down_ref, 1)
    started = run_copies(copies, sems)
    first = 1 + 4 * halves
    for copy in started[:first]:
        copy.wait()
    middle = x_ref[...].astype(F32) + dot(gated_ref[...], o_ref[...])
    r = scale_of(middle)
    n = middle * r
    fgain = fgain_ref[...]
    ffn_low = (n * fgain).astype(BF16)
    for copy in started[first:]:
        copy.wait()
    g = g_ref[...]
    up_pre = dot(ffn_low, up_ref[...])
    sigma = sigmoid(up_pre)
    hid_ref[...] = (up_pre * sigma).astype(BF16)
    gup_ref[...] = (dot_cols(g, down_ref[...]) * (sigma * (1.0 + up_pre * (1.0 - sigma)))).astype(BF16)
    g_in = dot_cols(gup_ref[...], up_ref[...])
    h = g_in * fgain
    g_mid = g.astype(F32) + r * (h - n * jnp.mean(h * n, axis=-1, keepdims=True))
    gmid_ref[...] = g_mid
    g_branch = g_mid.astype(BF16)
    leaving = run_copies([(gmid_ref, gmid_to)], out_sems.at[0:1])
    fg_ref[...] = jnp.sum(g_in * n, axis=0, keepdims=True)

    def leave(begin, rows, which):
        part = slice(begin, begin + rows)
        return run_copies(
            [(part_ref.at[j, part, :], (keep_to, send_to)[j % 2].at[j // 2, part, :]) for j in (1, 3, 0, 2)],
            part_sems.at[4 * which : 4 * which + 4],
        )

    grad = dot_rows(ffn_low, gup_ref[...]).astype(BF16)
    for j in range(4):
        part_ref[j, 0:dim, :] = grad[:, j * units : (j + 1) * units]
    leaving += leave(0, dim, 0)
    for which, (left, right) in enumerate(((hid_ref, g), (gated_ref, g_branch))):
        grad = dot_rows(left[...], right).astype(BF16)
        begin = dim + (1 - which) * halves * urows
        for j in range(4):
            for half in range(halves):
                part_ref[j, begin + half * urows : begin + (half + 1) * urows, :] = grad[
                    j * urows : (j + 1) * urows, half * units : (half + 1) * units
                ]
        leaving += leave(begin, halves * urows, 1 + which)
    ggated_ref[...] = dot_cols(g_branch, o_ref[...])
    out = (middle + dot(hid_ref[...], down_ref[...])).astype(BF16)
    toks = g_ref.shape[0]
    for half in range(halves):
        out_ref[half * toks : (half + 1) * toks, :] = out[:, half * units : (half + 1) * units]
    leaving += run_copies([(out_ref, out_to)], out_sems.at[1:2])
    for copy in leaving:
        copy.wait()


def attn_back_kernel(
    nc, nd, ggated_ref, rpre_ref, vpre_ref, ctx_ref, attn_ref, val_ref, zpre_ref, mpre_ref, xt_ref, z_ref, pt_ref,
    qg_ref, kg_ref, qb_ref,
    gv_to, gr_to, gz_ref, gmt_ref, carry_ref, small_ref, skip_ref, buf, gv_ref, gr_ref, sems, out_sems,
):
    width = xt_ref.shape[0] // SUBS
    rp = SUBS // nc
    z_pre = zpre_ref[...]
    sigma = sigmoid(z_pre)
    zeta = z_pre * sigma
    queries = (zeta * qg_ref[...] + qb_ref[...]).astype(BF16)
    keys = (zeta * kg_ref[...]).astype(BF16)
    scale = z_pre.shape[1] ** (-0.5)
    parts_q, parts_k = [], []
    for row in range(rp):
        rows = slice(row * width, (row + 1) * width)
        g_gated = ggated_ref[rows, :]
        r_pre = rpre_ref[rows, :]
        sr = sigmoid(r_pre)
        g_context = (g_gated * (r_pre * sr)).astype(BF16)
        gr_ref[rows, :] = (g_gated * ctx_ref[rows, :] * (sr * (1.0 + r_pre * (1.0 - sr)))).astype(BF16)
        attn = attn_ref[rows, :]
        g_values = dot_rows(attn.astype(BF16), g_context)
        gv_ref[rows, :] = (g_values * silu_slope(vpre_ref[rows, :])).astype(BF16)
        g_attn = dot_cols(g_context, val_ref[rows, :])
        g_scores = attn * (g_attn - jnp.sum(attn * g_attn, axis=-1, keepdims=True))
        parts_q.append(exact(g_scores, keys[rows, :], ((1,), (0,))) * scale)
        parts_k.append(exact(g_scores, queries[rows, :], ((0,), (0,))) * scale)
    leaving = run_copies([(gv_ref, gv_to), (gr_ref, gr_to)], out_sems)
    g_q = jnp.concatenate(parts_q, axis=0)
    g_k = jnp.concatenate(parts_k, axis=0)
    small_ref[...] = jnp.concatenate(
        [
            jnp.sum(g_q * zeta, axis=0, keepdims=True),
            jnp.sum(g_k * zeta, axis=0, keepdims=True),
            jnp.sum(g_q, axis=0, keepdims=True),
            jnp.zeros((SUBS - 3, z_pre.shape[1]), F32),
        ],
        axis=0,
    )
    g_z = (g_q * qg_ref[...] + g_k * kg_ref[...]) * (sigma * (1.0 + z_pre * (1.0 - sigma)))
    gz_ref[...] = g_z
    for row in range(rp):
        rows = slice(row * width, (row + 1) * width)
        for chunk in range(nc):
            at = row * nc + chunk
            lanes = slice(chunk * LANES, (chunk + 1) * LANES)
            g_mixed = exact(g_z[rows, :], z_ref[lanes, :], ((1,), (1,))) * silu_slope(mpre_ref[rows, lanes])
            gmt_ref[pl.ds(at, width, stride=SUBS), :] = g_mixed
    keep = [tile(pt_ref, nd + k) for k in range(nd)]

    def step(block, carries):
        carries = list(carries)
        for u in range(8):
            gm = step_tile(gmt_ref, width - 1 - (block * 8 + u))
            carries = [q * (c + gm) for q, c in zip(keep, carries)]
        return tuple(carries)

    zero = jnp.zeros((SUBS, LANES), F32)
    carries = lax.fori_loop(0, width // 8, step, (zero,) * nd)
    buf[...] = jnp.concatenate(carries, axis=0).astype(BF16)
    leaving += run_copies([(buf, carry_ref.at[at]) for at in range(carry_ref.shape[0])], sems)
    skips = []
    for at in range(SUBS):
        every = pl.ds(at, width, stride=SUBS)
        skips.append(jnp.sum(gmt_ref[every, :] * xt_ref[every, :], axis=0, keepdims=True))
    skip_ref[...] = jnp.concatenate(skips, axis=0)
    for copy in leaving:
        copy.wait()


def grads_kernel(
    nc, dim, zrows, low_at, gv_at, gr_at, mlow_at, gz_ref, keep_to, *refs
):
    sends, (zg_ref, low_ref, gv_ref, gr_ref, mlow_ref, part_ref, sems, part_sems) = refs[:-8], refs[-8:]
    units = gv_ref.shape[1] // nc
    chan = lax.axis_index(CHAN)
    started = run_copies([(mlow_at, mlow_ref), (low_at, low_ref), (gv_at, gv_ref), (gr_at, gr_ref)], sems)
    started[0].wait()
    zg_ref[...] = exact(mlow_ref[...], gz_ref[...], ((0,), (0,)))
    for copy in started[1:]:
        copy.wait()
    low = low_ref[...]
    used = 2 * dim + zrows
    spare = part_ref.shape[1] - used
    leaving = []
    for j in (1, 3, 0, 2):
        cols = slice(j * units, (j + 1) * units)
        part_ref[j, 0:dim, :] = dot_rows(low, gv_ref[:, cols]).astype(BF16)
        part_ref[j, dim : 2 * dim, :] = dot_rows(low, gr_ref[:, cols]).astype(BF16)
        start = pl.multiple_of(jnp.bitwise_xor(chan, j) * 2 * zrows, 2 * zrows)
        block = zg_ref[pl.ds(start, 2 * zrows), :]
        part_ref[j, 2 * dim : used, :] = jnp.concatenate([block[:zrows, :], block[zrows:, :]], axis=1).astype(BF16)
        part_ref[j, used:, :] = jnp.zeros((spare, units), BF16)
        if j % 2:
            copies = []
            total, each = part_ref.shape[1], sends[0].shape[0]
            begin = 0
            while begin < total:
                at = j // 2 * total + begin
                take = min(total - begin, each - at % each)
                to = sends[at // each].at[at % each : at % each + take, :]
                copies.append((part_ref.at[j, begin : begin + take, :], to))
                begin += take
        else:
            copies = [(part_ref.at[j], keep_to.at[j // 2])]
        leaving += run_copies(copies, part_sems.at[4 * j : 4 * j + len(copies)])
    for copy in leaving:
        copy.wait()


def scans_kernel(
    nd, dim, gv_at, gr_at, h0, h1, h2, h3, pt_ref, sin_at, xt_ref, gmt_ref,
    shared_to, acc_to, shared_ref, acc_ref, sin_ref, buf, gv_ref, gr_ref, sems,
):
    units = h0.shape[1]
    width = xt_ref.shape[0] // SUBS
    started = run_copies(
        [(sin_at, sin_ref), (gv_at, gv_ref), (gr_at, gr_ref)]
        + [(ref.at[0 : 2 * dim, :], buf.at[j]) for j, ref in enumerate((h0, h1, h2, h3))],
        sems,
    )
    started[0].wait()
    group = nd // 2

    def scan(begin):
        ks = list(range(begin, begin + group))
        keep = [tile(pt_ref, nd + k) for k in ks]

        def step(block, carry):
            s, d, a, b = [list(part) for part in carry]
            for u in range(8):
                t = block * 8 + u
                x = step_tile(xt_ref, t)
                gm = step_tile(gmt_ref, t)
                d = [q * di + si for q, di, si in zip(keep, d, s)]
                s = [q * si + x for q, si in zip(keep, s)]
                a = [ai + gm * si for ai, si in zip(a, s)]
                b = [bi + gm * di for bi, di in zip(b, d)]
            return tuple(s), tuple(d), tuple(a), tuple(b)

        zero = (jnp.zeros((SUBS, LANES), F32),) * group
        init = tuple(tile(sin_ref, k) for k in ks)
        s, d, a, b = lax.fori_loop(0, width // 8, step, (init, zero, zero, zero))
        rows = slice(begin * SUBS, (begin + group) * SUBS)
        acc_ref[0, rows, :] = jnp.concatenate(a, axis=0)
        acc_ref[1, rows, :] = jnp.concatenate(b, axis=0)
        acc_ref[2, rows, :] = jnp.concatenate(d, axis=0)

    scan(0)
    for copy in started[1:3]:
        copy.wait()
    shared = None
    for j in range(4):
        cols = slice(j * units, (j + 1) * units)
        started[3 + j].wait()
        term = dot_cols(gv_ref[:, cols], buf[j, 0:dim, :]) + dot_cols(gr_ref[:, cols], buf[j, dim:, :])
        shared = term if j == 0 else shared + term
    shared_ref[...] = shared
    leaving = run_copies([(shared_ref, shared_to)], sems.at[1:])
    scan(group)
    leaving += run_copies([(acc_ref, acc_to)], sems)
    for copy in leaving:
        copy.wait()


def rest_rows(nd):
    return -(-(3 * nd + 4) // 16) * 16


def last_kernel(
    nc, nd, ns, span, carry_ref, gmt_ref, pt_ref, shared_at, x_at, gain_at, gmid_at, ids_at, sums_at,
    small_ref, skip_ref, fg_ref,
    keep_ref, send1_ref, send3_ref, yt_ref, acc_ref, ema_ref, rest_ref, shared_ref, x_ref, gain_ref, gmid_ref, ids_ref, sums_ref,
    sems,
):
    started = run_copies(
        [
            (shared_at, shared_ref), (x_at, x_ref), (gain_at, gain_ref), (gmid_at, gmid_ref), (ids_at, ids_ref),
            (sums_at, sums_ref),
        ],
        sems,
    )
    width = gmt_ref.shape[0] // SUBS
    rp = SUBS // nc
    vocab = acc_ref.shape[0]
    place = lax.axis_index(SEQ)
    chan = lax.axis_index(CHAN)
    amp, keep_all, out_all, root = weights_of(pt_ref, nd)
    whole = whole_keep(keep_all, width)
    per = span // width
    last = place // per * per + per - 1

    def gather(n, state):
        return state * whole + carry_ref[last - n].astype(F32)

    start = lax.fori_loop(0, last - place, gather, jnp.zeros_like(whole))
    drive = amp * root
    weight_all = out_all * drive
    keep = split_tiles(keep_all, nd)
    weight = split_tiles(weight_all, nd)

    def step(block, carries):
        carries = list(carries)
        for u in range(8):
            t = width - 1 - (block * 8 + u)
            gm = step_tile(gmt_ref, t)
            adj = [c + gm for c in carries]
            yt_ref[pl.ds(pl.multiple_of(t * SUBS, SUBS), SUBS), :] = tree_sum(
                [w * s for w, s in zip(weight, adj)]
            )
            carries = [q * s for q, s in zip(keep, adj)]
        return tuple(carries)

    lax.fori_loop(0, width // 8, step, tuple(split_tiles(start, nd)))
    for copy in started:
        copy.wait()
    a = sums_ref[0]
    g_drive = out_all * a
    grad_out = drive * a
    grad_in = g_drive * root
    grad_keep = weight_all * (sums_ref[1] + sums_ref[2] * start) - g_drive * amp * keep_all / root
    for at, grad in enumerate((grad_in, grad_keep, grad_out)):
        ema_ref[at * nd * SUBS : (at + 1) * nd * SUBS, :] = grad
    skip = pt_ref[3 * nd * SUBS : 3 * nd * SUBS + SUBS, :]
    gain = gain_ref[...]
    for row in range(rp):
        toks = slice(row * width, (row + 1) * width)
        pieces = []
        for chunk in range(nc):
            at = row * nc + chunk
            lanes = slice(chunk * LANES, (chunk + 1) * LANES)
            gm = gmt_ref[pl.ds(at, width, stride=SUBS), :]
            pieces.append(
                shared_ref[toks, lanes] + skip[at : at + 1, :] * gm + yt_ref[pl.ds(at, width, stride=SUBS), :]
            )
        g_normed = jnp.concatenate(pieces, axis=1)
        x = x_ref[toks, :].astype(F32)
        r = scale_of(x)
        n = x * r
        h = g_normed * gain
        g_x = gmid_ref[toks, :] + r * (h - n * jnp.mean(h * n, axis=-1, keepdims=True))
        part = jnp.sum(g_normed * n, axis=0, keepdims=True)
        ag = part if row == 0 else ag + part
        ids = ids_ref[pl.ds(chan * rp + row, 1), :]
        onehot = jnp.where(lax.broadcasted_iota(jnp.int32, (vocab, width), 0) == ids, 1.0, 0.0).astype(BF16)
        term = exact(onehot, g_x, ((1,), (0,)))
        acc_ref[...] = term if row == 0 else acc_ref[...] + term
    rest_ref[...] = jnp.zeros_like(rest_ref)
    for chunk in range(nc):
        lanes = slice(chunk * LANES, (chunk + 1) * LANES)
        for at in range(3):
            total = None
            for row in range(rp):
                term = ema_ref[pl.ds(at * nd * SUBS + row * nc + chunk, nd, stride=SUBS), :]
                total = term if row == 0 else total + term
            rest_ref[chunk, at * nd : (at + 1) * nd, :] = total
        at = 3 * nd
        rest_ref[chunk, at : at + 1, :] = sum(
            skip_ref[row * nc + chunk : row * nc + chunk + 1, :] for row in range(rp)
        )
        rest_ref[chunk, at + 1 : at + 2, :] = ag[:, lanes]
        rest_ref[chunk, at + 2 : at + 3, :] = fg_ref[:, lanes]
        if chunk < 3:
            rest_ref[chunk, at + 3 : at + 4, :] = small_ref[chunk : chunk + 1, :]
    half = vocab // 2
    room = rest_ref.shape[1]
    for j in range(4):
        to = (keep_ref.at[0], send1_ref, keep_ref.at[1], send3_ref)[j]
        owner = jnp.bitwise_xor(chan, j)
        block = acc_ref[:, pl.ds(pl.multiple_of(owner * LANES, LANES), LANES)]
        to[0:half, :] = jnp.concatenate([block[:half, :], block[half:, :]], axis=1).astype(BF16)
        rest = rest_ref[owner]
        high = rest.astype(BF16)
        low = (rest - high.astype(F32)).astype(BF16)
        to[half : half + room, :] = jnp.concatenate([high, low], axis=1)
        to[half + room :, :] = jnp.zeros((to.shape[0] - half - room, to.shape[1]), BF16)


def sum_kernel(in_ref, out_ref, buf, sems):
    total = in_ref[0].astype(F32)
    for at in range(1, in_ref.shape[0]):
        total = total + in_ref[at].astype(F32)
    buf[...] = total.astype(BF16)
    for copy in run_copies([(buf, out_ref.at[at]) for at in range(out_ref.shape[0])], sems):
        copy.wait()


def spread(parts):
    scratch = [pltpu.VMEM(parts.shape[1:], BF16), pltpu.SemaphoreType.DMA((parts.shape[0],))]
    return call(sum_kernel, (shape_of(parts.shape, BF16),), (parts,), scratch=scratch, out_hbm=(0,))[0]


def finish_kernel(
    nc, nd, w0, w1, w2, w3, embed_ref, ag_ref, ei_ref, ek_ref, eo_ref, es_ref, fg_ref, qg_ref, kg_ref, qb_ref, rest_ref
):
    half = embed_ref.shape[0] // 2
    room = rest_ref.shape[1]
    chan = lax.axis_index(CHAN)
    for j, ref in enumerate((w0, w1, w2, w3)):
        owner = jnp.bitwise_xor(chan, j)
        lanes = pl.ds(pl.multiple_of(owner * LANES, LANES), LANES)
        block = ref[0:half, :].astype(F32)
        embed_ref[0:half, lanes] = block[:, :LANES]
        embed_ref[half:, lanes] = block[:, LANES:]
        rest = ref[half : half + room, :].astype(F32)
        rest = rest[:, :LANES] + rest[:, LANES:]
        rest_ref[owner] = rest
        if j == 0:
            for at, to in enumerate((ei_ref, ek_ref, eo_ref)):
                to[...] = rest[at * nd : (at + 1) * nd, :]
            es_ref[...] = rest[3 * nd : 3 * nd + 1, :]
        ag_ref[:, lanes] = rest[3 * nd + 1 : 3 * nd + 2, :]
        fg_ref[:, lanes] = rest[3 * nd + 2 : 3 * nd + 3, :]
    for at, to in enumerate((qg_ref, kg_ref, qb_ref)):
        to[...] = rest_ref[at, 3 * nd + 3 : 3 * nd + 4, :]


def unpack_first(dim, urows, parts, u_ref, v_ref, up_ref, o_ref, down_ref, s_ref):
    join(parts, u_ref, v_ref, s_ref)
    units = s_ref.shape[1]
    up_ref[...] = s_ref[0:dim, :].astype(F32)
    for at, ref in enumerate((o_ref, down_ref)):
        for half in range(dim // units):
            start = dim + (at * (dim // units) + half) * urows
            ref[:, half * units : (half + 1) * units] = s_ref[start : start + urows, :].astype(F32)


def unpack_second(dim, zrows, parts, u_ref, x_ref, v_ref, r_ref, z_ref, s_ref):
    join(parts, u_ref, x_ref, s_ref)
    v_ref[...] = s_ref[0:dim, :].astype(F32)
    r_ref[...] = s_ref[dim : 2 * dim, :].astype(F32)
    block = s_ref[2 * dim : 2 * dim + zrows, :].astype(F32)
    z_ref[0:zrows, :] = block[:, :LANES]
    z_ref[zrows:, :] = block[:, LANES:]


def join(parts, mine_ref, other_ref, to_ref):
    if parts is None:
        to_ref[...] = mine_ref[...]
    else:
        join_halves(0, parts, mine_ref, other_ref, to_ref)


def plus(left, right):
    return (left.astype(F32) + right.astype(F32)).astype(BF16)


def piece_sum(keep_ref, got, chunk, begin, rows):
    each = got[0].shape[0]
    pieces = []
    while rows:
        at = chunk * keep_ref.shape[1] + begin
        inner = at % each
        take = min(rows, each - inner)
        pieces.append(plus(keep_ref[chunk, begin : begin + take, :], got[at // each][inner : inner + take, :]))
        begin, rows = begin + take, rows - take
    return pieces[0] if len(pieces) == 1 else jnp.concatenate(pieces, axis=0)


def add_core_split(split, keep_ref, *refs):
    got, refs = refs[:-8], refs[-8:]
    (mine_to, theirs_to, keep_to, send_to), (mine_ref, theirs_ref, halves_ref, sems) = refs[:4], refs[4:]
    half = (keep_ref.shape[1] - split) // 2
    theirs_ref[...] = piece_sum(keep_ref, got, 1, 0, split)
    leaving = run_copies([(theirs_ref, theirs_to)], sems.at[0:1])
    for chunk in range(2):
        for side in range(2):
            halves_ref[side, chunk * half : (chunk + 1) * half, :] = piece_sum(
                keep_ref, got, chunk, split + side * half, half
            )
    bit = seq_bit(0)
    leaving += run_copies([(halves_ref.at[1 - bit], send_to), (halves_ref.at[bit], keep_to)], sems.at[1:3])
    mine_ref[...] = piece_sum(keep_ref, got, 0, 0, split)
    leaving += run_copies([(mine_ref, mine_to)], sems.at[3:4])
    for copy in leaving:
        copy.wait()


def turn_kernel(mine_ref, got_ref, keep_ref, other_ref, kept_ref, send_ref, own_ref, theirs_ref):
    half = kept_ref.shape[0]
    bit = seq_bit(0)
    for side, ref in ((bit, kept_ref), (1 - bit, send_ref)):
        rows = pl.ds(pl.multiple_of(side * half, 16), half)
        ref[...] = plus(mine_ref[rows, :], got_ref[rows, :])
    half = own_ref.shape[0]
    own_ref[...] = plus(keep_ref[0:half, :], other_ref[0:half, :])
    theirs_ref[...] = plus(keep_ref[half:, :], other_ref[half:, :])


def add_core_far(keep_ref, *refs):
    got, (mine_to, theirs_to, mine_ref, theirs_ref, sems) = refs[:-5], refs[-5:]
    leaving = []
    for chunk, ref, to in ((1, theirs_ref, theirs_to), (0, mine_ref, mine_to)):
        ref[...] = piece_sum(keep_ref, got, chunk, 0, keep_ref.shape[1])
        leaving += run_copies([(ref, to)], sems.at[chunk : chunk + 1])
    for copy in leaving:
        copy.wait()


def add_core(keep_ref, got_ref, other_ref, mine_ref, theirs_ref):
    mine_ref[...] = plus(keep_ref[0], got_ref[...])
    theirs_ref[...] = plus(keep_ref[1], other_ref[...])


def add_plain(mine_ref, got_ref, out_ref):
    out_ref[...] = plus(mine_ref[...], got_ref[...])


def seq_bit(level):
    return jnp.bitwise_and(lax.shift_right_logical(lax.axis_index(SEQ), level), 1)


def add_halves(level, parts, *refs):
    pairs, (keep_ref, send_ref) = refs[:-2], refs[-2:]
    bit = seq_bit(level)
    begin = 0
    for at in range(0, len(pairs), 2):
        mine_ref, got_ref = pairs[at : at + 2]
        inner = 0
        for rows in parts[at // 2]:
            half = rows // 2
            for side, ref in ((bit, keep_ref), (1 - bit, send_ref)):
                at_rows = pl.ds(pl.multiple_of(inner + side * half, 16), half)
                ref[begin : begin + half, :] = plus(mine_ref[at_rows, :], got_ref[at_rows, :])
            inner += rows
            begin += half


def join_halves(level, parts, mine_ref, got_ref, out_ref):
    bit = seq_bit(level)
    begin = 0
    for rows in parts:
        for side, ref in ((bit, mine_ref), (1 - bit, got_ref)):
            out_ref[pl.ds(pl.multiple_of(2 * begin + side * rows, 16), rows), :] = ref[begin : begin + rows, :]
        begin += rows


def join_part(begin, mine_ref, got_ref, out_ref):
    half = out_ref.shape[0] // 2
    bit = seq_bit(0)
    for side, ref in ((bit, mine_ref), (1 - bit, got_ref)):
        out_ref[pl.ds(pl.multiple_of(side * half, 16), half), :] = ref[begin : begin + half, :]


def output_kernel(w0, w1, w2, w3, out_ref):
    rows, width, dim = out_ref.shape
    units = w0.shape[1]
    toks = w0.shape[0] // (dim // units)
    chan = lax.axis_index(CHAN)
    for j, ref in enumerate((w0, w1, w2, w3)):
        for row in range(toks // width):
            for half in range(dim // units):
                start = half * toks + row * width
                out_ref[jnp.bitwise_xor(chan, j) * (toks // width) + row, :, half * units : (half + 1) * units] = ref[
                    start : start + width, :
                ]


def swap(value, mask, axis=CHAN):
    return lax.ppermute(value, axis, [(at, at ^ mask) for at in range(lax.axis_size(axis))])


def exchange(value, axis):
    return lax.all_to_all(value, axis, 0, 0, tiled=True)


def seq_sum(value, ns):
    rows = value.shape[0]
    parts = exchange(value.reshape(ns, rows // ns, value.shape[1]), SEQ)
    return exchange(spread(parts), SEQ).reshape(value.shape)


def body(
    token_ids, valid_counts, embed, attn_gain, ema_in, ema_keep, ema_out, ema_skip, z_proj, q_gain, k_gain, q_bias,
    v_proj, r_proj, o_proj, ffn_gain, up_proj, down_proj, grad_out,
):
    rows, width = token_ids.shape
    vocab, dim = embed.shape
    nd = ema_in.shape[1]
    units = v_proj.shape[1]
    zdim = z_proj.shape[1]
    nc = lax.axis_size(CHAN)
    ns = lax.axis_size(SEQ)
    ndev = nc * ns
    rp = rows // nc
    toks = rp * width
    span = min(width * ns, SEQMAX)
    urows = o_proj.shape[0]
    zrows = z_proj.shape[0] // 2
    prows = 3 * nd + SUBS
    w1_rows = 2 * dim + zrows
    w2_rows = 3 * dim
    row = lambda vector: vector.reshape(1, -1)
    TOKEN.clear()

    dma = pltpu.SemaphoreType.DMA
    (p_own,) = call(
        pack_params, (shape_of((prows, LANES)),), (ema_in.T, ema_keep.T, ema_out.T, row(ema_skip)),
        scratch=[dma((4,))], hbm=range(4), out_free=(0,), limit=8,
    )
    p_far, p_near = swap(p_own, 2), swap(p_own, 1)
    x, xt, low, own1, own2 = call(
        functools.partial(prepare_kernel, nc),
        (
            shape_of((toks, dim), BF16), shape_of((width * SUBS, LANES)), shape_of((toks, dim), BF16),
            shape_of((w1_rows, units), BF16), shape_of((w2_rows, units), BF16),
        ),
        (token_ids, embed, row(attn_gain), v_proj, r_proj, z_proj, up_proj, o_proj, down_proj),
        scratch=[
            pltpu.VMEM((rows, width), jnp.int32), pltpu.VMEM((vocab, dim), BF16), pltpu.VMEM((1, dim), F32),
            pltpu.VMEM((toks, dim), BF16), pltpu.VMEM((toks, dim), BF16), pltpu.VMEM((w1_rows, units), BF16),
            pltpu.VMEM((w2_rows, units), BF16), dma((3,)), dma((9,)), dma((4,)),
        ],
        hbm=range(9), out_hbm=(0, 2, 3, 4),
    )
    own1, own2, p_far = lax.optimization_barrier((own1, own2, p_far))
    p_both = swap(p_far, 1)
    far1 = swap(own1, 2)
    near1 = swap(own1, 1)
    far2 = swap(own2, 2)
    near2 = swap(own2, 1)
    pt, ends = call(
        functools.partial(scan_end_kernel, nc, nd),
        (shape_of((prows * SUBS, LANES)), shape_of((ns, nd * SUBS, LANES))),
        (p_own, p_near, p_far, p_both, xt),
        scratch=[pltpu.VMEM((nc, prows, LANES), F32), pltpu.VMEM((nd * SUBS, LANES), F32), dma((ns,))],
        free=range(4), out_hbm=(1,), limit=8,
    )
    far1, _ = lax.optimization_barrier((far1, pt))
    both1 = swap(far1, 1)
    first = (own1, near1, far1, both1)
    ends = exchange(ends, SEQ)
    v_pre, r_pre, values, z_all, values_far = call(
        functools.partial(project_kernel, dim),
        (
            shape_of((toks, nc * units)), shape_of((toks, nc * units)), shape_of((toks, nc * units), BF16),
            shape_of((dim, zdim), BF16), shape_of((toks, nc * units), BF16),
        ),
        (low,) + first,
        scratch=[
            pltpu.VMEM((toks, dim), BF16), pltpu.VMEM((toks, nc * units), F32), pltpu.VMEM((4, w1_rows, units), BF16),
            dma((5,)), dma((8,)),
        ],
        hbm=range(4), free=(4,), out_hbm=(0, 4), limit=16,
    )
    mixed_pre, mixed_low, z_pre, attn, context, gated, state_in = call(
        functools.partial(mix_kernel, nc, nd, span),
        (
            shape_of((toks, dim)), shape_of((toks, dim), BF16), shape_of((toks, zdim)), shape_of((toks, width)),
            shape_of((toks, nc * units)), shape_of((toks, nc * units), BF16), shape_of((nd * SUBS, LANES)),
        ),
        (
            valid_counts, ends, xt, pt, z_all, values, r_pre, row(q_gain), row(k_gain), row(q_bias),
        ), scratch=[pltpu.VMEM((width * SUBS, LANES), F32), pltpu.VMEM((nd * SUBS, LANES), F32), pltpu.VMEM((toks, dim), BF16), dma((2,))],
        smem=(0,), free=range(7, 10), out_hbm=(1, 6), limit=16,
    )
    far2, gated = lax.optimization_barrier((far2, gated))
    both2 = swap(far2, 1)
    second = (own2, near2, far2, both2)
    out_rows = toks * (dim // units)
    out, g_mid, g_gated, keep1, send1, ffn_grad = call(
        functools.partial(ffn_kernel, nc, dim),
        (
            shape_of((out_rows, units), BF16), shape_of((toks, dim)), shape_of((toks, nc * units)),
            shape_of((2, w2_rows, units), BF16), shape_of((2, w2_rows, units), BF16), shape_of((1, dim)),
        ),
        (gated,) + second + (x, grad_out, row(ffn_gain)),
        scratch=[
            pltpu.VMEM((toks, nc * units), BF16), pltpu.VMEM((toks, nc * units), BF16),
            pltpu.VMEM((toks, dim), BF16), pltpu.VMEM((out_rows, units), BF16), pltpu.VMEM((toks, dim), F32),
            pltpu.VMEM((toks, dim), BF16), pltpu.VMEM((dim, nc * units), BF16), pltpu.VMEM((nc * urows, dim), BF16),
            pltpu.VMEM((nc * urows, dim), BF16), pltpu.VMEM((4, w2_rows, units), BF16),
            dma((1 + 8 * (dim // units) + 4 + rp,)), dma((2,)), dma((12,)),
        ],
        hbm=(1, 2, 3, 5, 6), free=(4, 7), out_hbm=(0, 1, 3, 4), limit=32,
    )
    got1 = swap(send1, 1).reshape(2 * w2_rows, units)
    fast = ns == 8
    g2_rows = -(-w1_rows // (16 * ns)) * 16 * ns
    split1 = w2_rows - X_FIRST if fast else w2_rows
    split2 = g2_rows - X_ROWS if fast else g2_rows
    pieces = PIECES if fast else 2
    room = rest_rows(nd)
    f_rows = -(-(vocab // 2 + room) // (16 * ns)) * 16 * ns
    state = types.SimpleNamespace(out=out)
    parts_of = lambda rows, split: tuple(part // 2 for part in (split, rows - split) if part)
    parts1, parts2 = parts_of(w2_rows, split1), parts_of(g2_rows, split2)
    half_of = lambda parts: tuple(part // 2 for part in parts)
    bf = lambda rows: shape_of((rows, units), BF16)

    def halves(level, pairs, parts):
        rows = sum(sum(part) for part in parts) // 2
        return call(
            functools.partial(add_halves, level, parts), (bf(rows),) * 2, pairs, free=range(len(pairs)),
            out_free=range(2),
        )

    def joined(level, pair, parts):
        return call(
            functools.partial(join_halves, level, parts), (bf(2 * pair[0].shape[0]),), pair, free=range(2),
            out_free=(0,),
        )[0]

    def add_two(pair):
        return call(add_plain, (bf(pair[0].shape[0]),), pair, free=range(2), out_free=(0,))[0]

    def over_seq(value, mask):
        return swap(value, mask, SEQ)

    def core_whole(keep, gots, rows):
        mine, theirs = call(
            add_core_far, (bf(rows),) * 2, (keep, *gots),
            scratch=[pltpu.VMEM((rows, units), BF16), pltpu.VMEM((rows, units), BF16), dma((2,))],
            free=range(1 + len(gots)), out_hbm=range(2),
        )
        return mine, swap(theirs, 2)

    def tied(value):
        value, TOKEN[0] = lax.optimization_barrier((value, TOKEN[0]))
        return value

    def attn_back():
        grad_v, grad_r, g_z, gmt, carries, small, skip_grad = call(
            functools.partial(attn_back_kernel, nc, nd),
            (
                shape_of((toks, nc * units), BF16), shape_of((toks, nc * units), BF16), shape_of((toks, zdim)),
                shape_of((width * SUBS, LANES)), shape_of((ns, nd * SUBS, LANES), BF16), shape_of((SUBS, zdim)),
                shape_of((SUBS, LANES)),
            ),
            (
                g_gated, r_pre, v_pre, context, attn, values_far, z_pre, mixed_pre, xt, z_all, pt, row(q_gain),
                row(k_gain), row(q_bias),
            ),
            scratch=[
                pltpu.VMEM((nd * SUBS, LANES), BF16), pltpu.VMEM((toks, nc * units), BF16),
                pltpu.VMEM((toks, nc * units), BF16), dma((ns,)), dma((2,)),
            ],
            free=(2, 5, 11, 12, 13), out_hbm=(0, 1, 4), limit=20,
        )
        vars(state).update(
            grad_v=grad_v, grad_r=grad_r, g_z=g_z, gmt=gmt, carries=carries, small=small, skip_grad=skip_grad,
        )

    def core_parted(keep, gots, rows, split):
        if split == rows:
            return core_whole(keep, gots, rows)
        mine, theirs, kept, send = call(
            functools.partial(add_core_split, split), (bf(split),) * 2 + (bf(rows - split),) * 2, (keep, *gots),
            scratch=[
                pltpu.VMEM((split, units), BF16), pltpu.VMEM((split, units), BF16),
                pltpu.VMEM((2, rows - split, units), BF16), dma((4,)),
            ],
            free=range(1 + len(gots)), out_hbm=range(4),
        )
        return mine, swap(theirs, 2), kept, over_seq(send, 1)

    def turned(sums):
        if len(sums) == 2:
            keep, send = halves(0, sums, ((sums[0].shape[0],),))
            return keep, over_seq(send, 1)
        near, far = sums[0].shape[0] // 2, sums[2].shape[0] // 2
        kept, send, own, theirs = call(
            turn_kernel, (bf(near), bf(near), bf(far), bf(far)), sums, free=range(4), out_free=range(4)
        )
        return kept, over_seq(send, 1), own, swap(theirs, 2)

    def move_carry():
        state.carries = exchange(tied(state.carries), SEQ)

    def core_first():
        state.sums1 = core_parted(keep1, (got1,), w2_rows, split1)

    def grads():
        keep2, *sends = call(
            functools.partial(grads_kernel, nc, dim, zrows),
            (shape_of((2, g2_rows, units), BF16),) + (bf(2 * g2_rows // pieces),) * pieces,
            (low, state.grad_v, state.grad_r, mixed_low, state.g_z),
            scratch=[
                pltpu.VMEM((dim, zdim), F32), pltpu.VMEM((toks, dim), BF16), pltpu.VMEM((toks, nc * units), BF16),
                pltpu.VMEM((toks, nc * units), BF16), pltpu.VMEM((toks, dim), BF16),
                pltpu.VMEM((4, g2_rows, units), BF16), dma((4,)), dma((16,)),
            ],
            hbm=range(4), out_hbm=range(1 + pieces), limit=24,
        )
        vars(state).update(keep2=keep2, gots2=[swap(value, 1) for value in sends])

    def scans():
        state.shared, state.sums = call(
            functools.partial(scans_kernel, nd, dim), (shape_of((toks, dim)), shape_of((3, nd * SUBS, LANES))),
            (state.grad_v, state.grad_r) + first + (pt, state_in, xt, state.gmt),
            scratch=[
                pltpu.VMEM((toks, dim), F32), pltpu.VMEM((3, nd * SUBS, LANES), F32), pltpu.VMEM((nd * SUBS, LANES), F32),
                pltpu.VMEM((4, 2 * dim, units), BF16), pltpu.VMEM((toks, nc * units), BF16),
                pltpu.VMEM((toks, nc * units), BF16), dma((7,)),
            ],
            hbm=(0, 1, 2, 3, 4, 5, 7), out_hbm=range(2), limit=24,
        )

    def core_second():
        state.sums2 = core_parted(state.keep2, state.gots2, g2_rows, split2)

    def x_first():
        state.sums1 = turned(state.sums1)

    def last():
        state.f = call(
            functools.partial(last_kernel, nc, nd, ns, span),
            (shape_of((2, f_rows, units), BF16),) + (bf(f_rows),) * 2,
            (
                state.carries, state.gmt, pt, state.shared, x, row(attn_gain), g_mid, token_ids, state.sums,
                state.small, state.skip_grad, ffn_grad,
            ),
            scratch=[
                pltpu.VMEM((width * SUBS, LANES), F32), pltpu.VMEM((vocab, dim), F32),
                pltpu.VMEM((3 * nd * SUBS, LANES), F32), pltpu.VMEM((nc, room, LANES), F32),
                pltpu.VMEM((toks, dim), F32), pltpu.VMEM((toks, dim), BF16), pltpu.VMEM((1, dim), F32),
                pltpu.VMEM((toks, dim), F32), pltpu.VMEM((rows, width), jnp.int32),
                pltpu.VMEM((3, nd * SUBS, LANES), F32), dma((6,)),
            ],
            hbm=range(3, 9), out_free=range(3), limit=16,
        )

    def core_last():
        keep, send, other = state.f
        mine, theirs = call(
            add_core, (bf(f_rows),) * 2, (keep, swap(send, 1), swap(other, 1)), free=range(3),
            out_free=range(2),
        )
        state.sumsf = (mine, swap(theirs, 2))

    def x_last():
        keep, send = halves(0, state.sumsf, ((f_rows,),))
        state.sumsf = (keep, over_seq(send, 1))

    def turn_second():
        state.sums2 = turned(state.sums2)

    def z_first():
        keep, send = halves(1, state.sums1, tuple((rows,) for rows in parts1))
        state.sums1 = (keep, over_seq(send, 2))

    def z_second():
        keep, send = halves(1, state.sums2, tuple((rows,) for rows in parts2))
        state.sums2 = (keep, over_seq(send, 2))

    def added(sums, mask):
        value = add_two(sums)
        return value, over_seq(value, mask)

    def zz_first():
        state.sums1 = added(state.sums1, 4)

    def zz_second():
        state.sums2 = added(state.sums2, 4)

    def zz_last():
        state.sumsf = added(state.sumsf, 4)

    def sum_first():
        state.sums1 = added(state.sums1, 2)

    def sum_second():
        state.sums2 = added(state.sums2, 2)

    def sum_last():
        state.sumsf = added(state.sumsf, 2)

    def join_first():
        whole = joined(1, state.sums1, half_of(parts1))
        state.sums1 = (whole, over_seq(whole, 1))

    def join_second():
        whole = joined(1, state.sums2, half_of(parts2))
        state.sums2 = (whole, over_seq(whole, 1))

    def z_last():
        keep, send = halves(1, state.sumsf, ((f_rows // 2,),))
        state.sumsf = (keep, over_seq(send, 2))

    def join_last():
        whole = joined(1, state.sumsf, (f_rows // 4,))
        state.sumsf = (whole, over_seq(whole, 1))

    def move_out():
        state.out = tied(state.out)
        vars(state).update(out_far=swap(state.out, 2), out_near=swap(state.out, 1))

    def move_both():
        state.out_far = tied(state.out_far)
        state.out_both = swap(state.out_far, 1)

    def output():
        state.output = call(
            output_kernel, (shape_of((rows, width, dim), BF16),),
            (state.out, state.out_near, state.out_far, state.out_both), free=range(4),
            out_free=(0,), limit=8,
        )[0]

    def plain_sums():
        state.sums1, state.sums2, state.sumsf = [
            (seq_sum(add_two(sums), ns),) * 2 for sums in (state.sums1, state.sums2, state.sumsf)
        ]
        state.f_own = state.sumsf[0]

    def give_first():
        state.first = call(
            functools.partial(unpack_first, dim, urows, parts1 if fast else None),
            (shape_of(up_proj.shape), shape_of(o_proj.shape), shape_of(down_proj.shape)), state.sums1, free=range(2), out_free=range(3), scratch=[pltpu.VMEM((w2_rows, units), BF16)],
        )

    def give_second():
        state.second = call(
            functools.partial(unpack_second, dim, zrows, parts2 if fast else None),
            (shape_of(v_proj.shape), shape_of(r_proj.shape), shape_of(z_proj.shape)), state.sums2, free=range(2), out_free=range(3), scratch=[pltpu.VMEM((g2_rows, units), BF16)],
        )

    def collect():
        (state.f_own,) = call(
            functools.partial(join_part, 0), (bf(f_rows),), state.sumsf, free=range(2),
            out_free=(0,),
        )

    def finish():
        own = state.f_own
        far = swap(own, 2)
        state.finish = call(
            functools.partial(finish_kernel, nc, nd),
            (
                shape_of((vocab, dim)), shape_of((1, dim)), shape_of((nd, LANES)), shape_of((nd, LANES)),
                shape_of((nd, LANES)), shape_of((1, LANES)), shape_of((1, dim)), shape_of((1, zdim)),
                shape_of((1, zdim)), shape_of((1, zdim)),
            ),
            (own, swap(own, 1), far, swap(far, 1)), free=range(4), out_free=range(10),
            scratch=[pltpu.VMEM((nc, room, LANES), F32)], limit=8,
        )

    if fast:
        steps = (
            attn_back, core_first, grads, move_carry, scans, core_second, x_first, last, core_last, z_first, turn_second,
            zz_first, z_second, move_out, x_last, z_last, zz_second, sum_first, zz_last, join_first, sum_second, sum_last,
            move_both, join_second, join_last, output, give_first, collect, give_second, finish,
        )
    else:
        steps = (
            attn_back, move_carry, core_first, grads, scans, core_second, last, core_last, move_out, move_both, output,
            plain_sums, give_first, give_second, finish,
        )
    for step in steps:
        step()
    up_grad, o_grad, down_grad = state.first
    v_grad, r_grad, z_grad = state.second
    embed_grad, ag, gi, gk, go, gs, fg, qg, kg, qb = state.finish
    flat = lambda value: value.reshape(-1)
    return (
        state.output, embed_grad, flat(ag), gi.T, gk.T, go.T, flat(gs), z_grad, flat(qg), flat(kg), flat(qb), v_grad, r_grad,
        o_grad, flat(fg), up_grad, down_grad,
    )


def solution(mesh):
    placed = (
        P(None, SEQ), P(), P(), P(), P(CHAN, None), P(CHAN, None), P(CHAN, None), P(CHAN), P(CHAN, None),
        P(), P(), P(), P(None, CHAN), P(None, CHAN), P(CHAN, None), P(), P(None, CHAN), P(CHAN, None),
        P(None, SEQ, None),
    )
    return jax.shard_map(
        body,
        mesh=mesh,
        in_specs=placed,
        out_specs=(
            P(None, SEQ, None), P(), P(), P(CHAN, None), P(CHAN, None), P(CHAN, None), P(CHAN),
            P(CHAN, None), P(), P(), P(), P(None, CHAN), P(None, CHAN), P(CHAN, None), P(), P(None, CHAN),
            P(CHAN, None),
        ),
        check_vma=False,
    )
```

```python
import functools
import types

import jax
import jax.numpy as jnp
from jax import lax
from jax.experimental import pallas as pl
from jax.experimental.pallas import tpu as pltpu
from jax.sharding import PartitionSpec as P

SEQMAX = 4096
CHAN, SEQ = "chan", "seq"
EPS = 1e-06
F32 = jnp.float32
BF16 = jnp.bfloat16
LANES = 128
SUBS = 8
MIB = 1024 * 1024


def sigmoid(u):
    return 0.5 * jnp.tanh(0.5 * u) + 0.5


def silu_slope(pre):
    sigma = sigmoid(pre)
    return sigma * (1.0 + pre * (1.0 - sigma))


def mm(left, right, dims, precision=None):
    return lax.dot_general(
        left, right, ((dims[0], dims[1]), ((), ())), precision=precision, preferred_element_type=F32
    )


def dot(left, right):
    return mm(left, right, ((1,), (0,)))


def dot_rows(left, right):
    return mm(left, right, ((0,), (0,)))


def dot_cols(left, right):
    return mm(left, right, ((1,), (1,)))


def two_parts(value):
    high = value.astype(BF16)
    return high, (value - high.astype(F32)).astype(BF16)


def exact(left, right, dims):
    if left.dtype == BF16:
        high, low = two_parts(right)
        return mm(left, high, dims) + mm(left, low, dims)
    high, low = two_parts(left)
    return mm(high, right, dims) + mm(low, right, dims)


def shape_of(dims, dtype=F32):
    return jax.ShapeDtypeStruct(dims, dtype)


TOKEN = []
X_FIRST = 128
X_ROWS = 256
PIECES = 2


def call(
    kernel, outs, args, scratch=(), smem=(), hbm=(), free=(), far=(), out_hbm=(), out_free=(), out_far=(), limit=16
):
    waits = list(TOKEN)
    hbm, out_hbm = {*hbm, *far}, {*out_hbm, *out_far}
    count, made = len(args), len(outs)
    inner = kernel.func if isinstance(kernel, functools.partial) else kernel

    def run(*refs):
        rest = refs[count + len(waits) :]
        kernel(*refs[:count], *rest[:made], *rest[made + 1 :])

    def spec(at):
        if at >= count or (at in hbm and at not in far):
            return pl.BlockSpec(memory_space=pltpu.HBM)
        return pl.BlockSpec(memory_space=pltpu.SMEM if at in smem else pltpu.VMEM)

    def held(at, value):
        if at < count and (at in smem or at in free):
            return value
        return pltpu.with_memory_space_constraint(value, pltpu.HBM if at in hbm or at >= count else pltpu.VMEM)

    def result(at, out):
        if at in out_free:
            return out
        return (pltpu.HBM if at in out_hbm or at == made else pltpu.VMEM)(out.shape, out.dtype)

    shapes = list(outs) + [shape_of((SUBS, LANES))]
    *results, token = pl.pallas_call(
        run,
        out_shape=[result(at, out) for at, out in enumerate(shapes)],
        in_specs=[spec(at) for at in range(count + len(waits))],
        out_specs=[
            pl.BlockSpec(memory_space=pltpu.HBM if (at in out_hbm and at not in out_far) or at == made else pltpu.VMEM)
            for at in range(made + 1)
        ],
        scratch_shapes=list(scratch),
        name=inner.__name__,
        cost_estimate=pl.CostEstimate(flops=1, bytes_accessed=1, transcendentals=0),
        compiler_params=pltpu.CompilerParams(vmem_limit_bytes=limit * MIB),
    )(*[held(at, value) for at, value in enumerate([*args, *waits])])
    TOKEN[:] = [token]
    return results


def move(copies, sems):
    for copy in run_copies(copies, sems):
        copy.wait()


def run_copies(copies, sems):
    started = [pltpu.make_async_copy(src, dst, sems.at[at]) for at, (src, dst) in enumerate(copies)]
    for copy in started:
        copy.start()
    return started


def pack_params(in_ref, keep_ref, out_ref, skip_ref, p_ref, sems):
    nd, lanes = in_ref.shape
    copies = [(ref, p_ref.at[at * nd : (at + 1) * nd, :]) for at, ref in enumerate((in_ref, keep_ref, out_ref))]
    copies.append((skip_ref, p_ref.at[3 * nd : 3 * nd + 1, :]))
    move(copies, sems)
    rest = p_ref.shape[0] - 3 * nd
    p_ref[3 * nd :, :] = jnp.broadcast_to(p_ref[3 * nd : 3 * nd + 1, :], (rest, lanes))


def first_copies(v_ref, r_ref, z_ref, buf):
    dim = v_ref.shape[0]
    zrows = z_ref.shape[0] // 2
    copies = [(v_ref, buf.at[0:dim, :]), (r_ref, buf.at[dim : 2 * dim, :])]
    for half in range(2):
        copies.append(
            (
                z_ref.at[half * zrows : (half + 1) * zrows, :],
                buf.at[2 * dim : 2 * dim + zrows, half * LANES : (half + 1) * LANES],
            )
        )
    return copies


def second_copies(up_ref, o_ref, down_ref, buf):
    dim, units = up_ref.shape
    urows = o_ref.shape[0]
    copies = [(up_ref, buf.at[0:dim, :])]
    for at, ref in enumerate((o_ref, down_ref)):
        for half in range(dim // units):
            start = dim + (dim // units * at + half) * urows
            copies.append((ref.at[:, half * units : (half + 1) * units], buf.at[start : start + urows, :]))
    return copies


def prepare_kernel(
    nc, ids_at, table_at, gain_at, v_at, r_at, z_at, up_at, o_at, down_at,
    x_to, xt_ref, low_to, w1_to, w2_to,
    ids_ref, embed_ref, gain_ref, x_ref, low_ref, w1_ref, w2_ref, sems, w_sems, out_sems,
):
    entering = run_copies(first_copies(v_at, r_at, z_at, w1_ref), w_sems.at[0:4])
    started = run_copies([(ids_at, ids_ref), (table_at, embed_ref), (gain_at, gain_ref)], sems)
    later = run_copies(second_copies(up_at, o_at, down_at, w2_ref), w_sems.at[4:9])
    for copy in entering:
        copy.wait()
    leaving = run_copies([(w1_ref, w1_to)], out_sems.at[0:1])
    rp = x_ref.shape[0] // ids_ref.shape[1]
    width = ids_ref.shape[1]
    vocab = embed_ref.shape[0]
    chan = lax.axis_index(CHAN)
    for copy in started:
        copy.wait()
    for row in range(rp):
        ids = ids_ref[pl.ds(chan * rp + row, 1), :]
        onehot = jnp.where(lax.broadcasted_iota(jnp.int32, (vocab, width), 0) == ids, 1.0, 0.0).astype(BF16)
        x = dot_rows(onehot, embed_ref[...])
        x_ref[row * width : (row + 1) * width, :] = x.astype(BF16)
        normed = x * lax.rsqrt(jnp.mean(x * x, axis=-1, keepdims=True) + EPS) * gain_ref[...]
        low_ref[row * width : (row + 1) * width, :] = normed.astype(BF16)
        for chunk in range(nc):
            xt_ref[pl.ds(row * nc + chunk, width, stride=SUBS), :] = normed[
                :, chunk * LANES : (chunk + 1) * LANES
            ]
        for copy in later:
            copy.wait()
        later = []
        leaving += run_copies([(w2_ref, w2_to)], out_sems.at[1:2]) if row == 0 else []
    leaving += run_copies([(x_ref, x_to), (low_ref, low_to)], out_sems.at[2:4])
    for copy in leaving:
        copy.wait()


def tile(ref, at):
    return ref[at * SUBS : (at + 1) * SUBS, :]


def step_tile(ref, t):
    return ref[pl.ds(pl.multiple_of(t * SUBS, SUBS), SUBS), :]


def scan_end_kernel(nc, nd, p0, p1, p2, p3, xt_ref, pt_ref, end_ref, p_ref, buf, sems):
    width = xt_ref.shape[0] // SUBS
    prows = p_ref.shape[1]
    chan = lax.axis_index(CHAN)
    for j, ref in enumerate((p0, p1, p2, p3)):
        p_ref[jnp.bitwise_xor(chan, j)] = ref[...]
    for sub in range(SUBS):
        pt_ref[pl.ds(sub, prows, stride=SUBS), :] = p_ref[sub % nc]
    keep = [tile(pt_ref, nd + k) for k in range(nd)]

    def step(block, states):
        states = list(states)
        for u in range(8):
            x = step_tile(xt_ref, block * 8 + u)
            states = [q * s + x for q, s in zip(keep, states)]
        return tuple(states)

    zero = jnp.zeros((SUBS, LANES), F32)
    states = lax.fori_loop(0, width // 8, step, (zero,) * nd)
    buf[...] = jnp.concatenate(states, axis=0)
    for copy in run_copies([(buf, end_ref.at[at]) for at in range(end_ref.shape[0])], sems):
        copy.wait()


def project_kernel(
    dim, low_at, h0, h1, h2, h3, vpre_to, rpre_ref, val_ref, z_ref, val_to, low_ref, vpre_ref, buf, sems, out_sems
):
    chan = lax.axis_index(CHAN)
    units = h0.shape[1]
    zrows = h0.shape[0] - 2 * dim
    started = run_copies([(low_at, low_ref)] + [(ref, buf.at[j]) for j, ref in enumerate((h0, h1, h2, h3))], sems)
    started[0].wait()
    low = low_ref[...]
    leaving = []
    for j in range(4):
        started[1 + j].wait()
        w = buf.at[j]
        cols = slice(j * units, (j + 1) * units)
        v_pre = dot(low, w[0:dim, :])
        vpre_ref[:, cols] = v_pre
        val_ref[:, cols] = (v_pre * sigmoid(v_pre)).astype(BF16)
        leaving += run_copies(
            [(vpre_ref.at[:, cols], vpre_to.at[:, cols]), (val_ref.at[:, cols], val_to.at[:, cols])],
            out_sems.at[2 * j : 2 * j + 2],
        )
        rpre_ref[:, cols] = dot(low, w[dim : 2 * dim, :])
        start = pl.multiple_of(jnp.bitwise_xor(chan, j) * 2 * zrows, 2 * zrows)
        half = w[2 * dim : 2 * dim + zrows, :]
        z_ref[pl.ds(start, 2 * zrows), :] = jnp.concatenate([half[:, :LANES], half[:, LANES:]], axis=0)
    for copy in leaving:
        copy.wait()


def whole_keep(keep, width):
    whole = keep
    power = 1
    while power < width:
        whole = whole * whole
        power *= 2
    return whole


def weights_of(pt_ref, nd):
    amp = pt_ref[0 : nd * SUBS, :]
    keep = pt_ref[nd * SUBS : 2 * nd * SUBS, :]
    out = pt_ref[2 * nd * SUBS : 3 * nd * SUBS, :]
    root = jnp.sqrt(1.0 - keep * keep)
    return amp, keep, out, root


def split_tiles(value, nd):
    return [value[k * SUBS : (k + 1) * SUBS, :] for k in range(nd)]


def tree_sum(values):
    values = list(values)
    while len(values) > 1:
        values = [sum(values[i : i + 2][1:], values[i]) for i in range(0, len(values), 2)]
    return values[0]


def scale_of(x):
    return lax.rsqrt(jnp.mean(x * x, axis=-1, keepdims=True) + EPS)


def mix_kernel(
    nc, nd, span, counts_ref, ends_ref, xt_ref, pt_ref, z_ref, val_ref, rpre_ref, qg_ref, kg_ref, qb_ref,
    mpre_ref, mlow_to, zpre_ref, attn_ref, ctx_ref, gated_ref, sin_to, sm_ref, sin_ref, mlow_ref, sems,
):
    width = xt_ref.shape[0] // SUBS
    rp = SUBS // nc
    place = lax.axis_index(SEQ)
    chan = lax.axis_index(CHAN)
    amp, keep_all, out_all, root = weights_of(pt_ref, nd)
    whole = whole_keep(keep_all, width)
    per = span // width
    first = place // per * per

    def gather(n, state):
        return state * whole + ends_ref[n].astype(F32)

    start = lax.fori_loop(first, place, gather, jnp.zeros_like(whole))
    sin_ref[...] = start
    (leaving,) = run_copies([(sin_ref, sin_to)], sems.at[:1])
    keep = split_tiles(keep_all, nd)
    weight = split_tiles(out_all * amp * root, nd)

    def step(block, states):
        states = list(states)
        for u in range(8):
            t = block * 8 + u
            x = step_tile(xt_ref, t)
            states = [q * s + x for q, s in zip(keep, states)]
            sm_ref[pl.ds(pl.multiple_of(t * SUBS, SUBS), SUBS), :] = tree_sum(
                [w * s for w, s in zip(weight, states)]
            )
        return tuple(states)

    lax.fori_loop(0, width // 8, step, tuple(split_tiles(start, nd)))
    skip = pt_ref[3 * nd * SUBS : 3 * nd * SUBS + SUBS, :]
    for row in range(rp):
        rows = slice(row * width, (row + 1) * width)
        for chunk in range(nc):
            at = row * nc + chunk
            lanes = slice(chunk * LANES, (chunk + 1) * LANES)
            own = xt_ref[pl.ds(at, width, stride=SUBS), :]
            pre = sm_ref[pl.ds(at, width, stride=SUBS), :] + skip[at : at + 1, :] * own
            mpre_ref[rows, lanes] = pre
            mlow_ref[rows, lanes] = (pre * sigmoid(pre)).astype(BF16)
    (left,) = run_copies([(mlow_ref, mlow_to)], sems.at[1:])
    z_pre = dot(mlow_ref[...], z_ref[...])
    zpre_ref[...] = z_pre
    zeta = z_pre * sigmoid(z_pre)
    queries = (zeta * qg_ref[...] + qb_ref[...]).astype(BF16)
    keys = (zeta * kg_ref[...]).astype(BF16)
    scale = z_pre.shape[1] ** (-0.5)
    pieces = counts_ref.shape[0] // (rp * nc)
    begin = place * width
    piece = begin // span
    inner = begin - piece * span
    for row in range(rp):
        rows = slice(row * width, (row + 1) * width)
        count = counts_ref[(chan * rp + row) * pieces + piece]
        valid = lax.broadcasted_iota(jnp.int32, (width, width), 1) < count - inner
        scores = jnp.where(valid, dot_cols(queries[rows, :], keys[rows, :]) * scale, -1e30)
        top = jnp.max(scores, axis=-1, keepdims=True)
        weights = jnp.where(valid, jnp.exp(scores - top), 0.0)
        empty = jnp.where(count > inner, 0.0, 1.0)
        attn = weights / (jnp.sum(weights, axis=-1, keepdims=True) + empty)
        attn_ref[rows, :] = attn
        context = dot(attn.astype(BF16), val_ref[rows, :])
        ctx_ref[rows, :] = context
        r_pre = rpre_ref[rows, :]
        gated_ref[rows, :] = (r_pre * sigmoid(r_pre) * context).astype(BF16)
    leaving.wait()
    left.wait()


def ffn_kernel(
    nc, dim, gated_ref, h0, h1, h2, h3, x_at, grad_ref, fgain_ref,
    out_to, gmid_to, ggated_ref, keep_to, send_to, fg_ref,
    hid_ref, gup_ref, g_ref, out_ref, gmid_ref, x_ref, up_ref, o_ref, down_ref, part_ref, sems, out_sems, part_sems,
):
    units = h0.shape[1]
    rp = grad_ref.shape[0] // nc
    width = grad_ref.shape[1]
    chan = lax.axis_index(CHAN)
    urows = (h0.shape[0] - dim) // 4
    halves = dim // units
    hs = (h0, h1, h2, h3)

    def shards(ref, which):
        return [
            (
                h.at[dim + (which * halves + half) * urows : dim + (which * halves + half + 1) * urows, :],
                ref.at[j * urows : (j + 1) * urows, half * units : (half + 1) * units],
            )
            for j, h in enumerate(hs)
            for half in range(halves)
        ]

    copies = [(x_at, x_ref)] + shards(o_ref, 0)
    copies += [(h.at[0:dim, :], up_ref.at[:, j * units : (j + 1) * units]) for j, h in enumerate(hs)]
    copies += [(grad_ref.at[chan * rp + row], g_ref.at[row * width : (row + 1) * width, :]) for row in range(rp)]
    copies += shards(down_ref, 1)
    started = run_copies(copies, sems)
    first = 1 + 4 * halves
    for copy in started[:first]:
        copy.wait()
    middle = x_ref[...].astype(F32) + dot(gated_ref[...], o_ref[...])
    r = scale_of(middle)
    n = middle * r
    fgain = fgain_ref[...]
    ffn_low = (n * fgain).astype(BF16)
    for copy in started[first:]:
        copy.wait()
    g = g_ref[...]
    up_pre = dot(ffn_low, up_ref[...])
    sigma = sigmoid(up_pre)
    hid_ref[...] = (up_pre * sigma).astype(BF16)
    gup_ref[...] = (dot_cols(g, down_ref[...]) * (sigma * (1.0 + up_pre * (1.0 - sigma)))).astype(BF16)
    g_in = dot_cols(gup_ref[...], up_ref[...])
    h = g_in * fgain
    g_mid = g.astype(F32) + r * (h - n * jnp.mean(h * n, axis=-1, keepdims=True))
    gmid_ref[...] = g_mid
    g_branch = g_mid.astype(BF16)
    leaving = run_copies([(gmid_ref, gmid_to)], out_sems.at[0:1])
    fg_ref[...] = jnp.sum(g_in * n, axis=0, keepdims=True)

    def leave(begin, rows, which):
        part = slice(begin, begin + rows)
        return run_copies(
            [(part_ref.at[j, part, :], (keep_to, send_to)[j % 2].at[j // 2, part, :]) for j in (1, 3, 0, 2)],
            part_sems.at[4 * which : 4 * which + 4],
        )

    grad = dot_rows(ffn_low, gup_ref[...]).astype(BF16)
    for j in range(4):
        part_ref[j, 0:dim, :] = grad[:, j * units : (j + 1) * units]
    leaving += leave(0, dim, 0)
    for which, (left, right) in enumerate(((hid_ref, g), (gated_ref, g_branch))):
        grad = dot_rows(left[...], right).astype(BF16)
        begin = dim + (1 - which) * halves * urows
        for j in range(4):
            for half in range(halves):
                part_ref[j, begin + half * urows : begin + (half + 1) * urows, :] = grad[
                    j * urows : (j + 1) * urows, half * units : (half + 1) * units
                ]
        leaving += leave(begin, halves * urows, 1 + which)
    ggated_ref[...] = dot_cols(g_branch, o_ref[...])
    out = (middle + dot(hid_ref[...], down_ref[...])).astype(BF16)
    toks = g_ref.shape[0]
    for half in range(halves):
        out_ref[half * toks : (half + 1) * toks, :] = out[:, half * units : (half + 1) * units]
    leaving += run_copies([(out_ref, out_to)], out_sems.at[1:2])
    for copy in leaving:
        copy.wait()


def attn_back_kernel(
    nc, nd, ggated_ref, rpre_ref, vpre_ref, ctx_ref, attn_ref, val_ref, zpre_ref, mpre_ref, xt_ref, z_ref, pt_ref,
    qg_ref, kg_ref, qb_ref,
    gv_to, gr_to, gz_ref, gmt_ref, carry_ref, small_ref, skip_ref, buf, gv_ref, gr_ref, sems, out_sems,
):
    width = xt_ref.shape[0] // SUBS
    rp = SUBS // nc
    z_pre = zpre_ref[...]
    sigma = sigmoid(z_pre)
    zeta = z_pre * sigma
    queries = (zeta * qg_ref[...] + qb_ref[...]).astype(BF16)
    keys = (zeta * kg_ref[...]).astype(BF16)
    scale = z_pre.shape[1] ** (-0.5)
    parts_q, parts_k = [], []
    for row in range(rp):
        rows = slice(row * width, (row + 1) * width)
        g_gated = ggated_ref[rows, :]
        r_pre = rpre_ref[rows, :]
        sr = sigmoid(r_pre)
        g_context = (g_gated * (r_pre * sr)).astype(BF16)
        gr_ref[rows, :] = (g_gated * ctx_ref[rows, :] * (sr * (1.0 + r_pre * (1.0 - sr)))).astype(BF16)
        attn = attn_ref[rows, :]
        g_values = dot_rows(attn.astype(BF16), g_context)
        gv_ref[rows, :] = (g_values * silu_slope(vpre_ref[rows, :])).astype(BF16)
        g_attn = dot_cols(g_context, val_ref[rows, :])
        g_scores = attn * (g_attn - jnp.sum(attn * g_attn, axis=-1, keepdims=True))
        parts_q.append(exact(g_scores, keys[rows, :], ((1,), (0,))) * scale)
        parts_k.append(exact(g_scores, queries[rows, :], ((0,), (0,))) * scale)
    leaving = run_copies([(gv_ref, gv_to), (gr_ref, gr_to)], out_sems)
    g_q = jnp.concatenate(parts_q, axis=0)
    g_k = jnp.concatenate(parts_k, axis=0)
    small_ref[...] = jnp.concatenate(
        [
            jnp.sum(g_q * zeta, axis=0, keepdims=True),
            jnp.sum(g_k * zeta, axis=0, keepdims=True),
            jnp.sum(g_q, axis=0, keepdims=True),
            jnp.zeros((SUBS - 3, z_pre.shape[1]), F32),
        ],
        axis=0,
    )
    g_z = (g_q * qg_ref[...] + g_k * kg_ref[...]) * (sigma * (1.0 + z_pre * (1.0 - sigma)))
    gz_ref[...] = g_z
    for row in range(rp):
        rows = slice(row * width, (row + 1) * width)
        for chunk in range(nc):
            at = row * nc + chunk
            lanes = slice(chunk * LANES, (chunk + 1) * LANES)
            g_mixed = exact(g_z[rows, :], z_ref[lanes, :], ((1,), (1,))) * silu_slope(mpre_ref[rows, lanes])
            gmt_ref[pl.ds(at, width, stride=SUBS), :] = g_mixed
    keep = [tile(pt_ref, nd + k) for k in range(nd)]

    def step(block, carries):
        carries = list(carries)
        for u in range(8):
            gm = step_tile(gmt_ref, width - 1 - (block * 8 + u))
            carries = [q * (c + gm) for q, c in zip(keep, carries)]
        return tuple(carries)

    zero = jnp.zeros((SUBS, LANES), F32)
    carries = lax.fori_loop(0, width // 8, step, (zero,) * nd)
    buf[...] = jnp.concatenate(carries, axis=0).astype(BF16)
    leaving += run_copies([(buf, carry_ref.at[at]) for at in range(carry_ref.shape[0])], sems)
    skips = []
    for at in range(SUBS):
        every = pl.ds(at, width, stride=SUBS)
        skips.append(jnp.sum(gmt_ref[every, :] * xt_ref[every, :], axis=0, keepdims=True))
    skip_ref[...] = jnp.concatenate(skips, axis=0)
    for copy in leaving:
        copy.wait()


def grads_kernel(
    nc, dim, zrows, low_at, gv_at, gr_at, mlow_at, gz_ref, keep_to, *refs
):
    sends, (zg_ref, low_ref, gv_ref, gr_ref, mlow_ref, part_ref, sems, part_sems) = refs[:-8], refs[-8:]
    units = gv_ref.shape[1] // nc
    chan = lax.axis_index(CHAN)
    started = run_copies([(mlow_at, mlow_ref), (low_at, low_ref), (gv_at, gv_ref), (gr_at, gr_ref)], sems)
    started[0].wait()
    zg_ref[...] = exact(mlow_ref[...], gz_ref[...], ((0,), (0,)))
    for copy in started[1:]:
        copy.wait()
    low = low_ref[...]
    used = 2 * dim + zrows
    spare = part_ref.shape[1] - used
    leaving = []
    for j in (1, 3, 0, 2):
        cols = slice(j * units, (j + 1) * units)
        part_ref[j, 0:dim, :] = dot_rows(low, gv_ref[:, cols]).astype(BF16)
        part_ref[j, dim : 2 * dim, :] = dot_rows(low, gr_ref[:, cols]).astype(BF16)
        start = pl.multiple_of(jnp.bitwise_xor(chan, j) * 2 * zrows, 2 * zrows)
        block = zg_ref[pl.ds(start, 2 * zrows), :]
        part_ref[j, 2 * dim : used, :] = jnp.concatenate([block[:zrows, :], block[zrows:, :]], axis=1).astype(BF16)
        if spare:
            part_ref[j, used:, :] = jnp.zeros((spare, units), BF16)
        if j % 2:
            copies = []
            total, each = part_ref.shape[1], sends[0].shape[0]
            begin = 0
            while begin < total:
                at = j // 2 * total + begin
                take = min(total - begin, each - at % each)
                to = sends[at // each].at[at % each : at % each + take, :]
                copies.append((part_ref.at[j, begin : begin + take, :], to))
                begin += take
        else:
            copies = [(part_ref.at[j], keep_to.at[j // 2])]
        leaving += run_copies(copies, part_sems.at[4 * j : 4 * j + len(copies)])
    for copy in leaving:
        copy.wait()


def scans_kernel(
    nd, dim, gv_at, gr_at, h0, h1, h2, h3, pt_ref, sin_at, xt_ref, gmt_ref,
    shared_to, acc_to, shared_ref, acc_ref, sin_ref, buf, gv_ref, gr_ref, sems,
):
    units = h0.shape[1]
    width = xt_ref.shape[0] // SUBS
    started = run_copies(
        [(sin_at, sin_ref), (gv_at, gv_ref), (gr_at, gr_ref)]
        + [(ref.at[0 : 2 * dim, :], buf.at[j]) for j, ref in enumerate((h0, h1, h2, h3))],
        sems,
    )
    started[0].wait()
    group = nd // 2

    def scan(begin):
        ks = list(range(begin, begin + group))
        keep = [tile(pt_ref, nd + k) for k in ks]

        def step(block, carry):
            s, d, a, b = [list(part) for part in carry]
            for u in range(8):
                t = block * 8 + u
                x = step_tile(xt_ref, t)
                gm = step_tile(gmt_ref, t)
                d = [q * di + si for q, di, si in zip(keep, d, s)]
                s = [q * si + x for q, si in zip(keep, s)]
                a = [ai + gm * si for ai, si in zip(a, s)]
                b = [bi + gm * di for bi, di in zip(b, d)]
            return tuple(s), tuple(d), tuple(a), tuple(b)

        zero = (jnp.zeros((SUBS, LANES), F32),) * group
        init = tuple(tile(sin_ref, k) for k in ks)
        s, d, a, b = lax.fori_loop(0, width // 8, step, (init, zero, zero, zero))
        rows = slice(begin * SUBS, (begin + group) * SUBS)
        acc_ref[0, rows, :] = jnp.concatenate(a, axis=0)
        acc_ref[1, rows, :] = jnp.concatenate(b, axis=0)
        acc_ref[2, rows, :] = jnp.concatenate(d, axis=0)

    scan(0)
    for copy in started[1:3]:
        copy.wait()
    shared = None
    for j in range(4):
        cols = slice(j * units, (j + 1) * units)
        started[3 + j].wait()
        term = dot_cols(gv_ref[:, cols], buf[j, 0:dim, :]) + dot_cols(gr_ref[:, cols], buf[j, dim:, :])
        shared = term if j == 0 else shared + term
    shared_ref[...] = shared
    leaving = run_copies([(shared_ref, shared_to)], sems.at[1:])
    scan(group)
    leaving += run_copies([(acc_ref, acc_to)], sems)
    for copy in leaving:
        copy.wait()


def rest_rows(nd):
    return -(-(3 * nd + 4) // 16) * 16


def last_kernel(
    nc, nd, ns, span, carry_ref, gmt_ref, pt_ref, shared_at, x_at, gain_at, gmid_at, ids_at, sums_at,
    small_ref, skip_ref, fg_ref,
    keep_ref, send1_ref, send3_ref, yt_ref, acc_ref, ema_ref, rest_ref, shared_ref, x_ref, gain_ref, gmid_ref, ids_ref, sums_ref,
    sems,
):
    started = run_copies(
        [
            (shared_at, shared_ref), (x_at, x_ref), (gain_at, gain_ref), (gmid_at, gmid_ref), (ids_at, ids_ref),
            (sums_at, sums_ref),
        ],
        sems,
    )
    width = gmt_ref.shape[0] // SUBS
    rp = SUBS // nc
    vocab = acc_ref.shape[0]
    place = lax.axis_index(SEQ)
    chan = lax.axis_index(CHAN)
    amp, keep_all, out_all, root = weights_of(pt_ref, nd)
    whole = whole_keep(keep_all, width)
    per = span // width
    last = place // per * per + per - 1

    def gather(n, state):
        return state * whole + carry_ref[last - n].astype(F32)

    start = lax.fori_loop(0, last - place, gather, jnp.zeros_like(whole))
    drive = amp * root
    weight_all = out_all * drive
    keep = split_tiles(keep_all, nd)
    weight = split_tiles(weight_all, nd)

    def step(block, carries):
        carries = list(carries)
        for u in range(8):
            t = width - 1 - (block * 8 + u)
            gm = step_tile(gmt_ref, t)
            adj = [c + gm for c in carries]
            yt_ref[pl.ds(pl.multiple_of(t * SUBS, SUBS), SUBS), :] = tree_sum(
                [w * s for w, s in zip(weight, adj)]
            )
            carries = [q * s for q, s in zip(keep, adj)]
        return tuple(carries)

    lax.fori_loop(0, width // 8, step, tuple(split_tiles(start, nd)))
    for copy in started:
        copy.wait()
    a = sums_ref[0]
    g_drive = out_all * a
    grad_out = drive * a
    grad_in = g_drive * root
    grad_keep = weight_all * (sums_ref[1] + sums_ref[2] * start) - g_drive * amp * keep_all / root
    for at, grad in enumerate((grad_in, grad_keep, grad_out)):
        ema_ref[at * nd * SUBS : (at + 1) * nd * SUBS, :] = grad
    skip = pt_ref[3 * nd * SUBS : 3 * nd * SUBS + SUBS, :]
    gain = gain_ref[...]
    for row in range(rp):
        toks = slice(row * width, (row + 1) * width)
        pieces = []
        for chunk in range(nc):
            at = row * nc + chunk
            lanes = slice(chunk * LANES, (chunk + 1) * LANES)
            gm = gmt_ref[pl.ds(at, width, stride=SUBS), :]
            pieces.append(
                shared_ref[toks, lanes] + skip[at : at + 1, :] * gm + yt_ref[pl.ds(at, width, stride=SUBS), :]
            )
        g_normed = jnp.concatenate(pieces, axis=1)
        x = x_ref[toks, :].astype(F32)
        r = scale_of(x)
        n = x * r
        h = g_normed * gain
        g_x = gmid_ref[toks, :] + r * (h - n * jnp.mean(h * n, axis=-1, keepdims=True))
        part = jnp.sum(g_normed * n, axis=0, keepdims=True)
        ag = part if row == 0 else ag + part
        ids = ids_ref[pl.ds(chan * rp + row, 1), :]
        onehot = jnp.where(lax.broadcasted_iota(jnp.int32, (vocab, width), 0) == ids, 1.0, 0.0).astype(BF16)
        term = exact(onehot, g_x, ((1,), (0,)))
        acc_ref[...] = term if row == 0 else acc_ref[...] + term
    rest_ref[...] = jnp.zeros_like(rest_ref)
    for chunk in range(nc):
        lanes = slice(chunk * LANES, (chunk + 1) * LANES)
        for at in range(3):
            total = None
            for row in range(rp):
                term = ema_ref[pl.ds(at * nd * SUBS + row * nc + chunk, nd, stride=SUBS), :]
                total = term if row == 0 else total + term
            rest_ref[chunk, at * nd : (at + 1) * nd, :] = total
        at = 3 * nd
        rest_ref[chunk, at : at + 1, :] = sum(
            skip_ref[row * nc + chunk : row * nc + chunk + 1, :] for row in range(rp)
        )
        rest_ref[chunk, at + 1 : at + 2, :] = ag[:, lanes]
        rest_ref[chunk, at + 2 : at + 3, :] = fg_ref[:, lanes]
        if chunk < 3:
            rest_ref[chunk, at + 3 : at + 4, :] = small_ref[chunk : chunk + 1, :]
    half = vocab // 2
    room = rest_ref.shape[1]
    for j in range(4):
        to = (keep_ref.at[0], send1_ref, keep_ref.at[1], send3_ref)[j]
        owner = jnp.bitwise_xor(chan, j)
        block = acc_ref[:, pl.ds(pl.multiple_of(owner * LANES, LANES), LANES)]
        to[0:half, :] = jnp.concatenate([block[:half, :], block[half:, :]], axis=1).astype(BF16)
        rest = rest_ref[owner]
        high = rest.astype(BF16)
        low = (rest - high.astype(F32)).astype(BF16)
        to[half : half + room, :] = jnp.concatenate([high, low], axis=1)
        if to.shape[0] > half + room:
            to[half + room :, :] = jnp.zeros((to.shape[0] - half - room, to.shape[1]), BF16)


def sum_kernel(in_ref, out_ref, buf, sems):
    total = in_ref[0].astype(F32)
    for at in range(1, in_ref.shape[0]):
        total = total + in_ref[at].astype(F32)
    buf[...] = total.astype(BF16)
    for copy in run_copies([(buf, out_ref.at[at]) for at in range(out_ref.shape[0])], sems):
        copy.wait()


def spread(parts):
    scratch = [pltpu.VMEM(parts.shape[1:], BF16), pltpu.SemaphoreType.DMA((parts.shape[0],))]
    return call(sum_kernel, (shape_of(parts.shape, BF16),), (parts,), scratch=scratch, out_hbm=(0,))[0]


def finish_kernel(
    nc, nd, w0, w1, w2, w3, embed_ref, ag_ref, ei_ref, ek_ref, eo_ref, es_ref, fg_ref, qg_ref, kg_ref, qb_ref, rest_ref
):
    half = embed_ref.shape[0] // 2
    room = rest_ref.shape[1]
    chan = lax.axis_index(CHAN)
    for j, ref in enumerate((w0, w1, w2, w3)):
        owner = jnp.bitwise_xor(chan, j)
        lanes = pl.ds(pl.multiple_of(owner * LANES, LANES), LANES)
        block = ref[0:half, :].astype(F32)
        embed_ref[0:half, lanes] = block[:, :LANES]
        embed_ref[half:, lanes] = block[:, LANES:]
        rest = ref[half : half + room, :].astype(F32)
        rest = rest[:, :LANES] + rest[:, LANES:]
        rest_ref[owner] = rest
        if j == 0:
            for at, to in enumerate((ei_ref, ek_ref, eo_ref)):
                to[...] = rest[at * nd : (at + 1) * nd, :]
            es_ref[...] = rest[3 * nd : 3 * nd + 1, :]
        ag_ref[:, lanes] = rest[3 * nd + 1 : 3 * nd + 2, :]
        fg_ref[:, lanes] = rest[3 * nd + 2 : 3 * nd + 3, :]
    for at, to in enumerate((qg_ref, kg_ref, qb_ref)):
        to[...] = rest_ref[at, 3 * nd + 3 : 3 * nd + 4, :]


def unpack_first(dim, urows, parts, u_ref, v_ref, up_ref, o_ref, down_ref, s_ref):
    join(parts, u_ref, v_ref, s_ref)
    units = s_ref.shape[1]
    up_ref[...] = s_ref[0:dim, :].astype(F32)
    for at, ref in enumerate((o_ref, down_ref)):
        for half in range(dim // units):
            start = dim + (at * (dim // units) + half) * urows
            ref[:, half * units : (half + 1) * units] = s_ref[start : start + urows, :].astype(F32)


def unpack_second(dim, zrows, parts, u_ref, x_ref, v_ref, r_ref, z_ref, s_ref):
    join(parts, u_ref, x_ref, s_ref)
    v_ref[...] = s_ref[0:dim, :].astype(F32)
    r_ref[...] = s_ref[dim : 2 * dim, :].astype(F32)
    block = s_ref[2 * dim : 2 * dim + zrows, :].astype(F32)
    z_ref[0:zrows, :] = block[:, :LANES]
    z_ref[zrows:, :] = block[:, LANES:]


def join(parts, mine_ref, other_ref, to_ref):
    if parts is None:
        to_ref[...] = mine_ref[...]
    else:
        join_halves(0, parts, mine_ref, other_ref, to_ref)


def plus(left, right):
    return (left.astype(F32) + right.astype(F32)).astype(BF16)


def piece_sum(keep_ref, got, chunk, begin, rows):
    each = got[0].shape[0]
    pieces = []
    while rows:
        at = chunk * keep_ref.shape[1] + begin
        inner = at % each
        take = min(rows, each - inner)
        pieces.append(plus(keep_ref[chunk, begin : begin + take, :], got[at // each][inner : inner + take, :]))
        begin, rows = begin + take, rows - take
    return pieces[0] if len(pieces) == 1 else jnp.concatenate(pieces, axis=0)


def add_core_split(split, keep_ref, *refs):
    got, refs = refs[:-8], refs[-8:]
    (mine_to, theirs_to, keep_to, send_to), (mine_ref, theirs_ref, halves_ref, sems) = refs[:4], refs[4:]
    half = (keep_ref.shape[1] - split) // 2
    theirs_ref[...] = piece_sum(keep_ref, got, 1, 0, split)
    leaving = run_copies([(theirs_ref, theirs_to)], sems.at[0:1])
    for chunk in range(2):
        for side in range(2):
            halves_ref[side, chunk * half : (chunk + 1) * half, :] = piece_sum(
                keep_ref, got, chunk, split + side * half, half
            )
    bit = seq_bit(0)
    leaving += run_copies([(halves_ref.at[1 - bit], send_to), (halves_ref.at[bit], keep_to)], sems.at[1:3])
    mine_ref[...] = piece_sum(keep_ref, got, 0, 0, split)
    leaving += run_copies([(mine_ref, mine_to)], sems.at[3:4])
    for copy in leaving:
        copy.wait()


def turn_kernel(mine_ref, got_ref, keep_ref, other_ref, kept_ref, send_ref, own_ref, theirs_ref):
    half = kept_ref.shape[0]
    bit = seq_bit(0)
    for side, ref in ((bit, kept_ref), (1 - bit, send_ref)):
        rows = pl.ds(pl.multiple_of(side * half, 16), half)
        ref[...] = plus(mine_ref[rows, :], got_ref[rows, :])
    half = own_ref.shape[0]
    own_ref[...] = plus(keep_ref[0:half, :], other_ref[0:half, :])
    theirs_ref[...] = plus(keep_ref[half:, :], other_ref[half:, :])


def add_core_far(keep_ref, *refs):
    got, (mine_to, theirs_to, mine_ref, theirs_ref, sems) = refs[:-5], refs[-5:]
    leaving = []
    for chunk, ref, to in ((1, theirs_ref, theirs_to), (0, mine_ref, mine_to)):
        ref[...] = piece_sum(keep_ref, got, chunk, 0, keep_ref.shape[1])
        leaving += run_copies([(ref, to)], sems.at[chunk : chunk + 1])
    for copy in leaving:
        copy.wait()


def add_core(keep_ref, got_ref, other_ref, mine_ref, theirs_ref):
    mine_ref[...] = plus(keep_ref[0], got_ref[...])
    theirs_ref[...] = plus(keep_ref[1], other_ref[...])


def add_plain(mine_ref, got_ref, out_ref):
    out_ref[...] = plus(mine_ref[...], got_ref[...])


def seq_bit(level):
    return jnp.bitwise_and(lax.shift_right_logical(lax.axis_index(SEQ), level), 1)


def add_halves(level, parts, *refs):
    pairs, (keep_ref, send_ref) = refs[:-2], refs[-2:]
    bit = seq_bit(level)
    begin = 0
    for at in range(0, len(pairs), 2):
        mine_ref, got_ref = pairs[at : at + 2]
        inner = 0
        for rows in parts[at // 2]:
            half = rows // 2
            for side, ref in ((bit, keep_ref), (1 - bit, send_ref)):
                at_rows = pl.ds(pl.multiple_of(inner + side * half, 16), half)
                ref[begin : begin + half, :] = plus(mine_ref[at_rows, :], got_ref[at_rows, :])
            inner += rows
            begin += half


def join_halves(level, parts, mine_ref, got_ref, out_ref):
    bit = seq_bit(level)
    begin = 0
    for rows in parts:
        for side, ref in ((bit, mine_ref), (1 - bit, got_ref)):
            out_ref[pl.ds(pl.multiple_of(2 * begin + side * rows, 16), rows), :] = ref[begin : begin + rows, :]
        begin += rows


def join_part(begin, mine_ref, got_ref, out_ref):
    half = out_ref.shape[0] // 2
    bit = seq_bit(0)
    for side, ref in ((bit, mine_ref), (1 - bit, got_ref)):
        out_ref[pl.ds(pl.multiple_of(side * half, 16), half), :] = ref[begin : begin + half, :]


def output_kernel(w0, w1, w2, w3, out_ref):
    rows, width, dim = out_ref.shape
    units = w0.shape[1]
    toks = w0.shape[0] // (dim // units)
    chan = lax.axis_index(CHAN)
    for j, ref in enumerate((w0, w1, w2, w3)):
        for row in range(toks // width):
            for half in range(dim // units):
                start = half * toks + row * width
                out_ref[jnp.bitwise_xor(chan, j) * (toks // width) + row, :, half * units : (half + 1) * units] = ref[
                    start : start + width, :
                ]


def swap(value, mask, axis=CHAN):
    return lax.ppermute(value, axis, [(at, at ^ mask) for at in range(lax.axis_size(axis))])


def exchange(value, axis):
    return lax.all_to_all(value, axis, 0, 0, tiled=True)


def seq_sum(value, ns):
    rows = value.shape[0]
    parts = exchange(value.reshape(ns, rows // ns, value.shape[1]), SEQ)
    return exchange(spread(parts), SEQ).reshape(value.shape)


def body(
    token_ids, valid_counts, embed, attn_gain, ema_in, ema_keep, ema_out, ema_skip, z_proj, q_gain, k_gain, q_bias,
    v_proj, r_proj, o_proj, ffn_gain, up_proj, down_proj, grad_out,
):
    rows, width = token_ids.shape
    vocab, dim = embed.shape
    nd = ema_in.shape[1]
    units = v_proj.shape[1]
    zdim = z_proj.shape[1]
    nc = lax.axis_size(CHAN)
    ns = lax.axis_size(SEQ)
    ndev = nc * ns
    rp = rows // nc
    toks = rp * width
    span = min(width * ns, SEQMAX)
    urows = o_proj.shape[0]
    zrows = z_proj.shape[0] // 2
    prows = 3 * nd + SUBS
    w1_rows = 2 * dim + zrows
    w2_rows = 3 * dim
    row = lambda vector: vector.reshape(1, -1)
    TOKEN.clear()

    dma = pltpu.SemaphoreType.DMA
    (p_own,) = call(
        pack_params, (shape_of((prows, LANES)),), (ema_in.T, ema_keep.T, ema_out.T, row(ema_skip)),
        scratch=[dma((4,))], hbm=range(4), out_free=(0,), limit=8,
    )
    p_far, p_near = swap(p_own, 2), swap(p_own, 1)
    x, xt, low, own1, own2 = call(
        functools.partial(prepare_kernel, nc),
        (
            shape_of((toks, dim), BF16), shape_of((width * SUBS, LANES)), shape_of((toks, dim), BF16),
            shape_of((w1_rows, units), BF16), shape_of((w2_rows, units), BF16),
        ),
        (token_ids, embed, row(attn_gain), v_proj, r_proj, z_proj, up_proj, o_proj, down_proj),
        scratch=[
            pltpu.VMEM((rows, width), jnp.int32), pltpu.VMEM((vocab, dim), BF16), pltpu.VMEM((1, dim), F32),
            pltpu.VMEM((toks, dim), BF16), pltpu.VMEM((toks, dim), BF16), pltpu.VMEM((w1_rows, units), BF16),
            pltpu.VMEM((w2_rows, units), BF16), dma((3,)), dma((9,)), dma((4,)),
        ],
        hbm=range(9), out_hbm=(0, 2, 3, 4),
    )
    own1, own2, p_far = lax.optimization_barrier((own1, own2, p_far))
    p_both = swap(p_far, 1)
    far1 = swap(own1, 2)
    near1 = swap(own1, 1)
    far2 = swap(own2, 2)
    near2 = swap(own2, 1)
    pt, ends = call(
        functools.partial(scan_end_kernel, nc, nd),
        (shape_of((prows * SUBS, LANES)), shape_of((ns, nd * SUBS, LANES))),
        (p_own, p_near, p_far, p_both, xt),
        scratch=[pltpu.VMEM((nc, prows, LANES), F32), pltpu.VMEM((nd * SUBS, LANES), F32), dma((ns,))],
        free=range(4), out_hbm=(1,), limit=8,
    )
    far1, _ = lax.optimization_barrier((far1, pt))
    both1 = swap(far1, 1)
    first = (own1, near1, far1, both1)
    ends = exchange(ends, SEQ)
    v_pre, r_pre, values, z_all, values_far = call(
        functools.partial(project_kernel, dim),
        (
            shape_of((toks, nc * units)), shape_of((toks, nc * units)), shape_of((toks, nc * units), BF16),
            shape_of((dim, zdim), BF16), shape_of((toks, nc * units), BF16),
        ),
        (low,) + first,
        scratch=[
            pltpu.VMEM((toks, dim), BF16), pltpu.VMEM((toks, nc * units), F32), pltpu.VMEM((4, w1_rows, units), BF16),
            dma((5,)), dma((8,)),
        ],
        hbm=range(4), free=(4,), out_hbm=(0, 4), limit=16,
    )
    mixed_pre, mixed_low, z_pre, attn, context, gated, state_in = call(
        functools.partial(mix_kernel, nc, nd, span),
        (
            shape_of((toks, dim)), shape_of((toks, dim), BF16), shape_of((toks, zdim)), shape_of((toks, width)),
            shape_of((toks, nc * units)), shape_of((toks, nc * units), BF16), shape_of((nd * SUBS, LANES)),
        ),
        (
            valid_counts, ends, xt, pt, z_all, values, r_pre, row(q_gain), row(k_gain), row(q_bias),
        ), scratch=[pltpu.VMEM((width * SUBS, LANES), F32), pltpu.VMEM((nd * SUBS, LANES), F32), pltpu.VMEM((toks, dim), BF16), dma((2,))],
        smem=(0,), free=range(7, 10), out_hbm=(1, 6), limit=16,
    )
    far2, gated = lax.optimization_barrier((far2, gated))
    both2 = swap(far2, 1)
    second = (own2, near2, far2, both2)
    out_rows = toks * (dim // units)
    out, g_mid, g_gated, keep1, send1, ffn_grad = call(
        functools.partial(ffn_kernel, nc, dim),
        (
            shape_of((out_rows, units), BF16), shape_of((toks, dim)), shape_of((toks, nc * units)),
            shape_of((2, w2_rows, units), BF16), shape_of((2, w2_rows, units), BF16), shape_of((1, dim)),
        ),
        (gated,) + second + (x, grad_out, row(ffn_gain)),
        scratch=[
            pltpu.VMEM((toks, nc * units), BF16), pltpu.VMEM((toks, nc * units), BF16),
            pltpu.VMEM((toks, dim), BF16), pltpu.VMEM((out_rows, units), BF16), pltpu.VMEM((toks, dim), F32),
            pltpu.VMEM((toks, dim), BF16), pltpu.VMEM((dim, nc * units), BF16), pltpu.VMEM((nc * urows, dim), BF16),
            pltpu.VMEM((nc * urows, dim), BF16), pltpu.VMEM((4, w2_rows, units), BF16),
            dma((1 + 8 * (dim // units) + 4 + rp,)), dma((2,)), dma((12,)),
        ],
        hbm=(1, 2, 3, 5, 6), free=(4, 7), out_hbm=(0, 1, 3, 4), limit=32,
    )
    got1 = swap(send1, 1).reshape(2 * w2_rows, units)
    fast = ns == 8
    unit = 64 if fast else 16 * ns
    g2_rows = -(-w1_rows // unit) * unit
    split1 = w2_rows - X_FIRST if fast else w2_rows
    split2 = g2_rows - X_ROWS if fast else g2_rows
    pieces = PIECES if fast else 2
    room = rest_rows(nd)
    f_rows = -(-(vocab // 2 + room) // (16 * ns)) * 16 * ns
    state = types.SimpleNamespace(out=out)
    parts_of = lambda rows, split: tuple(part // 2 for part in (split, rows - split) if part)
    parts1, parts2 = parts_of(w2_rows, split1), parts_of(g2_rows, split2)
    half_of = lambda parts: tuple(part // 2 for part in parts)
    bf = lambda rows: shape_of((rows, units), BF16)

    def halves(level, pairs, parts):
        rows = sum(sum(part) for part in parts) // 2
        return call(
            functools.partial(add_halves, level, parts), (bf(rows),) * 2, pairs, free=range(len(pairs)),
            out_free=range(2),
        )

    def joined(level, pair, parts):
        return call(
            functools.partial(join_halves, level, parts), (bf(2 * pair[0].shape[0]),), pair, free=range(2),
            out_free=(0,),
        )[0]

    def add_two(pair):
        return call(add_plain, (bf(pair[0].shape[0]),), pair, free=range(2), out_free=(0,))[0]

    def over_seq(value, mask):
        return swap(value, mask, SEQ)

    def core_whole(keep, gots, rows):
        mine, theirs = call(
            add_core_far, (bf(rows),) * 2, (keep, *gots),
            scratch=[pltpu.VMEM((rows, units), BF16), pltpu.VMEM((rows, units), BF16), dma((2,))],
            free=range(1 + len(gots)), out_hbm=range(2),
        )
        return mine, swap(theirs, 2)

    def tied(value):
        value, TOKEN[0] = lax.optimization_barrier((value, TOKEN[0]))
        return value

    def attn_back():
        grad_v, grad_r, g_z, gmt, carries, small, skip_grad = call(
            functools.partial(attn_back_kernel, nc, nd),
            (
                shape_of((toks, nc * units), BF16), shape_of((toks, nc * units), BF16), shape_of((toks, zdim)),
                shape_of((width * SUBS, LANES)), shape_of((ns, nd * SUBS, LANES), BF16), shape_of((SUBS, zdim)),
                shape_of((SUBS, LANES)),
            ),
            (
                g_gated, r_pre, v_pre, context, attn, values_far, z_pre, mixed_pre, xt, z_all, pt, row(q_gain),
                row(k_gain), row(q_bias),
            ),
            scratch=[
                pltpu.VMEM((nd * SUBS, LANES), BF16), pltpu.VMEM((toks, nc * units), BF16),
                pltpu.VMEM((toks, nc * units), BF16), dma((ns,)), dma((2,)),
            ],
            free=(2, 5, 11, 12, 13), out_hbm=(0, 1, 4), limit=20,
        )
        vars(state).update(
            grad_v=grad_v, grad_r=grad_r, g_z=g_z, gmt=gmt, carries=carries, small=small, skip_grad=skip_grad,
        )

    def core_parted(keep, gots, rows, split):
        if split == rows:
            return core_whole(keep, gots, rows)
        mine, theirs, kept, send = call(
            functools.partial(add_core_split, split), (bf(split),) * 2 + (bf(rows - split),) * 2, (keep, *gots),
            scratch=[
                pltpu.VMEM((split, units), BF16), pltpu.VMEM((split, units), BF16),
                pltpu.VMEM((2, rows - split, units), BF16), dma((4,)),
            ],
            free=range(1 + len(gots)), out_hbm=range(4),
        )
        return mine, swap(theirs, 2), kept, over_seq(send, 1)

    def turned(sums):
        if len(sums) == 2:
            keep, send = halves(0, sums, ((sums[0].shape[0],),))
            return keep, over_seq(send, 1)
        near, far = sums[0].shape[0] // 2, sums[2].shape[0] // 2
        kept, send, own, theirs = call(
            turn_kernel, (bf(near), bf(near), bf(far), bf(far)), sums, free=range(4), out_free=range(4)
        )
        return kept, over_seq(send, 1), own, swap(theirs, 2)

    def move_carry():
        state.carries = exchange(tied(state.carries), SEQ)

    def core_first():
        state.sums1 = core_parted(keep1, (got1,), w2_rows, split1)

    def grads():
        keep2, *sends = call(
            functools.partial(grads_kernel, nc, dim, zrows),
            (shape_of((2, g2_rows, units), BF16),) + (bf(2 * g2_rows // pieces),) * pieces,
            (low, state.grad_v, state.grad_r, mixed_low, state.g_z),
            scratch=[
                pltpu.VMEM((dim, zdim), F32), pltpu.VMEM((toks, dim), BF16), pltpu.VMEM((toks, nc * units), BF16),
                pltpu.VMEM((toks, nc * units), BF16), pltpu.VMEM((toks, dim), BF16),
                pltpu.VMEM((4, g2_rows, units), BF16), dma((4,)), dma((16,)),
            ],
            hbm=range(4), out_hbm=range(1 + pieces), limit=24,
        )
        vars(state).update(keep2=keep2, gots2=[swap(value, 1) for value in sends])

    def scans():
        state.shared, state.sums = call(
            functools.partial(scans_kernel, nd, dim), (shape_of((toks, dim)), shape_of((3, nd * SUBS, LANES))),
            (state.grad_v, state.grad_r) + first + (pt, state_in, xt, state.gmt),
            scratch=[
                pltpu.VMEM((toks, dim), F32), pltpu.VMEM((3, nd * SUBS, LANES), F32), pltpu.VMEM((nd * SUBS, LANES), F32),
                pltpu.VMEM((4, 2 * dim, units), BF16), pltpu.VMEM((toks, nc * units), BF16),
                pltpu.VMEM((toks, nc * units), BF16), dma((7,)),
            ],
            hbm=(0, 1, 2, 3, 4, 5, 7), out_hbm=range(2), limit=24,
        )

    def core_second():
        state.sums2 = core_parted(state.keep2, state.gots2, g2_rows, split2)

    def x_first():
        state.sums1 = turned(state.sums1)

    def last():
        state.f = call(
            functools.partial(last_kernel, nc, nd, ns, span),
            (shape_of((2, f_rows, units), BF16),) + (bf(f_rows),) * 2,
            (
                state.carries, state.gmt, pt, state.shared, x, row(attn_gain), g_mid, token_ids, state.sums,
                state.small, state.skip_grad, ffn_grad,
            ),
            scratch=[
                pltpu.VMEM((width * SUBS, LANES), F32), pltpu.VMEM((vocab, dim), F32),
                pltpu.VMEM((3 * nd * SUBS, LANES), F32), pltpu.VMEM((nc, room, LANES), F32),
                pltpu.VMEM((toks, dim), F32), pltpu.VMEM((toks, dim), BF16), pltpu.VMEM((1, dim), F32),
                pltpu.VMEM((toks, dim), F32), pltpu.VMEM((rows, width), jnp.int32),
                pltpu.VMEM((3, nd * SUBS, LANES), F32), dma((6,)),
            ],
            hbm=range(3, 9), out_free=range(3), limit=16,
        )

    def core_last():
        keep, send, other = state.f
        mine, theirs = call(
            add_core, (bf(f_rows),) * 2, (keep, swap(send, 1), swap(other, 1)), free=range(3),
            out_free=range(2),
        )
        state.sumsf = (mine, swap(theirs, 2))

    def x_last():
        keep, send = halves(0, state.sumsf, ((f_rows,),))
        state.sumsf = (keep, over_seq(send, 1))

    def turn_second():
        state.sums2 = turned(state.sums2)

    def z_first():
        keep, send = halves(1, state.sums1, tuple((rows,) for rows in parts1))
        state.sums1 = (keep, over_seq(send, 2))

    def z_second():
        keep, send = halves(1, state.sums2, tuple((rows,) for rows in parts2))
        state.sums2 = (keep, over_seq(send, 2))

    def added(sums, mask):
        value = add_two(sums)
        return value, over_seq(value, mask)

    def zz_first():
        state.sums1 = added(state.sums1, 4)

    def zz_second():
        state.sums2 = added(state.sums2, 4)

    def zz_last():
        state.sumsf = added(state.sumsf, 4)

    def sum_first():
        state.sums1 = added(state.sums1, 2)

    def sum_second():
        state.sums2 = added(state.sums2, 2)

    def sum_last():
        state.sumsf = added(state.sumsf, 2)

    def join_first():
        whole = joined(1, state.sums1, half_of(parts1))
        state.sums1 = (whole, over_seq(whole, 1))

    def join_second():
        whole = joined(1, state.sums2, half_of(parts2))
        state.sums2 = (whole, over_seq(whole, 1))

    def z_last():
        keep, send = halves(1, state.sumsf, ((f_rows // 2,),))
        state.sumsf = (keep, over_seq(send, 2))

    def join_last():
        whole = joined(1, state.sumsf, (f_rows // 4,))
        state.sumsf = (whole, over_seq(whole, 1))

    def move_out():
        state.out = tied(state.out)
        vars(state).update(out_far=swap(state.out, 2), out_near=swap(state.out, 1))

    def move_both():
        state.out_far = tied(state.out_far)
        state.out_both = swap(state.out_far, 1)

    def output():
        state.output = call(
            output_kernel, (shape_of((rows, width, dim), BF16),),
            (state.out, state.out_near, state.out_far, state.out_both), free=range(4),
            out_free=(0,), limit=8,
        )[0]

    def plain_sums():
        state.sums1, state.sums2, state.sumsf = [
            (seq_sum(add_two(sums), ns),) * 2 for sums in (state.sums1, state.sums2, state.sumsf)
        ]
        state.f_own = state.sumsf[0]

    def give_first():
        state.first = call(
            functools.partial(unpack_first, dim, urows, parts1 if fast else None),
            (shape_of(up_proj.shape), shape_of(o_proj.shape), shape_of(down_proj.shape)), state.sums1, free=range(2), out_free=range(3), scratch=[pltpu.VMEM((w2_rows, units), BF16)],
        )

    def give_second():
        state.second = call(
            functools.partial(unpack_second, dim, zrows, parts2 if fast else None),
            (shape_of(v_proj.shape), shape_of(r_proj.shape), shape_of(z_proj.shape)), state.sums2, free=range(2), out_free=range(3), scratch=[pltpu.VMEM((g2_rows, units), BF16)],
        )

    def collect():
        (state.f_own,) = call(
            functools.partial(join_part, 0), (bf(f_rows),), state.sumsf, free=range(2),
            out_free=(0,),
        )

    def finish():
        own = state.f_own
        far = swap(own, 2)
        state.finish = call(
            functools.partial(finish_kernel, nc, nd),
            (
                shape_of((vocab, dim)), shape_of((1, dim)), shape_of((nd, LANES)), shape_of((nd, LANES)),
                shape_of((nd, LANES)), shape_of((1, LANES)), shape_of((1, dim)), shape_of((1, zdim)),
                shape_of((1, zdim)), shape_of((1, zdim)),
            ),
            (own, swap(own, 1), far, swap(far, 1)), free=range(4), out_free=range(10),
            scratch=[pltpu.VMEM((nc, room, LANES), F32)], limit=8,
        )

    if fast:
        steps = (
            attn_back, core_first, grads, move_carry, scans, core_second, x_first, last, core_last, z_first, turn_second, zz_first, z_second, move_out, x_last, z_last, zz_second, sum_first, zz_last, join_first, sum_second, sum_last, move_both, join_second, join_last, output, give_first, collect, give_second, finish,
        )
    else:
        steps = (
            attn_back, move_carry, core_first, grads, scans, core_second, last, core_last, move_out, move_both, output,
            plain_sums, give_first, give_second, finish,
        )
    for step in steps:
        step()
    up_grad, o_grad, down_grad = state.first
    v_grad, r_grad, z_grad = state.second
    embed_grad, ag, gi, gk, go, gs, fg, qg, kg, qb = state.finish
    flat = lambda value: value.reshape(-1)
    return (
        state.output, embed_grad, flat(ag), gi.T, gk.T, go.T, flat(gs), z_grad, flat(qg), flat(kg), flat(qb), v_grad, r_grad,
        o_grad, flat(fg), up_grad, down_grad,
    )


def solution(mesh):
    placed = (
        P(None, SEQ), P(), P(), P(), P(CHAN, None), P(CHAN, None), P(CHAN, None), P(CHAN), P(CHAN, None),
        P(), P(), P(), P(None, CHAN), P(None, CHAN), P(CHAN, None), P(), P(None, CHAN), P(CHAN, None),
        P(None, SEQ, None),
    )
    return jax.shard_map(
        body,
        mesh=mesh,
        in_specs=placed,
        out_specs=(
            P(None, SEQ, None), P(), P(), P(CHAN, None), P(CHAN, None), P(CHAN, None), P(CHAN),
            P(CHAN, None), P(), P(), P(), P(None, CHAN), P(None, CHAN), P(CHAN, None), P(), P(None, CHAN),
            P(CHAN, None),
        ),
        check_vma=False,
    )
```

```python
import functools
import types

import jax
import jax.numpy as jnp
from jax import lax
from jax.experimental import pallas as pl
from jax.experimental.pallas import tpu as pltpu
from jax.sharding import PartitionSpec as P

SEQMAX = 4096
CHAN, SEQ = "chan", "seq"
EPS = 1e-06
F32 = jnp.float32
BF16 = jnp.bfloat16
LANES = 128
SUBS = 8
MIB = 1024 * 1024


def sigmoid(u):
    return 0.5 * jnp.tanh(0.5 * u) + 0.5


def silu_slope(pre):
    sigma = sigmoid(pre)
    return sigma * (1.0 + pre * (1.0 - sigma))


def mm(left, right, dims, precision=None):
    return lax.dot_general(
        left, right, ((dims[0], dims[1]), ((), ())), precision=precision, preferred_element_type=F32
    )


def dot(left, right):
    return mm(left, right, ((1,), (0,)))


def dot_rows(left, right):
    return mm(left, right, ((0,), (0,)))


def dot_cols(left, right):
    return mm(left, right, ((1,), (1,)))


def two_parts(value):
    high = value.astype(BF16)
    return high, (value - high.astype(F32)).astype(BF16)


def exact(left, right, dims):
    if left.dtype == BF16:
        high, low = two_parts(right)
        return mm(left, high, dims) + mm(left, low, dims)
    high, low = two_parts(left)
    return mm(high, right, dims) + mm(low, right, dims)


def shape_of(dims, dtype=F32):
    return jax.ShapeDtypeStruct(dims, dtype)


TOKEN = []
X_FIRST = 128
X_ROWS = 256
PIECES = 2


def call(
    kernel, outs, args, scratch=(), smem=(), hbm=(), free=(), far=(), out_hbm=(), out_free=(), out_far=(), limit=16
):
    waits = list(TOKEN)
    hbm, out_hbm = {*hbm, *far}, {*out_hbm, *out_far}
    count, made = len(args), len(outs)
    inner = kernel.func if isinstance(kernel, functools.partial) else kernel

    def run(*refs):
        rest = refs[count + len(waits) :]
        kernel(*refs[:count], *rest[:made], *rest[made + 1 :])

    def spec(at):
        if at >= count or (at in hbm and at not in far):
            return pl.BlockSpec(memory_space=pltpu.HBM)
        return pl.BlockSpec(memory_space=pltpu.SMEM if at in smem else pltpu.VMEM)

    def held(at, value):
        if at < count and (at in smem or at in free):
            return value
        return pltpu.with_memory_space_constraint(value, pltpu.HBM if at in hbm or at >= count else pltpu.VMEM)

    def result(at, out):
        if at in out_free:
            return out
        return (pltpu.HBM if at in out_hbm or at == made else pltpu.VMEM)(out.shape, out.dtype)

    shapes = list(outs) + [shape_of((SUBS, LANES))]
    *results, token = pl.pallas_call(
        run,
        out_shape=[result(at, out) for at, out in enumerate(shapes)],
        in_specs=[spec(at) for at in range(count + len(waits))],
        out_specs=[
            pl.BlockSpec(memory_space=pltpu.HBM if (at in out_hbm and at not in out_far) or at == made else pltpu.VMEM)
            for at in range(made + 1)
        ],
        scratch_shapes=list(scratch),
        name=inner.__name__,
        cost_estimate=pl.CostEstimate(flops=1, bytes_accessed=1, transcendentals=0),
        compiler_params=pltpu.CompilerParams(vmem_limit_bytes=limit * MIB),
    )(*[held(at, value) for at, value in enumerate([*args, *waits])])
    TOKEN[:] = [token]
    return results


def move(copies, sems):
    for copy in run_copies(copies, sems):
        copy.wait()


def run_copies(copies, sems):
    started = [pltpu.make_async_copy(src, dst, sems.at[at]) for at, (src, dst) in enumerate(copies)]
    for copy in started:
        copy.start()
    return started


def pack_params(in_ref, keep_ref, out_ref, skip_ref, p_ref, sems):
    nd, lanes = in_ref.shape
    copies = [(ref, p_ref.at[at * nd : (at + 1) * nd, :]) for at, ref in enumerate((in_ref, keep_ref, out_ref))]
    copies.append((skip_ref, p_ref.at[3 * nd : 3 * nd + 1, :]))
    move(copies, sems)
    rest = p_ref.shape[0] - 3 * nd
    p_ref[3 * nd :, :] = jnp.broadcast_to(p_ref[3 * nd : 3 * nd + 1, :], (rest, lanes))


def first_copies(v_ref, r_ref, z_ref, buf):
    dim = v_ref.shape[0]
    zrows = z_ref.shape[0] // 2
    copies = [(v_ref, buf.at[0:dim, :]), (r_ref, buf.at[dim : 2 * dim, :])]
    for half in range(2):
        copies.append(
            (
                z_ref.at[half * zrows : (half + 1) * zrows, :],
                buf.at[2 * dim : 2 * dim + zrows, half * LANES : (half + 1) * LANES],
            )
        )
    return copies


def second_copies(up_ref, o_ref, down_ref, buf):
    dim, units = up_ref.shape
    urows = o_ref.shape[0]
    copies = [(up_ref, buf.at[0:dim, :])]
    for at, ref in enumerate((o_ref, down_ref)):
        for half in range(dim // units):
            start = dim + (dim // units * at + half) * urows
            copies.append((ref.at[:, half * units : (half + 1) * units], buf.at[start : start + urows, :]))
    return copies


def prepare_kernel(
    nc, ids_at, table_at, gain_at, v_at, r_at, z_at, up_at, o_at, down_at,
    x_to, xt_ref, low_to, w1_to, w2_to,
    ids_ref, embed_ref, gain_ref, x_ref, low_ref, w1_ref, w2_ref, sems, w_sems, out_sems,
):
    entering = run_copies(first_copies(v_at, r_at, z_at, w1_ref), w_sems.at[0:4])
    started = run_copies([(ids_at, ids_ref), (table_at, embed_ref), (gain_at, gain_ref)], sems)
    later = run_copies(second_copies(up_at, o_at, down_at, w2_ref), w_sems.at[4:9])
    for copy in entering:
        copy.wait()
    leaving = run_copies([(w1_ref, w1_to)], out_sems.at[0:1])
    rp = x_ref.shape[0] // ids_ref.shape[1]
    width = ids_ref.shape[1]
    vocab = embed_ref.shape[0]
    chan = lax.axis_index(CHAN)
    for copy in started:
        copy.wait()
    for row in range(rp):
        ids = ids_ref[pl.ds(chan * rp + row, 1), :]
        onehot = jnp.where(lax.broadcasted_iota(jnp.int32, (vocab, width), 0) == ids, 1.0, 0.0).astype(BF16)
        x = dot_rows(onehot, embed_ref[...])
        x_ref[row * width : (row + 1) * width, :] = x.astype(BF16)
        normed = x * lax.rsqrt(jnp.mean(x * x, axis=-1, keepdims=True) + EPS) * gain_ref[...]
        low_ref[row * width : (row + 1) * width, :] = normed.astype(BF16)
        for chunk in range(nc):
            xt_ref[pl.ds(row * nc + chunk, width, stride=SUBS), :] = normed[
                :, chunk * LANES : (chunk + 1) * LANES
            ]
        for copy in later:
            copy.wait()
        later = []
        leaving += run_copies([(w2_ref, w2_to)], out_sems.at[1:2]) if row == 0 else []
    leaving += run_copies([(x_ref, x_to), (low_ref, low_to)], out_sems.at[2:4])
    for copy in leaving:
        copy.wait()


def tile(ref, at):
    return ref[at * SUBS : (at + 1) * SUBS, :]


def step_tile(ref, t):
    return ref[pl.ds(pl.multiple_of(t * SUBS, SUBS), SUBS), :]


def scan_end_kernel(nc, nd, p0, p1, p2, p3, xt_ref, pt_ref, end_ref, p_ref, buf, sems):
    width = xt_ref.shape[0] // SUBS
    prows = p_ref.shape[1]
    chan = lax.axis_index(CHAN)
    for j, ref in enumerate((p0, p1, p2, p3)):
        p_ref[jnp.bitwise_xor(chan, j)] = ref[...]
    for sub in range(SUBS):
        pt_ref[pl.ds(sub, prows, stride=SUBS), :] = p_ref[sub % nc]
    keep = [tile(pt_ref, nd + k) for k in range(nd)]

    def step(block, states):
        states = list(states)
        for u in range(8):
            x = step_tile(xt_ref, block * 8 + u)
            states = [q * s + x for q, s in zip(keep, states)]
        return tuple(states)

    zero = jnp.zeros((SUBS, LANES), F32)
    states = lax.fori_loop(0, width // 8, step, (zero,) * nd)
    buf[...] = jnp.concatenate(states, axis=0)
    for copy in run_copies([(buf, end_ref.at[at]) for at in range(end_ref.shape[0])], sems):
        copy.wait()


def project_kernel(
    dim, low_at, h0, h1, h2, h3, vpre_to, rpre_ref, val_ref, z_ref, val_to, low_ref, vpre_ref, buf, sems, out_sems
):
    chan = lax.axis_index(CHAN)
    units = h0.shape[1]
    zrows = h0.shape[0] - 2 * dim
    started = run_copies([(low_at, low_ref)] + [(ref, buf.at[j]) for j, ref in enumerate((h0, h1, h2, h3))], sems)
    started[0].wait()
    low = low_ref[...]
    leaving = []
    for j in range(4):
        started[1 + j].wait()
        w = buf.at[j]
        cols = slice(j * units, (j + 1) * units)
        v_pre = dot(low, w[0:dim, :])
        vpre_ref[:, cols] = v_pre
        val_ref[:, cols] = (v_pre * sigmoid(v_pre)).astype(BF16)
        leaving += run_copies(
            [(vpre_ref.at[:, cols], vpre_to.at[:, cols]), (val_ref.at[:, cols], val_to.at[:, cols])],
            out_sems.at[2 * j : 2 * j + 2],
        )
        rpre_ref[:, cols] = dot(low, w[dim : 2 * dim, :])
        start = pl.multiple_of(jnp.bitwise_xor(chan, j) * 2 * zrows, 2 * zrows)
        half = w[2 * dim : 2 * dim + zrows, :]
        z_ref[pl.ds(start, 2 * zrows), :] = jnp.concatenate([half[:, :LANES], half[:, LANES:]], axis=0)
    for copy in leaving:
        copy.wait()


def whole_keep(keep, width):
    whole = keep
    power = 1
    while power < width:
        whole = whole * whole
        power *= 2
    return whole


def weights_of(pt_ref, nd):
    amp = pt_ref[0 : nd * SUBS, :]
    keep = pt_ref[nd * SUBS : 2 * nd * SUBS, :]
    out = pt_ref[2 * nd * SUBS : 3 * nd * SUBS, :]
    root = jnp.sqrt(1.0 - keep * keep)
    return amp, keep, out, root


def split_tiles(value, nd):
    return [value[k * SUBS : (k + 1) * SUBS, :] for k in range(nd)]


def tree_sum(values):
    values = list(values)
    while len(values) > 1:
        values = [sum(values[i : i + 2][1:], values[i]) for i in range(0, len(values), 2)]
    return values[0]


def scale_of(x):
    return lax.rsqrt(jnp.mean(x * x, axis=-1, keepdims=True) + EPS)


def mix_kernel(
    nc, nd, span, counts_ref, ends_ref, xt_ref, pt_ref, z_ref, val_ref, rpre_ref, qg_ref, kg_ref, qb_ref,
    mpre_ref, mlow_to, zpre_ref, attn_ref, ctx_ref, gated_ref, sin_to, sm_ref, sin_ref, mlow_ref, sems,
):
    width = xt_ref.shape[0] // SUBS
    rp = SUBS // nc
    place = lax.axis_index(SEQ)
    chan = lax.axis_index(CHAN)
    amp, keep_all, out_all, root = weights_of(pt_ref, nd)
    whole = whole_keep(keep_all, width)
    per = span // width
    first = place // per * per

    def gather(n, state):
        return state * whole + ends_ref[n].astype(F32)

    start = lax.fori_loop(first, place, gather, jnp.zeros_like(whole))
    sin_ref[...] = start
    (leaving,) = run_copies([(sin_ref, sin_to)], sems.at[:1])
    keep = split_tiles(keep_all, nd)
    weight = split_tiles(out_all * amp * root, nd)

    def step(block, states):
        states = list(states)
        for u in range(8):
            t = block * 8 + u
            x = step_tile(xt_ref, t)
            states = [q * s + x for q, s in zip(keep, states)]
            sm_ref[pl.ds(pl.multiple_of(t * SUBS, SUBS), SUBS), :] = tree_sum(
                [w * s for w, s in zip(weight, states)]
            )
        return tuple(states)

    lax.fori_loop(0, width // 8, step, tuple(split_tiles(start, nd)))
    skip = pt_ref[3 * nd * SUBS : 3 * nd * SUBS + SUBS, :]
    for row in range(rp):
        rows = slice(row * width, (row + 1) * width)
        for chunk in range(nc):
            at = row * nc + chunk
            lanes = slice(chunk * LANES, (chunk + 1) * LANES)
            own = xt_ref[pl.ds(at, width, stride=SUBS), :]
            pre = sm_ref[pl.ds(at, width, stride=SUBS), :] + skip[at : at + 1, :] * own
            mpre_ref[rows, lanes] = pre
            mlow_ref[rows, lanes] = (pre * sigmoid(pre)).astype(BF16)
    (left,) = run_copies([(mlow_ref, mlow_to)], sems.at[1:])
    z_pre = dot(mlow_ref[...], z_ref[...])
    zpre_ref[...] = z_pre
    zeta = z_pre * sigmoid(z_pre)
    queries = (zeta * qg_ref[...] + qb_ref[...]).astype(BF16)
    keys = (zeta * kg_ref[...]).astype(BF16)
    scale = z_pre.shape[1] ** (-0.5)
    pieces = counts_ref.shape[0] // (rp * nc)
    begin = place * width
    piece = begin // span
    inner = begin - piece * span
    for row in range(rp):
        rows = slice(row * width, (row + 1) * width)
        count = counts_ref[(chan * rp + row) * pieces + piece]
        valid = lax.broadcasted_iota(jnp.int32, (width, width), 1) < count - inner
        scores = jnp.where(valid, dot_cols(queries[rows, :], keys[rows, :]) * scale, -1e30)
        top = jnp.max(scores, axis=-1, keepdims=True)
        weights = jnp.where(valid, jnp.exp(scores - top), 0.0)
        empty = jnp.where(count > inner, 0.0, 1.0)
        attn = weights / (jnp.sum(weights, axis=-1, keepdims=True) + empty)
        attn_ref[rows, :] = attn
        context = dot(attn.astype(BF16), val_ref[rows, :])
        ctx_ref[rows, :] = context
        r_pre = rpre_ref[rows, :]
        gated_ref[rows, :] = (r_pre * sigmoid(r_pre) * context).astype(BF16)
    leaving.wait()
    left.wait()


def ffn_kernel(
    nc, dim, gated_ref, h0, h1, h2, h3, x_at, grad_ref, fgain_ref,
    out_to, gmid_to, ggated_ref, keep_to, send_to, fg_ref,
    hid_ref, gup_ref, g_ref, out_ref, gmid_ref, x_ref, up_ref, o_ref, down_ref, part_ref, sems, out_sems, part_sems,
):
    units = h0.shape[1]
    rp = grad_ref.shape[0] // nc
    width = grad_ref.shape[1]
    chan = lax.axis_index(CHAN)
    urows = (h0.shape[0] - dim) // 4
    halves = dim // units
    hs = (h0, h1, h2, h3)

    def shards(ref, which):
        return [
            (
                h.at[dim + (which * halves + half) * urows : dim + (which * halves + half + 1) * urows, :],
                ref.at[j * urows : (j + 1) * urows, half * units : (half + 1) * units],
            )
            for j, h in enumerate(hs)
            for half in range(halves)
        ]

    copies = [(x_at, x_ref)] + shards(o_ref, 0)
    copies += [(h.at[0:dim, :], up_ref.at[:, j * units : (j + 1) * units]) for j, h in enumerate(hs)]
    copies += [(grad_ref.at[chan * rp + row], g_ref.at[row * width : (row + 1) * width, :]) for row in range(rp)]
    copies += shards(down_ref, 1)
    started = run_copies(copies, sems)
    first = 1 + 4 * halves
    for copy in started[:first]:
        copy.wait()
    middle = x_ref[...].astype(F32) + dot(gated_ref[...], o_ref[...])
    r = scale_of(middle)
    n = middle * r
    fgain = fgain_ref[...]
    ffn_low = (n * fgain).astype(BF16)
    for copy in started[first : first + 4]:
        copy.wait()
    up_pre = dot(ffn_low, up_ref[...])
    sigma = sigmoid(up_pre)
    hid_ref[...] = (up_pre * sigma).astype(BF16)
    for copy in started[first + 4 :]:
        copy.wait()
    g = g_ref[...]
    gup_ref[...] = (dot_cols(g, down_ref[...]) * (sigma * (1.0 + up_pre * (1.0 - sigma)))).astype(BF16)
    g_in = dot_cols(gup_ref[...], up_ref[...])
    h = g_in * fgain
    g_mid = g.astype(F32) + r * (h - n * jnp.mean(h * n, axis=-1, keepdims=True))
    gmid_ref[...] = g_mid
    g_branch = g_mid.astype(BF16)
    leaving = run_copies([(gmid_ref, gmid_to)], out_sems.at[0:1])
    fg_ref[...] = jnp.sum(g_in * n, axis=0, keepdims=True)

    def leave(begin, rows, which):
        part = slice(begin, begin + rows)
        return run_copies(
            [(part_ref.at[j, part, :], (keep_to, send_to)[j % 2].at[j // 2, part, :]) for j in (1, 3, 0, 2)],
            part_sems.at[4 * which : 4 * which + 4],
        )

    grad = dot_rows(ffn_low, gup_ref[...]).astype(BF16)
    for j in range(4):
        part_ref[j, 0:dim, :] = grad[:, j * units : (j + 1) * units]
    leaving += leave(0, dim, 0)
    for which, (left, right) in enumerate(((hid_ref, g), (gated_ref, g_branch))):
        grad = dot_rows(left[...], right).astype(BF16)
        begin = dim + (1 - which) * halves * urows
        for j in range(4):
            for half in range(halves):
                part_ref[j, begin + half * urows : begin + (half + 1) * urows, :] = grad[
                    j * urows : (j + 1) * urows, half * units : (half + 1) * units
                ]
        leaving += leave(begin, halves * urows, 1 + which)
    ggated_ref[...] = dot_cols(g_branch, o_ref[...])
    out = (middle + dot(hid_ref[...], down_ref[...])).astype(BF16)
    toks = g_ref.shape[0]
    for half in range(halves):
        out_ref[half * toks : (half + 1) * toks, :] = out[:, half * units : (half + 1) * units]
    leaving += run_copies([(out_ref, out_to)], out_sems.at[1:2])
    for copy in leaving:
        copy.wait()


def attn_back_kernel(
    nc, nd, ggated_ref, rpre_ref, vpre_ref, ctx_ref, attn_ref, val_ref, zpre_ref, mpre_ref, xt_ref, z_ref, pt_ref,
    qg_ref, kg_ref, qb_ref,
    gv_to, gr_to, gz_ref, gmt_ref, carry_ref, small_ref, skip_ref, buf, gv_ref, gr_ref, sems, out_sems,
):
    width = xt_ref.shape[0] // SUBS
    rp = SUBS // nc
    z_pre = zpre_ref[...]
    sigma = sigmoid(z_pre)
    zeta = z_pre * sigma
    queries = (zeta * qg_ref[...] + qb_ref[...]).astype(BF16)
    keys = (zeta * kg_ref[...]).astype(BF16)
    scale = z_pre.shape[1] ** (-0.5)
    parts_q, parts_k = [], []
    for row in range(rp):
        rows = slice(row * width, (row + 1) * width)
        g_gated = ggated_ref[rows, :]
        r_pre = rpre_ref[rows, :]
        sr = sigmoid(r_pre)
        g_context = (g_gated * (r_pre * sr)).astype(BF16)
        gr_ref[rows, :] = (g_gated * ctx_ref[rows, :] * (sr * (1.0 + r_pre * (1.0 - sr)))).astype(BF16)
        attn = attn_ref[rows, :]
        g_values = dot_rows(attn.astype(BF16), g_context)
        gv_ref[rows, :] = (g_values * silu_slope(vpre_ref[rows, :])).astype(BF16)
        g_attn = dot_cols(g_context, val_ref[rows, :])
        g_scores = attn * (g_attn - jnp.sum(attn * g_attn, axis=-1, keepdims=True))
        parts_q.append(exact(g_scores, keys[rows, :], ((1,), (0,))) * scale)
        parts_k.append(exact(g_scores, queries[rows, :], ((0,), (0,))) * scale)
    leaving = run_copies([(gv_ref, gv_to), (gr_ref, gr_to)], out_sems)
    g_q = jnp.concatenate(parts_q, axis=0)
    g_k = jnp.concatenate(parts_k, axis=0)
    small_ref[...] = jnp.concatenate(
        [
            jnp.sum(g_q * zeta, axis=0, keepdims=True),
            jnp.sum(g_k * zeta, axis=0, keepdims=True),
            jnp.sum(g_q, axis=0, keepdims=True),
            jnp.zeros((SUBS - 3, z_pre.shape[1]), F32),
        ],
        axis=0,
    )
    g_z = (g_q * qg_ref[...] + g_k * kg_ref[...]) * (sigma * (1.0 + z_pre * (1.0 - sigma)))
    gz_ref[...] = g_z
    for row in range(rp):
        rows = slice(row * width, (row + 1) * width)
        for chunk in range(nc):
            at = row * nc + chunk
            lanes = slice(chunk * LANES, (chunk + 1) * LANES)
            g_mixed = exact(g_z[rows, :], z_ref[lanes, :], ((1,), (1,))) * silu_slope(mpre_ref[rows, lanes])
            gmt_ref[pl.ds(at, width, stride=SUBS), :] = g_mixed
    keep = [tile(pt_ref, nd + k) for k in range(nd)]

    def step(block, carries):
        carries = list(carries)
        for u in range(8):
            gm = step_tile(gmt_ref, width - 1 - (block * 8 + u))
            carries = [q * (c + gm) for q, c in zip(keep, carries)]
        return tuple(carries)

    zero = jnp.zeros((SUBS, LANES), F32)
    carries = lax.fori_loop(0, width // 8, step, (zero,) * nd)
    buf[...] = jnp.concatenate(carries, axis=0).astype(BF16)
    leaving += run_copies([(buf, carry_ref.at[at]) for at in range(carry_ref.shape[0])], sems)
    skips = []
    for at in range(SUBS):
        every = pl.ds(at, width, stride=SUBS)
        skips.append(jnp.sum(gmt_ref[every, :] * xt_ref[every, :], axis=0, keepdims=True))
    skip_ref[...] = jnp.concatenate(skips, axis=0)
    for copy in leaving:
        copy.wait()


def grads_kernel(
    nc, dim, zrows, low_at, gv_at, gr_at, mlow_at, gz_ref, keep_to, *refs
):
    sends, (zg_ref, low_ref, gv_ref, gr_ref, mlow_ref, part_ref, sems, part_sems) = refs[:-8], refs[-8:]
    units = gv_ref.shape[1] // nc
    chan = lax.axis_index(CHAN)
    started = run_copies([(mlow_at, mlow_ref), (low_at, low_ref), (gv_at, gv_ref), (gr_at, gr_ref)], sems)
    started[0].wait()
    zg_ref[...] = exact(mlow_ref[...], gz_ref[...], ((0,), (0,)))
    for copy in started[1:]:
        copy.wait()
    low = low_ref[...]
    used = 2 * dim + zrows
    spare = part_ref.shape[1] - used
    leaving = []
    for j in (1, 3, 0, 2):
        cols = slice(j * units, (j + 1) * units)
        part_ref[j, 0:dim, :] = dot_rows(low, gv_ref[:, cols]).astype(BF16)
        part_ref[j, dim : 2 * dim, :] = dot_rows(low, gr_ref[:, cols]).astype(BF16)
        start = pl.multiple_of(jnp.bitwise_xor(chan, j) * 2 * zrows, 2 * zrows)
        block = zg_ref[pl.ds(start, 2 * zrows), :]
        part_ref[j, 2 * dim : used, :] = jnp.concatenate([block[:zrows, :], block[zrows:, :]], axis=1).astype(BF16)
        if spare:
            part_ref[j, used:, :] = jnp.zeros((spare, units), BF16)
        if j % 2:
            copies = []
            total, each = part_ref.shape[1], sends[0].shape[0]
            begin = 0
            while begin < total:
                at = j // 2 * total + begin
                take = min(total - begin, each - at % each)
                to = sends[at // each].at[at % each : at % each + take, :]
                copies.append((part_ref.at[j, begin : begin + take, :], to))
                begin += take
        else:
            copies = [(part_ref.at[j], keep_to.at[j // 2])]
        leaving += run_copies(copies, part_sems.at[4 * j : 4 * j + len(copies)])
    for copy in leaving:
        copy.wait()


def scans_kernel(
    nd, dim, gv_at, gr_at, h0, h1, h2, h3, pt_ref, sin_at, xt_ref, gmt_ref,
    shared_to, acc_to, shared_ref, acc_ref, sin_ref, buf, gv_ref, gr_ref, sems,
):
    units = h0.shape[1]
    width = xt_ref.shape[0] // SUBS
    started = run_copies(
        [(sin_at, sin_ref), (gv_at, gv_ref), (gr_at, gr_ref)]
        + [(ref.at[0 : 2 * dim, :], buf.at[j]) for j, ref in enumerate((h0, h1, h2, h3))],
        sems,
    )
    started[0].wait()
    group = nd // 2

    def scan(begin):
        ks = list(range(begin, begin + group))
        keep = [tile(pt_ref, nd + k) for k in ks]

        def step(block, carry):
            s, d, a, b = [list(part) for part in carry]
            for u in range(8):
                t = block * 8 + u
                x = step_tile(xt_ref, t)
                gm = step_tile(gmt_ref, t)
                d = [q * di + si for q, di, si in zip(keep, d, s)]
                s = [q * si + x for q, si in zip(keep, s)]
                a = [ai + gm * si for ai, si in zip(a, s)]
                b = [bi + gm * di for bi, di in zip(b, d)]
            return tuple(s), tuple(d), tuple(a), tuple(b)

        zero = (jnp.zeros((SUBS, LANES), F32),) * group
        init = tuple(tile(sin_ref, k) for k in ks)
        s, d, a, b = lax.fori_loop(0, width // 8, step, (init, zero, zero, zero))
        rows = slice(begin * SUBS, (begin + group) * SUBS)
        acc_ref[0, rows, :] = jnp.concatenate(a, axis=0)
        acc_ref[1, rows, :] = jnp.concatenate(b, axis=0)
        acc_ref[2, rows, :] = jnp.concatenate(d, axis=0)

    scan(0)
    for copy in started[1:3]:
        copy.wait()
    shared = None
    for j in range(4):
        cols = slice(j * units, (j + 1) * units)
        started[3 + j].wait()
        term = dot_cols(gv_ref[:, cols], buf[j, 0:dim, :]) + dot_cols(gr_ref[:, cols], buf[j, dim:, :])
        shared = term if j == 0 else shared + term
    shared_ref[...] = shared
    leaving = run_copies([(shared_ref, shared_to)], sems.at[1:])
    scan(group)
    leaving += run_copies([(acc_ref, acc_to)], sems)
    for copy in leaving:
        copy.wait()


def rest_rows(nd):
    return -(-(3 * nd + 4) // 16) * 16


def last_kernel(
    nc, nd, ns, span, carry_ref, gmt_ref, pt_ref, shared_at, x_at, gain_at, gmid_at, ids_at, sums_at,
    small_ref, skip_ref, fg_ref,
    keep_ref, send1_ref, send3_ref, yt_ref, acc_ref, ema_ref, rest_ref, shared_ref, x_ref, gain_ref, gmid_ref, ids_ref, sums_ref,
    sems,
):
    started = run_copies(
        [
            (shared_at, shared_ref), (x_at, x_ref), (gain_at, gain_ref), (gmid_at, gmid_ref), (ids_at, ids_ref),
            (sums_at, sums_ref),
        ],
        sems,
    )
    width = gmt_ref.shape[0] // SUBS
    rp = SUBS // nc
    vocab = acc_ref.shape[0]
    place = lax.axis_index(SEQ)
    chan = lax.axis_index(CHAN)
    amp, keep_all, out_all, root = weights_of(pt_ref, nd)
    whole = whole_keep(keep_all, width)
    per = span // width
    last = place // per * per + per - 1

    def gather(n, state):
        return state * whole + carry_ref[last - n].astype(F32)

    start = lax.fori_loop(0, last - place, gather, jnp.zeros_like(whole))
    drive = amp * root
    weight_all = out_all * drive
    keep = split_tiles(keep_all, nd)
    weight = split_tiles(weight_all, nd)

    def step(block, carries):
        carries = list(carries)
        for u in range(8):
            t = width - 1 - (block * 8 + u)
            gm = step_tile(gmt_ref, t)
            adj = [c + gm for c in carries]
            yt_ref[pl.ds(pl.multiple_of(t * SUBS, SUBS), SUBS), :] = tree_sum(
                [w * s for w, s in zip(weight, adj)]
            )
            carries = [q * s for q, s in zip(keep, adj)]
        return tuple(carries)

    lax.fori_loop(0, width // 8, step, tuple(split_tiles(start, nd)))
    for copy in started:
        copy.wait()
    a = sums_ref[0]
    g_drive = out_all * a
    grad_out = drive * a
    grad_in = g_drive * root
    grad_keep = weight_all * (sums_ref[1] + sums_ref[2] * start) - g_drive * amp * keep_all / root
    for at, grad in enumerate((grad_in, grad_keep, grad_out)):
        ema_ref[at * nd * SUBS : (at + 1) * nd * SUBS, :] = grad
    skip = pt_ref[3 * nd * SUBS : 3 * nd * SUBS + SUBS, :]
    gain = gain_ref[...]
    for row in range(rp):
        toks = slice(row * width, (row + 1) * width)
        pieces = []
        for chunk in range(nc):
            at = row * nc + chunk
            lanes = slice(chunk * LANES, (chunk + 1) * LANES)
            gm = gmt_ref[pl.ds(at, width, stride=SUBS), :]
            pieces.append(
                shared_ref[toks, lanes] + skip[at : at + 1, :] * gm + yt_ref[pl.ds(at, width, stride=SUBS), :]
            )
        g_normed = jnp.concatenate(pieces, axis=1)
        x = x_ref[toks, :].astype(F32)
        r = scale_of(x)
        n = x * r
        h = g_normed * gain
        g_x = gmid_ref[toks, :] + r * (h - n * jnp.mean(h * n, axis=-1, keepdims=True))
        part = jnp.sum(g_normed * n, axis=0, keepdims=True)
        ag = part if row == 0 else ag + part
        ids = ids_ref[pl.ds(chan * rp + row, 1), :]
        onehot = jnp.where(lax.broadcasted_iota(jnp.int32, (vocab, width), 0) == ids, 1.0, 0.0).astype(BF16)
        term = exact(onehot, g_x, ((1,), (0,)))
        acc_ref[...] = term if row == 0 else acc_ref[...] + term
    rest_ref[...] = jnp.zeros_like(rest_ref)
    for chunk in range(nc):
        lanes = slice(chunk * LANES, (chunk + 1) * LANES)
        for at in range(3):
            total = None
            for row in range(rp):
                term = ema_ref[pl.ds(at * nd * SUBS + row * nc + chunk, nd, stride=SUBS), :]
                total = term if row == 0 else total + term
            rest_ref[chunk, at * nd : (at + 1) * nd, :] = total
        at = 3 * nd
        rest_ref[chunk, at : at + 1, :] = sum(
            skip_ref[row * nc + chunk : row * nc + chunk + 1, :] for row in range(rp)
        )
        rest_ref[chunk, at + 1 : at + 2, :] = ag[:, lanes]
        rest_ref[chunk, at + 2 : at + 3, :] = fg_ref[:, lanes]
        if chunk < 3:
            rest_ref[chunk, at + 3 : at + 4, :] = small_ref[chunk : chunk + 1, :]
    half = vocab // 2
    room = rest_ref.shape[1]
    for j in range(4):
        to = (keep_ref.at[0], send1_ref, keep_ref.at[1], send3_ref)[j]
        owner = jnp.bitwise_xor(chan, j)
        block = acc_ref[:, pl.ds(pl.multiple_of(owner * LANES, LANES), LANES)]
        to[0:half, :] = jnp.concatenate([block[:half, :], block[half:, :]], axis=1).astype(BF16)
        rest = rest_ref[owner]
        high = rest.astype(BF16)
        low = (rest - high.astype(F32)).astype(BF16)
        to[half : half + room, :] = jnp.concatenate([high, low], axis=1)
        if to.shape[0] > half + room:
            to[half + room :, :] = jnp.zeros((to.shape[0] - half - room, to.shape[1]), BF16)


def sum_kernel(in_ref, out_ref, buf, sems):
    total = in_ref[0].astype(F32)
    for at in range(1, in_ref.shape[0]):
        total = total + in_ref[at].astype(F32)
    buf[...] = total.astype(BF16)
    for copy in run_copies([(buf, out_ref.at[at]) for at in range(out_ref.shape[0])], sems):
        copy.wait()


def spread(parts):
    scratch = [pltpu.VMEM(parts.shape[1:], BF16), pltpu.SemaphoreType.DMA((parts.shape[0],))]
    return call(sum_kernel, (shape_of(parts.shape, BF16),), (parts,), scratch=scratch, out_hbm=(0,))[0]


def finish_kernel(
    nc, nd, w0, w1, w2, w3, embed_ref, ag_ref, ei_ref, ek_ref, eo_ref, es_ref, fg_ref, qg_ref, kg_ref, qb_ref, rest_ref
):
    half = embed_ref.shape[0] // 2
    room = rest_ref.shape[1]
    chan = lax.axis_index(CHAN)
    for j, ref in enumerate((w0, w1, w2, w3)):
        owner = jnp.bitwise_xor(chan, j)
        lanes = pl.ds(pl.multiple_of(owner * LANES, LANES), LANES)
        block = ref[0:half, :].astype(F32)
        embed_ref[0:half, lanes] = block[:, :LANES]
        embed_ref[half:, lanes] = block[:, LANES:]
        rest = ref[half : half + room, :].astype(F32)
        rest = rest[:, :LANES] + rest[:, LANES:]
        rest_ref[owner] = rest
        if j == 0:
            for at, to in enumerate((ei_ref, ek_ref, eo_ref)):
                to[...] = rest[at * nd : (at + 1) * nd, :]
            es_ref[...] = rest[3 * nd : 3 * nd + 1, :]
        ag_ref[:, lanes] = rest[3 * nd + 1 : 3 * nd + 2, :]
        fg_ref[:, lanes] = rest[3 * nd + 2 : 3 * nd + 3, :]
    for at, to in enumerate((qg_ref, kg_ref, qb_ref)):
        to[...] = rest_ref[at, 3 * nd + 3 : 3 * nd + 4, :]


def unpack_first(dim, urows, parts, u_ref, v_ref, up_ref, o_ref, down_ref, s_ref):
    join(parts, u_ref, v_ref, s_ref)
    units = s_ref.shape[1]
    up_ref[...] = s_ref[0:dim, :].astype(F32)
    for at, ref in enumerate((o_ref, down_ref)):
        for half in range(dim // units):
            start = dim + (at * (dim // units) + half) * urows
            ref[:, half * units : (half + 1) * units] = s_ref[start : start + urows, :].astype(F32)


def unpack_second(dim, zrows, parts, u_ref, x_ref, v_ref, r_ref, z_ref, s_ref):
    join(parts, u_ref, x_ref, s_ref)
    v_ref[...] = s_ref[0:dim, :].astype(F32)
    r_ref[...] = s_ref[dim : 2 * dim, :].astype(F32)
    block = s_ref[2 * dim : 2 * dim + zrows, :].astype(F32)
    z_ref[0:zrows, :] = block[:, :LANES]
    z_ref[zrows:, :] = block[:, LANES:]


def join(parts, mine_ref, other_ref, to_ref):
    if parts is None:
        to_ref[...] = mine_ref[...]
    else:
        join_halves(0, parts, mine_ref, other_ref, to_ref)


def plus(left, right):
    return (left.astype(F32) + right.astype(F32)).astype(BF16)


def piece_sum(keep_ref, got, chunk, begin, rows):
    each = got[0].shape[0]
    pieces = []
    while rows:
        at = chunk * keep_ref.shape[1] + begin
        inner = at % each
        take = min(rows, each - inner)
        pieces.append(plus(keep_ref[chunk, begin : begin + take, :], got[at // each][inner : inner + take, :]))
        begin, rows = begin + take, rows - take
    return pieces[0] if len(pieces) == 1 else jnp.concatenate(pieces, axis=0)


def add_core_split(split, keep_ref, *refs):
    got, refs = refs[:-8], refs[-8:]
    (mine_to, theirs_to, keep_to, send_to), (mine_ref, theirs_ref, halves_ref, sems) = refs[:4], refs[4:]
    half = (keep_ref.shape[1] - split) // 2
    theirs_ref[...] = piece_sum(keep_ref, got, 1, 0, split)
    leaving = run_copies([(theirs_ref, theirs_to)], sems.at[0:1])
    for chunk in range(2):
        for side in range(2):
            halves_ref[side, chunk * half : (chunk + 1) * half, :] = piece_sum(
                keep_ref, got, chunk, split + side * half, half
            )
    bit = seq_bit(0)
    leaving += run_copies([(halves_ref.at[1 - bit], send_to), (halves_ref.at[bit], keep_to)], sems.at[1:3])
    mine_ref[...] = piece_sum(keep_ref, got, 0, 0, split)
    leaving += run_copies([(mine_ref, mine_to)], sems.at[3:4])
    for copy in leaving:
        copy.wait()


def turn_kernel(mine_ref, got_ref, keep_ref, other_ref, kept_ref, send_ref, own_ref, theirs_ref):
    half = kept_ref.shape[0]
    bit = seq_bit(0)
    for side, ref in ((bit, kept_ref), (1 - bit, send_ref)):
        rows = pl.ds(pl.multiple_of(side * half, 16), half)
        ref[...] = plus(mine_ref[rows, :], got_ref[rows, :])
    half = own_ref.shape[0]
    own_ref[...] = plus(keep_ref[0:half, :], other_ref[0:half, :])
    theirs_ref[...] = plus(keep_ref[half:, :], other_ref[half:, :])


def add_core_far(keep_ref, *refs):
    got, (mine_to, theirs_to, mine_ref, theirs_ref, sems) = refs[:-5], refs[-5:]
    leaving = []
    for chunk, ref, to in ((1, theirs_ref, theirs_to), (0, mine_ref, mine_to)):
        ref[...] = piece_sum(keep_ref, got, chunk, 0, keep_ref.shape[1])
        leaving += run_copies([(ref, to)], sems.at[chunk : chunk + 1])
    for copy in leaving:
        copy.wait()


def add_core(keep_ref, got_ref, other_ref, mine_ref, theirs_ref):
    mine_ref[...] = plus(keep_ref[0], got_ref[...])
    theirs_ref[...] = plus(keep_ref[1], other_ref[...])


def add_plain(mine_ref, got_ref, out_ref):
    out_ref[...] = plus(mine_ref[...], got_ref[...])


def seq_bit(level):
    return jnp.bitwise_and(lax.shift_right_logical(lax.axis_index(SEQ), level), 1)


def add_halves(level, parts, *refs):
    pairs, (keep_ref, send_ref) = refs[:-2], refs[-2:]
    bit = seq_bit(level)
    begin = 0
    for at in range(0, len(pairs), 2):
        mine_ref, got_ref = pairs[at : at + 2]
        inner = 0
        for rows in parts[at // 2]:
            half = rows // 2
            for side, ref in ((bit, keep_ref), (1 - bit, send_ref)):
                at_rows = pl.ds(pl.multiple_of(inner + side * half, 16), half)
                ref[begin : begin + half, :] = plus(mine_ref[at_rows, :], got_ref[at_rows, :])
            inner += rows
            begin += half


def join_halves(level, parts, mine_ref, got_ref, out_ref):
    bit = seq_bit(level)
    begin = 0
    for rows in parts:
        for side, ref in ((bit, mine_ref), (1 - bit, got_ref)):
            out_ref[pl.ds(pl.multiple_of(2 * begin + side * rows, 16), rows), :] = ref[begin : begin + rows, :]
        begin += rows


def join_part(begin, mine_ref, got_ref, out_ref):
    half = out_ref.shape[0] // 2
    bit = seq_bit(0)
    for side, ref in ((bit, mine_ref), (1 - bit, got_ref)):
        out_ref[pl.ds(pl.multiple_of(side * half, 16), half), :] = ref[begin : begin + half, :]


def output_kernel(w0, w1, w2, w3, out_ref):
    rows, width, dim = out_ref.shape
    units = w0.shape[1]
    toks = w0.shape[0] // (dim // units)
    chan = lax.axis_index(CHAN)
    for j, ref in enumerate((w0, w1, w2, w3)):
        for row in range(toks // width):
            for half in range(dim // units):
                start = half * toks + row * width
                out_ref[jnp.bitwise_xor(chan, j) * (toks // width) + row, :, half * units : (half + 1) * units] = ref[
                    start : start + width, :
                ]


def swap(value, mask, axis=CHAN):
    return lax.ppermute(value, axis, [(at, at ^ mask) for at in range(lax.axis_size(axis))])


def exchange(value, axis):
    return lax.all_to_all(value, axis, 0, 0, tiled=True)


def seq_sum(value, ns):
    rows = value.shape[0]
    parts = exchange(value.reshape(ns, rows // ns, value.shape[1]), SEQ)
    return exchange(spread(parts), SEQ).reshape(value.shape)


def body(
    token_ids, valid_counts, embed, attn_gain, ema_in, ema_keep, ema_out, ema_skip, z_proj, q_gain, k_gain, q_bias,
    v_proj, r_proj, o_proj, ffn_gain, up_proj, down_proj, grad_out,
):
    rows, width = token_ids.shape
    vocab, dim = embed.shape
    nd = ema_in.shape[1]
    units = v_proj.shape[1]
    zdim = z_proj.shape[1]
    nc = lax.axis_size(CHAN)
    ns = lax.axis_size(SEQ)
    ndev = nc * ns
    rp = rows // nc
    toks = rp * width
    span = min(width * ns, SEQMAX)
    urows = o_proj.shape[0]
    zrows = z_proj.shape[0] // 2
    prows = 3 * nd + SUBS
    w1_rows = 2 * dim + zrows
    w2_rows = 3 * dim
    row = lambda vector: vector.reshape(1, -1)
    TOKEN.clear()

    dma = pltpu.SemaphoreType.DMA
    (p_own,) = call(
        pack_params, (shape_of((prows, LANES)),), (ema_in.T, ema_keep.T, ema_out.T, row(ema_skip)),
        scratch=[dma((4,))], hbm=range(4), out_free=(0,), limit=8,
    )
    p_far, p_near = swap(p_own, 2), swap(p_own, 1)
    x, xt, low, own1, own2 = call(
        functools.partial(prepare_kernel, nc),
        (
            shape_of((toks, dim), BF16), shape_of((width * SUBS, LANES)), shape_of((toks, dim), BF16),
            shape_of((w1_rows, units), BF16), shape_of((w2_rows, units), BF16),
        ),
        (token_ids, embed, row(attn_gain), v_proj, r_proj, z_proj, up_proj, o_proj, down_proj),
        scratch=[
            pltpu.VMEM((rows, width), jnp.int32), pltpu.VMEM((vocab, dim), BF16), pltpu.VMEM((1, dim), F32),
            pltpu.VMEM((toks, dim), BF16), pltpu.VMEM((toks, dim), BF16), pltpu.VMEM((w1_rows, units), BF16),
            pltpu.VMEM((w2_rows, units), BF16), dma((3,)), dma((9,)), dma((4,)),
        ],
        hbm=range(9), out_hbm=(0, 2, 3, 4),
    )
    own1, own2, p_far = lax.optimization_barrier((own1, own2, p_far))
    p_both = swap(p_far, 1)
    far1 = swap(own1, 2)
    near1 = swap(own1, 1)
    far2 = swap(own2, 2)
    near2 = swap(own2, 1)
    pt, ends = call(
        functools.partial(scan_end_kernel, nc, nd),
        (shape_of((prows * SUBS, LANES)), shape_of((ns, nd * SUBS, LANES))),
        (p_own, p_near, p_far, p_both, xt),
        scratch=[pltpu.VMEM((nc, prows, LANES), F32), pltpu.VMEM((nd * SUBS, LANES), F32), dma((ns,))],
        free=range(4), out_hbm=(1,), limit=8,
    )
    far1, _ = lax.optimization_barrier((far1, pt))
    both1 = swap(far1, 1)
    first = (own1, near1, far1, both1)
    ends = exchange(ends, SEQ)
    v_pre, r_pre, values, z_all, values_far = call(
        functools.partial(project_kernel, dim),
        (
            shape_of((toks, nc * units)), shape_of((toks, nc * units)), shape_of((toks, nc * units), BF16),
            shape_of((dim, zdim), BF16), shape_of((toks, nc * units), BF16),
        ),
        (low,) + first,
        scratch=[
            pltpu.VMEM((toks, dim), BF16), pltpu.VMEM((toks, nc * units), F32), pltpu.VMEM((4, w1_rows, units), BF16),
            dma((5,)), dma((8,)),
        ],
        hbm=range(4), free=(4,), out_hbm=(0, 4), limit=16,
    )
    mixed_pre, mixed_low, z_pre, attn, context, gated, state_in = call(
        functools.partial(mix_kernel, nc, nd, span),
        (
            shape_of((toks, dim)), shape_of((toks, dim), BF16), shape_of((toks, zdim)), shape_of((toks, width)),
            shape_of((toks, nc * units)), shape_of((toks, nc * units), BF16), shape_of((nd * SUBS, LANES)),
        ),
        (
            valid_counts, ends, xt, pt, z_all, values, r_pre, row(q_gain), row(k_gain), row(q_bias),
        ), scratch=[pltpu.VMEM((width * SUBS, LANES), F32), pltpu.VMEM((nd * SUBS, LANES), F32), pltpu.VMEM((toks, dim), BF16), dma((2,))],
        smem=(0,), free=range(7, 10), out_hbm=(1, 6), limit=16,
    )
    far2, gated = lax.optimization_barrier((far2, gated))
    both2 = swap(far2, 1)
    second = (own2, near2, far2, both2)
    out_rows = toks * (dim // units)
    out, g_mid, g_gated, keep1, send1, ffn_grad = call(
        functools.partial(ffn_kernel, nc, dim),
        (
            shape_of((out_rows, units), BF16), shape_of((toks, dim)), shape_of((toks, nc * units)),
            shape_of((2, w2_rows, units), BF16), shape_of((2, w2_rows, units), BF16), shape_of((1, dim)),
        ),
        (gated,) + second + (x, grad_out, row(ffn_gain)),
        scratch=[
            pltpu.VMEM((toks, nc * units), BF16), pltpu.VMEM((toks, nc * units), BF16),
            pltpu.VMEM((toks, dim), BF16), pltpu.VMEM((out_rows, units), BF16), pltpu.VMEM((toks, dim), F32),
            pltpu.VMEM((toks, dim), BF16), pltpu.VMEM((dim, nc * units), BF16), pltpu.VMEM((nc * urows, dim), BF16),
            pltpu.VMEM((nc * urows, dim), BF16), pltpu.VMEM((4, w2_rows, units), BF16),
            dma((1 + 8 * (dim // units) + 4 + rp,)), dma((2,)), dma((12,)),
        ],
        hbm=(1, 2, 3, 5, 6), free=(4, 7), out_hbm=(0, 1, 3, 4), limit=32,
    )
    got1 = swap(send1, 1).reshape(2 * w2_rows, units)
    fast = ns == 8
    unit = 64 if fast else 16 * ns
    g2_rows = -(-w1_rows // unit) * unit
    split1 = w2_rows - X_FIRST if fast else w2_rows
    split2 = g2_rows - X_ROWS if fast else g2_rows
    pieces = PIECES if fast else 2
    room = rest_rows(nd)
    f_rows = -(-(vocab // 2 + room) // (16 * ns)) * 16 * ns
    state = types.SimpleNamespace(out=out)
    parts_of = lambda rows, split: tuple(part // 2 for part in (split, rows - split) if part)
    parts1, parts2 = parts_of(w2_rows, split1), parts_of(g2_rows, split2)
    half_of = lambda parts: tuple(part // 2 for part in parts)
    bf = lambda rows: shape_of((rows, units), BF16)

    def halves(level, pairs, parts):
        rows = sum(sum(part) for part in parts) // 2
        return call(
            functools.partial(add_halves, level, parts), (bf(rows),) * 2, pairs, free=range(len(pairs)),
            out_free=range(2),
        )

    def joined(level, pair, parts):
        return call(
            functools.partial(join_halves, level, parts), (bf(2 * pair[0].shape[0]),), pair, free=range(2),
            out_free=(0,),
        )[0]

    def add_two(pair):
        return call(add_plain, (bf(pair[0].shape[0]),), pair, free=range(2), out_free=(0,))[0]

    def over_seq(value, mask):
        return swap(value, mask, SEQ)

    def core_whole(keep, gots, rows):
        mine, theirs = call(
            add_core_far, (bf(rows),) * 2, (keep, *gots),
            scratch=[pltpu.VMEM((rows, units), BF16), pltpu.VMEM((rows, units), BF16), dma((2,))],
            free=range(1 + len(gots)), out_hbm=range(2),
        )
        return mine, swap(theirs, 2)

    def tied(value):
        value, TOKEN[0] = lax.optimization_barrier((value, TOKEN[0]))
        return value

    def attn_back():
        grad_v, grad_r, g_z, gmt, carries, small, skip_grad = call(
            functools.partial(attn_back_kernel, nc, nd),
            (
                shape_of((toks, nc * units), BF16), shape_of((toks, nc * units), BF16), shape_of((toks, zdim)),
                shape_of((width * SUBS, LANES)), shape_of((ns, nd * SUBS, LANES), BF16), shape_of((SUBS, zdim)),
                shape_of((SUBS, LANES)),
            ),
            (
                g_gated, r_pre, v_pre, context, attn, values_far, z_pre, mixed_pre, xt, z_all, pt, row(q_gain),
                row(k_gain), row(q_bias),
            ),
            scratch=[
                pltpu.VMEM((nd * SUBS, LANES), BF16), pltpu.VMEM((toks, nc * units), BF16),
                pltpu.VMEM((toks, nc * units), BF16), dma((ns,)), dma((2,)),
            ],
            free=(2, 5, 11, 12, 13), out_hbm=(0, 1, 4), limit=20,
        )
        vars(state).update(
            grad_v=grad_v, grad_r=grad_r, g_z=g_z, gmt=gmt, carries=carries, small=small, skip_grad=skip_grad,
        )

    def core_parted(keep, gots, rows, split):
        if split == rows:
            return core_whole(keep, gots, rows)
        mine, theirs, kept, send = call(
            functools.partial(add_core_split, split), (bf(split),) * 2 + (bf(rows - split),) * 2, (keep, *gots),
            scratch=[
                pltpu.VMEM((split, units), BF16), pltpu.VMEM((split, units), BF16),
                pltpu.VMEM((2, rows - split, units), BF16), dma((4,)),
            ],
            free=range(1 + len(gots)), out_hbm=range(4),
        )
        return mine, swap(theirs, 2), kept, over_seq(send, 1)

    def turned(sums):
        if len(sums) == 2:
            keep, send = halves(0, sums, ((sums[0].shape[0],),))
            return keep, over_seq(send, 1)
        near, far = sums[0].shape[0] // 2, sums[2].shape[0] // 2
        kept, send, own, theirs = call(
            turn_kernel, (bf(near), bf(near), bf(far), bf(far)), sums, free=range(4), out_free=range(4)
        )
        return kept, over_seq(send, 1), own, swap(theirs, 2)

    def move_carry():
        state.carries = exchange(tied(state.carries), SEQ)

    def core_first():
        state.sums1 = core_parted(keep1, (got1,), w2_rows, split1)

    def grads():
        keep2, *sends = call(
            functools.partial(grads_kernel, nc, dim, zrows),
            (shape_of((2, g2_rows, units), BF16),) + (bf(2 * g2_rows // pieces),) * pieces,
            (low, state.grad_v, state.grad_r, mixed_low, state.g_z),
            scratch=[
                pltpu.VMEM((dim, zdim), F32), pltpu.VMEM((toks, dim), BF16), pltpu.VMEM((toks, nc * units), BF16),
                pltpu.VMEM((toks, nc * units), BF16), pltpu.VMEM((toks, dim), BF16),
                pltpu.VMEM((4, g2_rows, units), BF16), dma((4,)), dma((16,)),
            ],
            hbm=range(4), out_hbm=range(1 + pieces), limit=24,
        )
        vars(state).update(keep2=keep2, gots2=[swap(value, 1) for value in sends])

    def scans():
        state.shared, state.sums = call(
            functools.partial(scans_kernel, nd, dim), (shape_of((toks, dim)), shape_of((3, nd * SUBS, LANES))),
            (state.grad_v, state.grad_r) + first + (pt, state_in, xt, state.gmt),
            scratch=[
                pltpu.VMEM((toks, dim), F32), pltpu.VMEM((3, nd * SUBS, LANES), F32), pltpu.VMEM((nd * SUBS, LANES), F32),
                pltpu.VMEM((4, 2 * dim, units), BF16), pltpu.VMEM((toks, nc * units), BF16),
                pltpu.VMEM((toks, nc * units), BF16), dma((7,)),
            ],
            hbm=(0, 1, 2, 3, 4, 5, 7), out_hbm=range(2), limit=24,
        )

    def core_second():
        state.sums2 = core_parted(state.keep2, state.gots2, g2_rows, split2)

    def x_first():
        state.sums1 = turned(state.sums1)

    def last():
        state.f = call(
            functools.partial(last_kernel, nc, nd, ns, span),
            (shape_of((2, f_rows, units), BF16),) + (bf(f_rows),) * 2,
            (
                state.carries, state.gmt, pt, state.shared, x, row(attn_gain), g_mid, token_ids, state.sums,
                state.small, state.skip_grad, ffn_grad,
            ),
            scratch=[
                pltpu.VMEM((width * SUBS, LANES), F32), pltpu.VMEM((vocab, dim), F32),
                pltpu.VMEM((3 * nd * SUBS, LANES), F32), pltpu.VMEM((nc, room, LANES), F32),
                pltpu.VMEM((toks, dim), F32), pltpu.VMEM((toks, dim), BF16), pltpu.VMEM((1, dim), F32),
                pltpu.VMEM((toks, dim), F32), pltpu.VMEM((rows, width), jnp.int32),
                pltpu.VMEM((3, nd * SUBS, LANES), F32), dma((6,)),
            ],
            hbm=range(3, 9), out_free=range(3), limit=16,
        )

    def core_last():
        keep, send, other = state.f
        mine, theirs = call(
            add_core, (bf(f_rows),) * 2, (keep, swap(send, 1), swap(other, 1)), free=range(3),
            out_free=range(2),
        )
        state.sumsf = (mine, swap(theirs, 2))

    def x_last():
        keep, send = halves(0, state.sumsf, ((f_rows,),))
        state.sumsf = (keep, over_seq(send, 1))

    def turn_second():
        state.sums2 = turned(state.sums2)

    def z_first():
        keep, send = halves(1, state.sums1, tuple((rows,) for rows in parts1))
        state.sums1 = (keep, over_seq(send, 2))

    def z_second():
        keep, send = halves(1, state.sums2, tuple((rows,) for rows in parts2))
        state.sums2 = (keep, over_seq(send, 2))

    def added(sums, mask):
        value = add_two(sums)
        return value, over_seq(value, mask)

    def zz_first():
        state.sums1 = added(state.sums1, 4)

    def zz_second():
        state.sums2 = added(state.sums2, 4)

    def zz_last():
        state.sumsf = added(state.sumsf, 4)

    def sum_first():
        state.sums1 = added(state.sums1, 2)

    def sum_second():
        state.sums2 = added(state.sums2, 2)

    def sum_last():
        state.sumsf = added(state.sumsf, 2)

    def join_first():
        whole = joined(1, state.sums1, half_of(parts1))
        state.sums1 = (whole, over_seq(whole, 1))

    def join_second():
        whole = joined(1, state.sums2, half_of(parts2))
        state.sums2 = (whole, over_seq(whole, 1))

    def z_last():
        keep, send = halves(1, state.sumsf, ((f_rows // 2,),))
        state.sumsf = (keep, over_seq(send, 2))

    def join_last():
        whole = joined(1, state.sumsf, (f_rows // 4,))
        state.sumsf = (whole, over_seq(whole, 1))

    def move_out():
        state.out = tied(state.out)
        vars(state).update(out_far=swap(state.out, 2), out_near=swap(state.out, 1))

    def move_both():
        state.out_far = tied(state.out_far)
        state.out_both = swap(state.out_far, 1)

    def output():
        state.output = call(
            output_kernel, (shape_of((rows, width, dim), BF16),),
            (state.out, state.out_near, state.out_far, state.out_both), free=range(4),
            out_free=(0,), limit=8,
        )[0]

    def plain_sums():
        state.sums1, state.sums2, state.sumsf = [
            (seq_sum(add_two(sums), ns),) * 2 for sums in (state.sums1, state.sums2, state.sumsf)
        ]
        state.f_own = state.sumsf[0]

    def give_first():
        state.first = call(
            functools.partial(unpack_first, dim, urows, parts1 if fast else None),
            (shape_of(up_proj.shape), shape_of(o_proj.shape), shape_of(down_proj.shape)), state.sums1, free=range(2), out_free=range(3), scratch=[pltpu.VMEM((w2_rows, units), BF16)],
        )

    def give_second():
        state.second = call(
            functools.partial(unpack_second, dim, zrows, parts2 if fast else None),
            (shape_of(v_proj.shape), shape_of(r_proj.shape), shape_of(z_proj.shape)), state.sums2, free=range(2), out_free=range(3), scratch=[pltpu.VMEM((g2_rows, units), BF16)],
        )

    def collect():
        (state.f_own,) = call(
            functools.partial(join_part, 0), (bf(f_rows),), state.sumsf, free=range(2),
            out_free=(0,),
        )

    def finish():
        own = state.f_own
        far = swap(own, 2)
        state.finish = call(
            functools.partial(finish_kernel, nc, nd),
            (
                shape_of((vocab, dim)), shape_of((1, dim)), shape_of((nd, LANES)), shape_of((nd, LANES)),
                shape_of((nd, LANES)), shape_of((1, LANES)), shape_of((1, dim)), shape_of((1, zdim)),
                shape_of((1, zdim)), shape_of((1, zdim)),
            ),
            (own, swap(own, 1), far, swap(far, 1)), free=range(4), out_free=range(10),
            scratch=[pltpu.VMEM((nc, room, LANES), F32)], limit=8,
        )

    if fast:
        steps = (
            attn_back, core_first, grads, move_carry, scans, core_second, x_first, last, core_last, z_first, turn_second, zz_first, z_second, move_out, x_last, z_last, zz_second, sum_first, zz_last, join_first, sum_second, sum_last, move_both, join_second, join_last, output, give_first, collect, give_second, finish,
        )
    else:
        steps = (
            attn_back, move_carry, core_first, grads, scans, core_second, last, core_last, move_out, move_both, output,
            plain_sums, give_first, give_second, finish,
        )
    for step in steps:
        step()
    up_grad, o_grad, down_grad = state.first
    v_grad, r_grad, z_grad = state.second
    embed_grad, ag, gi, gk, go, gs, fg, qg, kg, qb = state.finish
    flat = lambda value: value.reshape(-1)
    return (
        state.output, embed_grad, flat(ag), gi.T, gk.T, go.T, flat(gs), z_grad, flat(qg), flat(kg), flat(qb), v_grad, r_grad,
        o_grad, flat(fg), up_grad, down_grad,
    )


def solution(mesh):
    placed = (
        P(None, SEQ), P(), P(), P(), P(CHAN, None), P(CHAN, None), P(CHAN, None), P(CHAN), P(CHAN, None),
        P(), P(), P(), P(None, CHAN), P(None, CHAN), P(CHAN, None), P(), P(None, CHAN), P(CHAN, None),
        P(None, SEQ, None),
    )
    return jax.shard_map(
        body,
        mesh=mesh,
        in_specs=placed,
        out_specs=(
            P(None, SEQ, None), P(), P(), P(CHAN, None), P(CHAN, None), P(CHAN, None), P(CHAN),
            P(CHAN, None), P(), P(), P(), P(None, CHAN), P(None, CHAN), P(CHAN, None), P(), P(None, CHAN),
            P(CHAN, None),
        ),
        check_vma=False,
    )
```
